32 devices in a mesh: tile: 8 (over z, x), chan: 4 (over y, core).
Axes of the slice: x: 2, y: 2, z: 4, core: 2. Of those that a mesh axis runs over, the one named last changes fastest.
Arguments:
- inputs: bfloat16 [8, 256, 1024], P('tile', 'chan'), may hold values from -6 to 6
- grad_out: bfloat16 [8, 256, 1024], P('tile', 'chan'), may hold values from -6 to 6
- kernel: bfloat16 [25, 256], P(None, 'chan'), may hold values from -1.25 to 1.25
- w_in: bfloat16 [256, 1024], replicated, may hold values from -0.375 to 0.375
- w_out: bfloat16 [1024, 256], replicated, may hold values from -0.1875 to 0.1875
- neighbours: int32 [8, 8], replicated, may hold values from 0 to 7, as said below
- rotations: int32 [8, 8], replicated, may hold values from 0 to 3, as said below
Outputs:
- outputs: bfloat16 [8, 256, 1024], P('tile', 'chan')
- grad_in: bfloat16 [8, 256, 1024], P('tile', 'chan')
- grad_w_in: float32 [256, 1024], replicated
- grad_w_out: float32 [1024, 256], replicated
- grad_kernel: float32 [25, 256], replicated
The draws below stay inside these ranges and needn't reach their ends.
Inputs may be any that keep to these rules, and one draw needn't show every extreme that they name: neighbours[t, d] is the tile that borders tile t in direction d; for every tile t and direction d exactly one tile s has neighbours[s, d] = t, namely s = neighbours[t, 7 - d]. rotations[t, d] is the number of quarter turns that brings the bordering tile into tile t's frame.
All inputs are finite; a program needn't handle non-finite values.
Results may differ from the reference program's by a relative error of at most 0.006.
Values may be sent and summed in bfloat16 or wider, within the bound.
No kernel may reach another device: no remote copies, remote signals or barrier semaphores. Data moves between devices by JAX's collectives and lax.ppermute only.
A program may use at most 64 MiB of HBM per device.

```python
import jax
import jax.numpy as jnp
from jax import lax

C = 256
HID = 1024
KSIZE = 5
SIDE = 32
PIX = 1024
TILES = 8


offsets = ((-1, -1), (-1, 0), (-1, 1), (0, -1), (0, 1), (1, -1), (1, 0), (1, 1))


def tile_layout(key):
    grid_cols = 4
    grid_rows = TILES // grid_cols
    placement = jax.random.permutation(jax.random.fold_in(key, 11), TILES).astype(jnp.int32)
    tile_at = jnp.zeros((TILES,), jnp.int32).at[placement].set(jnp.arange(TILES, dtype=jnp.int32))
    cell_row = placement // grid_cols
    cell_col = placement % grid_cols
    columns = []
    for step_row, step_col in offsets:
        grid_cell = (cell_row + step_row) % grid_rows * grid_cols + (cell_col + step_col) % grid_cols
        columns.append(tile_at[grid_cell])
    neighbour_table = jnp.stack(columns, axis=1).astype(jnp.int32)
    shuffled = jax.random.permutation(jax.random.fold_in(key, 23), TILES * 8).astype(jnp.int32)
    turn_codes = (shuffled % 4).reshape(TILES, 8).astype(jnp.int32)
    return (neighbour_table, turn_codes)


def draw_neighbours(key, part):
    return tile_layout(key)[0]


def draw_rotations(key, part):
    return tile_layout(key)[1]


def shard_levels(own_key, extent, split, least, largest):
    loudness, own = 1.0, jax.random.fold_in(own_key, 6)
    for position, shards_of in split:
        heights = jnp.exp(jax.random.uniform(jax.random.fold_in(own, position), (shards_of,), jnp.float32, least / len(split), largest / len(split)))
        loudness = loudness * jnp.repeat(heights, extent[position] // shards_of).reshape([-1 if axis == position else 1 for axis in range(len(extent))])
    return loudness


def noise(rng, extent, deviation, most, split=(), kind=jnp.bfloat16):
    values = jax.random.normal(rng, extent, jnp.float32) * deviation
    if len(split) > 0:
        values = shard_levels(rng, extent, split, -0.22, 0.18) * values
    return jnp.clip(values, min=-most, max=most).astype(kind)


def setup_inputs(seed: int = 0) -> dict:
    key_list = jax.random.split(jax.random.key(seed), 8)
    return {
        "inputs": noise(key_list[0], (TILES, C, PIX), 1.0, 6.0, ((0, 8), (1, 4))),
        "grad_out": noise(key_list[1], (TILES, C, PIX), 1.0, 6.0, ((0, 8), (1, 4))),
        "kernel": noise(key_list[2], (KSIZE * KSIZE, C), (KSIZE * KSIZE) ** -0.5, 1.25, ((1, 4),)),
        "w_in": noise(key_list[3], (C, HID), C ** -0.5, 0.375),
        "w_out": noise(key_list[4], (HID, C), HID ** -0.5, 0.1875),
        "neighbours": draw_neighbours(jax.random.fold_in(key_list[7], 71), 0),
        "rotations": draw_rotations(jax.random.fold_in(key_list[7], 71), 0),
    }


offsets = ((-1, -1), (-1, 0), (-1, 1), (0, -1), (0, 1), (1, -1), (1, 0), (1, 1))


def source_span(step_dir, edge_len, halo_width):
    if step_dir < 0:
        return (edge_len - halo_width, edge_len)
    if step_dir > 0:
        return (0, halo_width)
    return (0, edge_len)


def target_span(step_dir, edge_len, halo_width):
    if step_dir < 0:
        return (0, halo_width)
    if step_dir > 0:
        return (halo_width + edge_len, edge_len + 2 * halo_width)
    return (halo_width, halo_width + edge_len)


def rotate_tile(images, quarter):
    turn_code = jnp.reshape(quarter, quarter.shape + (1,) * (images.ndim - quarter.ndim))
    result = images
    for amount in range(1, 4):
        result = jnp.where(turn_code == amount, jnp.rot90(images, amount, axes=(-2, -1)), result)
    return result


def depthwise(padded, kernel, edge_len):
    result = jnp.zeros(padded.shape[:-2] + (edge_len, edge_len), jnp.float32)
    for tap_row in range(KSIZE):
        for tap_col in range(KSIZE):
            weight = kernel[tap_row * KSIZE + tap_col].astype(jnp.float32)[:, None, None]
            result = result + weight * padded[..., tap_row:tap_row + edge_len, tap_col:tap_col + edge_len].astype(jnp.float32)
    return result


def spread(grads, kernel, row_span, col_span):
    margin = KSIZE - 1
    widths = [(0, 0)] * (grads.ndim - 2) + [(margin, margin), (margin, margin)]
    widened = jnp.pad(grads, widths)
    result = jnp.zeros(grads.shape[:-2] + (row_span[1] - row_span[0], col_span[1] - col_span[0]), jnp.float32)
    for tap_row in range(KSIZE):
        for tap_col in range(KSIZE):
            weight = kernel[tap_row * KSIZE + tap_col].astype(jnp.float32)[:, None, None]
            result = result + weight * widened[..., row_span[0] + margin - tap_row:row_span[1] + margin - tap_row,
                                               col_span[0] + margin - tap_col:col_span[1] + margin - tap_col]
    return result


def kernel_grads(grad_tiles, padded, edge_len, sum_axes):
    columns = []
    for tap_row in range(KSIZE):
        for tap_col in range(KSIZE):
            window = padded[..., tap_row:tap_row + edge_len, tap_col:tap_col + edge_len].astype(jnp.float32)
            columns.append(jnp.sum(grad_tiles * window, axis=sum_axes))
    return jnp.stack(columns, axis=0)


def gelu_slope(values):
    cumul = 0.5 * (1.0 + lax.erf(values * 0.7071067811865476))
    return cumul + values * jnp.exp(-0.5 * values * values) * 0.3989422804014327


def reference(inputs, grad_out, kernel, w_in, w_out, neighbours, rotations):
    halo_width = KSIZE // 2
    ext_len = SIDE + 2 * halo_width
    images = inputs.reshape(TILES, C, SIDE, SIDE)
    padded = jnp.zeros((TILES, C, ext_len, ext_len), jnp.bfloat16)
    padded = padded.at[:, :, halo_width:halo_width + SIDE, halo_width:halo_width + SIDE].set(images)
    for direction, (step_row, step_col) in enumerate(offsets):
        turned = rotate_tile(images[neighbours[:, direction]], rotations[:, direction])
        src_rows = source_span(step_row, SIDE, halo_width)
        src_cols = source_span(step_col, SIDE, halo_width)
        dst_rows = target_span(step_row, SIDE, halo_width)
        dst_cols = target_span(step_col, SIDE, halo_width)
        padded = padded.at[:, :, dst_rows[0]:dst_rows[1], dst_cols[0]:dst_cols[1]].set(
            turned[:, :, src_rows[0]:src_rows[1], src_cols[0]:src_cols[1]])
    hidden = depthwise(padded, kernel, SIDE).astype(jnp.bfloat16).reshape(TILES, C, PIX)

    def per_tile(running, tile_pair):
        features, cotangent = tile_pair
        pre_act = lax.dot_general(w_in, features, (((0,), (0,)), ((), ())), preferred_element_type=jnp.float32)
        activated = jax.nn.gelu(pre_act, approximate=False).astype(jnp.bfloat16)
        branch_out = lax.dot_general(w_out, activated, (((0,), (0,)), ((), ())),
                                     preferred_element_type=jnp.float32).astype(jnp.bfloat16)
        grad_act = jnp.dot(w_out, cotangent, preferred_element_type=jnp.float32)
        grad_pre = (grad_act * gelu_slope(pre_act)).astype(jnp.bfloat16)
        grad_feat = jnp.dot(w_in, grad_pre, preferred_element_type=jnp.float32).astype(jnp.bfloat16)
        sum_in = running[0] + lax.dot_general(features, grad_pre, (((1,), (1,)), ((), ())),
                                              preferred_element_type=jnp.float32)
        sum_out = running[1] + lax.dot_general(activated, cotangent, (((1,), (1,)), ((), ())),
                                               preferred_element_type=jnp.float32)
        return (sum_in, sum_out), (branch_out, grad_feat)

    start_sums = (jnp.zeros((C, HID), jnp.float32), jnp.zeros((HID, C), jnp.float32))
    (sum_in, sum_out), (branch_out, grad_hidden) = lax.scan(per_tile, start_sums, (hidden, grad_out))
    outputs = (inputs.astype(jnp.float32) + branch_out.astype(jnp.float32)).astype(jnp.bfloat16)
    grad_tiles = grad_hidden.reshape(TILES, C, SIDE, SIDE).astype(jnp.float32)
    grad_padded = spread(grad_tiles, kernel, (0, ext_len), (0, ext_len))
    kernel_sum = kernel_grads(grad_tiles, padded, SIDE, (0, 2, 3))
    accum = grad_out.reshape(TILES, C, SIDE, SIDE).astype(jnp.float32)
    accum = accum + grad_padded[:, :, halo_width:halo_width + SIDE, halo_width:halo_width + SIDE]
    for direction, (step_row, step_col) in enumerate(offsets):
        src_rows = source_span(step_row, SIDE, halo_width)
        src_cols = source_span(step_col, SIDE, halo_width)
        dst_rows = target_span(step_row, SIDE, halo_width)
        dst_cols = target_span(step_col, SIDE, halo_width)
        placed = jnp.zeros((TILES, C, SIDE, SIDE), jnp.float32).at[:, :, src_rows[0]:src_rows[1], src_cols[0]:src_cols[1]].set(
            grad_padded[:, :, dst_rows[0]:dst_rows[1], dst_cols[0]:dst_cols[1]])
        back = rotate_tile(placed, (4 - rotations[:, direction]) % 4)
        accum = accum.at[neighbours[:, direction]].add(back)
    grad_in = accum.astype(jnp.bfloat16).reshape(TILES, C, PIX)
    grad_scale = (TILES * PIX) ** -0.5
    return (outputs, grad_in, sum_in * grad_scale, sum_out * grad_scale, kernel_sum * grad_scale)
```

```python
import functools
import math

import jax
import jax.numpy as jnp
from jax import lax
from jax.experimental import pallas as pl
from jax.experimental.pallas import tpu as pltpu
from jax.sharding import PartitionSpec as P

KSIZE = 5
HALO = KSIZE // 2
LANES = 128
SIDES = (0, 2, 3, 4, 5, 7)
BF16 = jnp.bfloat16
F32 = jnp.float32

VMEM = pl.BlockSpec(memory_space=pltpu.VMEM)
SMEM = pl.BlockSpec(memory_space=pltpu.SMEM)


def call(kernel, outs, scratch=(), limit=32):
    def run(*args):
        specs = [SMEM if a.ndim == 1 and a.dtype == jnp.int32 else VMEM for a in args]
        return pl.pallas_call(
            kernel,
            out_shape=[jax.ShapeDtypeStruct(s, d) for s, d in outs],
            in_specs=specs,
            out_specs=[VMEM] * len(outs),
            scratch_shapes=list(scratch),
            compiler_params=pltpu.CompilerParams(vmem_limit_bytes=limit * 1024 * 1024),
        )(*args)

    return run


def dot(a, b):
    return lax.dot_general(a, b, (((1,), (0,)), ((), ())), preferred_element_type=F32)


def dot_nt(a, b):
    return lax.dot_general(a, b, (((1,), (1,)), ((), ())), preferred_element_type=F32)


def one_hot(index, rows):
    row = lax.broadcasted_iota(jnp.int32, (rows, index.shape[1]), 0)
    return jnp.where(row == index, 1.0, 0.0).astype(BF16)


def rim_pixels(edge):
    band_len = HALO * edge
    lane = lax.broadcasted_iota(jnp.int32, (1, 4 * band_len), 1)
    band, at = lane // band_len, lane % band_len
    side = (at // HALO) * edge + at % HALO
    pixel = jnp.where(band == 0, at, (edge - HALO) * edge + at)
    return jnp.where(band == 2, side, jnp.where(band == 3, side + edge - HALO, pixel))


def rim_lane(row, col, edge):
    band_len = HALO * edge
    side = jnp.where(col < HALO, 2 * band_len + row * HALO + col,
                     3 * band_len + row * HALO + col - (edge - HALO))
    side = jnp.where(row >= edge - HALO, band_len + (row - (edge - HALO)) * edge + col, side)
    return jnp.where(row < HALO, row * edge + col, side)


def turned_lane(row, col, quarter, edge):
    last = edge - 1
    from_row = jnp.where(quarter == 1, col, jnp.where(
        quarter == 2, last - row, jnp.where(quarter == 3, last - col, row)))
    from_col = jnp.where(quarter == 1, last - row, jnp.where(
        quarter == 2, last - col, jnp.where(quarter == 3, row, col)))
    return rim_lane(from_row, from_col, edge)


def row_halo_maps(top_turn, bottom_turn, edge):
    rim = 4 * HALO * edge
    lane = lax.broadcasted_iota(jnp.int32, (1, LANES), 1)
    up = lane - (LANES - HALO * edge)
    top = turned_lane(edge - HALO + up // edge, up % edge, top_turn, edge)
    low = turned_lane(lane // edge, lane % edge, bottom_turn, edge)
    top = jnp.where(up >= 0, top, -1)
    low = jnp.where(lane < HALO * edge, low, -1)
    return one_hot(top, rim), one_hot(low, rim)


def side_map(turns, edge):
    rim = 4 * HALO * edge
    lane = lax.broadcasted_iota(jnp.int32, (1, 2 * LANES), 1)
    row, k = lane // (2 * HALO), lane % (2 * HALO)
    above, below, right = row < HALO, row >= HALO + edge, k >= HALO
    b_row = jnp.where(above, edge - HALO + row, jnp.where(below, row - HALO - edge, row - HALO))
    b_col = jnp.where(right, k - HALO, edge - HALO + k)
    slot = jnp.where(above, 0, jnp.where(below, 4, 2)) + right.astype(jnp.int32)
    quarter = jnp.zeros_like(slot)
    for position in range(len(SIDES)):
        quarter = jnp.where(slot == position, turns[position], quarter)
    index = slot * rim + turned_lane(b_row, b_col, quarter, edge)
    index = jnp.where(row < edge + 2 * HALO, index, -1)
    return one_hot(index, len(SIDES) * rim)


def spread_map(edge, wide):
    lane = lax.broadcasted_iota(jnp.int32, (1, wide), 1)
    row = lane // edge - (LANES // edge - HALO)
    col = lane % edge
    right_row, left_row = row - 1, row + 1
    rows = edge + 2 * HALO
    right = jnp.where((right_row >= 0) & (right_row < rows), right_row * 2 * HALO + HALO + col, -1)
    left = jnp.where((left_row >= 0) & (left_row < rows),
                     left_row * 2 * HALO + col - (edge - HALO), -1)
    index = jnp.where(col < HALO, right, jnp.where(col >= edge - HALO, left, -1))
    return one_hot(index, 2 * LANES)


def side_mask(shift, shape, edge):
    col = lax.broadcasted_iota(jnp.int32, shape, 1) % edge
    return col < shift if shift > 0 else col >= edge + shift


def roll(values, shift):
    size = values.shape[1]
    return values if shift % size == 0 else pltpu.roll(values, shift % size, axis=1)


def pack_kernel(edge, x_ref, rim_ref):
    pixels = x_ref.shape[1]
    pick = one_hot(rim_pixels(edge), pixels)
    rim = dot(x_ref[...], pick).astype(BF16)
    rim_ref[...] = jnp.broadcast_to(rim[None], rim_ref.shape)


def conv_kernel(edge, place_ref, nb_ref, rot_ref, x_ref, rims_ref, taps_ref,
                hidden_ref, padded_ref, side_ref, gathered):
    channels, pixels = x_ref.shape
    wide = pixels + 2 * LANES
    rim = rims_ref.shape[2]
    first = place_ref[0] * 8
    nb = [nb_ref[first + d] for d in range(8)]
    rot = [rot_ref[first + d] for d in range(8)]
    top, low = row_halo_maps(rot[1], rot[6], edge)
    padded_ref[:, :LANES] = dot(rims_ref[nb[1]], top).astype(BF16)
    padded_ref[:, LANES + pixels:] = dot(rims_ref[nb[6]], low).astype(BF16)
    padded_ref[:, LANES:LANES + pixels] = x_ref[...]
    for position, d in enumerate(SIDES):
        gathered[:, position * rim:(position + 1) * rim] = rims_ref[nb[d]]
    packed = dot(gathered[...], side_map([rot[d] for d in SIDES], edge)).astype(BF16)
    side_ref[...] = dot(packed, spread_map(edge, wide)).astype(BF16)

    def block(i, carry):
        at = pl.multiple_of(i * 16, 16)
        xs = padded_ref[pl.ds(at, 16), :].astype(F32)
        hs = side_ref[pl.ds(at, 16), :].astype(F32)
        halves = []
        for half in (0, 8):
            x, h = xs[half:half + 8], hs[half:half + 8]
            sums = [None] * KSIZE
            for b in range(KSIZE):
                shift = b - HALO
                moved = x
                if shift:
                    moved = roll(jnp.where(side_mask(shift, x.shape, edge), h, x), -shift)
                for a in range(KSIZE):
                    tap = taps_ref[a * KSIZE + b, pl.ds(at + half, 8), :]
                    term = jnp.tile(tap, (1, wide // LANES)) * moved
                    sums[a] = term if sums[a] is None else sums[a] + term
            total = None
            for a in range(KSIZE):
                part = roll(sums[a], -(a - HALO) * edge)[:, LANES:LANES + pixels]
                total = part if total is None else total + part
            halves.append(total)
        hidden_ref[pl.ds(at, 16), :] = jnp.concatenate(halves, axis=0).astype(BF16)
        return carry

    lax.fori_loop(0, channels // 16, block, 0)


def gelu_parts(pre, grad_act):
    cumul = 0.5 * (1.0 + lax.erf(pre * 0.7071067811865476))
    slope = cumul + pre * jnp.exp(-0.5 * pre * pre) * 0.3989422804014327
    return (pre * cumul).astype(BF16), (grad_act * slope).astype(BF16)


def hidden_block(w_in_t, w_out, feats_ref, cot_ref, pre, slope, act, gpre):
    pre[...] = dot(w_in_t, feats_ref[...])
    slope[...] = dot(w_out, cot_ref[...])

    def rows(i, carry):
        at = pl.multiple_of(i * 16, 16)
        act[pl.ds(at, 16), :], gpre[pl.ds(at, 16), :] = gelu_parts(
            pre[pl.ds(at, 16), :], slope[pl.ds(at, 16), :])
        return carry

    lax.fori_loop(0, pre.shape[0] // 16, rows, 0)


def weight_kernel(place_ref, feats_ref, cot_ref, w_in_t_ref, w_out_ref, out_ref,
                  pre, slope, act, gpre):
    units = pre.shape[0]
    full = feats_ref.shape[0]
    at = pl.multiple_of(place_ref[1] * units, units)
    hidden_block(w_in_t_ref[pl.ds(at, units), :], w_out_ref[pl.ds(at, units), :],
                 feats_ref, cot_ref, pre, slope, act, gpre)
    part_in = dot_nt(feats_ref[...], gpre[...]).astype(BF16)
    part_out = dot_nt(act[...], cot_ref[...]).astype(BF16)
    used = 0
    for column in range(0, units, LANES):
        out_ref[used:used + full, :] = part_in[:, column:column + LANES]
        used += full
    for column in range(0, full, LANES):
        out_ref[used:used + units, :] = part_out[:, column:column + LANES]
        used += units
    if used < out_ref.shape[0]:
        out_ref[used:, :] = jnp.zeros((out_ref.shape[0] - used, LANES), BF16)


def point_kernel(feats_ref, cot_ref, w_in_t_ref, w_out_ref, w_in_own_ref, w_out_own_ref, x_ref,
                 out_ref, grad_ref, pre, slope, act, gpre):
    units = pre.shape[0]
    hidden = w_out_ref.shape[0]
    branch = grad = None
    for at in range(0, hidden, units):
        hidden_block(w_in_t_ref[at:at + units, :], w_out_ref[at:at + units, :],
                     feats_ref, cot_ref, pre, slope, act, gpre)
        more = dot(w_out_own_ref[:, at:at + units], act[...])
        branch = more if branch is None else branch + more
        more = dot(w_in_own_ref[:, at:at + units], gpre[...])
        grad = more if grad is None else grad + more
    out_ref[...] = (x_ref[...].astype(F32) + branch.astype(BF16).astype(F32)).astype(BF16)
    grad_ref[...] = grad.astype(BF16)


def back_kernel(edge, place_ref, nb_ref, rot_ref, grad_ref, cot_ref, padded_ref, side_ref, taps_ref,
                accum_ref, send_ref, d_row, d_side, tap_grads, gathered):
    channels, pixels = grad_ref.shape
    wide = pixels + 2 * LANES
    tiles = send_ref.shape[0]
    rim = gathered.shape[2]
    lane = lax.broadcasted_iota(jnp.int32, (8, LANES), 1)

    def block(i, carry):
        at = pl.multiple_of(i * 16, 16)
        gs = grad_ref[pl.ds(at, 16), :].astype(F32)
        xs = padded_ref[pl.ds(at, 16), :].astype(F32)
        hs = side_ref[pl.ds(at, 16), :].astype(F32)
        edges = jnp.zeros((8, LANES), F32)
        rows, sides = [], []
        for half in (0, 8):
            x, h = xs[half:half + 8], hs[half:half + 8]
            g = jnp.concatenate([edges, gs[half:half + 8], edges], axis=1)
            turned = [roll(g, (a - HALO) * edge) for a in range(KSIZE)]
            d_x = d_h = None
            sums = jnp.zeros((8, LANES), F32)
            for b in range(KSIZE):
                shift = b - HALO
                moved = x
                if shift:
                    mask = side_mask(shift, x.shape, edge)
                    moved = roll(jnp.where(mask, h, x), -shift)
                back = None
                for a in range(KSIZE):
                    tap = taps_ref[a * KSIZE + b, pl.ds(at + half, 8), :]
                    term = jnp.tile(tap, (1, wide // LANES)) * turned[a]
                    back = term if back is None else back + term
                    product = turned[a] * moved
                    line = product[:, :LANES]
                    for column in range(LANES, wide, LANES):
                        line = line + product[:, column:column + LANES]
                    sums = jnp.where(lane == a * KSIZE + b,
                                     jnp.sum(line, axis=1, keepdims=True), sums)
                back = roll(back, shift)
                if shift:
                    inside = jnp.where(mask, 0.0, back)
                    outside = jnp.where(mask, back, 0.0)
                    d_h = outside if d_h is None else d_h + outside
                    d_x = inside if d_x is None else d_x + inside
                else:
                    d_x = back if d_x is None else d_x + back
            tap_grads[pl.ds(at + half, 8), :] = sums
            rows.append(d_x)
            sides.append(d_h)
        d_x = jnp.concatenate(rows, axis=0)
        accum_ref[pl.ds(at, 16), :] = (
            d_x[:, LANES:LANES + pixels] + cot_ref[pl.ds(at, 16), :].astype(F32))
        d_row[pl.ds(at, 16), :LANES] = d_x[:, :LANES].astype(BF16)
        d_row[pl.ds(at, 16), LANES:] = d_x[:, LANES + pixels:].astype(BF16)
        d_side[pl.ds(at, 16), :] = jnp.concatenate(sides, axis=0).astype(BF16)
        return carry

    lax.fori_loop(0, channels // 16, block, 0)

    first = place_ref[0] * 8
    nb = [nb_ref[first + d] for d in range(8)]
    rot = [rot_ref[first + d] for d in range(8)]
    gathered[...] = jnp.zeros(gathered.shape, F32)
    top, low = row_halo_maps(rot[1], rot[6], edge)
    gathered[nb[1]] += dot_nt(d_row[:, :LANES], top)
    gathered[nb[6]] += dot_nt(d_row[:, LANES:], low)
    packed = dot_nt(d_side[...], spread_map(edge, wide)).astype(BF16)
    picks = side_map([rot[d] for d in SIDES], edge)
    for position, d in enumerate(SIDES):
        gathered[nb[d]] += dot_nt(packed, picks[position * rim:(position + 1) * rim, :])
    sums = split_parts(tap_grads[...])

    def store(t, carry):
        send_ref[t, :, :rim] = gathered[t].astype(BF16)
        send_ref[t, :, rim:] = sums
        return carry

    lax.fori_loop(0, tiles, store, 0)


def split_parts(values):
    high = values.astype(BF16)
    left = (values - high.astype(F32)).astype(BF16).astype(F32)
    lane = lax.broadcasted_iota(jnp.int32, values.shape, 1)
    return jnp.where(lane < LANES // 2, high.astype(F32), roll(left, LANES // 2)).astype(BF16)


def join_parts(values):
    return values + roll(values, LANES // 2)


def border_kernel(edge, recv_ref, accum_ref, grad_ref, tap_ref):
    tiles, channels, _ = recv_ref.shape
    pixels = accum_ref.shape[1]
    rim = 4 * HALO * edge
    total = lax.fori_loop(
        0, tiles, lambda t, so_far: so_far + recv_ref[t].astype(F32),
        jnp.zeros(recv_ref.shape[1:], F32))
    rims = total[:, :rim]
    high = rims.astype(BF16)
    low = (rims - high.astype(F32)).astype(BF16)
    pick = one_hot(rim_pixels(edge), pixels)
    grad_ref[...] = (accum_ref[...] + dot_nt(high, pick) + dot_nt(low, pick)).astype(BF16)
    tap_ref[...] = split_parts(join_parts(total[:, rim:]))


def sum_kernel(recv_ref, out_ref):
    total = lax.fori_loop(
        0, recv_ref.shape[0], lambda t, so_far: so_far + recv_ref[t].astype(F32),
        jnp.zeros(recv_ref.shape[1:], F32))
    out_ref[...] = jnp.broadcast_to(total.astype(BF16)[None], out_ref.shape)


def final_kernel(groups, scale, place_ref, *refs):
    pieces, taps = refs[:groups], refs[groups:2 * groups]
    g_in_ref, g_out_ref, g_tap_ref, all_taps = refs[2 * groups:]
    full, hidden = g_in_ref.shape
    units = hidden // groups
    channels = taps[0].shape[0]
    for k in range(groups):
        owner = place_ref[1] ^ k
        start = pl.multiple_of(owner * units, units)
        used = 0
        for column in range(0, units, LANES):
            g_in_ref[:, pl.ds(pl.multiple_of(start + column, LANES), LANES)] = (
                pieces[k][used:used + full, :].astype(F32) * scale)
            used += full
        for column in range(0, full, LANES):
            g_out_ref[pl.ds(start, units), column:column + LANES] = (
                pieces[k][used:used + units, :].astype(F32) * scale)
            used += units
        all_taps[pl.ds(pl.multiple_of(owner * channels, channels), channels), :] = (
            join_parts(taps[k][...].astype(F32)) * scale)
    g_tap_ref[...] = all_taps[...].T[:KSIZE * KSIZE, :]


def gather_pieces(own, groups):
    pieces = {0: own}
    bit = groups // 2
    while bit:
        swap = [(i, i ^ bit) for i in range(groups)]
        for k in list(pieces):
            pieces[k ^ bit] = lax.ppermute(pieces[k], "chan", swap)
        bit //= 2
    return [pieces[k] for k in range(groups)]


def swap_rows(values):
    return lax.all_to_all(values, "tile", 0, 0, tiled=True)


def body(inputs, grad_out, kernel, w_in, w_out, neighbours, rotations):
    channels, pixels = inputs.shape[1:]
    edge = math.isqrt(pixels)
    full, hidden = w_in.shape
    groups = lax.axis_size("chan")
    tiles = lax.axis_size("tile")
    wide = pixels + 2 * LANES
    rim = 4 * HALO * edge
    units = hidden // groups
    scale = (tiles * pixels) ** -0.5
    place = jnp.stack([lax.axis_index("tile"), lax.axis_index("chan")]).astype(jnp.int32)
    nb, rot = neighbours.reshape(-1), rotations.reshape(-1)
    x, cot = inputs[0], grad_out[0]

    [rims] = call(functools.partial(pack_kernel, edge), [((tiles, channels, rim), BF16)])(x)
    rims = swap_rows(rims)
    cots = lax.all_gather(cot, "chan", axis=0, tiled=True)
    taps = jnp.broadcast_to(kernel.astype(F32)[:, :, None], (KSIZE * KSIZE, channels, LANES))
    w_in_t = w_in.T
    start = place[1] * channels
    w_in_own = lax.dynamic_slice_in_dim(w_in, start, channels, 0)
    w_out_own = lax.dynamic_slice_in_dim(w_out, start, channels, 1).T

    hid, padded, side = call(
        functools.partial(conv_kernel, edge),
        [((channels, pixels), BF16), ((channels, wide), BF16), ((channels, wide), BF16)],
        [pltpu.VMEM((channels, len(SIDES) * rim), BF16)],
    )(place, nb, rot, x, rims, taps)
    feats = lax.all_gather(hid, "chan", axis=0, tiled=True)

    used = 2 * full * units // LANES
    share = -(-used // (16 * tiles)) * 16
    scratch = [pltpu.VMEM((units, pixels), F32), pltpu.VMEM((units, pixels), F32),
               pltpu.VMEM((units, pixels), BF16), pltpu.VMEM((units, pixels), BF16)]
    [part] = call(weight_kernel, [((tiles * share, LANES), BF16)], scratch)(
        place, feats, cots, w_in_t, w_out)
    part = swap_rows(part.reshape(tiles, share, LANES))

    outputs, grad_hid = call(
        point_kernel, [((channels, pixels), BF16)] * 2, scratch
    )(feats, cots, w_in_t, w_out, w_in_own, w_out_own, x)

    [mine] = call(sum_kernel, [((tiles, share, LANES), BF16)])(part)
    weights = swap_rows(mine).reshape(tiles * share, LANES)

    accum, border = call(
        functools.partial(back_kernel, edge),
        [((channels, pixels), F32), ((tiles, channels, rim + LANES), BF16)],
        [pltpu.VMEM((channels, 2 * LANES), BF16), pltpu.VMEM((channels, wide), BF16),
         pltpu.VMEM((channels, LANES), F32), pltpu.VMEM((tiles, channels, rim), F32)],
    )(place, nb, rot, grad_hid, cot, padded, side, taps)
    border = swap_rows(border)
    pieces = gather_pieces(weights, groups)
    grad_in, tap_part = call(
        functools.partial(border_kernel, edge),
        [((channels, pixels), BF16), ((channels, LANES), BF16)],
    )(border, accum)
    tap_pieces = gather_pieces(tap_part, groups)
    grads = call(
        functools.partial(final_kernel, groups, scale),
        [((full, hidden), F32), ((hidden, full), F32), ((KSIZE * KSIZE, full), F32)],
        [pltpu.VMEM((full, LANES), F32)],
    )(place, *pieces, *tap_pieces)
    return (outputs[None], grad_in[None], *grads)


def solution(mesh):
    return jax.shard_map(
        body,
        mesh=mesh,
        in_specs=(
            P("tile", "chan", None),
            P("tile", "chan", None),
            P(None, "chan"),
            P(),
            P(),
            P(),
            P(),
        ),
        out_specs=(P("tile", "chan", None), P("tile", "chan", None), P(), P(), P()),
        check_vma=False,
    )
```

```python
import functools
import math

import jax
import jax.numpy as jnp
from jax import lax
from jax.experimental import pallas as pl
from jax.experimental.pallas import tpu as pltpu
from jax.sharding import PartitionSpec as P

KSIZE = 5
HALO = KSIZE // 2
LANES = 128
SIDES = (0, 2, 3, 4, 5, 7)
BF16 = jnp.bfloat16
F32 = jnp.float32

VMEM = pl.BlockSpec(memory_space=pltpu.VMEM)
SMEM = pl.BlockSpec(memory_space=pltpu.SMEM)


def call(kernel, outs, scratch=(), limit=16):
    def run(*args):
        specs = [SMEM if a.ndim == 1 and a.dtype == jnp.int32 else VMEM for a in args]
        return pl.pallas_call(
            kernel,
            out_shape=[jax.ShapeDtypeStruct(s, d) for s, d in outs],
            in_specs=specs,
            out_specs=[VMEM] * len(outs),
            scratch_shapes=list(scratch),
            compiler_params=pltpu.CompilerParams(vmem_limit_bytes=limit * 1024 * 1024),
        )(*args)

    return run


def dot(a, b):
    return lax.dot_general(a, b, (((1,), (0,)), ((), ())), preferred_element_type=F32)


def dot_nt(a, b):
    return lax.dot_general(a, b, (((1,), (1,)), ((), ())), preferred_element_type=F32)


def one_hot(index, rows):
    row = lax.broadcasted_iota(jnp.int32, (rows, index.shape[1]), 0)
    return jnp.where(row == index, 1.0, 0.0).astype(BF16)


def rim_pixels(edge):
    band_len = HALO * edge
    lane = lax.broadcasted_iota(jnp.int32, (1, 4 * band_len), 1)
    band, at = lane // band_len, lane % band_len
    side = (at // HALO) * edge + at % HALO
    pixel = jnp.where(band == 0, at, (edge - HALO) * edge + at)
    return jnp.where(band == 2, side, jnp.where(band == 3, side + edge - HALO, pixel))


def rim_lane(row, col, edge):
    band_len = HALO * edge
    side = jnp.where(col < HALO, 2 * band_len + row * HALO + col,
                     3 * band_len + row * HALO + col - (edge - HALO))
    side = jnp.where(row >= edge - HALO, band_len + (row - (edge - HALO)) * edge + col, side)
    return jnp.where(row < HALO, row * edge + col, side)


def turned_lane(row, col, quarter, edge):
    last = edge - 1
    from_row = jnp.where(quarter == 1, col, jnp.where(
        quarter == 2, last - row, jnp.where(quarter == 3, last - col, row)))
    from_col = jnp.where(quarter == 1, last - row, jnp.where(
        quarter == 2, last - col, jnp.where(quarter == 3, row, col)))
    return rim_lane(from_row, from_col, edge)


def row_halo_maps(top_turn, bottom_turn, edge):
    rim = 4 * HALO * edge
    lane = lax.broadcasted_iota(jnp.int32, (1, LANES), 1)
    up = lane - (LANES - HALO * edge)
    top = turned_lane(edge - HALO + up // edge, up % edge, top_turn, edge)
    low = turned_lane(lane // edge, lane % edge, bottom_turn, edge)
    top = jnp.where(up >= 0, top, -1)
    low = jnp.where(lane < HALO * edge, low, -1)
    return one_hot(top, rim), one_hot(low, rim)


def side_map(turns, edge):
    rim = 4 * HALO * edge
    lane = lax.broadcasted_iota(jnp.int32, (1, 2 * LANES), 1)
    row, k = lane // (2 * HALO), lane % (2 * HALO)
    above, below, right = row < HALO, row >= HALO + edge, k >= HALO
    b_row = jnp.where(above, edge - HALO + row, jnp.where(below, row - HALO - edge, row - HALO))
    b_col = jnp.where(right, k - HALO, edge - HALO + k)
    slot = jnp.where(above, 0, jnp.where(below, 4, 2)) + right.astype(jnp.int32)
    quarter = jnp.zeros_like(slot)
    for position in range(len(SIDES)):
        quarter = jnp.where(slot == position, turns[position], quarter)
    index = slot * rim + turned_lane(b_row, b_col, quarter, edge)
    index = jnp.where(row < edge + 2 * HALO, index, -1)
    return one_hot(index, len(SIDES) * rim)


def spread_map(edge, wide):
    lane = lax.broadcasted_iota(jnp.int32, (1, wide), 1)
    row = lane // edge - (LANES // edge - HALO)
    col = lane % edge
    right_row, left_row = row - 1, row + 1
    rows = edge + 2 * HALO
    right = jnp.where((right_row >= 0) & (right_row < rows), right_row * 2 * HALO + HALO + col, -1)
    left = jnp.where((left_row >= 0) & (left_row < rows),
                     left_row * 2 * HALO + col - (edge - HALO), -1)
    index = jnp.where(col < HALO, right, jnp.where(col >= edge - HALO, left, -1))
    return one_hot(index, 2 * LANES)


def side_mask(shift, shape, edge):
    col = lax.broadcasted_iota(jnp.int32, shape, 1) % edge
    return col < shift if shift > 0 else col >= edge + shift


def roll(values, shift):
    size = values.shape[1]
    return values if shift % size == 0 else pltpu.roll(values, shift % size, axis=1)


def pack_kernel(edge, x_ref, rim_ref):
    pixels = x_ref.shape[1]
    pick = one_hot(rim_pixels(edge), pixels)
    rim = dot(x_ref[...], pick).astype(BF16)
    rim_ref[...] = jnp.broadcast_to(rim[None], rim_ref.shape)


def conv_kernel(edge, place_ref, nb_ref, rot_ref, x_ref, rims_ref, taps_ref,
                hidden_ref, padded_ref, side_ref, gathered):
    channels, pixels = x_ref.shape
    wide = pixels + 2 * LANES
    rim = rims_ref.shape[2]
    first = place_ref[0] * 8
    nb = [nb_ref[first + d] for d in range(8)]
    rot = [rot_ref[first + d] for d in range(8)]
    top, low = row_halo_maps(rot[1], rot[6], edge)
    padded_ref[:, :LANES] = dot(rims_ref[nb[1]], top).astype(BF16)
    padded_ref[:, LANES + pixels:] = dot(rims_ref[nb[6]], low).astype(BF16)
    padded_ref[:, LANES:LANES + pixels] = x_ref[...]
    for position, d in enumerate(SIDES):
        gathered[:, position * rim:(position + 1) * rim] = rims_ref[nb[d]]
    packed = dot(gathered[...], side_map([rot[d] for d in SIDES], edge)).astype(BF16)
    side_ref[...] = dot(packed, spread_map(edge, wide)).astype(BF16)

    def block(i, carry):
        at = pl.multiple_of(i * 16, 16)
        xs = padded_ref[pl.ds(at, 16), :].astype(F32)
        hs = side_ref[pl.ds(at, 16), :].astype(F32)
        halves = []
        for half in (0, 8):
            x, h = xs[half:half + 8], hs[half:half + 8]
            sums = [None] * KSIZE
            for b in range(KSIZE):
                shift = b - HALO
                moved = x
                if shift:
                    moved = roll(jnp.where(side_mask(shift, x.shape, edge), h, x), -shift)
                for a in range(KSIZE):
                    tap = taps_ref[a * KSIZE + b, pl.ds(at + half, 8), :]
                    term = jnp.tile(tap, (1, wide // LANES)) * moved
                    sums[a] = term if sums[a] is None else sums[a] + term
            total = None
            for a in range(KSIZE):
                part = roll(sums[a], -(a - HALO) * edge)[:, LANES:LANES + pixels]
                total = part if total is None else total + part
            halves.append(total)
        hidden_ref[pl.ds(at, 16), :] = jnp.concatenate(halves, axis=0).astype(BF16)
        return carry

    lax.fori_loop(0, channels // 16, block, 0)


def gelu_parts(pre, grad_act):
    cumul = 0.5 * (1.0 + lax.erf(pre * 0.7071067811865476))
    slope = cumul + pre * jnp.exp(-0.5 * pre * pre) * 0.3989422804014327
    return (pre * cumul).astype(BF16), (grad_act * slope).astype(BF16)


def hidden_block(w_in_t, w_out, feats_ref, cot_ref, pre, slope, act, gpre):
    pre[...] = dot(w_in_t, feats_ref[...])
    slope[...] = dot(w_out, cot_ref[...])

    def rows(i, carry):
        at = pl.multiple_of(i * 16, 16)
        act[pl.ds(at, 16), :], gpre[pl.ds(at, 16), :] = gelu_parts(
            pre[pl.ds(at, 16), :], slope[pl.ds(at, 16), :])
        return carry

    lax.fori_loop(0, pre.shape[0] // 16, rows, 0)


def weight_kernel(place_ref, feats_ref, cot_ref, w_in_t_ref, w_out_ref, out_ref, act, gpre,
                  pre, slope):
    units = pre.shape[0]
    full = feats_ref.shape[0]
    at = pl.multiple_of(place_ref[1] * units, units)
    hidden_block(w_in_t_ref[pl.ds(at, units), :], w_out_ref[pl.ds(at, units), :],
                 feats_ref, cot_ref, pre, slope, act, gpre)
    part_in = dot_nt(feats_ref[...], gpre[...]).astype(BF16)
    part_out = dot_nt(act[...], cot_ref[...]).astype(BF16)
    used = 0
    for column in range(0, units, LANES):
        out_ref[used:used + full, :] = part_in[:, column:column + LANES]
        used += full
    for column in range(0, full, LANES):
        out_ref[used:used + units, :] = part_out[:, column:column + LANES]
        used += units
    if used < out_ref.shape[0]:
        out_ref[used:, :] = jnp.zeros((out_ref.shape[0] - used, LANES), BF16)


def point_kernel(groups, place_ref, feats_ref, cot_ref, w_in_t_ref, w_out_ref, w_in_own_ref,
                 w_out_own_ref, act_own, gpre_own, x_ref, out_ref, grad_ref,
                 pre, slope, act, gpre):
    units = pre.shape[0]

    def start(k):
        return pl.multiple_of((place_ref[1] ^ k) * units, units)

    mine = pl.ds(start(0), units)
    branch = dot(w_out_own_ref[:, mine], act_own[...])
    grad = dot(w_in_own_ref[:, mine], gpre_own[...])
    for k in range(1, groups):
        part = pl.ds(start(k), units)
        hidden_block(w_in_t_ref[part, :], w_out_ref[part, :],
                     feats_ref, cot_ref, pre, slope, act, gpre)
        branch = branch + dot(w_out_own_ref[:, part], act[...])
        grad = grad + dot(w_in_own_ref[:, part], gpre[...])
    out_ref[...] = (x_ref[...].astype(F32) + branch.astype(BF16).astype(F32)).astype(BF16)
    grad_ref[...] = grad.astype(BF16)


def prep_kernel(place_ref, w_in_ref, w_out_ref, w_in_t_ref, w_in_own_ref, w_out_own_ref):
    channels = w_in_own_ref.shape[0]
    start = place_ref[1] * channels
    w_in_t_ref[...] = w_in_ref[...].astype(F32).T.astype(BF16)
    w_in_own_ref[...] = w_in_ref[pl.ds(pl.multiple_of(start, channels), channels), :]
    row = lax.broadcasted_iota(jnp.int32, (channels, w_out_ref.shape[1]), 0)
    column = lax.broadcasted_iota(jnp.int32, (channels, w_out_ref.shape[1]), 1)
    pick = jnp.where(column == row + start, 1.0, 0.0).astype(BF16)
    w_out_own_ref[...] = dot_nt(pick, w_out_ref[...]).astype(BF16)


def join_kernel(place_ref, *refs):
    pieces, out_ref = refs[:-1], refs[-1]
    channels = pieces[0].shape[0]
    for k, piece in enumerate(pieces):
        start = pl.multiple_of((place_ref[1] ^ k) * channels, channels)
        out_ref[pl.ds(start, channels), :] = piece[...]


def back_kernel(edge, place_ref, nb_ref, rot_ref, grad_ref, cot_ref, padded_ref, side_ref, taps_ref,
                accum_ref, send_ref, tap_ref, d_row, d_side, turned_all, moved_all, gathered):
    channels, pixels = grad_ref.shape
    wide = pixels + 2 * LANES
    tiles, _, rim = send_ref.shape
    slots = tap_ref.shape[0]
    moved_all[KSIZE * 16:, :] = jnp.zeros((LANES - KSIZE * 16, wide), BF16)
    tap_ref[...] = jnp.zeros(tap_ref.shape, BF16)
    same = (lax.broadcasted_iota(jnp.int32, (16, KSIZE * LANES), 1) % 16
            == lax.broadcasted_iota(jnp.int32, (16, KSIZE * LANES), 0))
    line = lax.broadcasted_iota(jnp.int32, (KSIZE * LANES, LANES), 0)
    tap = lax.broadcasted_iota(jnp.int32, (KSIZE * LANES, LANES), 1)
    used = line % LANES < KSIZE * 16
    pick = jnp.where(used & (line // LANES * KSIZE + line % LANES // 16 == tap), 1.0, 0.0).astype(BF16)

    for block in range(channels // 16):
        at = block * 16
        gs = grad_ref[at:at + 16, :].astype(F32)
        xs = padded_ref[at:at + 16, :].astype(F32)
        hs = side_ref[at:at + 16, :].astype(F32)
        zeros = jnp.zeros((8, LANES), F32)
        turned_rows, moved_rows = [[] for _ in range(KSIZE)], [[] for _ in range(KSIZE)]
        rows, sides = [], []
        for half in (0, 8):
            x, h = xs[half:half + 8], hs[half:half + 8]
            g = jnp.concatenate([zeros, gs[half:half + 8], zeros], axis=1)
            turned = [roll(g, (a - HALO) * edge) for a in range(KSIZE)]
            d_x = d_h = None
            for b in range(KSIZE):
                shift = b - HALO
                back = None
                for a in range(KSIZE):
                    weight = taps_ref[a * KSIZE + b, at + half:at + half + 8, :]
                    term = jnp.tile(weight, (1, wide // LANES)) * turned[a]
                    back = term if back is None else back + term
                back = roll(back, shift)
                if shift:
                    mask = side_mask(shift, x.shape, edge)
                    moved_rows[b].append(roll(jnp.where(mask, h, x), -shift))
                    inside = jnp.where(mask, 0.0, back)
                    outside = jnp.where(mask, back, 0.0)
                    d_h = outside if d_h is None else d_h + outside
                    d_x = inside if d_x is None else d_x + inside
                else:
                    moved_rows[b].append(x)
                    d_x = back if d_x is None else d_x + back
            for a in range(KSIZE):
                turned_rows[a].append(turned[a])
            rows.append(d_x)
            sides.append(d_h)
        d_x = jnp.concatenate(rows, axis=0)
        accum_ref[at:at + 16, :] = (
            d_x[:, LANES:LANES + pixels] + cot_ref[at:at + 16, :].astype(F32))
        d_row[at:at + 16, :LANES] = d_x[:, :LANES].astype(BF16)
        d_row[at:at + 16, LANES:] = d_x[:, LANES + pixels:].astype(BF16)
        d_side[at:at + 16, :] = jnp.concatenate(sides, axis=0).astype(BF16)
        for a in range(KSIZE):
            turned_all[a * 16:a * 16 + 16, :] = jnp.concatenate(turned_rows[a], axis=0).astype(BF16)
            moved_all[a * 16:a * 16 + 16, :] = jnp.concatenate(moved_rows[a], axis=0).astype(BF16)
        products = dot_nt(turned_all[...], moved_all[...])
        side_by_side = jnp.concatenate(
            [products[a * 16:a * 16 + 16, :] for a in range(KSIZE)], axis=1)
        found = dot(jnp.where(same, side_by_side, 0.0).astype(BF16), pick)
        lane = lax.broadcasted_iota(jnp.int32, (16, LANES), 1)
        place = block % 4
        placed = jnp.where(lane // 32 == place, roll(found, 32 * place), 0.0)
        slot = slice(block // 4 * 16, block // 4 * 16 + 16)
        tap_ref[slot, :] = (tap_ref[slot, :].astype(F32) + placed).astype(BF16)

    first = place_ref[0] * 8
    nb = [nb_ref[first + d] for d in range(8)]
    rot = [rot_ref[first + d] for d in range(8)]
    gathered[...] = jnp.zeros(gathered.shape, F32)
    top, low = row_halo_maps(rot[1], rot[6], edge)
    gathered[nb[1]] += dot_nt(d_row[:, :LANES], top)
    gathered[nb[6]] += dot_nt(d_row[:, LANES:], low)
    packed = dot_nt(d_side[...], spread_map(edge, wide)).astype(BF16)
    picks = side_map([rot[d] for d in SIDES], edge)
    for position, d in enumerate(SIDES):
        gathered[nb[d]] += dot_nt(packed, picks[position * rim:(position + 1) * rim, :])

    def store(t, carry):
        send_ref[t] = gathered[t].astype(BF16)
        return carry

    lax.fori_loop(0, tiles, store, 0)


def border_kernel(edge, recv_ref, accum_ref, grad_ref):
    pixels = accum_ref.shape[1]
    rims = total_of(recv_ref)
    high = rims.astype(BF16)
    low = (rims - high.astype(F32)).astype(BF16)
    pick = one_hot(rim_pixels(edge), pixels)
    grad_ref[...] = (accum_ref[...] + dot_nt(high, pick) + dot_nt(low, pick)).astype(BF16)


def total_of(ref):
    return lax.fori_loop(1, ref.shape[0], lambda t, so_far: so_far + ref[t].astype(F32),
                         ref[0].astype(F32))


def sum_kernel(recv_ref, tap_ref, out_ref):
    share = recv_ref.shape[1]
    total = total_of(recv_ref).astype(BF16)

    def store(t, carry):
        out_ref[t, :share, :] = total
        out_ref[t, share:, :] = tap_ref[...]
        return carry

    lax.fori_loop(0, out_ref.shape[0], store, 0)


def final_kernel(groups, share, channels, scale, place_ref, *refs):
    pieces = refs[:groups]
    g_in_ref, g_out_ref, g_tap_ref, all_taps = refs[groups:]
    full, hidden = g_in_ref.shape
    units = hidden // groups
    tiles, rows, _ = pieces[0].shape
    for k in range(groups):
        owner = place_ref[1] ^ k
        start = pl.multiple_of(owner * units, units)
        for tile in range(tiles):
            for row, count, column, at, into_in in chunks(tile, share, units, full):
                values = pieces[k][tile, row:row + count, :].astype(F32) * scale
                if into_in:
                    g_in_ref[at:at + count, pl.ds(pl.multiple_of(start + column, LANES), LANES)] = values
                else:
                    g_out_ref[pl.ds(pl.multiple_of(start + at, 16), count), column:column + LANES] = values
        taps = pieces[k][0, share:, :].astype(F32)
        for tile in range(1, tiles):
            taps = taps + pieces[k][tile, share:, :].astype(F32)
        taps = taps * scale
        for block in range(channels // 16):
            values = taps[block // 4 * 16:block // 4 * 16 + 16, :]
            into = pl.ds(pl.multiple_of(owner * channels + block * 16, 16), 16)
            all_taps[into, :] = roll(values, -32 * (block % 4))
    g_tap_ref[...] = all_taps[...].T[:KSIZE * KSIZE, :]


def chunks(tile, share, units, full):
    inside, found = units // LANES * full, []
    row, end = tile * share, min((tile + 1) * share, 2 * units * full // LANES)
    while row < end:
        height = full if row < inside else units
        offset = row if row < inside else row - inside
        column, at = offset // height * LANES, offset % height
        count = min(end - row, height - at)
        found.append((row - tile * share, count, column, at, row < inside))
        row += count
    return found


def gather_pieces(own, groups):
    pieces = {0: own}
    bit = groups // 2
    while bit:
        swap = [(i, i ^ bit) for i in range(groups)]
        for k in list(pieces):
            pieces[k ^ bit] = lax.ppermute(pieces[k], "chan", swap)
        bit //= 2
    return [pieces[k] for k in range(groups)]


def swap_rows(values):
    return lax.all_to_all(values, "tile", 0, 0, tiled=True)


def body(inputs, grad_out, kernel, w_in, w_out, neighbours, rotations):
    channels, pixels = inputs.shape[1:]
    edge = math.isqrt(pixels)
    full, hidden = w_in.shape
    groups = lax.axis_size("chan")
    tiles = lax.axis_size("tile")
    wide = pixels + 2 * LANES
    rim = 4 * HALO * edge
    units = hidden // groups
    scale = (tiles * pixels) ** -0.5
    place = jnp.stack([lax.axis_index("tile"), lax.axis_index("chan")]).astype(jnp.int32)
    nb, rot = neighbours.reshape(-1), rotations.reshape(-1)
    x, cot = inputs[0], grad_out[0]

    [rims] = call(functools.partial(pack_kernel, edge), [((tiles, channels, rim), BF16)])(x)
    rims, kernel, w_in, w_out = lax.optimization_barrier((rims, kernel, w_in, w_out))
    rims = swap_rows(rims)
    cot_pieces = gather_pieces(cot, groups)
    taps = jnp.broadcast_to(kernel.astype(F32)[:, :, None], (KSIZE * KSIZE, channels, LANES))
    w_in_t, w_in_own, w_out_own = call(
        prep_kernel, [((hidden, full), BF16)] + [((channels, hidden), BF16)] * 2
    )(place, w_in, w_out)
    [cots] = call(join_kernel, [((full, pixels), BF16)])(place, *cot_pieces)
    rims, cots, taps, w_in_t, w_in_own, w_out_own = lax.optimization_barrier(
        (rims, cots, taps, w_in_t, w_in_own, w_out_own))

    hid, padded, side = call(
        functools.partial(conv_kernel, edge),
        [((channels, pixels), BF16), ((channels, wide), BF16), ((channels, wide), BF16)],
        [pltpu.VMEM((channels, len(SIDES) * rim), BF16)],
    )(place, nb, rot, x, rims, taps)
    feats = lax.all_gather(hid, "chan", axis=0, tiled=True)

    used = 2 * full * units // LANES
    share = -(-used // (16 * tiles)) * 16
    tap_rows = -(-channels // 64) * 16
    values = [pltpu.VMEM((units, pixels), F32)] * 2
    rounded = [((units, pixels), BF16)] * 2
    part, act, gpre = call(weight_kernel, [((tiles * share, LANES), BF16)] + rounded, values)(
        place, feats, cots, w_in_t, w_out)
    part = swap_rows(part.reshape(tiles, share, LANES))

    outputs, grad_hid = call(
        functools.partial(point_kernel, groups), [((channels, pixels), BF16)] * 2,
        values + [pltpu.VMEM(s, d) for s, d in rounded],
    )(place, feats, cots, w_in_t, w_out, w_in_own, w_out_own, act, gpre, x)
    accum, border, tap_part = call(
        functools.partial(back_kernel, edge),
        [((channels, pixels), F32), ((tiles, channels, rim), BF16), ((tap_rows, LANES), BF16)],
        [pltpu.VMEM((channels, 2 * LANES), BF16), pltpu.VMEM((channels, wide), BF16),
         pltpu.VMEM((KSIZE * 16, wide), BF16), pltpu.VMEM((LANES, wide), BF16),
         pltpu.VMEM((tiles, channels, rim), F32)],
    )(place, nb, rot, grad_hid, cot, padded, side, taps)

    [mine] = call(sum_kernel, [((tiles, share + tap_rows, LANES), BF16)])(part, tap_part)
    mine, border = lax.optimization_barrier((mine, border))
    weights = swap_rows(mine)
    border = swap_rows(border)
    pieces = gather_pieces(weights, groups)
    [grad_in] = call(
        functools.partial(border_kernel, edge), [((channels, pixels), BF16)])(border, accum)
    grads = call(
        functools.partial(final_kernel, groups, share, channels, scale),
        [((full, hidden), F32), ((hidden, full), F32), ((KSIZE * KSIZE, full), F32)],
        [pltpu.VMEM((full, LANES), F32)],
    )(place, *pieces)
    return (outputs[None], grad_in[None], *grads)


def solution(mesh):
    return jax.shard_map(
        body,
        mesh=mesh,
        in_specs=(
            P("tile", "chan", None),
            P("tile", "chan", None),
            P(None, "chan"),
            P(),
            P(),
            P(),
            P(),
        ),
        out_specs=(P("tile", "chan", None), P("tile", "chan", None), P(), P(), P()),
        check_vma=False,
    )
```

```python
import functools
import math

import jax
import jax.numpy as jnp
from jax import lax
from jax.experimental import pallas as pl
from jax.experimental.pallas import tpu as pltpu
from jax.sharding import PartitionSpec as P

KSIZE = 5
HALO = KSIZE // 2
LANES = 128
SIDES = (0, 2, 3, 4, 5, 7)
BF16 = jnp.bfloat16
F32 = jnp.float32

SCALAR, NEAR, FAR, RAW = "scalar", "near", "far", "raw"
SPACES = {SCALAR: pltpu.SMEM, NEAR: pltpu.VMEM, FAR: pltpu.HBM, RAW: pltpu.HBM}


class Loaded:
    def __init__(self, ref, copy=None):
        self.ref, self.copy = ref, copy
        if copy is not None:
            copy.start()

    def get(self):
        if self.copy is not None:
            self.copy.wait()
            self.copy = None
        return self.ref


class Stored:
    def __init__(self, ref, copy):
        self.ref, self.copy, self.started = ref, copy, False

    def send(self):
        if not self.started:
            self.copy.start()
            self.started = True


def call(kernel, ins, outs, scratch=(), limit=16):
    buffers = []
    for shape, dtype, place in [(a.shape, a.dtype, p) for a, p in ins] + list(outs):
        if place == FAR:
            buffers += [pltpu.VMEM(shape, dtype), pltpu.SemaphoreType.DMA]

    def run(*refs):
        ends = len(ins), len(ins) + len(outs), len(ins) + len(outs) + len(buffers)
        spare = list(refs[ends[1]:ends[2]])
        operands, results = [], []
        for ref, (_, place) in zip(refs, ins):
            if place == FAR:
                buffer, sem = spare.pop(0), spare.pop(0)
                operands.append(Loaded(buffer, pltpu.make_async_copy(ref, buffer, sem)))
            else:
                operands.append(Loaded(ref) if place == NEAR else ref)
        for ref, (_, _, place) in zip(refs[ends[0]:], outs):
            if place == FAR:
                buffer, sem = spare.pop(0), spare.pop(0)
                results.append(Stored(buffer, pltpu.make_async_copy(buffer, ref, sem)))
            else:
                results.append(ref)
        kernel(*operands, *results, *refs[ends[2]:])
        far = [result for result in results if isinstance(result, Stored)]
        for result in far:
            result.send()
        for result in far:
            result.copy.wait()

    return pl.pallas_call(
        run,
        out_shape=[jax.ShapeDtypeStruct(s, d) for s, d, _ in outs],
        in_specs=[pl.BlockSpec(memory_space=SPACES[p]) for _, p in ins],
        out_specs=[pl.BlockSpec(memory_space=SPACES[p]) for _, _, p in outs],
        scratch_shapes=buffers + list(scratch),
        compiler_params=pltpu.CompilerParams(vmem_limit_bytes=limit * 1024 * 1024),
    )(*[a for a, _ in ins])


def dot(a, b):
    return lax.dot_general(a, b, (((1,), (0,)), ((), ())), preferred_element_type=F32)


def dot_nt(a, b):
    return lax.dot_general(a, b, (((1,), (1,)), ((), ())), preferred_element_type=F32)


def one_hot(index, rows):
    row = lax.broadcasted_iota(jnp.int32, (rows, index.shape[1]), 0)
    return jnp.where(row == index, 1.0, 0.0).astype(BF16)


def rim_pixels(edge):
    band_len = HALO * edge
    lane = lax.broadcasted_iota(jnp.int32, (1, 4 * band_len), 1)
    band, at = lane // band_len, lane % band_len
    side = (at // HALO) * edge + at % HALO
    pixel = jnp.where(band == 0, at, (edge - HALO) * edge + at)
    return jnp.where(band == 2, side, jnp.where(band == 3, side + edge - HALO, pixel))


def rim_lane(row, col, edge):
    band_len = HALO * edge
    side = jnp.where(col < HALO, 2 * band_len + row * HALO + col,
                     3 * band_len + row * HALO + col - (edge - HALO))
    side = jnp.where(row >= edge - HALO, band_len + (row - (edge - HALO)) * edge + col, side)
    return jnp.where(row < HALO, row * edge + col, side)


def turned_lane(row, col, quarter, edge):
    last = edge - 1
    from_row = jnp.where(quarter == 1, col, jnp.where(
        quarter == 2, last - row, jnp.where(quarter == 3, last - col, row)))
    from_col = jnp.where(quarter == 1, last - row, jnp.where(
        quarter == 2, last - col, jnp.where(quarter == 3, row, col)))
    return rim_lane(from_row, from_col, edge)


def row_halo_maps(top_turn, bottom_turn, edge):
    rim = 4 * HALO * edge
    lane = lax.broadcasted_iota(jnp.int32, (1, LANES), 1)
    up = lane - (LANES - HALO * edge)
    top = turned_lane(edge - HALO + up // edge, up % edge, top_turn, edge)
    low = turned_lane(lane // edge, lane % edge, bottom_turn, edge)
    top = jnp.where(up >= 0, top, -1)
    low = jnp.where(lane < HALO * edge, low, -1)
    return one_hot(top, rim), one_hot(low, rim)


def side_map(turns, edge):
    rim = 4 * HALO * edge
    lane = lax.broadcasted_iota(jnp.int32, (1, 2 * LANES), 1)
    row, k = lane // (2 * HALO), lane % (2 * HALO)
    above, below, right = row < HALO, row >= HALO + edge, k >= HALO
    b_row = jnp.where(above, edge - HALO + row, jnp.where(below, row - HALO - edge, row - HALO))
    b_col = jnp.where(right, k - HALO, edge - HALO + k)
    slot = jnp.where(above, 0, jnp.where(below, 4, 2)) + right.astype(jnp.int32)
    quarter = jnp.zeros_like(slot)
    for position in range(len(SIDES)):
        quarter = jnp.where(slot == position, turns[position], quarter)
    index = slot * rim + turned_lane(b_row, b_col, quarter, edge)
    index = jnp.where(row < edge + 2 * HALO, index, -1)
    return one_hot(index, len(SIDES) * rim)


def spread_map(edge, wide):
    lane = lax.broadcasted_iota(jnp.int32, (1, wide), 1)
    row = lane // edge - (LANES // edge - HALO)
    col = lane % edge
    right_row, left_row = row - 1, row + 1
    rows = edge + 2 * HALO
    right = jnp.where((right_row >= 0) & (right_row < rows), right_row * 2 * HALO + HALO + col, -1)
    left = jnp.where((left_row >= 0) & (left_row < rows),
                     left_row * 2 * HALO + col - (edge - HALO), -1)
    index = jnp.where(col < HALO, right, jnp.where(col >= edge - HALO, left, -1))
    return one_hot(index, 2 * LANES)


def side_mask(shift, shape, edge):
    col = lax.broadcasted_iota(jnp.int32, shape, 1) % edge
    return col < shift if shift > 0 else col >= edge + shift


def roll(values, shift):
    size = values.shape[1]
    return values if shift % size == 0 else pltpu.roll(values, shift % size, axis=1)


def pack_kernel(edge, x, rims):
    pick = one_hot(rim_pixels(edge), edge * edge)
    rim = dot(x.get()[...], pick).astype(BF16)
    rims.ref[...] = jnp.broadcast_to(rim[None], rims.ref.shape)


def conv_kernel(edge, place_ref, nb_ref, rot_ref, x, rims, taps,
                hidden_ref, padded, side, gathered):
    padded_ref, side_ref = padded.ref, side.ref
    rims_ref, taps_ref = rims.get(), taps.get()
    channels, pixels = hidden_ref.shape
    wide = pixels + 2 * LANES
    rim = rims_ref.shape[2]
    first = place_ref[0] * 8
    nb = [nb_ref[first + d] for d in range(8)]
    rot = [rot_ref[first + d] for d in range(8)]
    top, low = row_halo_maps(rot[1], rot[6], edge)
    padded_ref[:, :LANES] = dot(rims_ref[nb[1]], top).astype(BF16)
    padded_ref[:, LANES + pixels:] = dot(rims_ref[nb[6]], low).astype(BF16)
    padded_ref[:, LANES:LANES + pixels] = x.get()[...]
    padded.send()
    for position, d in enumerate(SIDES):
        gathered[:, position * rim:(position + 1) * rim] = rims_ref[nb[d]]
    packed = dot(gathered[...], side_map([rot[d] for d in SIDES], edge)).astype(BF16)
    side_ref[...] = dot(packed, spread_map(edge, wide)).astype(BF16)
    side.send()

    def block(i, carry):
        at = pl.multiple_of(i * 16, 16)
        xs = padded_ref[pl.ds(at, 16), :].astype(F32)
        hs = side_ref[pl.ds(at, 16), :].astype(F32)
        halves = []
        for half in (0, 8):
            x, h = xs[half:half + 8], hs[half:half + 8]
            sums = [None] * KSIZE
            for b in range(KSIZE):
                shift = b - HALO
                moved = x
                if shift:
                    moved = roll(jnp.where(side_mask(shift, x.shape, edge), h, x), -shift)
                for a in range(KSIZE):
                    tap = taps_ref[a * KSIZE + b, pl.ds(at + half, 8), :]
                    term = jnp.tile(tap, (1, wide // LANES)) * moved
                    sums[a] = term if sums[a] is None else sums[a] + term
            total = None
            for a in range(KSIZE):
                part = roll(sums[a], -(a - HALO) * edge)[:, LANES:LANES + pixels]
                total = part if total is None else total + part
            halves.append(total)
        hidden_ref[pl.ds(at, 16), :] = jnp.concatenate(halves, axis=0).astype(BF16)
        return carry

    lax.fori_loop(0, channels // 16, block, 0)


def gelu_parts(pre, grad_act):
    cumul = 0.5 * (1.0 + lax.erf(pre * 0.7071067811865476))
    slope = cumul + pre * jnp.exp(-0.5 * pre * pre) * 0.3989422804014327
    return (pre * cumul).astype(BF16), (grad_act * slope).astype(BF16)


def hidden_block(w_in_t, w_out, feats, cots, pre, slope, act, gpre):
    pre[...] = dot(w_in_t, feats[...])
    slope[...] = dot(w_out, cots[...])

    def rows(i, carry):
        at = pl.multiple_of(i * 16, 16)
        act[pl.ds(at, 16), :], gpre[pl.ds(at, 16), :] = gelu_parts(
            pre[pl.ds(at, 16), :], slope[pl.ds(at, 16), :])
        return carry

    lax.fori_loop(0, pre.shape[0] // 16, rows, 0)


def weight_kernel(place_ref, feats, cots, w_in_t, w_out, part, act, gpre,
                  pre, slope, own_in, own_out, sems):
    units = pre.shape[0]
    at = pl.multiple_of(place_ref[1] * units, units)
    own_in = Loaded(own_in, pltpu.make_async_copy(w_in_t.at[pl.ds(at, units)], own_in, sems.at[0]))
    own_out = Loaded(own_out, pltpu.make_async_copy(w_out.at[pl.ds(at, units)], own_out, sems.at[1]))
    feats, cots = feats.get(), cots.get()
    full = feats.shape[0]
    hidden_block(own_in.get()[...], own_out.get()[...], feats, cots, pre, slope, act.ref, gpre.ref)
    act.send()
    gpre.send()
    part_in = dot_nt(feats[...], gpre.ref[...]).astype(BF16)
    part_out = dot_nt(act.ref[...], cots[...]).astype(BF16)
    used = 0
    for column in range(0, units, LANES):
        part.ref[used:used + full, :] = part_in[:, column:column + LANES]
        used += full
    for column in range(0, full, LANES):
        part.ref[used:used + units, :] = part_out[:, column:column + LANES]
        used += units
    if used < part.ref.shape[0]:
        part.ref[used:, :] = jnp.zeros((part.ref.shape[0] - used, LANES), BF16)


def point_kernel(groups, place_ref, feats, cots, w_in_t, w_out, w_in_own, w_out_own, act_own,
                 gpre_own, x, out, grad_ref, pre, slope, act, gpre):
    units = pre.shape[0]
    feats, cots, w_in_t, w_out = feats.get(), cots.get(), w_in_t.get(), w_out.get()

    def start(k):
        return pl.multiple_of((place_ref[1] ^ k) * units, units)

    branch = grad = None
    for k in range(1, groups):
        part = pl.ds(start(k), units)
        hidden_block(w_in_t[part, :], w_out[part, :], feats, cots, pre, slope, act, gpre)
        more = dot(w_out_own.get()[:, part], act[...])
        branch = more if branch is None else branch + more
        more = dot(w_in_own.get()[:, part], gpre[...])
        grad = more if grad is None else grad + more
    mine = pl.ds(start(0), units)
    branch = branch + dot(w_out_own.get()[:, mine], act_own.get()[...])
    out.ref[...] = (x.get()[...].astype(F32) + branch.astype(BF16).astype(F32)).astype(BF16)
    out.send()
    grad = grad + dot(w_in_own.get()[:, mine], gpre_own.get()[...])
    grad_ref[...] = grad.astype(BF16)


def prep_kernel(place_ref, w_in, w_out, w_in_t, w_in_own, w_out_own):
    channels = w_in_own.ref.shape[0]
    start = place_ref[1] * channels
    w_in, w_out = w_in.get(), w_out.get()
    w_in_own.ref[...] = w_in[pl.ds(pl.multiple_of(start, channels), channels), :]
    w_in_own.send()
    w_in_t.ref[...] = w_in[...].astype(F32).T.astype(BF16)
    w_in_t.send()
    row = lax.broadcasted_iota(jnp.int32, (channels, w_out.shape[1]), 0)
    column = lax.broadcasted_iota(jnp.int32, (channels, w_out.shape[1]), 1)
    pick = jnp.where(column == row + start, 1.0, 0.0).astype(BF16)
    w_out_own.ref[...] = dot_nt(pick, w_out[...]).astype(BF16)


def join_kernel(place_ref, *refs):
    pieces, out_ref, sems = refs[:-2], refs[-2], refs[-1]
    channels = pieces[0].shape[0]
    copies = []
    for k, piece in enumerate(pieces):
        start = pl.multiple_of((place_ref[1] ^ k) * channels, channels)
        copies.append(pltpu.make_async_copy(piece, out_ref.at[pl.ds(start, channels)], sems.at[k]))
    for copy in copies:
        copy.start()
    for copy in copies:
        copy.wait()


def back_kernel(edge, place_ref, nb_ref, rot_ref, grad, cot, padded, side, taps,
                accum, border, tap_ref, d_row, d_side, turned_all, moved_all, gathered):
    accum_ref, send_ref = accum.ref, border.ref
    grad_ref, taps_ref = grad.get(), taps.get()
    padded_ref, side_ref, cot_ref = padded.get(), side.get(), cot.get()
    channels, pixels = grad_ref.shape
    wide = pixels + 2 * LANES
    tiles, _, rim = send_ref.shape
    slots = tap_ref.shape[0]
    moved_all[KSIZE * 16:, :] = jnp.zeros((LANES - KSIZE * 16, wide), BF16)
    tap_ref[...] = jnp.zeros(tap_ref.shape, BF16)
    same = (lax.broadcasted_iota(jnp.int32, (16, KSIZE * LANES), 1) % 16
            == lax.broadcasted_iota(jnp.int32, (16, KSIZE * LANES), 0))
    line = lax.broadcasted_iota(jnp.int32, (KSIZE * LANES, LANES), 0)
    tap = lax.broadcasted_iota(jnp.int32, (KSIZE * LANES, LANES), 1)
    used = line % LANES < KSIZE * 16
    pick = jnp.where(used & (line // LANES * KSIZE + line % LANES // 16 == tap), 1.0, 0.0).astype(BF16)

    for block in range(channels // 16):
        at = block * 16
        gs = grad_ref[at:at + 16, :].astype(F32)
        xs = padded_ref[at:at + 16, :].astype(F32)
        hs = side_ref[at:at + 16, :].astype(F32)
        zeros = jnp.zeros((8, LANES), F32)
        turned_rows, moved_rows = [[] for _ in range(KSIZE)], [[] for _ in range(KSIZE)]
        rows, sides = [], []
        for half in (0, 8):
            x, h = xs[half:half + 8], hs[half:half + 8]
            g = jnp.concatenate([zeros, gs[half:half + 8], zeros], axis=1)
            turned = [roll(g, (a - HALO) * edge) for a in range(KSIZE)]
            d_x = d_h = None
            for b in range(KSIZE):
                shift = b - HALO
                back = None
                for a in range(KSIZE):
                    weight = taps_ref[a * KSIZE + b, at + half:at + half + 8, :]
                    term = jnp.tile(weight, (1, wide // LANES)) * turned[a]
                    back = term if back is None else back + term
                back = roll(back, shift)
                if shift:
                    mask = side_mask(shift, x.shape, edge)
                    moved_rows[b].append(roll(jnp.where(mask, h, x), -shift))
                    inside = jnp.where(mask, 0.0, back)
                    outside = jnp.where(mask, back, 0.0)
                    d_h = outside if d_h is None else d_h + outside
                    d_x = inside if d_x is None else d_x + inside
                else:
                    moved_rows[b].append(x)
                    d_x = back if d_x is None else d_x + back
            for a in range(KSIZE):
                turned_rows[a].append(turned[a])
            rows.append(d_x)
            sides.append(d_h)
        d_x = jnp.concatenate(rows, axis=0)
        accum_ref[at:at + 16, :] = (
            d_x[:, LANES:LANES + pixels] + cot_ref[at:at + 16, :].astype(F32))
        d_row[at:at + 16, :LANES] = d_x[:, :LANES].astype(BF16)
        d_row[at:at + 16, LANES:] = d_x[:, LANES + pixels:].astype(BF16)
        d_side[at:at + 16, :] = jnp.concatenate(sides, axis=0).astype(BF16)
        for a in range(KSIZE):
            turned_all[a * 16:a * 16 + 16, :] = jnp.concatenate(turned_rows[a], axis=0).astype(BF16)
            moved_all[a * 16:a * 16 + 16, :] = jnp.concatenate(moved_rows[a], axis=0).astype(BF16)
        products = dot_nt(turned_all[...], moved_all[...])
        side_by_side = jnp.concatenate(
            [products[a * 16:a * 16 + 16, :] for a in range(KSIZE)], axis=1)
        found = dot(jnp.where(same, side_by_side, 0.0).astype(BF16), pick)
        lane = lax.broadcasted_iota(jnp.int32, (16, LANES), 1)
        place = block % 4
        placed = jnp.where(lane // 32 == place, roll(found, 32 * place), 0.0)
        slot = slice(block // 4 * 16, block // 4 * 16 + 16)
        tap_ref[slot, :] = (tap_ref[slot, :].astype(F32) + placed).astype(BF16)

    accum.send()
    first = place_ref[0] * 8
    nb = [nb_ref[first + d] for d in range(8)]
    rot = [rot_ref[first + d] for d in range(8)]
    gathered[...] = jnp.zeros(gathered.shape, F32)
    top, low = row_halo_maps(rot[1], rot[6], edge)
    gathered[nb[1]] += dot_nt(d_row[:, :LANES], top)
    gathered[nb[6]] += dot_nt(d_row[:, LANES:], low)
    packed = dot_nt(d_side[...], spread_map(edge, wide)).astype(BF16)
    picks = side_map([rot[d] for d in SIDES], edge)
    for position, d in enumerate(SIDES):
        gathered[nb[d]] += dot_nt(packed, picks[position * rim:(position + 1) * rim, :])

    def store(t, carry):
        send_ref[t] = gathered[t].astype(BF16)
        return carry

    lax.fori_loop(0, tiles, store, 0)


def border_kernel(edge, recv, accum, grad):
    rims = total_of(recv.get())
    high = rims.astype(BF16)
    low = (rims - high.astype(F32)).astype(BF16)
    pick = one_hot(rim_pixels(edge), edge * edge)
    added = dot_nt(high, pick) + dot_nt(low, pick)
    grad.ref[...] = (accum.get()[...] + added).astype(BF16)


def total_of(ref):
    return lax.fori_loop(1, ref.shape[0], lambda t, so_far: so_far + ref[t].astype(F32),
                         ref[0].astype(F32))


def sum_kernel(recv, tap, out):
    recv = recv.get()
    share = recv.shape[1]
    total, taps = total_of(recv).astype(BF16), tap.get()[...]

    def store(t, carry):
        out.ref[t, :share, :] = total
        out.ref[t, share:, :] = taps
        return carry

    lax.fori_loop(0, out.ref.shape[0], store, 0)


def final_kernel(groups, share, channels, scale, place_ref, *refs):
    pieces = refs[:groups]
    g_in, g_out, g_tap_ref, buf_in, buf_out, all_taps, sems = refs[groups:]
    full, units = buf_in.shape[1:]
    tiles, rows, _ = pieces[0].ref.shape
    copies = []
    for k in range(groups):
        piece = pieces[k].get()
        owner = place_ref[1] ^ k
        start = pl.multiple_of(owner * units, units)
        for tile in range(tiles):
            for row, count, column, at, into_in in chunks(tile, share, units, full):
                values = piece[tile, row:row + count, :].astype(F32) * scale
                buffer = buf_in if into_in else buf_out
                buffer[k, at:at + count, column:column + LANES] = values
        copies.append(pltpu.make_async_copy(
            buf_in.at[k], g_in.at[:, pl.ds(start, units)], sems.at[0, k]))
        copies.append(pltpu.make_async_copy(
            buf_out.at[k], g_out.at[pl.ds(start, units)], sems.at[1, k]))
        for copy in copies[-2:]:
            copy.start()
        taps = piece[0, share:, :].astype(F32)
        for tile in range(1, tiles):
            taps = taps + piece[tile, share:, :].astype(F32)
        taps = taps * scale
        for block in range(channels // 16):
            values = taps[block // 4 * 16:block // 4 * 16 + 16, :]
            into = pl.ds(pl.multiple_of(owner * channels + block * 16, 16), 16)
            all_taps[into, :] = roll(values, -32 * (block % 4))
    g_tap_ref[...] = all_taps[...].T[:KSIZE * KSIZE, :]
    for copy in copies:
        copy.wait()


def chunks(tile, share, units, full):
    inside, found = units // LANES * full, []
    row, end = tile * share, min((tile + 1) * share, 2 * units * full // LANES)
    while row < end:
        height = full if row < inside else units
        offset = row if row < inside else row - inside
        column, at = offset // height * LANES, offset % height
        count = min(end - row, height - at)
        found.append((row - tile * share, count, column, at, row < inside))
        row += count
    return found


def gather_pieces(own, groups):
    pieces = {0: own}
    bit = groups // 2
    while bit:
        swap = [(i, i ^ bit) for i in range(groups)]
        for k in list(pieces):
            pieces[k ^ bit] = lax.ppermute(pieces[k], "chan", swap)
        bit //= 2
    return [pieces[k] for k in range(groups)]


def swap_rows(values):
    return lax.all_to_all(values, "tile", 0, 0, tiled=True)


def body(inputs, grad_out, kernel, w_in, w_out, neighbours, rotations):
    channels, pixels = inputs.shape[1:]
    edge = math.isqrt(pixels)
    full, hidden = w_in.shape
    groups = lax.axis_size("chan")
    tiles = lax.axis_size("tile")
    wide = pixels + 2 * LANES
    rim = 4 * HALO * edge
    units = hidden // groups
    scale = (tiles * pixels) ** -0.5
    place = jnp.stack([lax.axis_index("tile"), lax.axis_index("chan")]).astype(jnp.int32)
    nb, rot = neighbours.reshape(-1), rotations.reshape(-1)
    x, cot = inputs[0], grad_out[0]

    [rims] = call(functools.partial(pack_kernel, edge), [(x, FAR)],
                  [((tiles, channels, rim), BF16, FAR)])
    rims, kernel, w_in, w_out = lax.optimization_barrier((rims, kernel, w_in, w_out))
    rims = swap_rows(rims)
    cot_pieces = gather_pieces(cot, groups)
    taps = jnp.broadcast_to(kernel.astype(F32)[:, :, None], (KSIZE * KSIZE, channels, LANES))
    w_in_t, w_in_own, w_out_own = call(
        prep_kernel, [(place, SCALAR), (w_in, FAR), (w_out, FAR)],
        [((hidden, full), BF16, FAR)] + [((channels, hidden), BF16, FAR)] * 2)
    [cots] = call(join_kernel, [(place, SCALAR)] + [(piece, RAW) for piece in cot_pieces],
                  [((full, pixels), BF16, RAW)], [pltpu.SemaphoreType.DMA((groups,))])
    rims, cots, taps, w_in_t, w_in_own, w_out_own = lax.optimization_barrier(
        (rims, cots, taps, w_in_t, w_in_own, w_out_own))

    here = [(place, SCALAR), (nb, SCALAR), (rot, SCALAR)]
    hid, padded, side = call(
        functools.partial(conv_kernel, edge), here + [(x, FAR), (rims, NEAR), (taps, NEAR)],
        [((channels, pixels), BF16, NEAR), ((channels, wide), BF16, FAR),
         ((channels, wide), BF16, FAR)],
        [pltpu.VMEM((channels, len(SIDES) * rim), BF16)])
    feats = lax.all_gather(hid, "chan", axis=0, tiled=True)

    used = 2 * full * units // LANES
    share = -(-used // (16 * tiles)) * 16
    tap_rows = -(-channels // 64) * 16
    values = [pltpu.VMEM((units, pixels), F32)] * 2
    part, act, gpre = call(
        weight_kernel,
        [(place, SCALAR), (feats, NEAR), (cots, FAR), (w_in_t, RAW), (w_out, RAW)],
        [((tiles * share, LANES), BF16, FAR)] + [((units, pixels), BF16, FAR)] * 2,
        values + [pltpu.VMEM((units, full), BF16)] * 2 + [pltpu.SemaphoreType.DMA((2,))])
    part = swap_rows(part.reshape(tiles, share, LANES))

    outputs, grad_hid = call(
        functools.partial(point_kernel, groups),
        [(place, SCALAR), (feats, NEAR), (cots, FAR), (w_in_t, FAR), (w_out, FAR), (w_in_own, FAR),
         (w_out_own, FAR), (act, FAR), (gpre, FAR), (x, FAR)],
        [((channels, pixels), BF16, FAR), ((channels, pixels), BF16, NEAR)],
        values + [pltpu.VMEM((units, pixels), BF16)] * 2)
    accum, border, tap_part = call(
        functools.partial(back_kernel, edge),
        here + [(grad_hid, NEAR), (cot, FAR), (padded, FAR), (side, FAR), (taps, NEAR)],
        [((channels, pixels), F32, FAR), ((tiles, channels, rim), BF16, FAR),
         ((tap_rows, LANES), BF16, NEAR)],
        [pltpu.VMEM((channels, 2 * LANES), BF16), pltpu.VMEM((channels, wide), BF16),
         pltpu.VMEM((KSIZE * 16, wide), BF16), pltpu.VMEM((LANES, wide), BF16),
         pltpu.VMEM((tiles, channels, rim), F32)])

    [mine] = call(sum_kernel, [(part, NEAR), (tap_part, NEAR)],
                  [((tiles, share + tap_rows, LANES), BF16, FAR)])
    weights = swap_rows(mine)
    weights, border = lax.optimization_barrier((weights, border))
    border = swap_rows(border)
    pieces = gather_pieces(weights, groups)
    grads = call(
        functools.partial(final_kernel, groups, share, channels, scale),
        [(place, SCALAR)] + [(piece, NEAR) for piece in pieces],
        [((full, hidden), F32, RAW), ((hidden, full), F32, RAW),
         ((KSIZE * KSIZE, full), F32, NEAR)],
        [pltpu.VMEM((groups, full, units), F32), pltpu.VMEM((groups, units, full), F32),
         pltpu.VMEM((full, LANES), F32), pltpu.SemaphoreType.DMA((2, groups))])
    border, *grads = lax.optimization_barrier((border, *grads))
    [grad_in] = call(functools.partial(border_kernel, edge), [(border, NEAR), (accum, FAR)],
                     [((channels, pixels), BF16, FAR)])
    return (outputs[None], grad_in[None], *grads)


def solution(mesh):
    return jax.shard_map(
        body,
        mesh=mesh,
        in_specs=(
            P("tile", "chan", None),
            P("tile", "chan", None),
            P(None, "chan"),
            P(),
            P(),
            P(),
            P(),
        ),
        out_specs=(P("tile", "chan", None), P("tile", "chan", None), P(), P(), P()),
        check_vma=False,
    )
```

```python
import functools
import math

import jax
import jax.numpy as jnp
from jax import lax
from jax.experimental import pallas as pl
from jax.experimental.pallas import tpu as pltpu
from jax.sharding import PartitionSpec as P

KSIZE = 5
HALO = KSIZE // 2
LANES = 128
SIDES = (0, 2, 3, 4, 5, 7)
BF16 = jnp.bfloat16
F32 = jnp.float32

SCALAR, NEAR, FAR, RAW = "scalar", "near", "far", "raw"
SPACES = {SCALAR: pltpu.SMEM, NEAR: pltpu.VMEM, FAR: pltpu.HBM, RAW: pltpu.HBM}


class Loaded:
    def __init__(self, ref, copy=None):
        self.ref, self.copy = ref, copy
        if copy is not None:
            copy.start()

    def get(self):
        if self.copy is not None:
            self.copy.wait()
            self.copy = None
        return self.ref


class Stored:
    def __init__(self, ref, copy):
        self.ref, self.copy, self.started = ref, copy, False

    def send(self):
        if not self.started:
            self.copy.start()
            self.started = True


def call(kernel, ins, outs, scratch=(), time=1.0, after=(), aliases=None, limit=16):
    ins = list(ins) + [(a, RAW) for a in after]
    buffers = []
    for shape, dtype, place in [(a.shape, a.dtype, p) for a, p in ins] + list(outs):
        if place == FAR:
            buffers += [pltpu.VMEM(shape, dtype), pltpu.SemaphoreType.DMA]

    def run(*refs):
        ends = len(ins), len(ins) + len(outs), len(ins) + len(outs) + len(buffers)
        spare = list(refs[ends[1]:ends[2]])
        operands, results = [], []
        for ref, (_, place) in zip(refs, ins):
            if place == FAR:
                buffer, sem = spare.pop(0), spare.pop(0)
                operands.append(Loaded(buffer, pltpu.make_async_copy(ref, buffer, sem)))
            else:
                operands.append(Loaded(ref) if place == NEAR else ref)
        for ref, (_, _, place) in zip(refs[ends[0]:], outs):
            if place == FAR:
                buffer, sem = spare.pop(0), spare.pop(0)
                results.append(Stored(buffer, pltpu.make_async_copy(buffer, ref, sem)))
            else:
                results.append(ref)
        kernel(*operands[:len(ins) - len(after)], *results, *refs[ends[2]:])
        far = [result for result in results if isinstance(result, Stored)]
        for result in far:
            result.send()
        for result in far:
            result.copy.wait()

    return pl.pallas_call(
        run,
        out_shape=[pltpu.HBM(s, d) if p in (FAR, RAW) else jax.ShapeDtypeStruct(s, d)
                   for s, d, p in outs],
        in_specs=[pl.BlockSpec(memory_space=SPACES[p]) for _, p in ins],
        out_specs=[pl.BlockSpec(memory_space=SPACES[p]) for _, _, p in outs],
        scratch_shapes=buffers + list(scratch),
        input_output_aliases=aliases or {},
        cost_estimate=pl.CostEstimate(
            flops=int(time * 1e9), bytes_accessed=int(time * 3.5e6), transcendentals=0),
        compiler_params=pltpu.CompilerParams(vmem_limit_bytes=limit * 1024 * 1024),
    )(*[pltpu.with_memory_space_constraint(a, pltpu.HBM) if p in (FAR, RAW) else a
        for a, p in ins])


def dot(a, b):
    return lax.dot_general(a, b, (((1,), (0,)), ((), ())), preferred_element_type=F32)


def dot_nt(a, b):
    return lax.dot_general(a, b, (((1,), (1,)), ((), ())), preferred_element_type=F32)


def one_hot(index, rows):
    row = lax.broadcasted_iota(jnp.int32, (rows, index.shape[1]), 0)
    return jnp.where(row == index, 1.0, 0.0).astype(BF16)


def rim_pixels(edge):
    band_len = HALO * edge
    lane = lax.broadcasted_iota(jnp.int32, (1, 4 * band_len), 1)
    band, at = lane // band_len, lane % band_len
    side = (at // HALO) * edge + at % HALO
    pixel = jnp.where(band == 0, at, (edge - HALO) * edge + at)
    return jnp.where(band == 2, side, jnp.where(band == 3, side + edge - HALO, pixel))


def rim_lane(row, col, edge):
    band_len = HALO * edge
    side = jnp.where(col < HALO, 2 * band_len + row * HALO + col,
                     3 * band_len + row * HALO + col - (edge - HALO))
    side = jnp.where(row >= edge - HALO, band_len + (row - (edge - HALO)) * edge + col, side)
    return jnp.where(row < HALO, row * edge + col, side)


def turned_lane(row, col, quarter, edge):
    last = edge - 1
    from_row = jnp.where(quarter == 1, col, jnp.where(
        quarter == 2, last - row, jnp.where(quarter == 3, last - col, row)))
    from_col = jnp.where(quarter == 1, last - row, jnp.where(
        quarter == 2, last - col, jnp.where(quarter == 3, row, col)))
    return rim_lane(from_row, from_col, edge)


def row_halo_maps(top_turn, bottom_turn, edge):
    rim = 4 * HALO * edge
    lane = lax.broadcasted_iota(jnp.int32, (1, LANES), 1)
    up = lane - (LANES - HALO * edge)
    top = turned_lane(edge - HALO + up // edge, up % edge, top_turn, edge)
    low = turned_lane(lane // edge, lane % edge, bottom_turn, edge)
    top = jnp.where(up >= 0, top, -1)
    low = jnp.where(lane < HALO * edge, low, -1)
    return one_hot(top, rim), one_hot(low, rim)


def side_map(turns, edge):
    rim = 4 * HALO * edge
    lane = lax.broadcasted_iota(jnp.int32, (1, 2 * LANES), 1)
    row, k = lane // (2 * HALO), lane % (2 * HALO)
    above, below, right = row < HALO, row >= HALO + edge, k >= HALO
    b_row = jnp.where(above, edge - HALO + row, jnp.where(below, row - HALO - edge, row - HALO))
    b_col = jnp.where(right, k - HALO, edge - HALO + k)
    slot = jnp.where(above, 0, jnp.where(below, 4, 2)) + right.astype(jnp.int32)
    quarter = jnp.zeros_like(slot)
    for position in range(len(SIDES)):
        quarter = jnp.where(slot == position, turns[position], quarter)
    index = slot * rim + turned_lane(b_row, b_col, quarter, edge)
    index = jnp.where(row < edge + 2 * HALO, index, -1)
    return one_hot(index, len(SIDES) * rim)


def spread_map(edge, wide):
    lane = lax.broadcasted_iota(jnp.int32, (1, wide), 1)
    row = lane // edge - (LANES // edge - HALO)
    col = lane % edge
    right_row, left_row = row - 1, row + 1
    rows = edge + 2 * HALO
    right = jnp.where((right_row >= 0) & (right_row < rows), right_row * 2 * HALO + HALO + col, -1)
    left = jnp.where((left_row >= 0) & (left_row < rows),
                     left_row * 2 * HALO + col - (edge - HALO), -1)
    index = jnp.where(col < HALO, right, jnp.where(col >= edge - HALO, left, -1))
    return one_hot(index, 2 * LANES)


def side_mask(shift, shape, edge):
    col = lax.broadcasted_iota(jnp.int32, shape, 1) % edge
    return col < shift if shift > 0 else col >= edge + shift


def roll(values, shift):
    size = values.shape[1]
    return values if shift % size == 0 else pltpu.roll(values, shift % size, axis=1)


def pack_kernel(edge, x, rims):
    pick = one_hot(rim_pixels(edge), edge * edge)
    rim = dot(x.get()[...], pick).astype(BF16)
    rims.ref[...] = jnp.broadcast_to(rim[None], rims.ref.shape)


def conv_kernel(edge, place_ref, nb_ref, rot_ref, x, rims, taps,
                hidden_ref, padded, side, gathered):
    padded_ref, side_ref = padded.ref, side.ref
    rims_ref, taps_ref = rims.get(), taps.get()
    channels, pixels = hidden_ref.shape
    wide = pixels + 2 * LANES
    rim = rims_ref.shape[2]
    first = place_ref[0] * 8
    nb = [nb_ref[first + d] for d in range(8)]
    rot = [rot_ref[first + d] for d in range(8)]
    top, low = row_halo_maps(rot[1], rot[6], edge)
    padded_ref[:, :LANES] = dot(rims_ref[nb[1]], top).astype(BF16)
    padded_ref[:, LANES + pixels:] = dot(rims_ref[nb[6]], low).astype(BF16)
    for position, d in enumerate(SIDES):
        gathered[:, position * rim:(position + 1) * rim] = rims_ref[nb[d]]
    packed = dot(gathered[...], side_map([rot[d] for d in SIDES], edge)).astype(BF16)
    side_ref[...] = dot(packed, spread_map(edge, wide)).astype(BF16)
    side.send()
    padded_ref[:, LANES:LANES + pixels] = x.get()[...]
    padded.send()

    def block(i, carry):
        at = pl.multiple_of(i * 16, 16)
        xs = padded_ref[pl.ds(at, 16), :].astype(F32)
        hs = side_ref[pl.ds(at, 16), :].astype(F32)
        halves = []
        for half in (0, 8):
            x, h = xs[half:half + 8], hs[half:half + 8]
            sums = [None] * KSIZE
            for b in range(KSIZE):
                shift = b - HALO
                moved = x
                if shift:
                    moved = roll(jnp.where(side_mask(shift, x.shape, edge), h, x), -shift)
                for a in range(KSIZE):
                    tap = taps_ref[a * KSIZE + b, pl.ds(at + half, 8), :]
                    term = jnp.tile(tap, (1, wide // LANES)) * moved
                    sums[a] = term if sums[a] is None else sums[a] + term
            total = None
            for a in range(KSIZE):
                part = roll(sums[a], -(a - HALO) * edge)[:, LANES:LANES + pixels]
                total = part if total is None else total + part
            halves.append(total)
        hidden_ref[pl.ds(at, 16), :] = jnp.concatenate(halves, axis=0).astype(BF16)
        return carry

    lax.fori_loop(0, channels // 16, block, 0)


def gelu_parts(pre, grad_act):
    cumul = 0.5 * (1.0 + lax.erf(pre * 0.7071067811865476))
    slope = cumul + pre * jnp.exp(-0.5 * pre * pre) * 0.3989422804014327
    return (pre * cumul).astype(BF16), (grad_act * slope).astype(BF16)


def hidden_block(w_in_t, w_out, feats, cots, pre, slope, act, gpre):
    pre[...] = dot(w_in_t, feats[...])
    slope[...] = dot(w_out, cots[...])

    def rows(i, carry):
        at = pl.multiple_of(i * 16, 16)
        act[pl.ds(at, 16), :], gpre[pl.ds(at, 16), :] = gelu_parts(
            pre[pl.ds(at, 16), :], slope[pl.ds(at, 16), :])
        return carry

    lax.fori_loop(0, pre.shape[0] // 16, rows, 0)


def weight_kernel(feats, cots, w_in_t, w_out, part, pre, slope, act, gpre, stack, sems):
    feats, cots = feats.get(), cots.get()
    full, units = feats.shape[0], pre.shape[0]
    hidden_block(w_in_t.get()[...], w_out.get()[...], feats, cots, pre, slope, act, gpre)
    used, copies = 0, []
    for values, height in ((dot_nt(feats[...], gpre[...]), full),
                           (dot_nt(act[...], cots[...]), units)):
        first = used
        for column in range(0, values.shape[1], LANES):
            stack[used:used + height, :] = values[:, column:column + LANES].astype(BF16)
            used += height
        copies.append(pltpu.make_async_copy(
            stack.at[first:used], part.at[first:used], sems.at[len(copies)]))
        copies[-1].start()
    if used < part.shape[0]:
        stack[used:, :] = jnp.zeros((part.shape[0] - used, LANES), BF16)
        copies.append(pltpu.make_async_copy(stack.at[used:], part.at[used:], sems.at[2]))
        copies[-1].start()
    for copy in copies:
        copy.wait()


def point_kernel(feats, cots, w_in_t, w_out, w_in_own, w_out_own, x, out, grad_ref,
                 pre, slope, act, gpre):
    units = pre.shape[0]
    feats, cots, w_in_t, w_out = feats.get(), cots.get(), w_in_t.get(), w_out.get()
    branch = grad = None
    for at in range(0, w_out.shape[0], units):
        part = slice(at, at + units)
        hidden_block(w_in_t[part, :], w_out[part, :], feats, cots, pre, slope, act, gpre)
        more = dot(w_out_own.get()[:, part], act[...])
        branch = more if branch is None else branch + more
        more = dot(w_in_own.get()[:, part], gpre[...])
        grad = more if grad is None else grad + more
    out.ref[...] = (x.get()[...].astype(F32) + branch.astype(BF16).astype(F32)).astype(BF16)
    out.send()
    grad_ref[...] = grad.astype(BF16)


def prep_kernel(place_ref, w_in, w_out, w_in_t, w_in_own, w_out_own, part_in_ref, part_out_ref):
    channels, units = w_in_own.ref.shape[0], part_in_ref.shape[0]
    start = place_ref[1] * channels
    share = pl.ds(pl.multiple_of(place_ref[1] * units, units), units)
    w_in, w_out = w_in.get(), w_out.get()
    w_in_own.ref[...] = w_in[pl.ds(pl.multiple_of(start, channels), channels), :]
    w_in_own.send()
    w_in_t.ref[...] = w_in[...].astype(F32).T.astype(BF16)
    w_in_t.send()
    part_in_ref[...] = w_in_t.ref[share, :]
    part_out_ref[...] = w_out[share, :]
    row = lax.broadcasted_iota(jnp.int32, (channels, w_out.shape[1]), 0)
    column = lax.broadcasted_iota(jnp.int32, (channels, w_out.shape[1]), 1)
    pick = jnp.where(column == row + start, 1.0, 0.0).astype(BF16)
    w_out_own.ref[...] = dot_nt(pick, w_out[...]).astype(BF16)


def join_kernel(place_ref, *refs):
    pieces, out_ref = refs[:-1], refs[-1]
    for k, piece in enumerate(pieces):
        piece = piece.get()
        channels = piece.shape[0]
        start = pl.multiple_of((place_ref[1] ^ k) * channels, channels)
        out_ref[pl.ds(start, channels), :] = piece[...]


def tap_kernel(edge, grad, padded, side, tap_ref, turned_all, moved_all):
    channels, pixels = grad.ref.shape
    wide = pixels + 2 * LANES
    grad_ref = grad.get()
    moved_all[KSIZE * 16:, :] = jnp.zeros((LANES - KSIZE * 16, wide), BF16)
    same = (lax.broadcasted_iota(jnp.int32, (16, KSIZE * LANES), 1) % 16
            == lax.broadcasted_iota(jnp.int32, (16, KSIZE * LANES), 0))
    line = lax.broadcasted_iota(jnp.int32, (KSIZE * LANES, LANES), 0)
    tap = lax.broadcasted_iota(jnp.int32, (KSIZE * LANES, LANES), 1)
    used = line % LANES < KSIZE * 16
    pick = jnp.where(used & (line // LANES * KSIZE + line % LANES // 16 == tap), 1.0, 0.0).astype(BF16)
    mask = {b: side_mask(b - HALO, (16, wide), edge) for b in range(KSIZE) if b != HALO}
    lane = lax.broadcasted_iota(jnp.int32, (16, LANES), 1)
    zeros = jnp.zeros((16, LANES), F32)
    padded_ref, side_ref = padded.get(), side.get()
    found = []
    for at in range(0, channels, 16):
        g = jnp.concatenate([zeros, grad_ref[at:at + 16, :].astype(F32), zeros], axis=1)
        x = padded_ref[at:at + 16, :].astype(F32)
        h = side_ref[at:at + 16, :].astype(F32)
        for a in range(KSIZE):
            shift = a - HALO
            turned_all[a * 16:a * 16 + 16, :] = roll(g, shift * edge).astype(BF16)
            moved = roll(jnp.where(mask[a], h, x), -shift) if shift else x
            moved_all[a * 16:a * 16 + 16, :] = moved.astype(BF16)
        products = dot_nt(turned_all[...], moved_all[...])
        side_by_side = jnp.concatenate(
            [products[a * 16:a * 16 + 16, :] for a in range(KSIZE)], axis=1)
        taps = dot(jnp.where(same, side_by_side, 0.0).astype(BF16), pick)
        place = at // 16 % 4
        taps = jnp.where(lane // 32 == place, roll(taps, 32 * place), 0.0)
        if place == 0:
            found.append(taps)
        else:
            found[-1] = found[-1] + taps
    tap_ref[...] = jnp.concatenate(found, axis=0).astype(BF16)


def back_kernel(edge, place_ref, nb_ref, rot_ref, grad, cot, taps,
                accum, border, d_row, d_side, gathered):
    accum_ref, send_ref = accum.ref, border.ref
    grad_ref, taps_ref = grad.get(), taps.get()
    channels, pixels = grad_ref.shape
    wide = pixels + 2 * LANES
    tiles, _, rim = send_ref.shape
    cot_ref = cot.get()

    def block(i, carry):
        at = pl.multiple_of(i * 16, 16)
        gs = grad_ref[pl.ds(at, 16), :].astype(F32)
        zeros = jnp.zeros((8, LANES), F32)
        rows, sides = [], []
        for half in (0, 8):
            g = jnp.concatenate([zeros, gs[half:half + 8], zeros], axis=1)
            turned = [roll(g, (a - HALO) * edge) for a in range(KSIZE)]
            d_x = d_h = None
            for b in range(KSIZE):
                shift = b - HALO
                back = None
                for a in range(KSIZE):
                    weight = taps_ref[a * KSIZE + b, pl.ds(at + half, 8), :]
                    term = jnp.tile(weight, (1, wide // LANES)) * turned[a]
                    back = term if back is None else back + term
                back = roll(back, shift)
                if shift:
                    mask = side_mask(shift, back.shape, edge)
                    inside = jnp.where(mask, 0.0, back)
                    outside = jnp.where(mask, back, 0.0)
                    d_h = outside if d_h is None else d_h + outside
                    d_x = inside if d_x is None else d_x + inside
                else:
                    d_x = back if d_x is None else d_x + back
            rows.append(d_x)
            sides.append(d_h)
        d_x = jnp.concatenate(rows, axis=0)
        accum_ref[pl.ds(at, 16), :] = (
            d_x[:, LANES:LANES + pixels] + cot_ref[pl.ds(at, 16), :].astype(F32))
        d_row[pl.ds(at, 16), :LANES] = d_x[:, :LANES].astype(BF16)
        d_row[pl.ds(at, 16), LANES:] = d_x[:, LANES + pixels:].astype(BF16)
        d_side[pl.ds(at, 16), :] = jnp.concatenate(sides, axis=0).astype(BF16)
        return carry

    lax.fori_loop(0, channels // 16, block, 0)
    accum.send()
    first = place_ref[0] * 8
    nb = [nb_ref[first + d] for d in range(8)]
    rot = [rot_ref[first + d] for d in range(8)]
    gathered[...] = jnp.zeros(gathered.shape, F32)
    top, low = row_halo_maps(rot[1], rot[6], edge)
    gathered[nb[1]] += dot_nt(d_row[:, :LANES], top)
    gathered[nb[6]] += dot_nt(d_row[:, LANES:], low)
    packed = dot_nt(d_side[...], spread_map(edge, wide)).astype(BF16)
    picks = side_map([rot[d] for d in SIDES], edge)
    for position, d in enumerate(SIDES):
        gathered[nb[d]] += dot_nt(packed, picks[position * rim:(position + 1) * rim, :])

    def store(t, carry):
        send_ref[t] = gathered[t].astype(BF16)
        return carry

    lax.fori_loop(0, tiles, store, 0)


def border_kernel(edge, recv, accum, grad):
    rims = total_of(recv.get())
    high = rims.astype(BF16)
    low = (rims - high.astype(F32)).astype(BF16)
    pick = one_hot(rim_pixels(edge), edge * edge)
    added = dot_nt(high, pick) + dot_nt(low, pick)
    grad.ref[...] = (accum.get()[...] + added).astype(BF16)


def total_of(ref):
    return lax.fori_loop(1, ref.shape[0], lambda t, so_far: so_far + ref[t].astype(F32),
                         ref[0].astype(F32))


def sum_kernel(recv, tap, out):
    recv = recv.get()
    share = recv.shape[1]
    total, taps = total_of(recv).astype(BF16), tap.get()[...]

    def store(t, carry):
        out.ref[t, :share, :] = total
        out.ref[t, share:, :] = taps
        return carry

    lax.fori_loop(0, out.ref.shape[0], store, 0)


def final_kernel(which, last, share, channels, scale, place_ref, *refs):
    count = len(which)
    pieces, taps_in = refs[:count], refs[count]
    g_in, g_out, g_tap_ref, buf_in, buf_out, sems = refs[-6:]
    full, units = buf_in.shape[1:]
    tiles, rows, _ = pieces[0].ref.shape
    copies = []
    all_taps = taps_in.get()[...] if last else jnp.zeros((full, LANES), F32)
    row_of = lax.broadcasted_iota(jnp.int32, (full, LANES), 0)
    for i, k in enumerate(which):
        piece = pieces[i].get()
        owner = place_ref[1] ^ k
        start = pl.multiple_of(owner * units, units)
        for tile in range(tiles):
            for row, height, column, at, into_in in chunks(tile, share, units, full):
                values = piece[tile, row:row + height, :].astype(F32) * scale
                buffer = buf_in if into_in else buf_out
                buffer[i, at:at + height, column:column + LANES] = values
        copies.append(pltpu.make_async_copy(
            buf_in.at[i], g_in.at[:, pl.ds(start, units)], sems.at[0, i]))
        copies.append(pltpu.make_async_copy(
            buf_out.at[i], g_out.at[pl.ds(start, units)], sems.at[1, i]))
        for copy in copies[-2:]:
            copy.start()
        taps = piece[0, share:, :].astype(F32)
        for tile in range(1, tiles):
            taps = taps + piece[tile, share:, :].astype(F32)
        blocks = []
        for block in range(channels // 16):
            values = taps[block // 4 * 16:block // 4 * 16 + 16, :]
            blocks.append(roll(values, -32 * (block % 4)))
        own = jnp.concatenate(blocks * (full // channels), axis=0)
        all_taps = jnp.where(row_of // channels == owner, own, all_taps)
    if last:
        g_tap_ref[...] = all_taps.T[:KSIZE * KSIZE, :] * scale
    else:
        g_tap_ref[...] = all_taps
    for copy in copies:
        copy.wait()


def chunks(tile, share, units, full):
    inside, found = units // LANES * full, []
    row, end = tile * share, min((tile + 1) * share, 2 * units * full // LANES)
    while row < end:
        height = full if row < inside else units
        offset = row if row < inside else row - inside
        column, at = offset // height * LANES, offset % height
        count = min(end - row, height - at)
        found.append((row - tile * share, count, column, at, row < inside))
        row += count
    return found


def gather_pieces(own, groups):
    pieces = {0: own}
    bit = groups // 2
    while bit:
        swap = [(i, i ^ bit) for i in range(groups)]
        for k in list(pieces):
            pieces[k ^ bit] = lax.ppermute(pieces[k], "chan", swap)
        bit //= 2
    return [pieces[k] for k in range(groups)]


def swap_rows(values):
    return lax.all_to_all(values, "tile", 0, 0, tiled=True)


def body(inputs, grad_out, kernel, w_in, w_out, neighbours, rotations):
    channels, pixels = inputs.shape[1:]
    edge = math.isqrt(pixels)
    full, hidden = w_in.shape
    groups = lax.axis_size("chan")
    tiles = lax.axis_size("tile")
    wide = pixels + 2 * LANES
    rim = 4 * HALO * edge
    units = hidden // groups
    scale = (tiles * pixels) ** -0.5
    place = jnp.stack([lax.axis_index("tile"), lax.axis_index("chan")]).astype(jnp.int32)
    nb, rot = neighbours.reshape(-1), rotations.reshape(-1)
    x, cot = inputs[0], grad_out[0]

    [rims] = call(functools.partial(pack_kernel, edge), [(x, FAR)],
                  [((tiles, channels, rim), BF16, FAR)])
    _, kernel = lax.optimization_barrier((rims, kernel))
    taps = jnp.broadcast_to(kernel.astype(F32)[:, :, None], (KSIZE * KSIZE, channels, LANES))
    cot_pieces = gather_pieces(cot, groups)
    w_in_t, w_in_own, w_out_own, part_in, part_out = call(
        prep_kernel, [(place, SCALAR), (w_in, NEAR), (w_out, NEAR)],
        [((hidden, full), BF16, FAR)] + [((channels, hidden), BF16, FAR)] * 2
        + [((units, full), BF16, NEAR)] * 2, time=2.0, after=[rims])
    [cots] = call(join_kernel, [(place, SCALAR)] + [(piece, NEAR) for piece in cot_pieces],
                  [((full, pixels), BF16, NEAR)], time=0.6)
    rims = swap_rows(rims)

    here = [(place, SCALAR), (nb, SCALAR), (rot, SCALAR)]
    hid, padded, side = call(
        functools.partial(conv_kernel, edge), here + [(x, FAR), (rims, NEAR), (taps, NEAR)],
        [((channels, pixels), BF16, NEAR), ((channels, wide), BF16, FAR),
         ((channels, wide), BF16, FAR)],
        [pltpu.VMEM((channels, len(SIDES) * rim), BF16)], time=2.5)
    feats = lax.all_gather(hid, "chan", axis=0, tiled=True)

    used = 2 * full * units // LANES
    share = -(-used // (16 * tiles)) * 16
    tap_rows = -(-channels // 64) * 16
    values = [pltpu.VMEM((units, pixels), F32)] * 2 + [pltpu.VMEM((units, pixels), BF16)] * 2
    [part] = call(
        weight_kernel, [(feats, NEAR), (cots, NEAR), (part_in, NEAR), (part_out, NEAR)],
        [((tiles * share, LANES), BF16, RAW)],
        values + [pltpu.VMEM((tiles * share, LANES), BF16), pltpu.SemaphoreType.DMA((3,))],
        time=2.2)
    part = swap_rows(part.reshape(tiles, share, LANES))

    outputs, grad_hid = call(
        point_kernel,
        [(feats, NEAR), (cots, NEAR), (w_in_t, FAR), (w_out, FAR), (w_in_own, FAR),
         (w_out_own, FAR), (x, FAR)],
        [((channels, pixels), BF16, FAR), ((channels, pixels), BF16, NEAR)], values, time=5.5)
    [tap_part] = call(
        functools.partial(tap_kernel, edge), [(grad_hid, NEAR), (padded, FAR), (side, FAR)],
        [((tap_rows, LANES), BF16, NEAR)],
        [pltpu.VMEM((KSIZE * 16, wide), BF16), pltpu.VMEM((LANES, wide), BF16)], time=1.5)
    [mine] = call(sum_kernel, [(part, NEAR), (tap_part, NEAR)],
                  [((tiles, share + tap_rows, LANES), BF16, FAR)])
    weights = swap_rows(mine)

    accum, border = call(
        functools.partial(back_kernel, edge), here + [(grad_hid, NEAR), (cot, FAR), (taps, NEAR)],
        [((channels, pixels), F32, FAR), ((tiles, channels, rim), BF16, FAR)],
        [pltpu.VMEM((channels, 2 * LANES), BF16), pltpu.VMEM((channels, wide), BF16),
         pltpu.VMEM((tiles, channels, rim), F32)], time=4.0, after=[mine])
    weights, border = lax.optimization_barrier((weights, border))
    border = swap_rows(border)
    pieces = gather_pieces(weights, groups)
    grads, ends = [], [(0, groups, 2), (1, groups, 2)]
    for last, end in enumerate(ends):
        which = list(range(*end))
        tap_shape = (KSIZE * KSIZE, full) if last else (full, LANES)
        grads = call(
            functools.partial(final_kernel, which, last, share, channels, scale),
            [(place, SCALAR)] + [(pieces[k], NEAR) for k in which]
            + ([(grads[2], NEAR), (grads[0], RAW), (grads[1], RAW)] if last else []),
            [((full, hidden), F32, RAW), ((hidden, full), F32, RAW), (tap_shape, F32, NEAR)],
            [pltpu.VMEM((len(which), full, units), F32), pltpu.VMEM((len(which), units, full), F32),
             pltpu.SemaphoreType.DMA((2, len(which)))],
            time=1.3, aliases={2 + len(which): 0, 3 + len(which): 1} if last else None)
    [grad_in] = call(functools.partial(border_kernel, edge), [(border, NEAR), (accum, FAR)],
                     [((channels, pixels), BF16, FAR)])
    return (outputs[None], grad_in[None], *grads)


def solution(mesh):
    return jax.shard_map(
        body,
        mesh=mesh,
        in_specs=(
            P("tile", "chan", None),
            P("tile", "chan", None),
            P(None, "chan"),
            P(),
            P(),
            P(),
            P(),
        ),
        out_specs=(P("tile", "chan", None), P("tile", "chan", None), P(), P(), P()),
        check_vma=False,
    )
```

```python
import functools
import math

import jax
import jax.numpy as jnp
from jax import lax
from jax.experimental import pallas as pl
from jax.experimental.pallas import tpu as pltpu
from jax.sharding import PartitionSpec as P

KSIZE = 5
HALO = KSIZE // 2
LANES = 128
SIDES = (0, 2, 3, 4, 5, 7)
BF16 = jnp.bfloat16
F32 = jnp.float32

SCALAR, NEAR, FAR, RAW = "scalar", "near", "far", "raw"
SPACES = {SCALAR: pltpu.SMEM, NEAR: pltpu.VMEM, FAR: pltpu.HBM, RAW: pltpu.HBM}


class Loaded:
    def __init__(self, ref, copy=None):
        self.ref, self.copy = ref, copy
        if copy is not None:
            copy.start()

    def get(self):
        if self.copy is not None:
            self.copy.wait()
            self.copy = None
        return self.ref


class Stored:
    def __init__(self, ref, copy):
        self.ref, self.copy, self.started = ref, copy, False

    def send(self):
        if not self.started:
            self.copy.start()
            self.started = True


def call(kernel, ins, outs, scratch=(), time=1.0, after=(), aliases=None, limit=16):
    ins = list(ins) + list(after)
    buffers = []
    for shape, dtype, place in [(a.shape, a.dtype, p) for a, p in ins] + list(outs):
        if place == FAR:
            buffers += [pltpu.VMEM(shape, dtype), pltpu.SemaphoreType.DMA]

    def run(*refs):
        ends = len(ins), len(ins) + len(outs), len(ins) + len(outs) + len(buffers)
        spare = list(refs[ends[1]:ends[2]])
        operands, results = [], []
        for ref, (_, place) in zip(refs, ins):
            if place == FAR:
                buffer, sem = spare.pop(0), spare.pop(0)
                operands.append(Loaded(buffer, pltpu.make_async_copy(ref, buffer, sem)))
            else:
                operands.append(Loaded(ref) if place == NEAR else ref)
        for ref, (_, _, place) in zip(refs[ends[0]:], outs):
            if place == FAR:
                buffer, sem = spare.pop(0), spare.pop(0)
                results.append(Stored(buffer, pltpu.make_async_copy(buffer, ref, sem)))
            else:
                results.append(ref)
        kernel(*operands[:len(ins) - len(after)], *results, *refs[ends[2]:])
        far = [result for result in results if isinstance(result, Stored)]
        for result in far:
            result.send()
        for result in far:
            result.copy.wait()

    return pl.pallas_call(
        run,
        out_shape=[pltpu.HBM(s, d) if p in (FAR, RAW) else jax.ShapeDtypeStruct(s, d)
                   for s, d, p in outs],
        in_specs=[pl.BlockSpec(memory_space=SPACES[p]) for _, p in ins],
        out_specs=[pl.BlockSpec(memory_space=SPACES[p]) for _, _, p in outs],
        scratch_shapes=buffers + list(scratch),
        input_output_aliases=aliases or {},
        cost_estimate=pl.CostEstimate(
            flops=int(time * 1e9), bytes_accessed=int(time * 3.5e6), transcendentals=0),
        compiler_params=pltpu.CompilerParams(vmem_limit_bytes=limit * 1024 * 1024),
    )(*[pltpu.with_memory_space_constraint(a, pltpu.HBM) if p in (FAR, RAW) else a
        for a, p in ins])


def dot(a, b):
    return lax.dot_general(a, b, (((1,), (0,)), ((), ())), preferred_element_type=F32)


def dot_nt(a, b):
    return lax.dot_general(a, b, (((1,), (1,)), ((), ())), preferred_element_type=F32)


def one_hot(index, rows):
    row = lax.broadcasted_iota(jnp.int32, (rows, index.shape[1]), 0)
    return jnp.where(row == index, 1.0, 0.0).astype(BF16)


def rim_pixels(edge):
    band_len = HALO * edge
    lane = lax.broadcasted_iota(jnp.int32, (1, 4 * band_len), 1)
    band, at = lane // band_len, lane % band_len
    side = (at // HALO) * edge + at % HALO
    pixel = jnp.where(band == 0, at, (edge - HALO) * edge + at)
    return jnp.where(band == 2, side, jnp.where(band == 3, side + edge - HALO, pixel))


def rim_lane(row, col, edge):
    band_len = HALO * edge
    side = jnp.where(col < HALO, 2 * band_len + row * HALO + col,
                     3 * band_len + row * HALO + col - (edge - HALO))
    side = jnp.where(row >= edge - HALO, band_len + (row - (edge - HALO)) * edge + col, side)
    return jnp.where(row < HALO, row * edge + col, side)


def turned_lane(row, col, quarter, edge):
    last = edge - 1
    from_row = jnp.where(quarter == 1, col, jnp.where(
        quarter == 2, last - row, jnp.where(quarter == 3, last - col, row)))
    from_col = jnp.where(quarter == 1, last - row, jnp.where(
        quarter == 2, last - col, jnp.where(quarter == 3, row, col)))
    return rim_lane(from_row, from_col, edge)


def row_halo_maps(top_turn, bottom_turn, edge):
    rim = 4 * HALO * edge
    lane = lax.broadcasted_iota(jnp.int32, (1, LANES), 1)
    up = lane - (LANES - HALO * edge)
    top = turned_lane(edge - HALO + up // edge, up % edge, top_turn, edge)
    low = turned_lane(lane // edge, lane % edge, bottom_turn, edge)
    top = jnp.where(up >= 0, top, -1)
    low = jnp.where(lane < HALO * edge, low, -1)
    return one_hot(top, rim), one_hot(low, rim)


def side_map(turns, edge):
    rim = 4 * HALO * edge
    lane = lax.broadcasted_iota(jnp.int32, (1, 2 * LANES), 1)
    row, k = lane // (2 * HALO), lane % (2 * HALO)
    above, below, right = row < HALO, row >= HALO + edge, k >= HALO
    b_row = jnp.where(above, edge - HALO + row, jnp.where(below, row - HALO - edge, row - HALO))
    b_col = jnp.where(right, k - HALO, edge - HALO + k)
    slot = jnp.where(above, 0, jnp.where(below, 4, 2)) + right.astype(jnp.int32)
    quarter = jnp.zeros_like(slot)
    for position in range(len(SIDES)):
        quarter = jnp.where(slot == position, turns[position], quarter)
    index = slot * rim + turned_lane(b_row, b_col, quarter, edge)
    index = jnp.where(row < edge + 2 * HALO, index, -1)
    return one_hot(index, len(SIDES) * rim)


def spread_map(edge, wide):
    lane = lax.broadcasted_iota(jnp.int32, (1, wide), 1)
    row = lane // edge - (LANES // edge - HALO)
    col = lane % edge
    right_row, left_row = row - 1, row + 1
    rows = edge + 2 * HALO
    right = jnp.where((right_row >= 0) & (right_row < rows), right_row * 2 * HALO + HALO + col, -1)
    left = jnp.where((left_row >= 0) & (left_row < rows),
                     left_row * 2 * HALO + col - (edge - HALO), -1)
    index = jnp.where(col < HALO, right, jnp.where(col >= edge - HALO, left, -1))
    return one_hot(index, 2 * LANES)


def side_mask(shift, shape, edge):
    col = lax.broadcasted_iota(jnp.int32, shape, 1) % edge
    return col < shift if shift > 0 else col >= edge + shift


def roll(values, shift):
    size = values.shape[1]
    return values if shift % size == 0 else pltpu.roll(values, shift % size, axis=1)


def pack_kernel(edge, x, rims, rim, sems):
    pick = one_hot(rim_pixels(edge), edge * edge)
    rim[...] = dot(x.get()[...], pick).astype(BF16)
    copies = [pltpu.make_async_copy(rim, rims.at[t], sems.at[t]) for t in range(rims.shape[0])]
    for copy in copies:
        copy.start()
    for copy in copies:
        copy.wait()


def conv_kernel(edge, place_ref, nb_ref, rot_ref, x, rims, taps,
                hidden_ref, padded, side, gathered):
    padded_ref, side_ref = padded.ref, side.ref
    rims_ref, taps_ref = rims.get(), taps.get()
    channels, pixels = hidden_ref.shape
    wide = pixels + 2 * LANES
    rim = rims_ref.shape[2]
    nb = [nb_ref[place_ref[0], d] for d in range(8)]
    rot = [rot_ref[place_ref[0], d] for d in range(8)]
    top, low = row_halo_maps(rot[1], rot[6], edge)
    padded_ref[:, :LANES] = dot(rims_ref[nb[1]], top).astype(BF16)
    padded_ref[:, LANES + pixels:] = dot(rims_ref[nb[6]], low).astype(BF16)
    for position, d in enumerate(SIDES):
        gathered[:, position * rim:(position + 1) * rim] = rims_ref[nb[d]]
    packed = dot(gathered[...], side_map([rot[d] for d in SIDES], edge)).astype(BF16)
    side_ref[...] = dot(packed, spread_map(edge, wide)).astype(BF16)
    side.send()
    padded_ref[:, LANES:LANES + pixels] = x.get()[...]
    padded.send()

    def block(i, carry):
        at = pl.multiple_of(i * 16, 16)
        xs = padded_ref[pl.ds(at, 16), :].astype(F32)
        hs = side_ref[pl.ds(at, 16), :].astype(F32)
        halves = []
        for half in (0, 8):
            x, h = xs[half:half + 8], hs[half:half + 8]
            sums = [None] * KSIZE
            for b in range(KSIZE):
                shift = b - HALO
                moved = x
                if shift:
                    moved = roll(jnp.where(side_mask(shift, x.shape, edge), h, x), -shift)
                for a in range(KSIZE):
                    tap = taps_ref[a * KSIZE + b, pl.ds(at + half, 8), :]
                    term = jnp.tile(tap, (1, wide // LANES)) * moved
                    sums[a] = term if sums[a] is None else sums[a] + term
            total = None
            for a in range(KSIZE):
                part = roll(sums[a], -(a - HALO) * edge)[:, LANES:LANES + pixels]
                total = part if total is None else total + part
            halves.append(total)
        hidden_ref[pl.ds(at, 16), :] = jnp.concatenate(halves, axis=0).astype(BF16)
        return carry

    lax.fori_loop(0, channels // 16, block, 0)


def gelu_parts(pre, grad_act):
    cumul = 0.5 * (1.0 + lax.erf(pre * 0.7071067811865476))
    slope = cumul + pre * jnp.exp(-0.5 * pre * pre) * 0.3989422804014327
    return (pre * cumul).astype(BF16), (grad_act * slope).astype(BF16)


def hidden_block(w_in_t, w_out, feats, cots, pre, slope, act, gpre):
    pre[...] = dot(w_in_t, feats[...])
    slope[...] = dot(w_out, cots[...])

    def rows(i, carry):
        at = pl.multiple_of(i * 16, 16)
        act[pl.ds(at, 16), :], gpre[pl.ds(at, 16), :] = gelu_parts(
            pre[pl.ds(at, 16), :], slope[pl.ds(at, 16), :])
        return carry

    lax.fori_loop(0, pre.shape[0] // 16, rows, 0)


def weight_kernel(feats, cots, w_in_t, w_out, part, pre, slope, act, gpre, stack, sems):
    feats, cots = feats.get(), cots.get()
    full, units = feats.shape[0], pre.shape[0]
    hidden_block(w_in_t.get()[...], w_out.get()[...], feats, cots, pre, slope, act, gpre)
    used, copies = 0, []
    for values, height in ((dot_nt(feats[...], gpre[...]), full),
                           (dot_nt(act[...], cots[...]), units)):
        first = used
        for column in range(0, values.shape[1], LANES):
            stack[used:used + height, :] = values[:, column:column + LANES].astype(BF16)
            used += height
        copies.append(pltpu.make_async_copy(
            stack.at[first:used], part.at[first:used], sems.at[len(copies)]))
        copies[-1].start()
    if used < part.shape[0]:
        stack[used:, :] = jnp.zeros((part.shape[0] - used, LANES), BF16)
        copies.append(pltpu.make_async_copy(stack.at[used:], part.at[used:], sems.at[2]))
        copies[-1].start()
    for copy in copies:
        copy.wait()


def point_kernel(edge, place_ref, feats, cots, w_in, w_in_t, w_out, x, padded, side,
                 out, grad_ref, tap_ref, pre, slope, act, gpre, turned_all, moved_all):
    units, channels = pre.shape[0], grad_ref.shape[0]
    feats, cots, w_in_t, w_out = feats.get(), cots.get(), w_in_t.get(), w_out.get()
    start = place_ref[1] * channels
    own = pl.ds(pl.multiple_of(start, channels), channels)
    row = lax.broadcasted_iota(jnp.int32, (channels, w_out.shape[1]), 0)
    column = lax.broadcasted_iota(jnp.int32, (channels, w_out.shape[1]), 1)
    pick = jnp.where(column == row + start, 1.0, 0.0).astype(BF16)
    branch = grad = None
    for at in range(0, w_out.shape[0], units):
        part = slice(at, at + units)
        hidden_block(w_in_t[part, :], w_out[part, :], feats, cots, pre, slope, act, gpre)
        more = dot(dot_nt(pick, w_out[part, :]).astype(BF16), act[...])
        branch = more if branch is None else branch + more
        more = dot(w_in.get()[own, part], gpre[...])
        grad = more if grad is None else grad + more
    out.ref[...] = (x.get()[...].astype(F32) + branch.astype(BF16).astype(F32)).astype(BF16)
    out.send()
    grad_ref[...] = grad.astype(BF16)
    tap_terms(edge, grad_ref, padded.get(), side.get(), tap_ref, turned_all, moved_all)


def prep_kernel(place_ref, w_in, w_out, w_in_t_ref, part_in_ref, part_out_ref):
    w_in_t_ref[...] = w_in.get()[...].astype(F32).T.astype(BF16)
    units = part_in_ref.shape[0]
    mine = pl.ds(pl.multiple_of(place_ref[1] * units, units), units)
    part_in_ref[...] = w_in_t_ref[mine, :]
    part_out_ref[...] = w_out.get()[mine, :]


def join_kernel(place_ref, *refs):
    pieces, out_ref = refs[:-1], refs[-1]
    for k, piece in enumerate(pieces):
        piece = piece.get()
        channels = piece.shape[0]
        start = pl.multiple_of((place_ref[1] ^ k) * channels, channels)
        out_ref[pl.ds(start, channels), :] = piece[...]


def tap_terms(edge, grad_ref, padded_ref, side_ref, tap_ref, turned_all, moved_all):
    channels, pixels = grad_ref.shape
    wide = pixels + 2 * LANES
    moved_all[KSIZE * 16:, :] = jnp.zeros((LANES - KSIZE * 16, wide), BF16)
    same = (lax.broadcasted_iota(jnp.int32, (16, KSIZE * LANES), 1) % 16
            == lax.broadcasted_iota(jnp.int32, (16, KSIZE * LANES), 0))
    line = lax.broadcasted_iota(jnp.int32, (KSIZE * LANES, LANES), 0)
    tap = lax.broadcasted_iota(jnp.int32, (KSIZE * LANES, LANES), 1)
    used = line % LANES < KSIZE * 16
    pick = jnp.where(used & (line // LANES * KSIZE + line % LANES // 16 == tap), 1.0, 0.0).astype(BF16)
    mask = {b: side_mask(b - HALO, (16, wide), edge) for b in range(KSIZE) if b != HALO}
    lane = lax.broadcasted_iota(jnp.int32, (16, LANES), 1)
    zeros = jnp.zeros((16, LANES), F32)
    found = []
    for at in range(0, channels, 16):
        g = jnp.concatenate([zeros, grad_ref[at:at + 16, :].astype(F32), zeros], axis=1)
        x = padded_ref[at:at + 16, :].astype(F32)
        h = side_ref[at:at + 16, :].astype(F32)
        for a in range(KSIZE):
            shift = a - HALO
            turned_all[a * 16:a * 16 + 16, :] = roll(g, shift * edge).astype(BF16)
            moved = roll(jnp.where(mask[a], h, x), -shift) if shift else x
            moved_all[a * 16:a * 16 + 16, :] = moved.astype(BF16)
        products = dot_nt(turned_all[...], moved_all[...])
        side_by_side = jnp.concatenate(
            [products[a * 16:a * 16 + 16, :] for a in range(KSIZE)], axis=1)
        taps = dot(jnp.where(same, side_by_side, 0.0).astype(BF16), pick)
        place = at // 16 % 4
        taps = jnp.where(lane // 32 == place, roll(taps, 32 * place), 0.0)
        if place == 0:
            found.append(taps)
        else:
            found[-1] = found[-1] + taps
    tap_ref[...] = jnp.concatenate(found, axis=0).astype(BF16)


def back_kernel(edge, place_ref, nb_ref, rot_ref, grad, taps,
                accum, border, d_row, d_side, gathered):
    accum_ref, send_ref = accum.ref, border.ref
    grad_ref, taps_ref = grad.get(), taps.get()
    channels, pixels = grad_ref.shape
    wide = pixels + 2 * LANES
    tiles, _, rim = send_ref.shape

    def block(i, carry):
        at = pl.multiple_of(i * 16, 16)
        gs = grad_ref[pl.ds(at, 16), :].astype(F32)
        zeros = jnp.zeros((8, LANES), F32)
        rows, sides = [], []
        for half in (0, 8):
            g = jnp.concatenate([zeros, gs[half:half + 8], zeros], axis=1)
            turned = [roll(g, (a - HALO) * edge) for a in range(KSIZE)]
            d_x = d_h = None
            for b in range(KSIZE):
                shift = b - HALO
                back = None
                for a in range(KSIZE):
                    weight = taps_ref[a * KSIZE + b, pl.ds(at + half, 8), :]
                    term = jnp.tile(weight, (1, wide // LANES)) * turned[a]
                    back = term if back is None else back + term
                back = roll(back, shift)
                if shift:
                    mask = side_mask(shift, back.shape, edge)
                    inside = jnp.where(mask, 0.0, back)
                    outside = jnp.where(mask, back, 0.0)
                    d_h = outside if d_h is None else d_h + outside
                    d_x = inside if d_x is None else d_x + inside
                else:
                    d_x = back if d_x is None else d_x + back
            rows.append(d_x)
            sides.append(d_h)
        d_x = jnp.concatenate(rows, axis=0)
        accum_ref[pl.ds(at, 16), :] = d_x[:, LANES:LANES + pixels]
        d_row[pl.ds(at, 16), :LANES] = d_x[:, :LANES].astype(BF16)
        d_row[pl.ds(at, 16), LANES:] = d_x[:, LANES + pixels:].astype(BF16)
        d_side[pl.ds(at, 16), :] = jnp.concatenate(sides, axis=0).astype(BF16)
        return carry

    lax.fori_loop(0, channels // 16, block, 0)
    accum.send()
    nb = [nb_ref[place_ref[0], d] for d in range(8)]
    rot = [rot_ref[place_ref[0], d] for d in range(8)]
    gathered[...] = jnp.zeros(gathered.shape, F32)
    top, low = row_halo_maps(rot[1], rot[6], edge)
    gathered[nb[1]] += dot_nt(d_row[:, :LANES], top)
    gathered[nb[6]] += dot_nt(d_row[:, LANES:], low)
    packed = dot_nt(d_side[...], spread_map(edge, wide)).astype(BF16)
    picks = side_map([rot[d] for d in SIDES], edge)
    for position, d in enumerate(SIDES):
        gathered[nb[d]] += dot_nt(packed, picks[position * rim:(position + 1) * rim, :])

    def store(t, carry):
        send_ref[t] = gathered[t].astype(BF16)
        return carry

    lax.fori_loop(0, tiles, store, 0)


def border_kernel(edge, recv, accum, cot, grad):
    rims = total_of(recv.get())
    high = rims.astype(BF16)
    low = (rims - high.astype(F32)).astype(BF16)
    pick = one_hot(rim_pixels(edge), edge * edge)
    added = dot_nt(high, pick) + dot_nt(low, pick)
    added = added + cot.get()[...].astype(F32)
    grad.ref[...] = (accum.get()[...] + added).astype(BF16)


def total_of(ref):
    return lax.fori_loop(1, ref.shape[0], lambda t, so_far: so_far + ref[t].astype(F32),
                         ref[0].astype(F32))


def sum_kernel(recv, tap, out):
    recv = recv.get()
    share = recv.shape[1]
    total, taps = total_of(recv).astype(BF16), tap.get()[...]

    def store(t, carry):
        out.ref[t, :share, :] = total
        out.ref[t, share:, :] = taps
        return carry

    lax.fori_loop(0, out.ref.shape[0], store, 0)


def final_kernel(which, last, share, channels, scale, place_ref, *refs):
    count = len(which)
    pieces, taps_in = refs[:count], refs[count]
    g_in, g_out, g_tap_ref, buf_in, buf_out, sems = refs[-6:]
    full, units = buf_in.shape[1:]
    tiles, rows, _ = pieces[0].ref.shape
    copies = []
    all_taps = taps_in.get()[...] if last else jnp.zeros((full, LANES), F32)
    row_of = lax.broadcasted_iota(jnp.int32, (full, LANES), 0)
    for i, k in enumerate(which):
        piece = pieces[i].get()
        owner = place_ref[1] ^ k
        start = pl.multiple_of(owner * units, units)
        for in_in, buffer, target in ((True, buf_in, g_in.at[:, pl.ds(start, units)]),
                                      (False, buf_out, g_out.at[pl.ds(start, units)])):
            for tile in range(tiles):
                for row, height, column, at, into_in in chunks(tile, share, units, full):
                    if into_in == in_in:
                        values = piece[tile, row:row + height, :].astype(F32) * scale
                        buffer[i, at:at + height, column:column + LANES] = values
            copies.append(pltpu.make_async_copy(buffer.at[i], target, sems.at[int(in_in), i]))
            copies[-1].start()
        taps = piece[0, share:, :].astype(F32)
        for tile in range(1, tiles):
            taps = taps + piece[tile, share:, :].astype(F32)
        blocks = []
        for block in range(channels // 16):
            values = taps[block // 4 * 16:block // 4 * 16 + 16, :]
            blocks.append(roll(values, -32 * (block % 4)))
        own = jnp.concatenate(blocks * (full // channels), axis=0)
        all_taps = jnp.where(row_of // channels == owner, own, all_taps)
    if last:
        g_tap_ref[...] = all_taps.T[:KSIZE * KSIZE, :] * scale
    else:
        g_tap_ref[...] = all_taps
    for copy in copies:
        copy.wait()


def chunks(tile, share, units, full):
    inside, found = units // LANES * full, []
    row, end = tile * share, min((tile + 1) * share, 2 * units * full // LANES)
    while row < end:
        height = full if row < inside else units
        offset = row if row < inside else row - inside
        column, at = offset // height * LANES, offset % height
        count = min(end - row, height - at)
        found.append((row - tile * share, count, column, at, row < inside))
        row += count
    return found


def gather_pieces(own, groups):
    pieces = {0: own}
    bit = groups // 2
    while bit:
        swap = [(i, i ^ bit) for i in range(groups)]
        for k in list(pieces):
            pieces[k ^ bit] = lax.ppermute(pieces[k], "chan", swap)
        bit //= 2
    return [pieces[k] for k in range(groups)]


def swap_rows(values):
    return lax.all_to_all(values, "tile", 0, 0, tiled=True)


def body(inputs, grad_out, kernel, w_in, w_out, neighbours, rotations):
    channels, pixels = inputs.shape[1:]
    edge = math.isqrt(pixels)
    full, hidden = w_in.shape
    groups = lax.axis_size("chan")
    tiles = lax.axis_size("tile")
    wide = pixels + 2 * LANES
    rim = 4 * HALO * edge
    units = hidden // groups
    scale = (tiles * pixels) ** -0.5
    place = jnp.stack([lax.axis_index("tile"), lax.axis_index("chan")]).astype(jnp.int32)
    x, cot = inputs[0], grad_out[0]

    [rims] = call(functools.partial(pack_kernel, edge), [(x, FAR)],
                  [((tiles, channels, rim), BF16, RAW)],
                  [pltpu.VMEM((channels, rim), BF16), pltpu.SemaphoreType.DMA((tiles,))])
    _, kernel = lax.optimization_barrier((rims, kernel))
    taps = jnp.broadcast_to(kernel.astype(F32)[:, :, None], (KSIZE * KSIZE, channels, LANES))
    cot_pieces = gather_pieces(cot, groups)
    w_in_t, part_in, part_out = call(
        prep_kernel, [(place, SCALAR), (w_in, NEAR), (w_out, NEAR)],
        [((hidden, full), BF16, NEAR)] + [((units, full), BF16, NEAR)] * 2, time=0.7,
        after=[(rims, RAW), (taps, NEAR)])
    rims = swap_rows(rims)

    here = [(place, SCALAR), (neighbours, SCALAR), (rotations, SCALAR)]
    hid, padded, side = call(
        functools.partial(conv_kernel, edge), here + [(x, FAR), (rims, NEAR), (taps, NEAR)],
        [((channels, pixels), BF16, NEAR), ((channels, wide), BF16, FAR),
         ((channels, wide), BF16, FAR)],
        [pltpu.VMEM((channels, len(SIDES) * rim), BF16)], time=2.5, after=[(part_in, NEAR)])
    feats = lax.all_gather(hid, "chan", axis=0, tiled=True)
    [cots] = call(join_kernel, [(place, SCALAR)] + [(piece, NEAR) for piece in cot_pieces],
                  [((full, pixels), BF16, NEAR)], time=0.6, after=[(feats, NEAR)])

    used = 2 * full * units // LANES
    share = -(-used // (16 * tiles)) * 16
    tap_rows = -(-channels // 64) * 16
    values = [pltpu.VMEM((units, pixels), F32)] * 2 + [pltpu.VMEM((units, pixels), BF16)] * 2
    [part] = call(
        weight_kernel,
        [(feats, NEAR), (cots, NEAR), (part_in, NEAR), (part_out, NEAR)],
        [((tiles * share, LANES), BF16, RAW)],
        values + [pltpu.VMEM((tiles * share, LANES), BF16), pltpu.SemaphoreType.DMA((3,))],
        time=2.2)
    part = swap_rows(part.reshape(tiles, share, LANES))

    outputs, grad_hid, tap_part = call(
        functools.partial(point_kernel, edge),
        [(place, SCALAR), (feats, NEAR), (cots, NEAR), (w_in, FAR), (w_in_t, NEAR), (w_out, NEAR),
         (x, FAR), (padded, FAR), (side, FAR)],
        [((channels, pixels), BF16, FAR), ((channels, pixels), BF16, NEAR),
         ((tap_rows, LANES), BF16, NEAR)],
        values + [pltpu.VMEM((KSIZE * 16, wide), BF16), pltpu.VMEM((LANES, wide), BF16)],
        time=7.0)
    [mine] = call(sum_kernel, [(part, NEAR), (tap_part, NEAR)],
                  [((tiles, share + tap_rows, LANES), BF16, FAR)])
    weights = swap_rows(mine)

    accum, border = call(
        functools.partial(back_kernel, edge), here + [(grad_hid, NEAR), (taps, NEAR)],
        [((channels, pixels), F32, FAR), ((tiles, channels, rim), BF16, FAR)],
        [pltpu.VMEM((channels, 2 * LANES), BF16), pltpu.VMEM((channels, wide), BF16),
         pltpu.VMEM((tiles, channels, rim), F32)], time=4.0, after=[(mine, RAW)])
    weights, border = lax.optimization_barrier((weights, border))
    border = swap_rows(border)
    pieces = gather_pieces(weights, groups)
    grads, ends = [], [(0, groups, 2), (1, groups, 2)]
    for last, end in enumerate(ends):
        which = list(range(*end))
        tap_shape = (KSIZE * KSIZE, full) if last else (full, LANES)
        grads = call(
            functools.partial(final_kernel, which, last, share, channels, scale),
            [(place, SCALAR)] + [(pieces[k], NEAR) for k in which]
            + ([(grads[2], NEAR), (grads[0], RAW), (grads[1], RAW)] if last else []),
            [((full, hidden), F32, RAW), ((hidden, full), F32, RAW), (tap_shape, F32, NEAR)],
            [pltpu.VMEM((len(which), full, units), F32), pltpu.VMEM((len(which), units, full), F32),
             pltpu.SemaphoreType.DMA((2, len(which)))],
            time=1.3, aliases={2 + len(which): 0, 3 + len(which): 1} if last else None)
    [grad_in] = call(functools.partial(border_kernel, edge), [(border, NEAR), (accum, FAR), (cot, FAR)],
                     [((channels, pixels), BF16, FAR)], after=[(grads[0], RAW)])
    return (outputs[None], grad_in[None], *grads)


def solution(mesh):
    return jax.shard_map(
        body,
        mesh=mesh,
        in_specs=(
            P("tile", "chan", None),
            P("tile", "chan", None),
            P(None, "chan"),
            P(),
            P(),
            P(),
            P(),
        ),
        out_specs=(P("tile", "chan", None), P("tile", "chan", None), P(), P(), P()),
        check_vma=False,
    )
```

```python
import functools
import math

import jax
import jax.numpy as jnp
from jax import lax
from jax.experimental import pallas as pl
from jax.experimental.pallas import tpu as pltpu
from jax.sharding import PartitionSpec as P

KSIZE = 5
HALO = KSIZE // 2
LANES = 128
SIDES = (0, 2, 3, 4, 5, 7)
BF16 = jnp.bfloat16
F32 = jnp.float32

NEAR, FAR, RAW = "near", "far", "raw"
SPACES = {NEAR: pltpu.VMEM, FAR: pltpu.HBM, RAW: pltpu.HBM}


class Loaded:
    def __init__(self, ref, copy=None):
        self.ref, self.copy = ref, copy
        if copy is not None:
            copy.start()

    def get(self):
        if self.copy is not None:
            self.copy.wait()
            self.copy = None
        return self.ref


class Stored:
    def __init__(self, ref, copy):
        self.ref, self.copy, self.started = ref, copy, False

    def send(self):
        if not self.started:
            self.copy.start()
            self.started = True


def call(kernel, ins, outs, scratch=(), time=1.0, after=(), aliases=None, limit=16):
    ins = list(ins) + list(after)
    buffers = []
    for shape, dtype, place in [(a.shape, a.dtype, p) for a, p in ins] + list(outs):
        if place == FAR:
            buffers += [pltpu.VMEM(shape, dtype), pltpu.SemaphoreType.DMA]

    def run(*refs):
        ends = len(ins), len(ins) + len(outs), len(ins) + len(outs) + len(buffers)
        spare = list(refs[ends[1]:ends[2]])
        operands, results = [], []
        for ref, (_, place) in zip(refs, ins):
            if place == FAR:
                buffer, sem = spare.pop(0), spare.pop(0)
                operands.append(Loaded(buffer, pltpu.make_async_copy(ref, buffer, sem)))
            else:
                operands.append(Loaded(ref) if place == NEAR else ref)
        for ref, (_, _, place) in zip(refs[ends[0]:], outs):
            if place == FAR:
                buffer, sem = spare.pop(0), spare.pop(0)
                results.append(Stored(buffer, pltpu.make_async_copy(buffer, ref, sem)))
            else:
                results.append(ref)
        kernel(*operands[:len(ins) - len(after)], *results, *refs[ends[2]:])
        far = [result for result in results if isinstance(result, Stored)]
        for result in far:
            result.send()
        for result in far:
            result.copy.wait()

    return pl.pallas_call(
        run,
        out_shape=[pltpu.HBM(s, d) if p in (FAR, RAW) else jax.ShapeDtypeStruct(s, d)
                   for s, d, p in outs],
        in_specs=[pl.BlockSpec(memory_space=SPACES[p]) for _, p in ins],
        out_specs=[pl.BlockSpec(memory_space=SPACES[p]) for _, _, p in outs],
        scratch_shapes=buffers + list(scratch),
        input_output_aliases=aliases or {},
        cost_estimate=pl.CostEstimate(
            flops=int(time * 1e9), bytes_accessed=int(time * 3.5e6), transcendentals=0),
        compiler_params=pltpu.CompilerParams(vmem_limit_bytes=limit * 1024 * 1024),
    )(*[pltpu.with_memory_space_constraint(a, pltpu.HBM) if p in (FAR, RAW) else a
        for a, p in ins])


def tile_row(table):
    row = table.get()[pl.ds(lax.axis_index("tile"), 1), :]
    return [row[0, d] for d in range(8)]


def dot(a, b):
    return lax.dot_general(a, b, (((1,), (0,)), ((), ())), preferred_element_type=F32)


def dot_nt(a, b):
    return lax.dot_general(a, b, (((1,), (1,)), ((), ())), preferred_element_type=F32)


def one_hot(index, rows):
    row = lax.broadcasted_iota(jnp.int32, (rows, index.shape[1]), 0)
    return jnp.where(row == index, 1.0, 0.0).astype(BF16)


def rim_pixels(edge):
    band_len = HALO * edge
    lane = lax.broadcasted_iota(jnp.int32, (1, 4 * band_len), 1)
    band, at = lane // band_len, lane % band_len
    side = (at // HALO) * edge + at % HALO
    pixel = jnp.where(band == 0, at, (edge - HALO) * edge + at)
    return jnp.where(band == 2, side, jnp.where(band == 3, side + edge - HALO, pixel))


def rim_lane(row, col, edge):
    band_len = HALO * edge
    side = jnp.where(col < HALO, 2 * band_len + row * HALO + col,
                     3 * band_len + row * HALO + col - (edge - HALO))
    side = jnp.where(row >= edge - HALO, band_len + (row - (edge - HALO)) * edge + col, side)
    return jnp.where(row < HALO, row * edge + col, side)


def turned_lane(row, col, quarter, edge):
    last = edge - 1
    from_row = jnp.where(quarter == 1, col, jnp.where(
        quarter == 2, last - row, jnp.where(quarter == 3, last - col, row)))
    from_col = jnp.where(quarter == 1, last - row, jnp.where(
        quarter == 2, last - col, jnp.where(quarter == 3, row, col)))
    return rim_lane(from_row, from_col, edge)


def row_halo_maps(top_turn, bottom_turn, edge):
    rim = 4 * HALO * edge
    lane = lax.broadcasted_iota(jnp.int32, (1, LANES), 1)
    up = lane - (LANES - HALO * edge)
    top = turned_lane(edge - HALO + up // edge, up % edge, top_turn, edge)
    low = turned_lane(lane // edge, lane % edge, bottom_turn, edge)
    top = jnp.where(up >= 0, top, -1)
    low = jnp.where(lane < HALO * edge, low, -1)
    return one_hot(top, rim), one_hot(low, rim)


def side_map(turns, edge):
    rim = 4 * HALO * edge
    lane = lax.broadcasted_iota(jnp.int32, (1, 2 * LANES), 1)
    row, k = lane // (2 * HALO), lane % (2 * HALO)
    above, below, right = row < HALO, row >= HALO + edge, k >= HALO
    b_row = jnp.where(above, edge - HALO + row, jnp.where(below, row - HALO - edge, row - HALO))
    b_col = jnp.where(right, k - HALO, edge - HALO + k)
    slot = jnp.where(above, 0, jnp.where(below, 4, 2)) + right.astype(jnp.int32)
    quarter = jnp.zeros_like(slot)
    for position in range(len(SIDES)):
        quarter = jnp.where(slot == position, turns[position], quarter)
    index = slot * rim + turned_lane(b_row, b_col, quarter, edge)
    index = jnp.where(row < edge + 2 * HALO, index, -1)
    return one_hot(index, len(SIDES) * rim)


def spread_map(edge, wide):
    lane = lax.broadcasted_iota(jnp.int32, (1, wide), 1)
    row = lane // edge - (LANES // edge - HALO)
    col = lane % edge
    right_row, left_row = row - 1, row + 1
    rows = edge + 2 * HALO
    right = jnp.where((right_row >= 0) & (right_row < rows), right_row * 2 * HALO + HALO + col, -1)
    left = jnp.where((left_row >= 0) & (left_row < rows),
                     left_row * 2 * HALO + col - (edge - HALO), -1)
    index = jnp.where(col < HALO, right, jnp.where(col >= edge - HALO, left, -1))
    return one_hot(index, 2 * LANES)


def side_mask(shift, shape, edge):
    col = lax.broadcasted_iota(jnp.int32, shape, 1) % edge
    return col < shift if shift > 0 else col >= edge + shift


def roll(values, shift):
    size = values.shape[1]
    return values if shift % size == 0 else pltpu.roll(values, shift % size, axis=1)


def pack_kernel(edge, x, rims, rim, sems):
    pick = one_hot(rim_pixels(edge), edge * edge)
    rim[...] = dot(x.get()[...], pick).astype(BF16)
    copies = [pltpu.make_async_copy(rim, rims.at[t], sems.at[t]) for t in range(rims.shape[0])]
    for copy in copies:
        copy.start()
    for copy in copies:
        copy.wait()


def conv_kernel(edge, neighbours, rotations, x, rims, taps,
                hidden_ref, padded, side, gathered):
    padded_ref, side_ref = padded.ref, side.ref
    rims_ref, taps_ref = rims.get(), taps.get()
    channels, pixels = hidden_ref.shape
    wide = pixels + 2 * LANES
    rim = rims_ref.shape[2]
    nb, rot = tile_row(neighbours), tile_row(rotations)
    top, low = row_halo_maps(rot[1], rot[6], edge)
    padded_ref[:, :LANES] = dot(rims_ref[nb[1]], top).astype(BF16)
    padded_ref[:, LANES + pixels:] = dot(rims_ref[nb[6]], low).astype(BF16)
    for position, d in enumerate(SIDES):
        gathered[:, position * rim:(position + 1) * rim] = rims_ref[nb[d]]
    packed = dot(gathered[...], side_map([rot[d] for d in SIDES], edge)).astype(BF16)
    side_ref[...] = dot(packed, spread_map(edge, wide)).astype(BF16)
    side.send()
    padded_ref[:, LANES:LANES + pixels] = x.get()[...]
    padded.send()

    def block(i, carry):
        at = pl.multiple_of(i * 16, 16)
        xs = padded_ref[pl.ds(at, 16), :].astype(F32)
        hs = side_ref[pl.ds(at, 16), :].astype(F32)
        taps = [taps_ref[tap, pl.ds(at, 16), :].astype(F32) for tap in range(KSIZE * KSIZE)]
        halves = []
        for half in (0, 8):
            x, h = xs[half:half + 8], hs[half:half + 8]
            sums = [None] * KSIZE
            for b in range(KSIZE):
                shift = b - HALO
                moved = x
                if shift:
                    moved = roll(jnp.where(side_mask(shift, x.shape, edge), h, x), -shift)
                for a in range(KSIZE):
                    term = jnp.tile(taps[a * KSIZE + b][half:half + 8], (1, wide // LANES)) * moved
                    sums[a] = term if sums[a] is None else sums[a] + term
            total = None
            for a in range(KSIZE):
                part = roll(sums[a], -(a - HALO) * edge)[:, LANES:LANES + pixels]
                total = part if total is None else total + part
            halves.append(total)
        hidden_ref[pl.ds(at, 16), :] = jnp.concatenate(halves, axis=0).astype(BF16)
        return carry

    lax.fori_loop(0, channels // 16, block, 0)


def gelu_parts(pre, grad_act):
    cumul = 0.5 * (1.0 + lax.erf(pre * 0.7071067811865476))
    slope = cumul + pre * jnp.exp(-0.5 * pre * pre) * 0.3989422804014327
    return (pre * cumul).astype(BF16), (grad_act * slope).astype(BF16)


def hidden_block(w_in_t, w_out, feats, cots, pre, slope, act, gpre):
    pre[...] = dot(w_in_t, feats[...])
    slope[...] = dot(w_out, cots[...])

    def rows(i, carry):
        at = pl.multiple_of(i * 16, 16)
        act[pl.ds(at, 16), :], gpre[pl.ds(at, 16), :] = gelu_parts(
            pre[pl.ds(at, 16), :], slope[pl.ds(at, 16), :])
        return carry

    lax.fori_loop(0, pre.shape[0] // 16, rows, 0)


def weight_kernel(feats, cots, w_in_t, w_out, part, pre, slope, act, gpre, stack, sems):
    feats, cots = feats.get(), cots.get()
    full, units = feats.shape[0], pre.shape[0]
    hidden_block(w_in_t.get()[...], w_out.get()[...], feats, cots, pre, slope, act, gpre)
    used, copies = 0, []
    for values, height in ((dot_nt(feats[...], gpre[...]), full),
                           (dot_nt(act[...], cots[...]), units)):
        first = used
        for column in range(0, values.shape[1], LANES):
            stack[used:used + height, :] = values[:, column:column + LANES].astype(BF16)
            used += height
        copies.append(pltpu.make_async_copy(
            stack.at[first:used], part.at[first:used], sems.at[len(copies)]))
        copies[-1].start()
    if used < part.shape[0]:
        stack[used:, :] = jnp.zeros((part.shape[0] - used, LANES), BF16)
        copies.append(pltpu.make_async_copy(stack.at[used:], part.at[used:], sems.at[2]))
        copies[-1].start()
    for copy in copies:
        copy.wait()


def point_kernel(edge, feats, cots, w_in, w_in_t, w_out, x, padded, side,
                 out, grad_ref, tap_ref, pre, slope, act, gpre, turned_all, moved_all):
    channels = grad_ref.shape[0]
    start = pl.multiple_of(lax.axis_index("chan") * channels, channels)
    w_out = w_out.get()
    hidden_block(w_in_t.get()[...], w_out[...], feats.get(), cots.get(), pre, slope, act, gpre)
    grad_ref[...] = dot(w_in.get()[pl.ds(start, channels), :], gpre[...]).astype(BF16)
    row = lax.broadcasted_iota(jnp.int32, (channels, w_out.shape[1]), 0)
    column = lax.broadcasted_iota(jnp.int32, (channels, w_out.shape[1]), 1)
    pick = jnp.where(column == row + start, 1.0, 0.0).astype(BF16)
    branch = dot(dot_nt(pick, w_out[...]).astype(BF16), act[...])
    out.ref[...] = (x.get()[...].astype(F32) + branch.astype(BF16).astype(F32)).astype(BF16)
    out.send()
    tap_terms(edge, grad_ref, padded.get(), side.get(), tap_ref, turned_all, moved_all)


def prep_kernel(w_in, x, neighbours, rotations, w_in_t_ref, x_ref, nb_ref, rot_ref):
    nb_ref[...], rot_ref[...] = neighbours.get()[...], rotations.get()[...]
    w_in_t_ref[...] = w_in.get()[...].astype(F32).T.astype(BF16)
    x_ref[...] = x.get()[...]


def join_kernel(w_in_t, w_out, *refs):
    pieces, (out_ref, part_in_ref, part_out_ref) = refs[:-3], refs[-3:]
    chan = lax.axis_index("chan")
    for k, piece in enumerate(pieces):
        piece = piece.get()
        channels = piece.shape[0]
        start = pl.multiple_of((chan ^ k) * channels, channels)
        out_ref[pl.ds(start, channels), :] = piece[...]
    units = part_in_ref.shape[0]
    mine = pl.ds(pl.multiple_of(chan * units, units), units)
    part_in_ref[...] = w_in_t.get()[mine, :]
    part_out_ref[...] = w_out.get()[mine, :]


def tap_terms(edge, grad_ref, padded_ref, side_ref, tap_ref, turned_all, moved_all):
    channels, pixels = grad_ref.shape
    wide = pixels + 2 * LANES
    moved_all[KSIZE * 16:, :] = jnp.zeros((LANES - KSIZE * 16, wide), BF16)
    same = (lax.broadcasted_iota(jnp.int32, (16, KSIZE * LANES), 1) % 16
            == lax.broadcasted_iota(jnp.int32, (16, KSIZE * LANES), 0))
    line = lax.broadcasted_iota(jnp.int32, (KSIZE * LANES, LANES), 0)
    tap = lax.broadcasted_iota(jnp.int32, (KSIZE * LANES, LANES), 1)
    used = line % LANES < KSIZE * 16
    pick = jnp.where(used & (line // LANES * KSIZE + line % LANES // 16 == tap), 1.0, 0.0).astype(BF16)
    mask = {b: side_mask(b - HALO, (16, wide), edge) for b in range(KSIZE) if b != HALO}
    lane = lax.broadcasted_iota(jnp.int32, (16, LANES), 1)
    zeros = jnp.zeros((16, LANES), F32)
    found = []
    for at in range(0, channels, 16):
        g = jnp.concatenate([zeros, grad_ref[at:at + 16, :].astype(F32), zeros], axis=1)
        x = padded_ref[at:at + 16, :].astype(F32)
        h = side_ref[at:at + 16, :].astype(F32)
        for a in range(KSIZE):
            shift = a - HALO
            turned_all[a * 16:a * 16 + 16, :] = roll(g, shift * edge).astype(BF16)
            moved = roll(jnp.where(mask[a], h, x), -shift) if shift else x
            moved_all[a * 16:a * 16 + 16, :] = moved.astype(BF16)
        products = dot_nt(turned_all[...], moved_all[...])
        side_by_side = jnp.concatenate(
            [products[a * 16:a * 16 + 16, :] for a in range(KSIZE)], axis=1)
        taps = dot(jnp.where(same, side_by_side, 0.0).astype(BF16), pick)
        place = at // 16 % 4
        taps = jnp.where(lane // 32 == place, roll(taps, 32 * place), 0.0)
        if place == 0:
            found.append(taps)
        else:
            found[-1] = found[-1] + taps
    tap_ref[...] = jnp.concatenate(found, axis=0).astype(BF16)


def back_kernel(edge, neighbours, rotations, grad, taps, cot,
                accum_ref, border, d_row, d_side, gathered):
    send_ref = border.ref
    grad_ref, taps_ref = grad.get(), taps.get()
    channels, pixels = grad_ref.shape
    wide = pixels + 2 * LANES
    tiles, _, rim = send_ref.shape

    def block(i, carry):
        at = pl.multiple_of(i * 16, 16)
        gs = grad_ref[pl.ds(at, 16), :].astype(F32)
        taps_of = [taps_ref[tap, pl.ds(at, 16), :].astype(F32) for tap in range(KSIZE * KSIZE)]
        zeros = jnp.zeros((8, LANES), F32)
        rows, sides = [], []
        for half in (0, 8):
            g = jnp.concatenate([zeros, gs[half:half + 8], zeros], axis=1)
            turned = [roll(g, (a - HALO) * edge) for a in range(KSIZE)]
            d_x = d_h = None
            for b in range(KSIZE):
                shift = b - HALO
                back = None
                for a in range(KSIZE):
                    weight = taps_of[a * KSIZE + b][half:half + 8]
                    term = jnp.tile(weight, (1, wide // LANES)) * turned[a]
                    back = term if back is None else back + term
                back = roll(back, shift)
                if shift:
                    mask = side_mask(shift, back.shape, edge)
                    inside = jnp.where(mask, 0.0, back)
                    outside = jnp.where(mask, back, 0.0)
                    d_h = outside if d_h is None else d_h + outside
                    d_x = inside if d_x is None else d_x + inside
                else:
                    d_x = back if d_x is None else d_x + back
            rows.append(d_x)
            sides.append(d_h)
        d_x = jnp.concatenate(rows, axis=0)
        accum_ref[pl.ds(at, 16), :] = d_x[:, LANES:LANES + pixels]
        d_row[pl.ds(at, 16), :LANES] = d_x[:, :LANES].astype(BF16)
        d_row[pl.ds(at, 16), LANES:] = d_x[:, LANES + pixels:].astype(BF16)
        d_side[pl.ds(at, 16), :] = jnp.concatenate(sides, axis=0).astype(BF16)
        return carry

    lax.fori_loop(0, channels // 16, block, 0)
    accum_ref[...] += cot.get()[...].astype(F32)
    nb, rot = tile_row(neighbours), tile_row(rotations)
    gathered[...] = jnp.zeros(gathered.shape, F32)
    top, low = row_halo_maps(rot[1], rot[6], edge)
    gathered[nb[1]] += dot_nt(d_row[:, :LANES], top)
    gathered[nb[6]] += dot_nt(d_row[:, LANES:], low)
    packed = dot_nt(d_side[...], spread_map(edge, wide)).astype(BF16)
    picks = side_map([rot[d] for d in SIDES], edge)
    for position, d in enumerate(SIDES):
        gathered[nb[d]] += dot_nt(packed, picks[position * rim:(position + 1) * rim, :])

    def store(t, carry):
        send_ref[t] = gathered[t].astype(BF16)
        return carry

    lax.fori_loop(0, tiles, store, 0)


def border_kernel(edge, recv, accum, grad):
    rims = total_of(recv.get())
    high = rims.astype(BF16)
    low = (rims - high.astype(F32)).astype(BF16)
    pick = one_hot(rim_pixels(edge), edge * edge)
    added = dot_nt(high, pick) + dot_nt(low, pick)
    grad.ref[...] = (accum.get()[...] + added).astype(BF16)


def total_of(ref):
    return lax.fori_loop(1, ref.shape[0], lambda t, so_far: so_far + ref[t].astype(F32),
                         ref[0].astype(F32))


def sum_kernel(recv, tap, out, total, sems):
    recv = recv.get()
    share = recv.shape[1]
    total[:share, :] = total_of(recv).astype(BF16)
    total[share:, :] = tap.get()[...]
    copies = [pltpu.make_async_copy(total, out.at[t], sems.at[t]) for t in range(out.shape[0])]
    for copy in copies:
        copy.start()
    for copy in copies:
        copy.wait()


def final_kernel(which, last, share, channels, scale, *refs):
    count = len(which)
    pieces, taps_in = refs[:count], refs[count]
    g_in, g_out, g_tap_ref, buf_in, buf_out, sems = refs[-6:]
    full, units = buf_in.shape[1:]
    tiles, rows, _ = pieces[0].ref.shape
    copies = []
    all_taps = taps_in.get()[...] if last else jnp.zeros((full, LANES), F32)
    row_of = lax.broadcasted_iota(jnp.int32, (full, LANES), 0)
    for i, k in enumerate(which):
        piece = pieces[i].get()
        owner = lax.axis_index("chan") ^ k
        start = pl.multiple_of(owner * units, units)
        for in_in, buffer, target in ((True, buf_in, g_in.at[:, pl.ds(start, units)]),
                                      (False, buf_out, g_out.at[pl.ds(start, units)])):
            for tile in range(tiles):
                for row, height, column, at, into_in in chunks(tile, share, units, full):
                    if into_in == in_in:
                        values = piece[tile, row:row + height, :].astype(F32) * scale
                        buffer[i, at:at + height, column:column + LANES] = values
            copies.append(pltpu.make_async_copy(buffer.at[i], target, sems.at[int(in_in), i]))
            copies[-1].start()
        taps = piece[0, share:, :].astype(F32)
        for tile in range(1, tiles):
            taps = taps + piece[tile, share:, :].astype(F32)
        blocks = []
        for block in range(channels // 16):
            values = taps[block // 4 * 16:block // 4 * 16 + 16, :]
            blocks.append(roll(values, -32 * (block % 4)))
        own = jnp.concatenate(blocks * (full // channels), axis=0)
        all_taps = jnp.where(row_of // channels == owner, own, all_taps)
    if last:
        g_tap_ref[...] = all_taps.T[:KSIZE * KSIZE, :] * scale
    else:
        g_tap_ref[...] = all_taps
    for copy in copies:
        copy.wait()


def chunks(tile, share, units, full):
    inside, found = units // LANES * full, []
    row, end = tile * share, min((tile + 1) * share, 2 * units * full // LANES)
    while row < end:
        height = full if row < inside else units
        offset = row if row < inside else row - inside
        column, at = offset // height * LANES, offset % height
        count = min(end - row, height - at)
        found.append((row - tile * share, count, column, at, row < inside))
        row += count
    return found


def gather_pieces(own, groups):
    pieces = {0: own}
    bit = groups // 2
    while bit:
        swap = [(i, i ^ bit) for i in range(groups)]
        for k in list(pieces):
            pieces[k ^ bit] = lax.ppermute(pieces[k], "chan", swap)
        bit //= 2
    return [pieces[k] for k in range(groups)]


def swap_rows(values):
    return lax.all_to_all(values, "tile", 0, 0, tiled=True)


def body(inputs, grad_out, kernel, w_in, w_out, neighbours, rotations):
    channels, pixels = inputs.shape[1:]
    edge = math.isqrt(pixels)
    full, hidden = w_in.shape
    groups = lax.axis_size("chan")
    tiles = lax.axis_size("tile")
    wide = pixels + 2 * LANES
    rim = 4 * HALO * edge
    units = hidden // groups
    scale = (tiles * pixels) ** -0.5
    x, cot = inputs[0], grad_out[0]

    [rims] = call(functools.partial(pack_kernel, edge), [(x, FAR)],
                  [((tiles, channels, rim), BF16, RAW)],
                  [pltpu.VMEM((channels, rim), BF16), pltpu.SemaphoreType.DMA((tiles,))])
    _, kernel = lax.optimization_barrier((rims, kernel))
    taps = jnp.broadcast_to(kernel[:, :, None], (KSIZE * KSIZE, channels, LANES))
    cot_pieces = gather_pieces(cot, groups)
    table = neighbours.shape
    w_in_t, x_near, nb_near, rot_near = call(
        prep_kernel, [(w_in, NEAR), (x, FAR), (neighbours, NEAR), (rotations, NEAR)],
        [((hidden, full), BF16, NEAR), ((channels, pixels), BF16, NEAR)]
        + [(neighbours.shape, jnp.int32, NEAR)] * 2, time=1.2,
        after=[(rims, RAW), (taps, NEAR)])
    rims = swap_rows(rims)

    hid, padded, side = call(
        functools.partial(conv_kernel, edge),
        [(nb_near, NEAR), (rot_near, NEAR), (x_near, NEAR), (rims, NEAR), (taps, NEAR)],
        [((channels, pixels), BF16, NEAR)] + [((channels, wide), BF16, FAR)] * 2,
        [pltpu.VMEM((channels, len(SIDES) * rim), BF16)], time=2.5,
        after=[(w_in_t, NEAR)])
    feats = lax.all_gather(hid, "chan", axis=0, tiled=True)
    cots, part_in, part_out = call(
        join_kernel, [(w_in_t, NEAR), (w_out, NEAR)] + [(piece, NEAR) for piece in cot_pieces],
        [((full, pixels), BF16, NEAR)] + [((units, full), BF16, NEAR)] * 2, time=0.6,
        after=[(feats, NEAR)])

    used = 2 * full * units // LANES
    share = -(-used // (16 * tiles)) * 16
    tap_rows = -(-channels // 64) * 16
    values = [pltpu.VMEM((units, pixels), F32)] * 2 + [pltpu.VMEM((units, pixels), BF16)] * 2
    [part] = call(
        weight_kernel,
        [(feats, NEAR), (cots, NEAR), (part_in, NEAR), (part_out, NEAR)],
        [((tiles * share, LANES), BF16, RAW)],
        values + [pltpu.VMEM((tiles * share, LANES), BF16), pltpu.SemaphoreType.DMA((3,))],
        time=2.2)
    part = swap_rows(part.reshape(tiles, share, LANES))

    outputs, grad_hid, tap_part = call(
        functools.partial(point_kernel, edge),
        [(feats, NEAR), (cots, NEAR), (w_in, FAR), (w_in_t, NEAR), (w_out, NEAR),
         (x, FAR), (padded, FAR), (side, FAR)],
        [((channels, pixels), BF16, FAR), ((channels, pixels), BF16, NEAR),
         ((tap_rows, LANES), BF16, NEAR)],
        [pltpu.VMEM((hidden, pixels), F32)] * 2 + [pltpu.VMEM((hidden, pixels), BF16)] * 2
        + [pltpu.VMEM((KSIZE * 16, wide), BF16), pltpu.VMEM((LANES, wide), BF16)],
        time=5.5, limit=32)
    [mine] = call(sum_kernel, [(part, NEAR), (tap_part, NEAR)],
                  [((tiles, share + tap_rows, LANES), BF16, RAW)],
                  [pltpu.VMEM((share + tap_rows, LANES), BF16), pltpu.SemaphoreType.DMA((tiles,))])
    weights = swap_rows(mine)

    accum, border = call(
        functools.partial(back_kernel, edge),
        [(neighbours, NEAR), (rotations, NEAR), (grad_hid, NEAR), (taps, NEAR), (cot, FAR)],
        [((channels, pixels), F32, NEAR), ((tiles, channels, rim), BF16, FAR)],
        [pltpu.VMEM((channels, 2 * LANES), BF16), pltpu.VMEM((channels, wide), BF16),
         pltpu.VMEM((tiles, channels, rim), F32)], time=4.0, after=[(mine, RAW)])
    weights, border = lax.optimization_barrier((weights, border))
    border = swap_rows(border)
    pieces = gather_pieces(weights, groups)
    grads, ends = [], [(0, groups, 2), (1, groups, 2)]
    for last, end in enumerate(ends):
        which = list(range(*end))
        tap_shape = (KSIZE * KSIZE, full) if last else (full, LANES)
        grads = call(
            functools.partial(final_kernel, which, last, share, channels, scale),
            [(pieces[k], NEAR) for k in which]
            + ([(grads[2], NEAR), (grads[0], RAW), (grads[1], RAW)] if last else []),
            [((full, hidden), F32, RAW), ((hidden, full), F32, RAW), (tap_shape, F32, NEAR)],
            [pltpu.VMEM((len(which), full, units), F32), pltpu.VMEM((len(which), units, full), F32),
             pltpu.SemaphoreType.DMA((2, len(which)))],
            time=1.3, aliases={1 + len(which): 0, 2 + len(which): 1} if last else None)
    [grad_in] = call(functools.partial(border_kernel, edge), [(border, NEAR), (accum, NEAR)],
                     [((channels, pixels), BF16, FAR)], after=[(grads[0], RAW)])
    return (outputs[None], grad_in[None], *grads)


def solution(mesh):
    return jax.shard_map(
        body,
        mesh=mesh,
        in_specs=(
            P("tile", "chan", None),
            P("tile", "chan", None),
            P(None, "chan"),
            P(),
            P(),
            P(),
            P(),
        ),
        out_specs=(P("tile", "chan", None), P("tile", "chan", None), P(), P(), P()),
        check_vma=False,
    )
```

```python
import functools
import math

import jax
import jax.numpy as jnp
from jax import lax
from jax.experimental import pallas as pl
from jax.experimental.pallas import tpu as pltpu
from jax.sharding import PartitionSpec as P

KSIZE = 5
HALO = KSIZE // 2
LANES = 128
SIDES = (0, 2, 3, 4, 5, 7)
BF16 = jnp.bfloat16
F32 = jnp.float32

NEAR, FAR, RAW = "near", "far", "raw"
SPACES = {NEAR: pltpu.VMEM, FAR: pltpu.HBM, RAW: pltpu.HBM}


class Loaded:
    def __init__(self, ref, copy=None):
        self.ref, self.copy = ref, copy
        if copy is not None:
            copy.start()

    def get(self):
        if self.copy is not None:
            self.copy.wait()
            self.copy = None
        return self.ref


class Stored:
    def __init__(self, ref, copy):
        self.ref, self.copy, self.started = ref, copy, False

    def send(self):
        if not self.started:
            self.copy.start()
            self.started = True


def call(kernel, ins, outs, scratch=(), time=1.0, after=(), aliases=None, limit=16):
    ins = list(ins) + list(after)
    buffers = []
    for shape, dtype, place in [(a.shape, a.dtype, p) for a, p in ins] + list(outs):
        if place == FAR:
            buffers += [pltpu.VMEM(shape, dtype), pltpu.SemaphoreType.DMA]

    def run(*refs):
        ends = len(ins), len(ins) + len(outs), len(ins) + len(outs) + len(buffers)
        spare = list(refs[ends[1]:ends[2]])
        operands, results = [], []
        for ref, (_, place) in zip(refs, ins):
            if place == FAR:
                buffer, sem = spare.pop(0), spare.pop(0)
                operands.append(Loaded(buffer, pltpu.make_async_copy(ref, buffer, sem)))
            else:
                operands.append(Loaded(ref) if place == NEAR else ref)
        for ref, (_, _, place) in zip(refs[ends[0]:], outs):
            if place == FAR:
                buffer, sem = spare.pop(0), spare.pop(0)
                results.append(Stored(buffer, pltpu.make_async_copy(buffer, ref, sem)))
            else:
                results.append(ref)
        kernel(*operands[:len(ins) - len(after)], *results, *refs[ends[2]:])
        far = [result for result in results if isinstance(result, Stored)]
        for result in far:
            result.send()
        for result in far:
            result.copy.wait()

    return pl.pallas_call(
        run,
        out_shape=[pltpu.HBM(s, d) if p in (FAR, RAW) else jax.ShapeDtypeStruct(s, d)
                   for s, d, p in outs],
        in_specs=[pl.BlockSpec(memory_space=SPACES[p]) for _, p in ins],
        out_specs=[pl.BlockSpec(memory_space=SPACES[p]) for _, _, p in outs],
        scratch_shapes=buffers + list(scratch),
        input_output_aliases=aliases or {},
        cost_estimate=pl.CostEstimate(
            flops=int(time * 1e9), bytes_accessed=int(time * 3.5e6), transcendentals=0),
        compiler_params=pltpu.CompilerParams(vmem_limit_bytes=limit * 1024 * 1024),
    )(*[pltpu.with_memory_space_constraint(a, pltpu.HBM) if p in (FAR, RAW) else a
        for a, p in ins])


def tile_row(table):
    row = table.get()[pl.ds(lax.axis_index("tile"), 1), :]
    return [row[0, d] for d in range(8)]


def dot(a, b):
    return lax.dot_general(a, b, (((1,), (0,)), ((), ())), preferred_element_type=F32)


def dot_nt(a, b):
    return lax.dot_general(a, b, (((1,), (1,)), ((), ())), preferred_element_type=F32)


def one_hot(index, rows):
    row = lax.broadcasted_iota(jnp.int32, (rows, index.shape[1]), 0)
    return jnp.where(row == index, 1.0, 0.0).astype(BF16)


def rim_pixels(edge):
    band_len = HALO * edge
    lane = lax.broadcasted_iota(jnp.int32, (1, 4 * band_len), 1)
    band, at = lane // band_len, lane % band_len
    side = (at // HALO) * edge + at % HALO
    pixel = jnp.where(band == 0, at, (edge - HALO) * edge + at)
    return jnp.where(band == 2, side, jnp.where(band == 3, side + edge - HALO, pixel))


def rim_lane(row, col, edge):
    band_len = HALO * edge
    side = jnp.where(col < HALO, 2 * band_len + row * HALO + col,
                     3 * band_len + row * HALO + col - (edge - HALO))
    side = jnp.where(row >= edge - HALO, band_len + (row - (edge - HALO)) * edge + col, side)
    return jnp.where(row < HALO, row * edge + col, side)


def turned_lane(row, col, quarter, edge):
    last = edge - 1
    from_row = jnp.where(quarter == 1, col, jnp.where(
        quarter == 2, last - row, jnp.where(quarter == 3, last - col, row)))
    from_col = jnp.where(quarter == 1, last - row, jnp.where(
        quarter == 2, last - col, jnp.where(quarter == 3, row, col)))
    return rim_lane(from_row, from_col, edge)


def row_halo_maps(top_turn, bottom_turn, edge):
    rim = 4 * HALO * edge
    lane = lax.broadcasted_iota(jnp.int32, (1, LANES), 1)
    up = lane - (LANES - HALO * edge)
    top = turned_lane(edge - HALO + up // edge, up % edge, top_turn, edge)
    low = turned_lane(lane // edge, lane % edge, bottom_turn, edge)
    top = jnp.where(up >= 0, top, -1)
    low = jnp.where(lane < HALO * edge, low, -1)
    return one_hot(top, rim), one_hot(low, rim)


def side_map(turns, edge):
    rim = 4 * HALO * edge
    lane = lax.broadcasted_iota(jnp.int32, (1, 2 * LANES), 1)
    row, k = lane // (2 * HALO), lane % (2 * HALO)
    above, below, right = row < HALO, row >= HALO + edge, k >= HALO
    b_row = jnp.where(above, edge - HALO + row, jnp.where(below, row - HALO - edge, row - HALO))
    b_col = jnp.where(right, k - HALO, edge - HALO + k)
    slot = jnp.where(above, 0, jnp.where(below, 4, 2)) + right.astype(jnp.int32)
    quarter = jnp.zeros_like(slot)
    for position in range(len(SIDES)):
        quarter = jnp.where(slot == position, turns[position], quarter)
    index = turned_lane(b_row, b_col, quarter, edge)
    index = jnp.where(row < edge + 2 * HALO, index, -1)
    return one_hot(index, rim), slot


def spread_map(edge, wide):
    lane = lax.broadcasted_iota(jnp.int32, (1, wide), 1)
    row = lane // edge - (LANES // edge - HALO)
    col = lane % edge
    right_row, left_row = row - 1, row + 1
    rows = edge + 2 * HALO
    right = jnp.where((right_row >= 0) & (right_row < rows), right_row * 2 * HALO + HALO + col, -1)
    left = jnp.where((left_row >= 0) & (left_row < rows),
                     left_row * 2 * HALO + col - (edge - HALO), -1)
    index = jnp.where(col < HALO, right, jnp.where(col >= edge - HALO, left, -1))
    return one_hot(index, 2 * LANES)


def side_mask(shift, shape, edge):
    col = lax.broadcasted_iota(jnp.int32, shape, 1) % edge
    return col < shift if shift > 0 else col >= edge + shift


def roll(values, shift):
    size = values.shape[1]
    return values if shift % size == 0 else pltpu.roll(values, shift % size, axis=1)


def pack_kernel(edge, x, rims, rim, sems):
    pick = one_hot(rim_pixels(edge), edge * edge)
    rim[...] = dot(x.get()[...], pick).astype(BF16)
    copies = [pltpu.make_async_copy(rim, rims.at[t], sems.at[t]) for t in range(rims.shape[0])]
    for copy in copies:
        copy.start()
    for copy in copies:
        copy.wait()


def conv_kernel(edge, neighbours, rotations, x, rims, taps,
                hidden_ref, padded, side, gathered):
    padded_ref, side_ref = padded.ref, side.ref
    rims_ref, taps_ref = rims.get(), taps.get()
    channels, pixels = hidden_ref.shape
    wide = pixels + 2 * LANES
    nb, rot = tile_row(neighbours), tile_row(rotations)
    top, low = row_halo_maps(rot[1], rot[6], edge)
    padded_ref[:, :LANES] = dot(rims_ref[nb[1]], top).astype(BF16)
    padded_ref[:, LANES + pixels:] = dot(rims_ref[nb[6]], low).astype(BF16)
    for position, d in enumerate(SIDES):
        gathered[position * channels:(position + 1) * channels, :] = rims_ref[nb[d]]
    pick, slot = side_map([rot[d] for d in SIDES], edge)
    candidates = dot(gathered[...], pick)
    packed = candidates[:channels, :]
    for position in range(1, len(SIDES)):
        packed = jnp.where(slot == position,
                           candidates[position * channels:(position + 1) * channels, :], packed)
    packed = packed.astype(BF16)
    side_ref[...] = dot(packed, spread_map(edge, wide)).astype(BF16)
    side.send()
    padded_ref[:, LANES:LANES + pixels] = x.get()[...]
    padded.send()

    def block(i, carry):
        at = pl.multiple_of(i * 16, 16)
        xs = padded_ref[pl.ds(at, 16), :].astype(F32)
        hs = side_ref[pl.ds(at, 16), :].astype(F32)
        taps = [taps_ref[tap, pl.ds(at, 16), :].astype(F32) for tap in range(KSIZE * KSIZE)]
        halves = []
        for half in (0, 8):
            x, h = xs[half:half + 8], hs[half:half + 8]
            sums = [None] * KSIZE
            for b in range(KSIZE):
                shift = b - HALO
                moved = x
                if shift:
                    moved = roll(jnp.where(side_mask(shift, x.shape, edge), h, x), -shift)
                for a in range(KSIZE):
                    term = jnp.tile(taps[a * KSIZE + b][half:half + 8], (1, wide // LANES)) * moved
                    sums[a] = term if sums[a] is None else sums[a] + term
            total = None
            for a in range(KSIZE):
                part = roll(sums[a], -(a - HALO) * edge)[:, LANES:LANES + pixels]
                total = part if total is None else total + part
            halves.append(total)
        hidden_ref[pl.ds(at, 16), :] = jnp.concatenate(halves, axis=0).astype(BF16)
        return carry

    lax.fori_loop(0, channels // 16, block, 0)


def normal_below(values):
    return 0.5 * (1.0 + lax.erf(values * 0.7071067811865476))


def gelu_slope(values, below):
    return below + values * jnp.exp(-0.5 * values * values) * 0.3989422804014327


def column_steps(ref):
    return [slice(at, at + 2 * LANES) for at in range(0, ref.shape[1], 2 * LANES)]


def over_units(units, block, body):
    def step(i, carry):
        body(pl.ds(pl.multiple_of(i * block, block), block))
        return carry

    lax.fori_loop(0, units // block, step, 0)


def weight_kernel(feats, cots, w_in_t, w_out, part, act, gpre, stack, sems):
    feats, cots = feats.get(), cots.get()
    full, units = feats.shape[0], act.shape[0]
    w_in_t, w_out = w_in_t.get()[...], w_out.get()[...]
    for part_of in column_steps(feats):
        pre = dot(w_in_t, feats[:, part_of])
        below = normal_below(pre)
        act[:, part_of] = (pre * below).astype(BF16)
        slope = gelu_slope(pre, below)
        gpre[:, part_of] = (dot(w_out, cots[:, part_of]) * slope).astype(BF16)
    used, copies = 0, []
    for values, height in ((dot_nt(feats[...], gpre[...]), full),
                           (dot_nt(act[...], cots[...]), units)):
        first = used
        for column in range(0, values.shape[1], LANES):
            stack[used:used + height, :] = values[:, column:column + LANES].astype(BF16)
            used += height
        copies.append(pltpu.make_async_copy(
            stack.at[first:used], part.at[first:used], sems.at[len(copies)]))
        copies[-1].start()
    if used < part.shape[0]:
        stack[used:, :] = jnp.zeros((part.shape[0] - used, LANES), BF16)
        copies.append(pltpu.make_async_copy(stack.at[used:], part.at[used:], sems.at[2]))
        copies[-1].start()
    for copy in copies:
        copy.wait()


def out_kernel(block, feats, w_in_t, w_out, x, out, act):
    feats, w_in_t, w_out = feats.get(), w_in_t.get(), w_out.get()

    def units(rows):
        for part_of in column_steps(feats):
            pre = dot(w_in_t[rows, :], feats[:, part_of])
            act[rows, part_of] = (pre * normal_below(pre)).astype(BF16)

    over_units(w_out.shape[0], block, units)
    channels = out.ref.shape[0]
    row = lax.broadcasted_iota(jnp.int32, (channels, w_out.shape[1]), 0)
    column = lax.broadcasted_iota(jnp.int32, (channels, w_out.shape[1]), 1)
    pick = jnp.where(column == row + lax.axis_index("chan") * channels, 1.0, 0.0).astype(BF16)
    branch = dot(dot_nt(pick, w_out[...]).astype(BF16), act[...])
    out.ref[...] = (x.get()[...].astype(F32) + branch.astype(BF16).astype(F32)).astype(BF16)


def back_kernel(edge, block, tiles, feats, cots, w_in, w_in_t, w_out, padded, side, cot, neighbours,
                rotations, taps, accum_ref, tap_ref, *refs):
    outs, (gpre, grad_ref, turned_all, moved_all, d_row, d_side, gathered) = refs[:-7], refs[-7:]
    channels = grad_ref.shape[0]
    feats, cots, w_in_t, w_out = feats.get(), cots.get(), w_in_t.get(), w_out.get()

    def units(rows):
        for part_of in column_steps(feats):
            pre = dot(w_in_t[rows, :], feats[:, part_of])
            slope = gelu_slope(pre, normal_below(pre))
            gpre[rows, part_of] = (dot(w_out[rows, :], cots[:, part_of]) * slope).astype(BF16)

    over_units(w_out.shape[0], block, units)
    own = pl.ds(pl.multiple_of(lax.axis_index("chan") * channels, channels), channels)
    grad_ref[...] = dot(w_in.get()[own, :], gpre[...]).astype(BF16)
    tap_terms(edge, grad_ref, padded.get(), side.get(), tap_ref, turned_all, moved_all)
    halo_adjoint(edge, neighbours, rotations, grad_ref, taps.get(), cot.get(), accum_ref, outs,
                 d_row, d_side, gathered)


def prep_kernel(w_in, x, neighbours, rotations, w_in_t_ref, x_ref, nb_ref, rot_ref):
    nb_ref[...], rot_ref[...] = neighbours.get()[...], rotations.get()[...]
    w_in_t_ref[...] = w_in.get()[...].astype(F32).T.astype(BF16)
    x_ref[...] = x.get()[...]


def join_kernel(w_in_t, w_out, *refs):
    pieces, (out_ref, part_in_ref, part_out_ref) = refs[:-3], refs[-3:]
    chan = lax.axis_index("chan")
    for k, piece in enumerate(pieces):
        piece = piece.get()
        channels = piece.shape[0]
        start = pl.multiple_of((chan ^ k) * channels, channels)
        out_ref[pl.ds(start, channels), :] = piece[...]
    units = part_in_ref.shape[0]
    mine = pl.ds(pl.multiple_of(chan * units, units), units)
    part_in_ref[...] = w_in_t.get()[mine, :]
    part_out_ref[...] = w_out.get()[mine, :]


def tap_terms(edge, grad_ref, padded_ref, side_ref, tap_ref, turned_all, moved_all):
    channels, pixels = grad_ref.shape
    wide = pixels + 2 * LANES
    moved_all[KSIZE * 16:, :] = jnp.zeros((LANES - KSIZE * 16, wide), BF16)
    same = (lax.broadcasted_iota(jnp.int32, (16, KSIZE * LANES), 1) % 16
            == lax.broadcasted_iota(jnp.int32, (16, KSIZE * LANES), 0))
    line = lax.broadcasted_iota(jnp.int32, (KSIZE * LANES, LANES), 0)
    tap = lax.broadcasted_iota(jnp.int32, (KSIZE * LANES, LANES), 1)
    used = line % LANES < KSIZE * 16
    pick = jnp.where(used & (line // LANES * KSIZE + line % LANES // 16 == tap), 1.0, 0.0).astype(BF16)
    mask = {b: side_mask(b - HALO, (16, wide), edge) for b in range(KSIZE) if b != HALO}
    lane = lax.broadcasted_iota(jnp.int32, (16, LANES), 1)
    zeros = jnp.zeros((16, LANES), F32)
    found = []
    for at in range(0, channels, 16):
        g = jnp.concatenate([zeros, grad_ref[at:at + 16, :].astype(F32), zeros], axis=1)
        x = padded_ref[at:at + 16, :].astype(F32)
        h = side_ref[at:at + 16, :].astype(F32)
        for a in range(KSIZE):
            shift = a - HALO
            turned_all[a * 16:a * 16 + 16, :] = roll(g, shift * edge).astype(BF16)
            moved = roll(jnp.where(mask[a], h, x), -shift) if shift else x
            moved_all[a * 16:a * 16 + 16, :] = moved.astype(BF16)
        products = dot_nt(turned_all[...], moved_all[...])
        side_by_side = jnp.concatenate(
            [products[a * 16:a * 16 + 16, :] for a in range(KSIZE)], axis=1)
        taps = dot(jnp.where(same, side_by_side, 0.0).astype(BF16), pick)
        place = at // 16 % 4
        taps = jnp.where(lane // 32 == place, roll(taps, 32 * place), 0.0)
        if place == 0:
            found.append(taps)
        else:
            found[-1] = found[-1] + taps
    tap_ref[...] = jnp.concatenate(found, axis=0).astype(BF16)


def halo_adjoint(edge, neighbours, rotations, grad_ref, taps_ref, cot_ref, accum_ref, outs,
                 d_row, d_side, gathered):
    channels, pixels = grad_ref.shape
    wide = pixels + 2 * LANES
    tiles = gathered.shape[0]

    def block(i, carry):
        at = pl.multiple_of(i * 16, 16)
        gs = grad_ref[pl.ds(at, 16), :].astype(F32)
        taps_of = [taps_ref[tap, pl.ds(at, 16), :].astype(F32) for tap in range(KSIZE * KSIZE)]
        zeros = jnp.zeros((8, LANES), F32)
        rows, sides = [], []
        for half in (0, 8):
            g = jnp.concatenate([zeros, gs[half:half + 8], zeros], axis=1)
            turned = [roll(g, (a - HALO) * edge) for a in range(KSIZE)]
            d_x = d_h = None
            for b in range(KSIZE):
                shift = b - HALO
                back = None
                for a in range(KSIZE):
                    weight = taps_of[a * KSIZE + b][half:half + 8]
                    term = jnp.tile(weight, (1, wide // LANES)) * turned[a]
                    back = term if back is None else back + term
                back = roll(back, shift)
                if shift:
                    mask = side_mask(shift, back.shape, edge)
                    inside = jnp.where(mask, 0.0, back)
                    outside = jnp.where(mask, back, 0.0)
                    d_h = outside if d_h is None else d_h + outside
                    d_x = inside if d_x is None else d_x + inside
                else:
                    d_x = back if d_x is None else d_x + back
            rows.append(d_x)
            sides.append(d_h)
        d_x = jnp.concatenate(rows, axis=0)
        accum_ref[pl.ds(at, 16), :] = d_x[:, LANES:LANES + pixels]
        d_row[pl.ds(at, 16), :LANES] = d_x[:, :LANES].astype(BF16)
        d_row[pl.ds(at, 16), LANES:] = d_x[:, LANES + pixels:].astype(BF16)
        d_side[pl.ds(at, 16), :] = jnp.concatenate(sides, axis=0).astype(BF16)
        return carry

    lax.fori_loop(0, channels // 16, block, 0)
    accum_ref[...] += cot_ref[...].astype(F32)
    nb, rot = tile_row(neighbours), tile_row(rotations)
    gathered[...] = jnp.zeros(gathered.shape, F32)
    top, low = row_halo_maps(rot[1], rot[6], edge)
    gathered[slot_of(nb[1], tiles)] += dot_nt(d_row[:, :LANES], top)
    gathered[slot_of(nb[6], tiles)] += dot_nt(d_row[:, LANES:], low)
    packed = dot_nt(d_side[...], spread_map(edge, wide))
    pick, slot = side_map([rot[d] for d in SIDES], edge)
    for position, d in enumerate(SIDES):
        own = jnp.where(slot == position, packed, 0.0).astype(BF16)
        gathered[slot_of(nb[d], tiles)] += dot_nt(own, pick)
    store_parts(gathered, outs)


def store_parts(values, outs):
    for part, out in enumerate(outs):
        out = out.ref if isinstance(out, Stored) else out
        rows = out.shape[0]

        def store(t, carry, out=out, first=part * rows):
            out[t] = values[first + t].astype(BF16)
            return carry

        lax.fori_loop(0, rows, store, 0)


def halves(tiles):
    return tiles & (tiles - 1) == 0


def slot_of(tile, tiles):
    if not halves(tiles):
        return tile
    apart, slot = tile ^ lax.axis_index("tile"), 0
    for bit in range(tiles.bit_length() - 1):
        slot = slot * 2 + ((apart >> bit) & 1)
    return slot


def pair_kernel(kept, other, *refs):
    outs, total = refs[:-1], refs[-1]
    total[...] = kept.get()[...].astype(F32) + other.get()[...].astype(F32)
    store_parts(total, outs)


def border_kernel(edge, accum, *refs):
    parts, grad = refs[:-1], refs[-1]
    rims = None
    for part in parts:
        more = total_of(part.get())
        rims = more if rims is None else rims + more
    high = rims.astype(BF16)
    low = (rims - high.astype(F32)).astype(BF16)
    pick = one_hot(rim_pixels(edge), edge * edge)
    added = dot_nt(high, pick) + dot_nt(low, pick)
    grad.ref[...] = (accum.get()[...] + added).astype(BF16)


def total_of(ref):
    return lax.fori_loop(1, ref.shape[0], lambda t, so_far: so_far + ref[t].astype(F32),
                         ref[0].astype(F32))


def sum_kernel(recv, tap, out, total, sems):
    recv = recv.get()
    share = recv.shape[1]
    total[:share, :] = total_of(recv).astype(BF16)
    total[share:, :] = tap.get()[...]
    copies = [pltpu.make_async_copy(total, out.at[t], sems.at[t]) for t in range(out.shape[0])]
    for copy in copies:
        copy.start()
    for copy in copies:
        copy.wait()


def final_kernel(which, last, share, channels, scale, *refs):
    count = len(which)
    pieces, taps_in = refs[:count], refs[count]
    g_in, g_out, g_tap_ref, buf_in, buf_out, sems = refs[-6:]
    full, units = buf_in.shape[1:]
    tiles, rows, _ = pieces[0].ref.shape
    copies = []
    all_taps = taps_in.get()[...] if last else jnp.zeros((full, LANES), F32)
    row_of = lax.broadcasted_iota(jnp.int32, (full, LANES), 0)
    for i, k in enumerate(which):
        piece = pieces[i].get()
        owner = lax.axis_index("chan") ^ k
        start = pl.multiple_of(owner * units, units)
        for in_in, buffer, target in ((True, buf_in, g_in.at[:, pl.ds(start, units)]),
                                      (False, buf_out, g_out.at[pl.ds(start, units)])):
            for tile in range(tiles):
                for row, height, column, at, into_in in chunks(tile, share, units, full):
                    if into_in == in_in:
                        values = piece[tile, row:row + height, :].astype(F32) * scale
                        buffer[i, at:at + height, column:column + LANES] = values
            copies.append(pltpu.make_async_copy(buffer.at[i], target, sems.at[int(in_in), i]))
            copies[-1].start()
        taps = piece[0, share:, :].astype(F32)
        for tile in range(1, tiles):
            taps = taps + piece[tile, share:, :].astype(F32)
        blocks = []
        for block in range(channels // 16):
            values = taps[block // 4 * 16:block // 4 * 16 + 16, :]
            blocks.append(roll(values, -32 * (block % 4)))
        own = jnp.concatenate(blocks * (full // channels), axis=0)
        all_taps = jnp.where(row_of // channels == owner, own, all_taps)
    if last:
        g_tap_ref[...] = all_taps.T[:KSIZE * KSIZE, :] * scale
    else:
        g_tap_ref[...] = all_taps
    for copy in copies:
        copy.wait()


def chunks(tile, share, units, full):
    inside, found = units // LANES * full, []
    row, end = tile * share, min((tile + 1) * share, 2 * units * full // LANES)
    while row < end:
        height = full if row < inside else units
        offset = row if row < inside else row - inside
        column, at = offset // height * LANES, offset % height
        count = min(end - row, height - at)
        found.append((row - tile * share, count, column, at, row < inside))
        row += count
    return found


def gather_pieces(own, groups, beside=()):
    pieces = {0: own}
    bit = groups // 2
    while bit:
        swap = [(i, i ^ bit) for i in range(groups)]
        for k in list(pieces):
            pieces[k ^ bit] = lax.ppermute(pieces[k], "chan", swap)
        if len(pieces) == 2 and beside:
            pieces[bit], *beside = lax.optimization_barrier((pieces[bit], *beside))
        bit //= 2
    return [pieces[k] for k in range(groups)], beside


def swap_rows(values):
    return lax.all_to_all(values, "tile", 0, 0, tiled=True)


def halve(parts, bit, after):
    kept, given = parts
    half = ((kept.shape[0] // 2, *kept.shape[1:]), BF16, NEAR)
    return call(pair_kernel, [(kept, NEAR), (swap_bit(given, bit), NEAR)], [half] * 2,
                [pltpu.VMEM(kept.shape, F32)], time=0.3, after=after)


def swap_bit(values, bit):
    return lax.ppermute(values, "tile", [(t, t ^ bit) for t in range(lax.axis_size("tile"))])


def body(inputs, grad_out, kernel, w_in, w_out, neighbours, rotations):
    channels, pixels = inputs.shape[1:]
    edge = math.isqrt(pixels)
    full, hidden = w_in.shape
    groups = lax.axis_size("chan")
    tiles = lax.axis_size("tile")
    wide = pixels + 2 * LANES
    rim = 4 * HALO * edge
    units = hidden // groups
    scale = (tiles * pixels) ** -0.5
    x, cot = inputs[0], grad_out[0]

    [rims] = call(functools.partial(pack_kernel, edge), [(x, FAR)],
                  [((tiles, channels, rim), BF16, RAW)],
                  [pltpu.VMEM((channels, rim), BF16), pltpu.SemaphoreType.DMA((tiles,))])
    _, kernel = lax.optimization_barrier((rims, kernel))
    taps = jnp.broadcast_to(kernel[:, :, None], (KSIZE * KSIZE, channels, LANES))
    cot_pieces, _ = gather_pieces(cot, groups)
    table = neighbours.shape
    w_in_t, x_near, nb_near, rot_near = call(
        prep_kernel, [(w_in, NEAR), (x, FAR), (neighbours, NEAR), (rotations, NEAR)],
        [((hidden, full), BF16, NEAR), ((channels, pixels), BF16, NEAR)]
        + [(neighbours.shape, jnp.int32, NEAR)] * 2, time=1.2,
        after=[(rims, RAW), (taps, NEAR)])
    rims = swap_rows(rims)

    hid, padded, side = call(
        functools.partial(conv_kernel, edge),
        [(nb_near, NEAR), (rot_near, NEAR), (x_near, NEAR), (rims, NEAR), (taps, NEAR)],
        [((channels, pixels), BF16, NEAR)] + [((channels, wide), BF16, FAR)] * 2,
        [pltpu.VMEM((len(SIDES) * channels, rim), BF16)], time=2.0,
        after=[(w_in_t, NEAR)])
    feats = lax.all_gather(hid, "chan", axis=0, tiled=True)
    cots, part_in, part_out = call(
        join_kernel, [(w_in_t, NEAR), (w_out, NEAR)] + [(piece, NEAR) for piece in cot_pieces],
        [((full, pixels), BF16, NEAR)] + [((units, full), BF16, NEAR)] * 2, time=0.6,
        after=[(feats, NEAR)])

    used = 2 * full * units // LANES
    share = -(-used // (16 * tiles)) * 16
    tap_rows = -(-channels // 64) * 16
    block = 2 * LANES
    [part] = call(
        weight_kernel,
        [(feats, NEAR), (cots, NEAR), (part_in, NEAR), (part_out, NEAR)],
        [((tiles * share, LANES), BF16, RAW)],
        [pltpu.VMEM((units, pixels), BF16)] * 2
        + [pltpu.VMEM((tiles * share, LANES), BF16), pltpu.SemaphoreType.DMA((3,))],
        time=2.2)
    part = swap_rows(part.reshape(tiles, share, LANES))

    parts = 2 if halves(tiles) else 1
    placed = ((tiles // parts, channels, rim), BF16, NEAR if parts > 1 else FAR)
    accum, tap_part, *border = call(
        functools.partial(back_kernel, edge, block, tiles),
        [(feats, NEAR), (cots, NEAR), (w_in, FAR), (w_in_t, NEAR), (w_out, NEAR), (padded, FAR),
         (side, FAR), (cot, FAR), (neighbours, NEAR), (rotations, NEAR), (taps, NEAR)],
        [((channels, pixels), F32, NEAR), ((tap_rows, LANES), BF16, NEAR)] + [placed] * parts,
        [pltpu.VMEM((hidden, pixels), BF16), pltpu.VMEM((channels, pixels), BF16),
         pltpu.VMEM((KSIZE * 16, wide), BF16), pltpu.VMEM((LANES, wide), BF16),
         pltpu.VMEM((channels, 2 * LANES), BF16), pltpu.VMEM((channels, wide), BF16),
         pltpu.VMEM((tiles, channels, rim), F32)], time=7.5, limit=32)
    [mine] = call(sum_kernel, [(part, NEAR), (tap_part, NEAR)],
                  [((tiles, share + tap_rows, LANES), BF16, RAW)],
                  [pltpu.VMEM((share + tap_rows, LANES), BF16), pltpu.SemaphoreType.DMA((tiles,))])
    weights = swap_rows(mine)

    [outputs] = call(
        functools.partial(out_kernel, block),
        [(feats, NEAR), (w_in_t, NEAR), (w_out, NEAR), (x, FAR)], [((channels, pixels), BF16, FAR)],
        [pltpu.VMEM((hidden, pixels), BF16)], time=4.0, limit=32, after=[(mine, RAW)])
    bit = 1
    while bit * 2 < tiles and parts > 1:
        border, bit = halve(border, bit, [(outputs, RAW)] if bit > 1 else []), bit * 2
    weights, outputs, *border = lax.optimization_barrier((weights, outputs, *border))
    border = [border[0], swap_bit(border[1], bit)] if parts > 1 else [swap_rows(border[0])]
    [grad_in] = call(functools.partial(border_kernel, edge),
                     [(accum, NEAR)] + [(part, NEAR) for part in border],
                     [((channels, pixels), BF16, FAR)])
    pieces, [grad_in] = gather_pieces(weights, groups, [grad_in])
    grads, ends = [], [(0, groups, 2), (1, groups, 2)]
    for last, end in enumerate(ends):
        which = list(range(*end))
        tap_shape = (KSIZE * KSIZE, full) if last else (full, LANES)
        grads = call(
            functools.partial(final_kernel, which, last, share, channels, scale),
            [(pieces[k], NEAR) for k in which]
            + ([(grads[2], NEAR), (grads[0], RAW), (grads[1], RAW)] if last else []),
            [((full, hidden), F32, RAW), ((hidden, full), F32, RAW), (tap_shape, F32, NEAR)],
            [pltpu.VMEM((len(which), full, units), F32), pltpu.VMEM((len(which), units, full), F32),
             pltpu.SemaphoreType.DMA((2, len(which)))],
            time=1.3, aliases={1 + len(which): 0, 2 + len(which): 1} if last else None)
    return (outputs[None], grad_in[None], *grads)


def solution(mesh):
    return jax.shard_map(
        body,
        mesh=mesh,
        in_specs=(
            P("tile", "chan", None),
            P("tile", "chan", None),
            P(None, "chan"),
            P(),
            P(),
            P(),
            P(),
        ),
        out_specs=(P("tile", "chan", None), P("tile", "chan", None), P(), P(), P()),
        check_vma=False,
    )
```

```python
import functools
import math

import jax
import jax.numpy as jnp
from jax import lax
from jax.experimental import pallas as pl
from jax.experimental.pallas import tpu as pltpu
from jax.sharding import PartitionSpec as P

KSIZE = 5
HALO = KSIZE // 2
LANES = 128
SIDES = (0, 2, 3, 4, 5, 7)
BF16 = jnp.bfloat16
F32 = jnp.float32

NEAR, FAR, RAW = "near", "far", "raw"
SPACES = {NEAR: pltpu.VMEM, FAR: pltpu.HBM, RAW: pltpu.HBM}


class Loaded:
    def __init__(self, ref, copy=None):
        self.ref, self.copy = ref, copy
        if copy is not None:
            copy.start()

    def get(self):
        if self.copy is not None:
            self.copy.wait()
            self.copy = None
        return self.ref


class Stored:
    def __init__(self, ref, copy):
        self.ref, self.copy, self.started = ref, copy, False

    def send(self):
        if not self.started:
            self.copy.start()
            self.started = True


def call(kernel, ins, outs, scratch=(), time=1.0, after=(), aliases=None, limit=16):
    ins = list(ins) + list(after)
    buffers = []
    for shape, dtype, place in [(a.shape, a.dtype, p) for a, p in ins] + list(outs):
        if place == FAR:
            buffers += [pltpu.VMEM(shape, dtype), pltpu.SemaphoreType.DMA]

    def run(*refs):
        ends = len(ins), len(ins) + len(outs), len(ins) + len(outs) + len(buffers)
        spare = list(refs[ends[1]:ends[2]])
        operands, results = [], []
        for ref, (_, place) in zip(refs, ins):
            if place == FAR:
                buffer, sem = spare.pop(0), spare.pop(0)
                operands.append(Loaded(buffer, pltpu.make_async_copy(ref, buffer, sem)))
            else:
                operands.append(Loaded(ref) if place == NEAR else ref)
        for ref, (_, _, place) in zip(refs[ends[0]:], outs):
            if place == FAR:
                buffer, sem = spare.pop(0), spare.pop(0)
                results.append(Stored(buffer, pltpu.make_async_copy(buffer, ref, sem)))
            else:
                results.append(ref)
        kernel(*operands[:len(ins) - len(after)], *results, *refs[ends[2]:])
        far = [result for result in results if isinstance(result, Stored)]
        for result in far:
            result.send()
        for result in far:
            result.copy.wait()

    return pl.pallas_call(
        run,
        out_shape=[pltpu.HBM(s, d) if p in (FAR, RAW) else jax.ShapeDtypeStruct(s, d)
                   for s, d, p in outs],
        in_specs=[pl.BlockSpec(memory_space=SPACES[p]) for _, p in ins],
        out_specs=[pl.BlockSpec(memory_space=SPACES[p]) for _, _, p in outs],
        scratch_shapes=buffers + list(scratch),
        input_output_aliases=aliases or {},
        cost_estimate=pl.CostEstimate(
            flops=int(time * 1e9), bytes_accessed=int(time * 3.5e6), transcendentals=0),
        compiler_params=pltpu.CompilerParams(vmem_limit_bytes=limit * 1024 * 1024),
    )(*[pltpu.with_memory_space_constraint(a, pltpu.HBM) if p in (FAR, RAW) else a
        for a, p in ins])


def tile_row(table):
    row = table.get()[pl.ds(lax.axis_index("tile"), 1), :]
    return [row[0, d] for d in range(8)]


def dot(a, b):
    return lax.dot_general(a, b, (((1,), (0,)), ((), ())), preferred_element_type=F32)


def dot_nt(a, b):
    return lax.dot_general(a, b, (((1,), (1,)), ((), ())), preferred_element_type=F32)


def one_hot(index, rows):
    row = lax.broadcasted_iota(jnp.int32, (rows, index.shape[1]), 0)
    return jnp.where(row == index, 1.0, 0.0).astype(BF16)


def rim_pixels(edge):
    band_len = HALO * edge
    lane = lax.broadcasted_iota(jnp.int32, (1, 4 * band_len), 1)
    band, at = lane // band_len, lane % band_len
    side = (at // HALO) * edge + at % HALO
    pixel = jnp.where(band == 0, at, (edge - HALO) * edge + at)
    return jnp.where(band == 2, side, jnp.where(band == 3, side + edge - HALO, pixel))


def rim_lane(row, col, edge):
    band_len = HALO * edge
    side = jnp.where(col < HALO, 2 * band_len + row * HALO + col,
                     3 * band_len + row * HALO + col - (edge - HALO))
    side = jnp.where(row >= edge - HALO, band_len + (row - (edge - HALO)) * edge + col, side)
    return jnp.where(row < HALO, row * edge + col, side)


def turned_lane(row, col, quarter, edge):
    last = edge - 1
    from_row = jnp.where(quarter == 1, col, jnp.where(
        quarter == 2, last - row, jnp.where(quarter == 3, last - col, row)))
    from_col = jnp.where(quarter == 1, last - row, jnp.where(
        quarter == 2, last - col, jnp.where(quarter == 3, row, col)))
    return rim_lane(from_row, from_col, edge)


def row_halo_maps(top_turn, bottom_turn, edge):
    rim = 4 * HALO * edge
    lane = lax.broadcasted_iota(jnp.int32, (1, LANES), 1)
    up = lane - (LANES - HALO * edge)
    top = turned_lane(edge - HALO + up // edge, up % edge, top_turn, edge)
    low = turned_lane(lane // edge, lane % edge, bottom_turn, edge)
    top = jnp.where(up >= 0, top, -1)
    low = jnp.where(lane < HALO * edge, low, -1)
    return one_hot(top, rim), one_hot(low, rim)


def side_map(turns, edge):
    rim = 4 * HALO * edge
    lane = lax.broadcasted_iota(jnp.int32, (1, 2 * LANES), 1)
    row, k = lane // (2 * HALO), lane % (2 * HALO)
    above, below, right = row < HALO, row >= HALO + edge, k >= HALO
    b_row = jnp.where(above, edge - HALO + row, jnp.where(below, row - HALO - edge, row - HALO))
    b_col = jnp.where(right, k - HALO, edge - HALO + k)
    slot = jnp.where(above, 0, jnp.where(below, 4, 2)) + right.astype(jnp.int32)
    quarter = jnp.zeros_like(slot)
    for position in range(len(SIDES)):
        quarter = jnp.where(slot == position, turns[position], quarter)
    index = turned_lane(b_row, b_col, quarter, edge)
    index = jnp.where(row < edge + 2 * HALO, index, -1)
    return one_hot(index, rim), slot


def spread_map(edge, wide):
    lane = lax.broadcasted_iota(jnp.int32, (1, wide), 1)
    row = lane // edge - (LANES // edge - HALO)
    col = lane % edge
    right_row, left_row = row - 1, row + 1
    rows = edge + 2 * HALO
    right = jnp.where((right_row >= 0) & (right_row < rows), right_row * 2 * HALO + HALO + col, -1)
    left = jnp.where((left_row >= 0) & (left_row < rows),
                     left_row * 2 * HALO + col - (edge - HALO), -1)
    index = jnp.where(col < HALO, right, jnp.where(col >= edge - HALO, left, -1))
    return one_hot(index, 2 * LANES)


def side_mask(shift, shape, edge):
    col = lax.broadcasted_iota(jnp.int32, shape, 1) % edge
    return col < shift if shift > 0 else col >= edge + shift


def roll(values, shift):
    size = values.shape[1]
    return values if shift % size == 0 else pltpu.roll(values, shift % size, axis=1)


def pack_kernel(edge, x, rims, rim, sems):
    pick = one_hot(rim_pixels(edge), edge * edge)
    rim[...] = dot(x.get()[...], pick).astype(BF16)
    copies = [pltpu.make_async_copy(rim, rims.at[t], sems.at[t]) for t in range(rims.shape[0])]
    for copy in copies:
        copy.start()
    for copy in copies:
        copy.wait()


def conv_kernel(edge, neighbours, top, low, pick, slot, spread, x, rims, taps,
                hidden_ref, padded, side, gathered):
    padded_ref, side_ref = padded.ref, side.ref
    rims_ref, taps_ref = rims.get(), taps.get()
    channels, pixels = hidden_ref.shape
    wide = pixels + 2 * LANES
    nb = tile_row(neighbours)
    padded_ref[:, :LANES] = dot(rims_ref[nb[1]], top.get()[...]).astype(BF16)
    padded_ref[:, LANES + pixels:] = dot(rims_ref[nb[6]], low.get()[...]).astype(BF16)
    for position, d in enumerate(SIDES):
        gathered[position * channels:(position + 1) * channels, :] = rims_ref[nb[d]]
    candidates, slot = dot(gathered[...], pick.get()[...]), slot.get()[...]
    packed = candidates[:channels, :]
    for position in range(1, len(SIDES)):
        packed = jnp.where(slot == position,
                           candidates[position * channels:(position + 1) * channels, :], packed)
    packed = packed.astype(BF16)
    side_ref[...] = dot(packed, spread.get()[...]).astype(BF16)
    side.send()
    padded_ref[:, LANES:LANES + pixels] = x.get()[...]
    padded.send()

    def block(i, carry):
        at = pl.multiple_of(i * 16, 16)
        xs = padded_ref[pl.ds(at, 16), :].astype(F32)
        hs = side_ref[pl.ds(at, 16), :].astype(F32)
        taps = [taps_ref[tap, pl.ds(at, 16), :].astype(F32) for tap in range(KSIZE * KSIZE)]
        halves = []
        for half in (0, 8):
            x, h = xs[half:half + 8], hs[half:half + 8]
            sums = [None] * KSIZE
            for b in range(KSIZE):
                shift = b - HALO
                moved = x
                if shift:
                    moved = roll(jnp.where(side_mask(shift, x.shape, edge), h, x), -shift)
                for a in range(KSIZE):
                    term = jnp.tile(taps[a * KSIZE + b][half:half + 8], (1, wide // LANES)) * moved
                    sums[a] = term if sums[a] is None else sums[a] + term
            total = None
            for a in range(KSIZE):
                part = roll(sums[a], -(a - HALO) * edge)[:, LANES:LANES + pixels]
                total = part if total is None else total + part
            halves.append(total)
        hidden_ref[pl.ds(at, 16), :] = jnp.concatenate(halves, axis=0).astype(BF16)
        return carry

    lax.fori_loop(0, channels // 16, block, 0)


def normal_below(values):
    return 0.5 * (1.0 + lax.erf(values * 0.7071067811865476))


def gelu_slope(values, below):
    return below + values * jnp.exp(-0.5 * values * values) * 0.3989422804014327


def column_steps(ref):
    return [slice(at, at + 2 * LANES) for at in range(0, ref.shape[1], 2 * LANES)]


def over_units(units, block, body):
    def step(i, carry):
        body(pl.ds(pl.multiple_of(i * block, block), block))
        return carry

    lax.fori_loop(0, units // block, step, 0)


def weight_kernel(feats, cots, w_in_t, w_out, part, act, gpre, stack, sems):
    feats, cots = feats.get(), cots.get()
    full, units = feats.shape[0], act.shape[0]
    w_in_t, w_out = w_in_t.get()[...], w_out.get()[...]
    for part_of in column_steps(feats):
        pre = dot(w_in_t, feats[:, part_of])
        below = normal_below(pre)
        act[:, part_of] = (pre * below).astype(BF16)
        slope = gelu_slope(pre, below)
        gpre[:, part_of] = (dot(w_out, cots[:, part_of]) * slope).astype(BF16)
    used, copies = 0, []
    for values, height in ((dot_nt(feats[...], gpre[...]), full),
                           (dot_nt(act[...], cots[...]), units)):
        first = used
        for column in range(0, values.shape[1], LANES):
            stack[used:used + height, :] = values[:, column:column + LANES].astype(BF16)
            used += height
        copies.append(pltpu.make_async_copy(
            stack.at[first:used], part.at[first:used], sems.at[len(copies)]))
        copies[-1].start()
    if used < part.shape[0]:
        stack[used:, :] = jnp.zeros((part.shape[0] - used, LANES), BF16)
        copies.append(pltpu.make_async_copy(stack.at[used:], part.at[used:], sems.at[2]))
        copies[-1].start()
    for copy in copies:
        copy.wait()


def out_kernel(block, feats, w_in_t, w_out, x, out, act):
    feats, w_in_t, w_out = feats.get(), w_in_t.get(), w_out.get()

    def units(rows):
        for part_of in column_steps(feats):
            pre = dot(w_in_t[rows, :], feats[:, part_of])
            act[rows, part_of] = (pre * normal_below(pre)).astype(BF16)

    over_units(w_out.shape[0], block, units)
    channels = out.ref.shape[0]
    row = lax.broadcasted_iota(jnp.int32, (channels, w_out.shape[1]), 0)
    column = lax.broadcasted_iota(jnp.int32, (channels, w_out.shape[1]), 1)
    pick = jnp.where(column == row + lax.axis_index("chan") * channels, 1.0, 0.0).astype(BF16)
    branch = dot(dot_nt(pick, w_out[...]).astype(BF16), act[...])
    out.ref[...] = (x.get()[...].astype(F32) + branch.astype(BF16).astype(F32)).astype(BF16)


def back_kernel(edge, block, tiles, feats, cots, w_in, w_in_t, w_out, padded, side, cot, neighbours,
                rotations, taps, accum_ref, tap_ref, *refs):
    outs, (gpre, grad_ref, turned_all, moved_all, d_row, d_side, gathered) = refs[:-7], refs[-7:]
    channels = grad_ref.shape[0]
    feats, cots, w_in_t, w_out = feats.get(), cots.get(), w_in_t.get(), w_out.get()

    def units(rows):
        for part_of in column_steps(feats):
            pre = dot(w_in_t[rows, :], feats[:, part_of])
            slope = gelu_slope(pre, normal_below(pre))
            gpre[rows, part_of] = (dot(w_out[rows, :], cots[:, part_of]) * slope).astype(BF16)

    over_units(w_out.shape[0], block, units)
    own = pl.ds(pl.multiple_of(lax.axis_index("chan") * channels, channels), channels)
    grad_ref[...] = dot(w_in.get()[own, :], gpre[...]).astype(BF16)
    tap_terms(edge, grad_ref, padded.get(), side.get(), tap_ref, turned_all, moved_all)
    halo_adjoint(edge, neighbours, rotations, grad_ref, taps.get(), cot.get(), accum_ref, outs,
                 d_row, d_side, gathered)


def prep_kernel(edge, w_in, x, neighbours, rotations, w_in_t_ref, x_ref, nb_ref, *map_refs):
    nb_ref[...] = neighbours.get()[...]
    rot = tile_row(rotations)
    pick, slot = side_map([rot[d] for d in SIDES], edge)
    wide = x_ref.shape[1] + 2 * LANES
    maps = (*row_halo_maps(rot[1], rot[6], edge), pick, slot, spread_map(edge, wide))
    for ref, values in zip(map_refs, maps):
        ref[...] = values
    w_in_t_ref[...] = w_in.get()[...].astype(F32).T.astype(BF16)
    x_ref[...] = x.get()[...]


def join_kernel(w_in_t, w_out, *refs):
    pieces, (out_ref, part_in_ref, part_out_ref) = refs[:-3], refs[-3:]
    chan = lax.axis_index("chan")
    for k, piece in enumerate(pieces):
        piece = piece.get()
        channels = piece.shape[0]
        start = pl.multiple_of((chan ^ k) * channels, channels)
        out_ref[pl.ds(start, channels), :] = piece[...]
    units = part_in_ref.shape[0]
    mine = pl.ds(pl.multiple_of(chan * units, units), units)
    part_in_ref[...] = w_in_t.get()[mine, :]
    part_out_ref[...] = w_out.get()[mine, :]


def tap_terms(edge, grad_ref, padded_ref, side_ref, tap_ref, turned_all, moved_all):
    channels, pixels = grad_ref.shape
    wide = pixels + 2 * LANES
    moved_all[KSIZE * 16:, :] = jnp.zeros((LANES - KSIZE * 16, wide), BF16)
    same = (lax.broadcasted_iota(jnp.int32, (16, KSIZE * LANES), 1) % 16
            == lax.broadcasted_iota(jnp.int32, (16, KSIZE * LANES), 0))
    line = lax.broadcasted_iota(jnp.int32, (KSIZE * LANES, LANES), 0)
    tap = lax.broadcasted_iota(jnp.int32, (KSIZE * LANES, LANES), 1)
    used = line % LANES < KSIZE * 16
    pick = jnp.where(used & (line // LANES * KSIZE + line % LANES // 16 == tap), 1.0, 0.0).astype(BF16)
    mask = {b: side_mask(b - HALO, (16, wide), edge) for b in range(KSIZE) if b != HALO}
    lane = lax.broadcasted_iota(jnp.int32, (16, LANES), 1)
    zeros = jnp.zeros((16, LANES), F32)
    found = []
    for at in range(0, channels, 16):
        g = jnp.concatenate([zeros, grad_ref[at:at + 16, :].astype(F32), zeros], axis=1)
        x = padded_ref[at:at + 16, :].astype(F32)
        h = side_ref[at:at + 16, :].astype(F32)
        for a in range(KSIZE):
            shift = a - HALO
            turned_all[a * 16:a * 16 + 16, :] = roll(g, shift * edge).astype(BF16)
            moved = roll(jnp.where(mask[a], h, x), -shift) if shift else x
            moved_all[a * 16:a * 16 + 16, :] = moved.astype(BF16)
        products = dot_nt(turned_all[...], moved_all[...])
        side_by_side = jnp.concatenate(
            [products[a * 16:a * 16 + 16, :] for a in range(KSIZE)], axis=1)
        taps = dot(jnp.where(same, side_by_side, 0.0).astype(BF16), pick)
        place = at // 16 % 4
        taps = jnp.where(lane // 32 == place, roll(taps, 32 * place), 0.0)
        if place == 0:
            found.append(taps)
        else:
            found[-1] = found[-1] + taps
    tap_ref[...] = jnp.concatenate(found, axis=0).astype(BF16)


def halo_adjoint(edge, neighbours, rotations, grad_ref, taps_ref, cot_ref, accum_ref, outs,
                 d_row, d_side, gathered):
    channels, pixels = grad_ref.shape
    wide = pixels + 2 * LANES
    tiles = gathered.shape[0]

    def block(i, carry):
        at = pl.multiple_of(i * 16, 16)
        gs = grad_ref[pl.ds(at, 16), :].astype(F32)
        taps_of = [taps_ref[tap, pl.ds(at, 16), :].astype(F32) for tap in range(KSIZE * KSIZE)]
        zeros = jnp.zeros((8, LANES), F32)
        rows, sides = [], []
        for half in (0, 8):
            g = jnp.concatenate([zeros, gs[half:half + 8], zeros], axis=1)
            turned = [roll(g, (a - HALO) * edge) for a in range(KSIZE)]
            d_x = d_h = None
            for b in range(KSIZE):
                shift = b - HALO
                back = None
                for a in range(KSIZE):
                    weight = taps_of[a * KSIZE + b][half:half + 8]
                    term = jnp.tile(weight, (1, wide // LANES)) * turned[a]
                    back = term if back is None else back + term
                back = roll(back, shift)
                if shift:
                    mask = side_mask(shift, back.shape, edge)
                    inside = jnp.where(mask, 0.0, back)
                    outside = jnp.where(mask, back, 0.0)
                    d_h = outside if d_h is None else d_h + outside
                    d_x = inside if d_x is None else d_x + inside
                else:
                    d_x = back if d_x is None else d_x + back
            rows.append(d_x)
            sides.append(d_h)
        d_x = jnp.concatenate(rows, axis=0)
        accum_ref[pl.ds(at, 16), :] = d_x[:, LANES:LANES + pixels]
        d_row[pl.ds(at, 16), :LANES] = d_x[:, :LANES].astype(BF16)
        d_row[pl.ds(at, 16), LANES:] = d_x[:, LANES + pixels:].astype(BF16)
        d_side[pl.ds(at, 16), :] = jnp.concatenate(sides, axis=0).astype(BF16)
        return carry

    lax.fori_loop(0, channels // 16, block, 0)
    accum_ref[...] += cot_ref[...].astype(F32)
    nb, rot = tile_row(neighbours), tile_row(rotations)
    gathered[...] = jnp.zeros(gathered.shape, F32)
    top, low = row_halo_maps(rot[1], rot[6], edge)
    gathered[slot_of(nb[1], tiles)] += dot_nt(d_row[:, :LANES], top)
    gathered[slot_of(nb[6], tiles)] += dot_nt(d_row[:, LANES:], low)
    packed = dot_nt(d_side[...], spread_map(edge, wide))
    pick, slot = side_map([rot[d] for d in SIDES], edge)
    for position, d in enumerate(SIDES):
        own = jnp.where(slot == position, packed, 0.0).astype(BF16)
        gathered[slot_of(nb[d], tiles)] += dot_nt(own, pick)
    store_parts(gathered, outs)


def store_parts(values, outs):
    for part, out in enumerate(outs):
        out = out.ref if isinstance(out, Stored) else out
        rows = out.shape[0]

        def store(t, carry, out=out, first=part * rows):
            out[t] = values[first + t].astype(BF16)
            return carry

        lax.fori_loop(0, rows, store, 0)


def halves(tiles):
    return tiles & (tiles - 1) == 0


def slot_of(tile, tiles):
    if not halves(tiles):
        return tile
    apart, slot = tile ^ lax.axis_index("tile"), 0
    for bit in halving_bits(tiles):
        slot = slot * 2 + jnp.where(apart & bit != 0, 1, 0)
    return slot


def halving_bits(tiles):
    return [1 << i for i in range(tiles.bit_length() - 2, 0, -2)] + [1, 2][:tiles.bit_length() - 2]


def pair_kernel(kept, other, *refs):
    outs, total = refs[:-1], refs[-1]
    total[...] = kept.get()[...].astype(F32) + other.get()[...].astype(F32)
    store_parts(total, outs)


def border_kernel(edge, accum, *refs):
    parts, grad = refs[:-1], refs[-1]
    rims = None
    for part in parts:
        more = total_of(part.get())
        rims = more if rims is None else rims + more
    high = rims.astype(BF16)
    low = (rims - high.astype(F32)).astype(BF16)
    pick = one_hot(rim_pixels(edge), edge * edge)
    added = dot_nt(high, pick) + dot_nt(low, pick)
    grad.ref[...] = (accum.get()[...] + added).astype(BF16)


def total_of(ref):
    return lax.fori_loop(1, ref.shape[0], lambda t, so_far: so_far + ref[t].astype(F32),
                         ref[0].astype(F32))


def sum_kernel(recv, tap, out, total, sems):
    recv = recv.get()
    share = recv.shape[1]
    total[:share, :] = total_of(recv).astype(BF16)
    total[share:, :] = tap.get()[...]
    copies = [pltpu.make_async_copy(total, out.at[t], sems.at[t]) for t in range(out.shape[0])]
    for copy in copies:
        copy.start()
    for copy in copies:
        copy.wait()


def compact_kernel(share, values, out):
    values = values.get()
    tiles, rows, _ = values.shape
    for tile in range(tiles):
        out[tile * share:(tile + 1) * share, :] = values[tile, :share, :]
    taps = values[0, share:, :].astype(F32)
    for tile in range(1, tiles):
        taps = taps + values[tile, share:, :].astype(F32)
    out[tiles * share:, :] = taps.astype(BF16)


def final_kernel(which, channels, tap_rows, scale, last, *refs):
    pieces, taps_in = refs[:len(which)], refs[len(which)]
    g_in, g_out, g_tap_ref, buf_in, buf_out, sems = refs[-6:]
    full, units = buf_in.shape[1:]
    copies = []
    all_taps = taps_in.get()[...]
    row_of = lax.broadcasted_iota(jnp.int32, (full, LANES), 0)
    for i, k in enumerate(which):
        piece = pieces[i].get()
        owner = lax.axis_index("chan") ^ k
        start = pl.multiple_of(owner * units, units)
        used = 0
        for buffer, target in ((buf_in, g_in.at[:, pl.ds(start, units)]),
                               (buf_out, g_out.at[pl.ds(start, units)])):
            height, width = buffer.shape[1:]
            for column in range(0, width, LANES):
                buffer[i, :, column:column + LANES] = piece[used:used + height, :].astype(F32) * scale
                used += height
            copies.append(pltpu.make_async_copy(buffer.at[i], target, sems.at[len(copies)]))
            copies[-1].start()
        taps = piece[piece.shape[0] - tap_rows:, :].astype(F32)
        blocks = []
        for block in range(channels // 16):
            values = taps[block // 4 * 16:block // 4 * 16 + 16, :]
            blocks.append(roll(values, -32 * (block % 4)))
        own = jnp.concatenate(blocks * (full // channels), axis=0)
        all_taps = jnp.where(row_of // channels == owner, own, all_taps)
    if last:
        g_tap_ref[...] = all_taps.T[:KSIZE * KSIZE, :] * scale
    else:
        g_tap_ref[...] = all_taps
    for copy in copies:
        copy.wait()


def swap_chan(values, bit):
    return lax.ppermute(values, "chan", [(i, i ^ bit) for i in range(lax.axis_size("chan"))])


def gather_pieces(own, groups):
    pieces = {0: own}
    bit = groups // 2
    while bit:
        for k in list(pieces):
            pieces[k ^ bit] = swap_chan(pieces[k], bit)
        bit //= 2
    return [pieces[k] for k in range(groups)]


def swap_rows(values):
    return lax.all_to_all(values, "tile", 0, 0, tiled=True)


def halve(parts, bit, after):
    kept, given = parts
    half = ((kept.shape[0] // 2, *kept.shape[1:]), BF16, NEAR)
    return call(pair_kernel, [(kept, NEAR), (swap_bit(given, bit), NEAR)], [half] * 2,
                [pltpu.VMEM(kept.shape, F32)], time=0.3, after=after)


def swap_bit(values, bit):
    return lax.ppermute(values, "tile", [(t, t ^ bit) for t in range(lax.axis_size("tile"))])


def body(inputs, grad_out, kernel, w_in, w_out, neighbours, rotations):
    channels, pixels = inputs.shape[1:]
    edge = math.isqrt(pixels)
    full, hidden = w_in.shape
    groups = lax.axis_size("chan")
    tiles = lax.axis_size("tile")
    wide = pixels + 2 * LANES
    rim = 4 * HALO * edge
    units = hidden // groups
    scale = (tiles * pixels) ** -0.5
    x, cot = inputs[0], grad_out[0]

    [rims] = call(functools.partial(pack_kernel, edge), [(x, FAR)],
                  [((tiles, channels, rim), BF16, RAW)],
                  [pltpu.VMEM((channels, rim), BF16), pltpu.SemaphoreType.DMA((tiles,))])
    _, kernel = lax.optimization_barrier((rims, kernel))
    taps = jnp.broadcast_to(kernel[:, :, None], (KSIZE * KSIZE, channels, LANES))
    cot_pieces = gather_pieces(cot, groups)
    table = neighbours.shape
    w_in_t, x_near, nb_near, *maps = call(
        functools.partial(prep_kernel, edge),
        [(w_in, NEAR), (x, FAR), (neighbours, NEAR), (rotations, NEAR)],
        [((hidden, full), BF16, NEAR), ((channels, pixels), BF16, NEAR),
         (neighbours.shape, jnp.int32, NEAR), ((rim, LANES), BF16, NEAR), ((rim, LANES), BF16, NEAR),
         ((rim, 2 * LANES), BF16, NEAR), ((1, 2 * LANES), jnp.int32, NEAR),
         ((2 * LANES, wide), BF16, NEAR)], time=1.2,
        after=[(rims, RAW), (taps, NEAR)])
    rims = swap_rows(rims)

    hid, padded, side = call(
        functools.partial(conv_kernel, edge),
        [(a, NEAR) for a in (nb_near, *maps, x_near, rims, taps)],
        [((channels, pixels), BF16, NEAR)] + [((channels, wide), BF16, FAR)] * 2,
        [pltpu.VMEM((len(SIDES) * channels, rim), BF16)], time=2.0,
        after=[(w_in_t, NEAR)])
    feats = lax.all_gather(hid, "chan", axis=0, tiled=True)
    cots, part_in, part_out = call(
        join_kernel, [(w_in_t, NEAR), (w_out, NEAR)] + [(piece, NEAR) for piece in cot_pieces],
        [((full, pixels), BF16, NEAR)] + [((units, full), BF16, NEAR)] * 2, time=0.6,
        after=[(feats, NEAR)])

    used = 2 * full * units // LANES
    share = -(-used // (16 * tiles)) * 16
    tap_rows = -(-channels // 64) * 16
    block = 2 * LANES
    [part] = call(
        weight_kernel,
        [(feats, NEAR), (cots, NEAR), (part_in, NEAR), (part_out, NEAR)],
        [((tiles * share, LANES), BF16, RAW)],
        [pltpu.VMEM((units, pixels), BF16)] * 2
        + [pltpu.VMEM((tiles * share, LANES), BF16), pltpu.SemaphoreType.DMA((3,))],
        time=2.2)
    part = swap_rows(part.reshape(tiles, share, LANES))

    parts = 2 if halves(tiles) else 1
    placed = ((tiles // parts, channels, rim), BF16, NEAR if parts > 1 else FAR)
    accum, tap_part, *border = call(
        functools.partial(back_kernel, edge, block, tiles),
        [(feats, NEAR), (cots, NEAR), (w_in, FAR), (w_in_t, NEAR), (w_out, NEAR), (padded, FAR),
         (side, FAR), (cot, FAR), (neighbours, NEAR), (rotations, NEAR), (taps, NEAR)],
        [((channels, pixels), F32, NEAR), ((tap_rows, LANES), BF16, NEAR)] + [placed] * parts,
        [pltpu.VMEM((hidden, pixels), BF16), pltpu.VMEM((channels, pixels), BF16),
         pltpu.VMEM((KSIZE * 16, wide), BF16), pltpu.VMEM((LANES, wide), BF16),
         pltpu.VMEM((channels, 2 * LANES), BF16), pltpu.VMEM((channels, wide), BF16),
         pltpu.VMEM((tiles, channels, rim), F32)], time=7.5, limit=32)
    [mine] = call(sum_kernel, [(part, NEAR), (tap_part, NEAR)],
                  [((tiles, share + tap_rows, LANES), BF16, RAW)],
                  [pltpu.VMEM((share + tap_rows, LANES), BF16), pltpu.SemaphoreType.DMA((tiles,))])
    [weights] = call(functools.partial(compact_kernel, share), [(swap_rows(mine), NEAR)],
                     [((tiles * share + tap_rows, LANES), BF16, NEAR)], time=0.1)

    [outputs] = call(
        functools.partial(out_kernel, block),
        [(feats, NEAR), (w_in_t, NEAR), (w_out, NEAR), (x, FAR)], [((channels, pixels), BF16, FAR)],
        [pltpu.VMEM((hidden, pixels), BF16)], time=4.0, limit=32, after=[(mine, RAW)])
    bits = halving_bits(tiles) if parts > 1 else [0]
    for step, bit in enumerate(bits[:-1]):
        border = halve(border, bit, [(outputs, RAW)] if step else [])
    weights, outputs, *border = lax.optimization_barrier((weights, outputs, *border))
    border = [border[0], swap_bit(border[1], bits[-1])] if parts > 1 else [swap_rows(border[0])]
    [grad_in] = call(functools.partial(border_kernel, edge),
                     [(accum, NEAR)] + [(part, NEAR) for part in border],
                     [((channels, pixels), BF16, FAR)])

    def place(which, grads, last):
        tap_shape = (KSIZE * KSIZE, full) if last else (full, LANES)
        more = [(grads[0], RAW), (grads[1], RAW)] if grads[0] is not None else []
        return call(
            functools.partial(final_kernel, which, channels, tap_rows, scale, last),
            [(pieces[k], NEAR) for k in which] + [(grads[2], NEAR)] + more,
            [((full, hidden), F32, RAW), ((hidden, full), F32, RAW), (tap_shape, F32, NEAR)],
            [pltpu.VMEM((len(which), full, units), F32), pltpu.VMEM((len(which), units, full), F32),
             pltpu.SemaphoreType.DMA((2 * len(which),))],
            time=1.2, aliases={1 + len(which): 0, 2 + len(which): 1} if more else None)

    pieces = {0: weights}
    bit = groups // 2
    while bit > 1:
        for k in [k for k in pieces if k % 2 == 0]:
            pieces[k ^ bit] = swap_chan(pieces[k], bit)
        bit //= 2
    pieces[1] = swap_chan(weights, 1)
    even, odd = list(range(2, groups, 2)), list(range(3, groups, 2))
    for k in even:
        pieces[k], grad_in = lax.optimization_barrier((pieces[k], grad_in))
    for k in odd:
        pieces[k] = swap_chan(pieces[k ^ 1], 1)
    grads = place([0, 1, *even], [None, None, jnp.zeros((full, LANES), F32)], False)
    grads = place(odd, grads, True)
    return (outputs[None], grad_in[None], *grads)


def solution(mesh):
    return jax.shard_map(
        body,
        mesh=mesh,
        in_specs=(
            P("tile", "chan", None),
            P("tile", "chan", None),
            P(None, "chan"),
            P(),
            P(),
            P(),
            P(),
        ),
        out_specs=(P("tile", "chan", None), P("tile", "chan", None), P(), P(), P()),
        check_vma=False,
    )
```

```python
import functools
import math

import jax
import jax.numpy as jnp
from jax import lax
from jax.experimental import pallas as pl
from jax.experimental.pallas import tpu as pltpu
from jax.sharding import PartitionSpec as P

KSIZE = 5
HALO = KSIZE // 2
LANES = 128
SIDES = (0, 2, 3, 4, 5, 7)
BF16 = jnp.bfloat16
F32 = jnp.float32

NEAR, FAR, RAW, PINNED = "near", "far", "raw", "pinned"
SPACES = {NEAR: pltpu.VMEM, FAR: pltpu.HBM, RAW: pltpu.HBM, PINNED: pltpu.VMEM}


class Loaded:
    def __init__(self, ref, copy=None):
        self.ref, self.copy = ref, copy
        if copy is not None:
            copy.start()

    def get(self):
        if self.copy is not None:
            self.copy.wait()
            self.copy = None
        return self.ref


class Stored:
    def __init__(self, ref, copy):
        self.ref, self.copy, self.started = ref, copy, False

    def send(self):
        if not self.started:
            self.copy.start()
            self.started = True


def call(kernel, ins, outs, scratch=(), time=1.0, after=(), aliases=None, limit=16):
    ins = list(ins) + list(after)
    buffers = []
    for shape, dtype, place in [(a.shape, a.dtype, p) for a, p in ins] + list(outs):
        if place == FAR:
            buffers += [pltpu.VMEM(shape, dtype), pltpu.SemaphoreType.DMA]

    def run(*refs):
        ends = len(ins), len(ins) + len(outs), len(ins) + len(outs) + len(buffers)
        spare = list(refs[ends[1]:ends[2]])
        operands, results = [], []
        for ref, (_, place) in zip(refs, ins):
            if place == FAR:
                buffer, sem = spare.pop(0), spare.pop(0)
                operands.append(Loaded(buffer, pltpu.make_async_copy(ref, buffer, sem)))
            else:
                operands.append(Loaded(ref) if place == NEAR else ref)
        for ref, (_, _, place) in zip(refs[ends[0]:], outs):
            if place == FAR:
                buffer, sem = spare.pop(0), spare.pop(0)
                results.append(Stored(buffer, pltpu.make_async_copy(buffer, ref, sem)))
            else:
                results.append(ref)
        kernel(*operands[:len(ins) - len(after)], *results, *refs[ends[2]:])
        far = [result for result in results if isinstance(result, Stored)]
        for result in far:
            result.send()
        for result in far:
            result.copy.wait()

    return pl.pallas_call(
        run,
        out_shape=[SPACES[p](s, d) if p != NEAR else jax.ShapeDtypeStruct(s, d)
                   for s, d, p in outs],
        in_specs=[pl.BlockSpec(memory_space=SPACES[p]) for _, p in ins],
        out_specs=[pl.BlockSpec(memory_space=SPACES[p]) for _, _, p in outs],
        scratch_shapes=buffers + list(scratch),
        input_output_aliases=aliases or {},
        cost_estimate=pl.CostEstimate(
            flops=int(time * 1e9), bytes_accessed=int(time * 3.5e6), transcendentals=0),
        compiler_params=pltpu.CompilerParams(vmem_limit_bytes=limit * 1024 * 1024),
    )(*[pltpu.with_memory_space_constraint(a, pltpu.HBM) if p in (FAR, RAW) else a
        for a, p in ins])


def tile_row(table):
    row = table.get()[pl.ds(lax.axis_index("tile"), 1), :]
    return [row[0, d] for d in range(8)]


def dot(a, b):
    return lax.dot_general(a, b, (((1,), (0,)), ((), ())), preferred_element_type=F32)


def dot_nt(a, b):
    return lax.dot_general(a, b, (((1,), (1,)), ((), ())), preferred_element_type=F32)


def one_hot(index, rows):
    row = lax.broadcasted_iota(jnp.int32, (rows, index.shape[1]), 0)
    return jnp.where(row == index, 1.0, 0.0).astype(BF16)


def rim_pixels(edge):
    band_len = HALO * edge
    lane = lax.broadcasted_iota(jnp.int32, (1, 4 * band_len), 1)
    band, at = lane // band_len, lane % band_len
    side = (at // HALO) * edge + at % HALO
    pixel = jnp.where(band == 0, at, (edge - HALO) * edge + at)
    return jnp.where(band == 2, side, jnp.where(band == 3, side + edge - HALO, pixel))


def rim_lane(row, col, edge):
    band_len = HALO * edge
    side = jnp.where(col < HALO, 2 * band_len + row * HALO + col,
                     3 * band_len + row * HALO + col - (edge - HALO))
    side = jnp.where(row >= edge - HALO, band_len + (row - (edge - HALO)) * edge + col, side)
    return jnp.where(row < HALO, row * edge + col, side)


def turned_lane(row, col, quarter, edge):
    last = edge - 1
    from_row = jnp.where(quarter == 1, col, jnp.where(
        quarter == 2, last - row, jnp.where(quarter == 3, last - col, row)))
    from_col = jnp.where(quarter == 1, last - row, jnp.where(
        quarter == 2, last - col, jnp.where(quarter == 3, row, col)))
    return rim_lane(from_row, from_col, edge)


def row_halo_maps(top_turn, bottom_turn, edge):
    rim = 4 * HALO * edge
    lane = lax.broadcasted_iota(jnp.int32, (1, LANES), 1)
    up = lane - (LANES - HALO * edge)
    top = turned_lane(edge - HALO + up // edge, up % edge, top_turn, edge)
    low = turned_lane(lane // edge, lane % edge, bottom_turn, edge)
    top = jnp.where(up >= 0, top, -1)
    low = jnp.where(lane < HALO * edge, low, -1)
    return one_hot(top, rim), one_hot(low, rim)


def side_map(turns, edge):
    rim = 4 * HALO * edge
    lane = lax.broadcasted_iota(jnp.int32, (1, 2 * LANES), 1)
    row, k = lane // (2 * HALO), lane % (2 * HALO)
    above, below, right = row < HALO, row >= HALO + edge, k >= HALO
    b_row = jnp.where(above, edge - HALO + row, jnp.where(below, row - HALO - edge, row - HALO))
    b_col = jnp.where(right, k - HALO, edge - HALO + k)
    slot = jnp.where(above, 0, jnp.where(below, 4, 2)) + right.astype(jnp.int32)
    quarter = jnp.zeros_like(slot)
    for position in range(len(SIDES)):
        quarter = jnp.where(slot == position, turns[position], quarter)
    index = turned_lane(b_row, b_col, quarter, edge)
    index = jnp.where(row < edge + 2 * HALO, index, -1)
    return one_hot(index, rim), slot


def spread_map(edge, wide):
    lane = lax.broadcasted_iota(jnp.int32, (1, wide), 1)
    row = lane // edge - (LANES // edge - HALO)
    col = lane % edge
    right_row, left_row = row - 1, row + 1
    rows = edge + 2 * HALO
    right = jnp.where((right_row >= 0) & (right_row < rows), right_row * 2 * HALO + HALO + col, -1)
    left = jnp.where((left_row >= 0) & (left_row < rows),
                     left_row * 2 * HALO + col - (edge - HALO), -1)
    index = jnp.where(col < HALO, right, jnp.where(col >= edge - HALO, left, -1))
    return one_hot(index, 2 * LANES)


def side_mask(shift, shape, edge):
    col = lax.broadcasted_iota(jnp.int32, shape, 1) % edge
    return col < shift if shift > 0 else col >= edge + shift


def roll(values, shift):
    size = values.shape[1]
    return values if shift % size == 0 else pltpu.roll(values, shift % size, axis=1)


def pack_kernel(edge, x, rims, rim, sems):
    pick = one_hot(rim_pixels(edge), edge * edge)
    rim[...] = dot(x.get()[...], pick).astype(BF16)
    copies = [pltpu.make_async_copy(rim, rims.at[t], sems.at[t]) for t in range(rims.shape[0])]
    for copy in copies:
        copy.start()
    for copy in copies:
        copy.wait()


def shifted(values, shift, edge):
    if not shift:
        return values
    return roll(jnp.where(side_mask(shift, values.shape, edge), 0.0, values), -shift)


def tap_rows_of(taps_ref, at):
    return [taps_ref[tap, pl.ds(at, 16), :].astype(F32) for tap in range(KSIZE * KSIZE)]


def center_conv(edge, x_ref, taps_ref, out_ref):
    channels, pixels = x_ref.shape
    wide = pixels + 2 * LANES

    def block(i, carry):
        at = pl.multiple_of(i * 16, 16)
        xs = x_ref[pl.ds(at, 16), :].astype(F32)
        taps = tap_rows_of(taps_ref, at)
        zeros = jnp.zeros((8, LANES), F32)
        halves = []
        for half in (0, 8):
            x = jnp.concatenate([zeros, xs[half:half + 8], zeros], axis=1)
            sums = [None] * KSIZE
            for b in range(KSIZE):
                moved = shifted(x, b - HALO, edge)
                for a in range(KSIZE):
                    term = jnp.tile(taps[a * KSIZE + b][half:half + 8], (1, wide // LANES)) * moved
                    sums[a] = term if sums[a] is None else sums[a] + term
            total = None
            for a in range(KSIZE):
                part = roll(sums[a], -(a - HALO) * edge)[:, LANES:LANES + pixels]
                total = part if total is None else total + part
            halves.append(total)
        out_ref[pl.ds(at, 16), :] = jnp.concatenate(halves, axis=0)
        return carry

    lax.fori_loop(0, channels // 16, block, 0)


def row_terms(rows, taps, edge, below):
    lane = lax.broadcasted_iota(jnp.int32, rows.shape, 1)
    total = None
    for a in range(KSIZE):
        far = a - HALO if below else HALO - a
        if far <= 0:
            continue
        sums = None
        for b in range(KSIZE):
            term = taps[a * KSIZE + b] * shifted(rows, b - HALO, edge)
            sums = term if sums is None else sums + term
        if below:
            part = jnp.where(lane >= LANES - far * edge, roll(sums, LANES - far * edge), 0.0)
        else:
            part = jnp.where(lane < far * edge, roll(sums, far * edge - LANES), 0.0)
        total = part if total is None else total + part
    return total


def side_terms(packed, taps, edge):
    place = lax.broadcasted_iota(jnp.int32, packed.shape, 1) % (2 * HALO)
    beside = jnp.where(place == 0, roll(packed, -1), jnp.where(place == 3, roll(packed, 1), 0.0))
    total = None
    for a in range(KSIZE):
        def tap(b):
            return jnp.tile(taps[a * KSIZE + b], (1, packed.shape[1] // LANES))

        terms = (jnp.where(place < HALO, tap(0), tap(4)) * packed
                 + jnp.where(place == 0, tap(1), tap(3)) * beside)
        part = roll(terms, -a * 2 * HALO)[:, :2 * HALO * edge]
        total = part if total is None else total + part
    return total


def column_map(edge):
    pixel = lax.broadcasted_iota(jnp.int32, (1, edge * edge), 1)
    row, col = pixel // edge, pixel % edge
    index = jnp.where(col < HALO, row * 2 * HALO + col, row * 2 * HALO + col - (edge - 2 * HALO))
    return one_hot(jnp.where((col < HALO) | (col >= edge - HALO), index, -1), 2 * HALO * edge)


def conv_kernel(edge, neighbours, top, low, pick, slot, columns, center, rims, taps,
                hidden_ref, halo, gathered, sides):
    rims_ref, taps_ref, halo_ref = rims.get(), taps.get(), halo.ref
    channels, pixels = hidden_ref.shape
    nb = tile_row(neighbours)
    halo_ref[:, :LANES] = dot(rims_ref[nb[1]], top.get()[...]).astype(BF16)
    halo_ref[:, LANES:2 * LANES] = dot(rims_ref[nb[6]], low.get()[...]).astype(BF16)
    for position, d in enumerate(SIDES):
        gathered[position * channels:(position + 1) * channels, :] = rims_ref[nb[d]]
    candidates, slot = dot(gathered[...], pick.get()[...]), slot.get()[...]
    packed = candidates[:channels, :]
    for position in range(1, len(SIDES)):
        packed = jnp.where(slot == position,
                           candidates[position * channels:(position + 1) * channels, :], packed)
    halo_ref[:, 2 * LANES:] = packed.astype(BF16)
    halo.send()
    center = center.get()
    ends = []
    for at in range(0, channels, 16):
        halos = halo_ref[at:at + 16, :].astype(F32)
        taps_of = tap_rows_of(taps_ref, at)
        ends.append((row_terms(halos[:, :LANES], taps_of, edge, False),
                     row_terms(halos[:, LANES:2 * LANES], taps_of, edge, True)))
        sides[at:at + 16, :] = side_terms(halos[:, 2 * LANES:], taps_of, edge)
    high = sides[...].astype(BF16)
    low = (sides[...] - high.astype(F32)).astype(BF16)
    columns = columns.get()[...]
    hidden = center[...] + dot(high, columns) + dot(low, columns)
    hidden_ref[:, LANES:pixels - LANES] = hidden[:, LANES:pixels - LANES].astype(BF16)
    first = jnp.concatenate([end[0] for end in ends], axis=0)
    last = jnp.concatenate([end[1] for end in ends], axis=0)
    hidden_ref[:, :LANES] = (hidden[:, :LANES] + first).astype(BF16)
    hidden_ref[:, pixels - LANES:] = (hidden[:, pixels - LANES:] + last).astype(BF16)


def normal_below(values):
    return 0.5 * (1.0 + lax.erf(values * 0.7071067811865476))


def gelu_slope(values, below):
    return below + values * jnp.exp(-0.5 * values * values) * 0.3989422804014327


def column_steps(ref):
    return [slice(at, at + 2 * LANES) for at in range(0, ref.shape[1], 2 * LANES)]


def over_units(units, block, body):
    def step(i, carry):
        body(pl.ds(pl.multiple_of(i * block, block), block))
        return carry

    lax.fori_loop(0, units // block, step, 0)


def weight_kernel(feats, cots, w_in_t, w_out, part, gpre, act, stack, sems):
    feats, cots = feats.get(), cots.get()
    full, units = feats.shape[0], act.shape[0]
    w_in_t, w_out = w_in_t.get()[...], w_out.get()[...]
    for part_of in column_steps(feats):
        pre = dot(w_in_t, feats[:, part_of])
        below = normal_below(pre)
        act[:, part_of] = (pre * below).astype(BF16)
        slope = gelu_slope(pre, below)
        gpre[:, part_of] = (dot(w_out, cots[:, part_of]) * slope).astype(BF16)
    used, copies = 0, []
    for values, height in ((dot_nt(feats[...], gpre[...]), full),
                           (dot_nt(act[...], cots[...]), units)):
        first = used
        for column in range(0, values.shape[1], LANES):
            stack[used:used + height, :] = values[:, column:column + LANES].astype(BF16)
            used += height
        copies.append(pltpu.make_async_copy(
            stack.at[first:used], part.at[first:used], sems.at[len(copies)]))
        copies[-1].start()
    if used < part.shape[0]:
        stack[used:, :] = jnp.zeros((part.shape[0] - used, LANES), BF16)
        copies.append(pltpu.make_async_copy(stack.at[used:], part.at[used:], sems.at[2]))
        copies[-1].start()
    for copy in copies:
        copy.wait()


def out_kernel(block, feats, w_in_t, w_out, x, out, act):
    feats, w_in_t, w_out = feats.get(), w_in_t.get(), w_out.get()

    def units(rows):
        for part_of in column_steps(feats):
            pre = dot(w_in_t[rows, :], feats[:, part_of])
            act[rows, part_of] = (pre * normal_below(pre)).astype(BF16)

    over_units(w_out.shape[0], block, units)
    channels = out.ref.shape[0]
    row = lax.broadcasted_iota(jnp.int32, (channels, w_out.shape[1]), 0)
    column = lax.broadcasted_iota(jnp.int32, (channels, w_out.shape[1]), 1)
    pick = jnp.where(column == row + lax.axis_index("chan") * channels, 1.0, 0.0).astype(BF16)
    branch = dot(dot_nt(pick, w_out[...]).astype(BF16), act[...])
    out.ref[...] = (x.get()[...].astype(F32) + branch.astype(BF16).astype(F32)).astype(BF16)


def back_kernel(edge, groups, tiles, feats, cots, w_in, w_in_t, w_out, gpre_own, x, halo, cot,
                neighbours, rotations, taps, accum_ref, tap_ref, *refs):
    outs, (gpre, grad_ref, padded_ref, side_ref, turned_all, moved_all, d_row, d_side, gathered) = (
        refs[:-9], refs[-9:])
    channels, pixels = grad_ref.shape
    feats, cots, w_in_t, w_out = feats.get(), cots.get(), w_in_t.get(), w_out.get()

    chan, units = lax.axis_index("chan"), gpre_own.ref.shape[0]

    def others(k, carry):
        rows = pl.ds(pl.multiple_of((chan ^ k) * units, units), units)
        for part_of in column_steps(feats):
            pre = dot(w_in_t[rows, :], feats[:, part_of])
            slope = gelu_slope(pre, normal_below(pre))
            gpre[rows, part_of] = (dot(w_out[rows, :], cots[:, part_of]) * slope).astype(BF16)
        return carry

    lax.fori_loop(1, groups, others, 0)
    gpre[pl.ds(pl.multiple_of(chan * units, units), units), :] = gpre_own.get()[...]
    own = pl.ds(pl.multiple_of(lax.axis_index("chan") * channels, channels), channels)
    grad_ref[...] = dot(w_in.get()[own, :], gpre[...]).astype(BF16)
    halo = halo.get()
    padded_ref[:, :LANES] = halo[:, :LANES]
    padded_ref[:, LANES:LANES + pixels] = x.get()[...]
    padded_ref[:, LANES + pixels:] = halo[:, LANES:2 * LANES]
    spread = spread_map(edge, padded_ref.shape[1])
    side_ref[...] = dot(halo[:, 2 * LANES:], spread).astype(BF16)
    tap_terms(edge, grad_ref, padded_ref, side_ref, tap_ref, turned_all, moved_all)
    halo_adjoint(edge, neighbours, rotations, spread, grad_ref, taps.get(), cot.get(), accum_ref,
                 outs, d_row, d_side, gathered)


def prep_kernel(edge, w_in, x, neighbours, rotations, taps, w_in_t_ref, center_ref, nb_ref,
                *map_refs):
    nb_ref[...] = neighbours.get()[...]
    rot = tile_row(rotations)
    pick, slot = side_map([rot[d] for d in SIDES], edge)
    maps = (*row_halo_maps(rot[1], rot[6], edge), pick, slot, column_map(edge))
    for ref, values in zip(map_refs, maps):
        ref[...] = values
    w_in_t_ref[...] = w_in.get()[...].astype(F32).T.astype(BF16)
    center_conv(edge, x.get(), taps.get(), center_ref)


def join_kernel(w_in_t, w_out, *refs):
    pieces, (out_ref, part_in_ref, part_out_ref) = refs[:-3], refs[-3:]
    chan = lax.axis_index("chan")
    for k, piece in enumerate(pieces):
        piece = piece.get()
        channels = piece.shape[0]
        start = pl.multiple_of((chan ^ k) * channels, channels)
        out_ref[pl.ds(start, channels), :] = piece[...]
    units = part_in_ref.shape[0]
    mine = pl.ds(pl.multiple_of(chan * units, units), units)
    part_in_ref[...] = w_in_t.get()[mine, :]
    part_out_ref[...] = w_out.get()[mine, :]


def tap_terms(edge, grad_ref, padded_ref, side_ref, tap_ref, turned_all, moved_all):
    channels, pixels = grad_ref.shape
    wide = pixels + 2 * LANES
    moved_all[KSIZE * 16:, :] = jnp.zeros((LANES - KSIZE * 16, wide), BF16)
    same = (lax.broadcasted_iota(jnp.int32, (16, KSIZE * LANES), 1) % 16
            == lax.broadcasted_iota(jnp.int32, (16, KSIZE * LANES), 0))
    line = lax.broadcasted_iota(jnp.int32, (KSIZE * LANES, LANES), 0)
    tap = lax.broadcasted_iota(jnp.int32, (KSIZE * LANES, LANES), 1)
    used = line % LANES < KSIZE * 16
    pick = jnp.where(used & (line // LANES * KSIZE + line % LANES // 16 == tap), 1.0, 0.0).astype(BF16)
    mask = {b: side_mask(b - HALO, (16, wide), edge) for b in range(KSIZE) if b != HALO}
    lane = lax.broadcasted_iota(jnp.int32, (16, LANES), 1)
    zeros = jnp.zeros((16, LANES), F32)
    found = []
    for at in range(0, channels, 16):
        g = jnp.concatenate([zeros, grad_ref[at:at + 16, :].astype(F32), zeros], axis=1)
        x = padded_ref[at:at + 16, :].astype(F32)
        h = side_ref[at:at + 16, :].astype(F32)
        for a in range(KSIZE):
            shift = a - HALO
            turned_all[a * 16:a * 16 + 16, :] = roll(g, shift * edge).astype(BF16)
            moved = roll(jnp.where(mask[a], h, x), -shift) if shift else x
            moved_all[a * 16:a * 16 + 16, :] = moved.astype(BF16)
        products = dot_nt(turned_all[...], moved_all[...])
        side_by_side = jnp.concatenate(
            [products[a * 16:a * 16 + 16, :] for a in range(KSIZE)], axis=1)
        taps = dot(jnp.where(same, side_by_side, 0.0).astype(BF16), pick)
        place = at // 16 % 4
        taps = jnp.where(lane // 32 == place, roll(taps, 32 * place), 0.0)
        if place == 0:
            found.append(taps)
        else:
            found[-1] = found[-1] + taps
    tap_ref[...] = jnp.concatenate(found, axis=0).astype(BF16)


def halo_adjoint(edge, neighbours, rotations, spread, grad_ref, taps_ref, cot_ref, accum_ref, outs,
                 d_row, d_side, gathered):
    channels, pixels = grad_ref.shape
    wide = pixels + 2 * LANES
    tiles = gathered.shape[0]

    def block(i, carry):
        at = pl.multiple_of(i * 16, 16)
        gs = grad_ref[pl.ds(at, 16), :].astype(F32)
        taps_of = [taps_ref[tap, pl.ds(at, 16), :].astype(F32) for tap in range(KSIZE * KSIZE)]
        zeros = jnp.zeros((8, LANES), F32)
        rows, sides = [], []
        for half in (0, 8):
            g = jnp.concatenate([zeros, gs[half:half + 8], zeros], axis=1)
            turned = [roll(g, (a - HALO) * edge) for a in range(KSIZE)]
            d_x = d_h = None
            for b in range(KSIZE):
                shift = b - HALO
                back = None
                for a in range(KSIZE):
                    weight = taps_of[a * KSIZE + b][half:half + 8]
                    term = jnp.tile(weight, (1, wide // LANES)) * turned[a]
                    back = term if back is None else back + term
                back = roll(back, shift)
                if shift:
                    mask = side_mask(shift, back.shape, edge)
                    inside = jnp.where(mask, 0.0, back)
                    outside = jnp.where(mask, back, 0.0)
                    d_h = outside if d_h is None else d_h + outside
                    d_x = inside if d_x is None else d_x + inside
                else:
                    d_x = back if d_x is None else d_x + back
            rows.append(d_x)
            sides.append(d_h)
        d_x = jnp.concatenate(rows, axis=0)
        accum_ref[pl.ds(at, 16), :] = d_x[:, LANES:LANES + pixels]
        d_row[pl.ds(at, 16), :LANES] = d_x[:, :LANES].astype(BF16)
        d_row[pl.ds(at, 16), LANES:] = d_x[:, LANES + pixels:].astype(BF16)
        d_side[pl.ds(at, 16), :] = jnp.concatenate(sides, axis=0).astype(BF16)
        return carry

    lax.fori_loop(0, channels // 16, block, 0)
    accum_ref[...] += cot_ref[...].astype(F32)
    nb, rot = tile_row(neighbours), tile_row(rotations)
    gathered[...] = jnp.zeros(gathered.shape, F32)
    top, low = row_halo_maps(rot[1], rot[6], edge)
    gathered[slot_of(nb[1], tiles)] += dot_nt(d_row[:, :LANES], top)
    gathered[slot_of(nb[6], tiles)] += dot_nt(d_row[:, LANES:], low)
    packed = dot_nt(d_side[...], spread)
    pick, slot = side_map([rot[d] for d in SIDES], edge)
    for position, d in enumerate(SIDES):
        own = jnp.where(slot == position, packed, 0.0).astype(BF16)
        gathered[slot_of(nb[d], tiles)] += dot_nt(own, pick)
    store_parts(gathered, outs)


def store_parts(values, outs):
    for part, out in enumerate(outs):
        out = out.ref if isinstance(out, Stored) else out
        rows = out.shape[0]

        def store(t, carry, out=out, first=part * rows):
            out[t] = values[first + t].astype(BF16)
            return carry

        lax.fori_loop(0, rows, store, 0)


def halves(tiles):
    return tiles > 1 and tiles & (tiles - 1) == 0


def slot_of(tile, tiles):
    if not halves(tiles):
        return tile
    apart, slot = tile ^ lax.axis_index("tile"), 0
    for bit in halving_bits(tiles):
        slot = slot * 2 + jnp.where(apart & bit != 0, 1, 0)
    return slot


def halving_bits(tiles):
    bits = [1 << i for i in range(tiles.bit_length() - 1)]
    return bits[1:2] + bits[:1] + bits[2:]


def pair_kernel(kept, other, *refs):
    outs, total = refs[:-1], refs[-1]
    total[...] = kept.get()[...].astype(F32) + other.get()[...].astype(F32)
    store_parts(total, outs)


def border_kernel(edge, accum, *refs):
    parts, grad_ref = refs[:-1], refs[-1]
    rims = None
    for part in parts:
        more = total_of(part.get())
        rims = more if rims is None else rims + more
    high = rims.astype(BF16)
    low = (rims - high.astype(F32)).astype(BF16)
    pick = one_hot(rim_pixels(edge), edge * edge)
    added = dot_nt(high, pick) + dot_nt(low, pick)
    grad_ref[...] = (accum.get()[...] + added).astype(BF16)


def total_of(ref):
    return lax.fori_loop(1, ref.shape[0], lambda t, so_far: so_far + ref[t].astype(F32),
                         ref[0].astype(F32))


def sum_kernel(recv, tap, out, total, sems):
    recv = recv.get()
    share = recv.shape[1]
    total[:share, :] = total_of(recv).astype(BF16)
    total[share:, :] = tap.get()[...]
    copies = [pltpu.make_async_copy(total, out.at[t], sems.at[t]) for t in range(out.shape[0])]
    for copy in copies:
        copy.start()
    for copy in copies:
        copy.wait()


def compact_kernel(share, values, out):
    values = values.get()
    tiles, rows, _ = values.shape
    for tile in range(tiles):
        out[tile * share:(tile + 1) * share, :] = values[tile, :share, :]
    taps = values[0, share:, :].astype(F32)
    for tile in range(1, tiles):
        taps = taps + values[tile, share:, :].astype(F32)
    out[tiles * share:, :] = taps.astype(BF16)


def final_kernel(which, channels, tap_rows, scale, last, *refs):
    pieces, taps_in = refs[:len(which)], refs[len(which)]
    copies = []
    if last:
        g_in, g_out, g_tap_ref, buf_in, buf_out, sems = refs[-6:]
    else:
        g_in, g_out, g_tap_ref, copied, buf_in, buf_out, sems = refs[-7:]
        copies.append(pltpu.make_async_copy(refs[len(which) + 1].get(), copied, sems.at[0]))
        copies[0].start()
    full, units = buf_in.shape[1:]
    all_taps = taps_in.get()[...]
    row_of = lax.broadcasted_iota(jnp.int32, (full, LANES), 0)
    for i, k in enumerate(which):
        piece = pieces[i].get()
        owner = lax.axis_index("chan") ^ k
        start = pl.multiple_of(owner * units, units)
        used = 0
        for buffer, target in ((buf_in, g_in.at[:, pl.ds(start, units)]),
                               (buf_out, g_out.at[pl.ds(start, units)])):
            height, width = buffer.shape[1:]
            for column in range(0, width, LANES):
                buffer[i, :, column:column + LANES] = piece[used:used + height, :].astype(F32) * scale
                used += height
            copies.append(pltpu.make_async_copy(buffer.at[i], target, sems.at[len(copies)]))
            copies[-1].start()
        taps = piece[piece.shape[0] - tap_rows:, :].astype(F32)
        blocks = []
        for block in range(channels // 16):
            values = taps[block // 4 * 16:block // 4 * 16 + 16, :]
            blocks.append(roll(values, -32 * (block % 4)))
        own = jnp.concatenate(blocks * (full // channels), axis=0)
        all_taps = jnp.where(row_of // channels == owner, own, all_taps)
    if last:
        g_tap_ref[...] = all_taps.T[:KSIZE * KSIZE, :] * scale
    else:
        g_tap_ref[...] = all_taps
    for copy in copies:
        copy.wait()


def swap_chan(values, bit):
    return lax.ppermute(values, "chan", [(i, i ^ bit) for i in range(lax.axis_size("chan"))])


def gather_pieces(own, groups):
    pieces = {0: own}
    bit = groups // 2
    while bit:
        for k in list(pieces):
            pieces[k ^ bit] = swap_chan(pieces[k], bit)
        bit //= 2
    return [pieces[k] for k in range(groups)]


def swap_rows(values):
    return lax.all_to_all(values, "tile", 0, 0, tiled=True)


def halve(parts, bit, after):
    kept, given = parts
    half = ((kept.shape[0] // 2, *kept.shape[1:]), BF16, NEAR)
    return call(pair_kernel, [(kept, NEAR), (swap_bit(given, bit), NEAR)], [half] * 2,
                [pltpu.VMEM(kept.shape, F32)], time=0.3, after=after)


def swap_bit(values, bit):
    return lax.ppermute(values, "tile", [(t, t ^ bit) for t in range(lax.axis_size("tile"))])


def body(inputs, grad_out, kernel, w_in, w_out, neighbours, rotations):
    channels, pixels = inputs.shape[1:]
    edge = math.isqrt(pixels)
    full, hidden = w_in.shape
    groups = lax.axis_size("chan")
    tiles = lax.axis_size("tile")
    wide = pixels + 2 * LANES
    rim = 4 * HALO * edge
    units = hidden // groups
    scale = (tiles * pixels) ** -0.5
    x, cot = inputs[0], grad_out[0]

    [rims] = call(functools.partial(pack_kernel, edge), [(x, FAR)],
                  [((tiles, channels, rim), BF16, RAW)],
                  [pltpu.VMEM((channels, rim), BF16), pltpu.SemaphoreType.DMA((tiles,))])
    _, kernel = lax.optimization_barrier((rims, kernel))
    taps = jnp.broadcast_to(kernel[:, :, None], (KSIZE * KSIZE, channels, LANES))
    cot_pieces = gather_pieces(cot, groups)
    table = neighbours.shape
    w_in_t, center, nb_near, *maps = call(
        functools.partial(prep_kernel, edge),
        [(w_in, NEAR), (x, FAR), (neighbours, NEAR), (rotations, NEAR), (taps, NEAR)],
        [((hidden, full), BF16, NEAR), ((channels, pixels), F32, NEAR),
         (neighbours.shape, jnp.int32, NEAR), ((rim, LANES), BF16, NEAR), ((rim, LANES), BF16, NEAR),
         ((rim, 2 * LANES), BF16, NEAR), ((1, 2 * LANES), jnp.int32, NEAR),
         ((2 * HALO * edge, pixels), BF16, NEAR)], time=2.0, after=[(rims, RAW)])
    rims = swap_rows(rims)

    hid, halo = call(
        functools.partial(conv_kernel, edge),
        [(a, NEAR) for a in (nb_near, *maps, center, rims, taps)],
        [((channels, pixels), BF16, NEAR), ((channels, 4 * LANES), BF16, FAR)],
        [pltpu.VMEM((len(SIDES) * channels, rim), BF16),
         pltpu.VMEM((channels, 2 * HALO * edge), F32)], time=1.0, after=[(w_in_t, NEAR)])
    feats = lax.all_gather(hid, "chan", axis=0, tiled=True)
    cots, part_in, part_out = call(
        join_kernel, [(w_in_t, NEAR), (w_out, NEAR)] + [(piece, NEAR) for piece in cot_pieces],
        [((full, pixels), BF16, NEAR)] + [((units, full), BF16, NEAR)] * 2, time=0.6,
        after=[(feats, NEAR)])

    used = 2 * full * units // LANES
    share = -(-used // (16 * tiles)) * 16
    tap_rows = -(-channels // 64) * 16
    block = 2 * LANES
    part, gpre = call(
        weight_kernel,
        [(feats, NEAR), (cots, NEAR), (part_in, NEAR), (part_out, NEAR)],
        [((tiles * share, LANES), BF16, RAW), ((units, pixels), BF16, NEAR)],
        [pltpu.VMEM((units, pixels), BF16)]
        + [pltpu.VMEM((tiles * share, LANES), BF16), pltpu.SemaphoreType.DMA((3,))],
        time=2.2)
    part = swap_rows(part.reshape(tiles, share, LANES))

    parts = 2 if halves(tiles) else 1
    placed = ((tiles // parts, channels, rim), BF16, NEAR if parts > 1 else FAR)
    accum, tap_part, *border = call(
        functools.partial(back_kernel, edge, groups, tiles),
        [(feats, NEAR), (cots, NEAR), (w_in, FAR), (w_in_t, NEAR), (w_out, NEAR), (gpre, FAR), (x, FAR),
         (halo, FAR), (cot, FAR), (neighbours, NEAR), (rotations, NEAR), (taps, NEAR)],
        [((channels, pixels), F32, NEAR), ((tap_rows, LANES), BF16, NEAR)] + [placed] * parts,
        [pltpu.VMEM((hidden, pixels), BF16), pltpu.VMEM((channels, pixels), BF16),
         pltpu.VMEM((channels, wide), BF16), pltpu.VMEM((channels, wide), BF16),
         pltpu.VMEM((KSIZE * 16, wide), BF16), pltpu.VMEM((LANES, wide), BF16),
         pltpu.VMEM((channels, 2 * LANES), BF16), pltpu.VMEM((channels, wide), BF16),
         pltpu.VMEM((tiles, channels, rim), F32)], time=7.5, limit=32)
    [mine] = call(sum_kernel, [(part, NEAR), (tap_part, NEAR)],
                  [((tiles, share + tap_rows, LANES), BF16, RAW)],
                  [pltpu.VMEM((share + tap_rows, LANES), BF16), pltpu.SemaphoreType.DMA((tiles,))])
    [weights] = call(functools.partial(compact_kernel, share), [(swap_rows(mine), NEAR)],
                     [((tiles * share + tap_rows, LANES), BF16, NEAR)], time=0.1)

    [outputs] = call(
        functools.partial(out_kernel, block),
        [(feats, NEAR), (w_in_t, NEAR), (w_out, NEAR), (x, FAR)], [((channels, pixels), BF16, FAR)],
        [pltpu.VMEM((hidden, pixels), BF16)], time=4.0, limit=32, after=[(mine, RAW)])
    bits = halving_bits(tiles) if parts > 1 else [0]
    for step, bit in enumerate(bits[:-1]):
        border = halve(border, bit, [(outputs, RAW)] if step else [])
    weights, outputs, *border = lax.optimization_barrier((weights, outputs, *border))
    border = [border[0], swap_bit(border[1], bits[-1])] if parts > 1 else [swap_rows(border[0])]
    [grad_in] = call(functools.partial(border_kernel, edge),
                     [(accum, NEAR)] + [(part, NEAR) for part in border],
                     [((channels, pixels), BF16, PINNED)])

    def place(which, taps_so_far, more, last):
        tap_shape = (KSIZE * KSIZE, full) if last else (full, LANES)
        copied = [] if last else [(more[0][0].shape, more[0][0].dtype, RAW)]
        return call(
            functools.partial(final_kernel, which, channels, tap_rows, scale, last),
            [(pieces[k], NEAR) for k in which] + [(taps_so_far, NEAR)] + more,
            [((full, hidden), F32, RAW), ((hidden, full), F32, RAW), (tap_shape, F32, NEAR)] + copied,
            [pltpu.VMEM((len(which), full, units), F32), pltpu.VMEM((len(which), units, full), F32),
             pltpu.SemaphoreType.DMA((2 * len(which) + 1,))],
            time=1.2, aliases={1 + len(which): 0, 2 + len(which): 1} if last else None)

    pieces = {0: weights}
    bit = groups // 2
    while bit > 1:
        for k in [k for k in pieces if k % 2 == 0]:
            pieces[k ^ bit] = swap_chan(pieces[k], bit)
        bit //= 2
    pieces[1] = swap_chan(weights, 1)
    even, odd = list(range(2, groups, 2)), list(range(3, groups, 2))
    for k in even:
        pieces[k], grad_in = lax.optimization_barrier((pieces[k], grad_in))
    for k in odd:
        pieces[k] = swap_chan(pieces[k ^ 1], 1)
    g_in, g_out, taps_so_far, grad_in = place(
        [0, 1, *even], jnp.zeros((full, LANES), F32), [(grad_in, NEAR)], False)
    grads = place(odd, taps_so_far, [(g_in, RAW), (g_out, RAW)], True)
    return (outputs[None], grad_in[None], *grads)


def solution(mesh):
    return jax.shard_map(
        body,
        mesh=mesh,
        in_specs=(
            P("tile", "chan", None),
            P("tile", "chan", None),
            P(None, "chan"),
            P(),
            P(),
            P(),
            P(),
        ),
        out_specs=(P("tile", "chan", None), P("tile", "chan", None), P(), P(), P()),
        check_vma=False,
    )
```

```python
import functools
import math

import jax
import jax.numpy as jnp
from jax import lax
from jax.experimental import pallas as pl
from jax.experimental.pallas import tpu as pltpu
from jax.sharding import PartitionSpec as P

KSIZE = 5
HALO = KSIZE // 2
LANES = 128
SIDES = (0, 2, 3, 4, 5, 7)
BF16 = jnp.bfloat16
F32 = jnp.float32

NEAR, FAR, RAW, PINNED = "near", "far", "raw", "pinned"
SPACES = {NEAR: pltpu.VMEM, FAR: pltpu.HBM, RAW: pltpu.HBM, PINNED: pltpu.VMEM}


class Loaded:
    def __init__(self, ref, copy=None):
        self.ref, self.copy = ref, copy
        if copy is not None:
            copy.start()

    def get(self):
        if self.copy is not None:
            self.copy.wait()
            self.copy = None
        return self.ref


class Stored:
    def __init__(self, ref, copy):
        self.ref, self.copy, self.started = ref, copy, False

    def send(self):
        if not self.started:
            self.copy.start()
            self.started = True


def call(kernel, ins, outs, scratch=(), time=1.0, after=(), aliases=None, limit=16):
    ins = list(ins) + list(after)
    buffers = []
    for shape, dtype, place in [(a.shape, a.dtype, p) for a, p in ins] + list(outs):
        if place == FAR:
            buffers += [pltpu.VMEM(shape, dtype), pltpu.SemaphoreType.DMA]

    def run(*refs):
        ends = len(ins), len(ins) + len(outs), len(ins) + len(outs) + len(buffers)
        spare = list(refs[ends[1]:ends[2]])
        operands, results = [], []
        for ref, (_, place) in zip(refs, ins):
            if place == FAR:
                buffer, sem = spare.pop(0), spare.pop(0)
                operands.append(Loaded(buffer, pltpu.make_async_copy(ref, buffer, sem)))
            else:
                operands.append(Loaded(ref) if place == NEAR else ref)
        for ref, (_, _, place) in zip(refs[ends[0]:], outs):
            if place == FAR:
                buffer, sem = spare.pop(0), spare.pop(0)
                results.append(Stored(buffer, pltpu.make_async_copy(buffer, ref, sem)))
            else:
                results.append(ref)
        kernel(*operands[:len(ins) - len(after)], *results, *refs[ends[2]:])
        far = [result for result in results if isinstance(result, Stored)]
        for result in far:
            result.send()
        for result in far:
            result.copy.wait()

    return pl.pallas_call(
        run,
        out_shape=[SPACES[p](s, d) if p != NEAR else jax.ShapeDtypeStruct(s, d)
                   for s, d, p in outs],
        in_specs=[pl.BlockSpec(memory_space=SPACES[p]) for _, p in ins],
        out_specs=[pl.BlockSpec(memory_space=SPACES[p]) for _, _, p in outs],
        scratch_shapes=buffers + list(scratch),
        input_output_aliases=aliases or {},
        cost_estimate=pl.CostEstimate(
            flops=int(time * 1e9), bytes_accessed=int(time * 3.5e6), transcendentals=0),
        compiler_params=pltpu.CompilerParams(vmem_limit_bytes=limit * 1024 * 1024),
    )(*[pltpu.with_memory_space_constraint(a, pltpu.HBM) if p in (FAR, RAW) else a
        for a, p in ins])


def tile_row(table):
    row = table.get()[pl.ds(lax.axis_index("tile"), 1), :]
    return [row[0, d] for d in range(8)]


def dot(a, b):
    return lax.dot_general(a, b, (((1,), (0,)), ((), ())), preferred_element_type=F32)


def dot_nt(a, b):
    return lax.dot_general(a, b, (((1,), (1,)), ((), ())), preferred_element_type=F32)


def one_hot(index, rows):
    row = lax.broadcasted_iota(jnp.int32, (rows, index.shape[1]), 0)
    return jnp.where(row == index, 1.0, 0.0).astype(BF16)


def rim_pixels(edge):
    band_len = HALO * edge
    lane = lax.broadcasted_iota(jnp.int32, (1, 4 * band_len), 1)
    band, at = lane // band_len, lane % band_len
    side = (at // HALO) * edge + at % HALO
    pixel = jnp.where(band == 0, at, (edge - HALO) * edge + at)
    return jnp.where(band == 2, side, jnp.where(band == 3, side + edge - HALO, pixel))


def rim_lane(row, col, edge):
    band_len = HALO * edge
    side = jnp.where(col < HALO, 2 * band_len + row * HALO + col,
                     3 * band_len + row * HALO + col - (edge - HALO))
    side = jnp.where(row >= edge - HALO, band_len + (row - (edge - HALO)) * edge + col, side)
    return jnp.where(row < HALO, row * edge + col, side)


def turned_lane(row, col, quarter, edge):
    last = edge - 1
    from_row = jnp.where(quarter == 1, col, jnp.where(
        quarter == 2, last - row, jnp.where(quarter == 3, last - col, row)))
    from_col = jnp.where(quarter == 1, last - row, jnp.where(
        quarter == 2, last - col, jnp.where(quarter == 3, row, col)))
    return rim_lane(from_row, from_col, edge)


def row_halo_maps(top_turn, bottom_turn, edge):
    rim = 4 * HALO * edge
    lane = lax.broadcasted_iota(jnp.int32, (1, LANES), 1)
    up = lane - (LANES - HALO * edge)
    top = turned_lane(edge - HALO + up // edge, up % edge, top_turn, edge)
    low = turned_lane(lane // edge, lane % edge, bottom_turn, edge)
    top = jnp.where(up >= 0, top, -1)
    low = jnp.where(lane < HALO * edge, low, -1)
    return one_hot(top, rim), one_hot(low, rim)


def side_map(turns, edge):
    rim = 4 * HALO * edge
    lane = lax.broadcasted_iota(jnp.int32, (1, 2 * LANES), 1)
    row, k = lane // (2 * HALO), lane % (2 * HALO)
    above, below, right = row < HALO, row >= HALO + edge, k >= HALO
    b_row = jnp.where(above, edge - HALO + row, jnp.where(below, row - HALO - edge, row - HALO))
    b_col = jnp.where(right, k - HALO, edge - HALO + k)
    slot = jnp.where(above, 0, jnp.where(below, 4, 2)) + right.astype(jnp.int32)
    quarter = jnp.zeros_like(slot)
    for position in range(len(SIDES)):
        quarter = jnp.where(slot == position, turns[position], quarter)
    index = turned_lane(b_row, b_col, quarter, edge)
    index = jnp.where(row < edge + 2 * HALO, index, -1)
    return one_hot(index, rim), slot


def spread_map(edge, wide):
    lane = lax.broadcasted_iota(jnp.int32, (1, wide), 1)
    row = lane // edge - (LANES // edge - HALO)
    col = lane % edge
    right_row, left_row = row - 1, row + 1
    rows = edge + 2 * HALO
    right = jnp.where((right_row >= 0) & (right_row < rows), right_row * 2 * HALO + HALO + col, -1)
    left = jnp.where((left_row >= 0) & (left_row < rows),
                     left_row * 2 * HALO + col - (edge - HALO), -1)
    index = jnp.where(col < HALO, right, jnp.where(col >= edge - HALO, left, -1))
    return one_hot(index, 2 * LANES)


def side_mask(shift, shape, edge):
    col = lax.broadcasted_iota(jnp.int32, shape, 1) % edge
    return col < shift if shift > 0 else col >= edge + shift


def roll(values, shift):
    size = values.shape[1]
    return values if shift % size == 0 else pltpu.roll(values, shift % size, axis=1)


def pack_kernel(edge, x, rims, rim, sems):
    pick = one_hot(rim_pixels(edge), edge * edge)
    rim[...] = dot(x.get()[...], pick).astype(BF16)
    copies = [pltpu.make_async_copy(rim, rims.at[t], sems.at[t]) for t in range(rims.shape[0])]
    for copy in copies:
        copy.start()
    for copy in copies:
        copy.wait()


def shifted(values, shift, edge):
    if not shift:
        return values
    return roll(jnp.where(side_mask(shift, values.shape, edge), 0.0, values), -shift)


def tap_rows_of(taps_ref, at):
    return [taps_ref[tap, pl.ds(at, 16), :].astype(F32) for tap in range(KSIZE * KSIZE)]


def center_conv(edge, x_ref, taps_ref, out_ref):
    channels, pixels = x_ref.shape
    wide = pixels + 2 * LANES

    def block(i, carry):
        at = pl.multiple_of(i * 16, 16)
        xs = x_ref[pl.ds(at, 16), :].astype(F32)
        taps = tap_rows_of(taps_ref, at)
        zeros = jnp.zeros((8, LANES), F32)
        halves = []
        for half in (0, 8):
            x = jnp.concatenate([zeros, xs[half:half + 8], zeros], axis=1)
            sums = [None] * KSIZE
            for b in range(KSIZE):
                moved = shifted(x, b - HALO, edge)
                for a in range(KSIZE):
                    term = jnp.tile(taps[a * KSIZE + b][half:half + 8], (1, wide // LANES)) * moved
                    sums[a] = term if sums[a] is None else sums[a] + term
            total = None
            for a in range(KSIZE):
                part = roll(sums[a], -(a - HALO) * edge)[:, LANES:LANES + pixels]
                total = part if total is None else total + part
            halves.append(total)
        out_ref[pl.ds(at, 16), :] = jnp.concatenate(halves, axis=0)
        return carry

    lax.fori_loop(0, channels // 16, block, 0)


def row_terms(rows, taps, edge, below):
    lane = lax.broadcasted_iota(jnp.int32, rows.shape, 1)
    total = None
    for a in range(KSIZE):
        far = a - HALO if below else HALO - a
        if far <= 0:
            continue
        sums = None
        for b in range(KSIZE):
            term = taps[a * KSIZE + b] * shifted(rows, b - HALO, edge)
            sums = term if sums is None else sums + term
        if below:
            part = jnp.where(lane >= LANES - far * edge, roll(sums, LANES - far * edge), 0.0)
        else:
            part = jnp.where(lane < far * edge, roll(sums, far * edge - LANES), 0.0)
        total = part if total is None else total + part
    return total


def side_terms(packed, taps, edge):
    place = lax.broadcasted_iota(jnp.int32, packed.shape, 1) % (2 * HALO)
    beside = jnp.where(place == 0, roll(packed, -1), jnp.where(place == 3, roll(packed, 1), 0.0))
    total = None
    for a in range(KSIZE):
        def tap(b):
            return jnp.tile(taps[a * KSIZE + b], (1, packed.shape[1] // LANES))

        terms = (jnp.where(place < HALO, tap(0), tap(4)) * packed
                 + jnp.where(place == 0, tap(1), tap(3)) * beside)
        part = roll(terms, -a * 2 * HALO)[:, :2 * HALO * edge]
        total = part if total is None else total + part
    return total


def column_map(edge):
    pixel = lax.broadcasted_iota(jnp.int32, (1, edge * edge), 1)
    row, col = pixel // edge, pixel % edge
    index = jnp.where(col < HALO, row * 2 * HALO + col, row * 2 * HALO + col - (edge - 2 * HALO))
    return one_hot(jnp.where((col < HALO) | (col >= edge - HALO), index, -1), 2 * HALO * edge)


def conv_kernel(edge, neighbours, top, low, pick, slot, columns, center, rims, taps,
                hidden_ref, halo, gathered, sides):
    rims_ref, taps_ref, halo_ref = rims.get(), taps.get(), halo.ref
    channels, pixels = hidden_ref.shape
    tiles = rims_ref.shape[0]
    nb = [lax.rem(tile + tiles - first_tile(tiles), tiles) for tile in tile_row(neighbours)]
    halo_ref[:, :LANES] = dot(rims_ref[nb[1]], top.get()[...]).astype(BF16)
    halo_ref[:, LANES:2 * LANES] = dot(rims_ref[nb[6]], low.get()[...]).astype(BF16)
    for position, d in enumerate(SIDES):
        gathered[position * channels:(position + 1) * channels, :] = rims_ref[nb[d]]
    candidates, slot = dot(gathered[...], pick.get()[...]), slot.get()[...]
    packed = candidates[:channels, :]
    for position in range(1, len(SIDES)):
        packed = jnp.where(slot == position,
                           candidates[position * channels:(position + 1) * channels, :], packed)
    halo_ref[:, 2 * LANES:] = packed.astype(BF16)
    halo.send()
    center = center.get()
    ends = []
    for at in range(0, channels, 16):
        halos = halo_ref[at:at + 16, :].astype(F32)
        taps_of = tap_rows_of(taps_ref, at)
        ends.append((row_terms(halos[:, :LANES], taps_of, edge, False),
                     row_terms(halos[:, LANES:2 * LANES], taps_of, edge, True)))
        sides[at:at + 16, :] = side_terms(halos[:, 2 * LANES:], taps_of, edge)
    high = sides[...].astype(BF16)
    low = (sides[...] - high.astype(F32)).astype(BF16)
    columns = columns.get()[...]
    hidden = center[...] + dot(high, columns) + dot(low, columns)
    hidden_ref[:, LANES:pixels - LANES] = hidden[:, LANES:pixels - LANES].astype(BF16)
    first = jnp.concatenate([end[0] for end in ends], axis=0)
    last = jnp.concatenate([end[1] for end in ends], axis=0)
    hidden_ref[:, :LANES] = (hidden[:, :LANES] + first).astype(BF16)
    hidden_ref[:, pixels - LANES:] = (hidden[:, pixels - LANES:] + last).astype(BF16)


def normal_below(values):
    return 0.5 * (1.0 + lax.erf(values * 0.7071067811865476))


def gelu_slope(values, below):
    return below + values * jnp.exp(-0.5 * values * values) * 0.3989422804014327


def column_steps(ref):
    return [slice(at, at + 2 * LANES) for at in range(0, ref.shape[1], 2 * LANES)]


def over_units(units, block, body):
    def step(i, carry):
        body(pl.ds(pl.multiple_of(i * block, block), block))
        return carry

    lax.fori_loop(0, units // block, step, 0)


def weight_kernel(feats, cots, w_in_t, w_out, part, gpre, act, stack, sems):
    feats, cots = feats.get(), cots.get()
    full, units = feats.shape[0], act.shape[0]
    w_in_t, w_out = w_in_t.get()[...], w_out.get()[...]
    for part_of in column_steps(feats):
        pre = dot(w_in_t, feats[:, part_of])
        below = normal_below(pre)
        act[:, part_of] = (pre * below).astype(BF16)
        slope = gelu_slope(pre, below)
        gpre[:, part_of] = (dot(w_out, cots[:, part_of]) * slope).astype(BF16)
    used, copies = 0, []
    for values, height in ((dot_nt(feats[...], gpre[...]), full),
                           (dot_nt(act[...], cots[...]), units)):
        first = used
        for column in range(0, values.shape[1], LANES):
            stack[used:used + height, :] = values[:, column:column + LANES].astype(BF16)
            used += height
        copies.append(pltpu.make_async_copy(
            stack.at[first:used], part.at[first:used], sems.at[len(copies)]))
        copies[-1].start()
    if used < part.shape[0]:
        stack[used:, :] = jnp.zeros((part.shape[0] - used, LANES), BF16)
        copies.append(pltpu.make_async_copy(stack.at[used:], part.at[used:], sems.at[2]))
        copies[-1].start()
    for copy in copies:
        copy.wait()


def out_kernel(block, feats, w_in_t, w_out, x, out, act):
    feats, w_in_t, w_out = feats.get(), w_in_t.get(), w_out.get()

    def units(rows):
        for part_of in column_steps(feats):
            pre = dot(w_in_t[rows, :], feats[:, part_of])
            act[rows, part_of] = (pre * normal_below(pre)).astype(BF16)

    over_units(w_out.shape[0], block, units)
    channels = out.ref.shape[0]
    row = lax.broadcasted_iota(jnp.int32, (channels, w_out.shape[1]), 0)
    column = lax.broadcasted_iota(jnp.int32, (channels, w_out.shape[1]), 1)
    pick = jnp.where(column == row + lax.axis_index("chan") * channels, 1.0, 0.0).astype(BF16)
    branch = dot(dot_nt(pick, w_out[...]).astype(BF16), act[...])
    out.ref[...] = (x.get()[...].astype(F32) + branch.astype(BF16).astype(F32)).astype(BF16)


def back_kernel(edge, groups, tiles, feats, cots, w_in, w_in_t, w_out, gpre_own, x, halo, cot,
                neighbours, rotations, taps, accum_ref, tap_ref, *refs):
    outs, (gpre, grad_ref, padded_ref, side_ref, turned_all, moved_all, d_row, d_side, gathered) = (
        refs[:-9], refs[-9:])
    channels, pixels = grad_ref.shape
    feats, cots, w_in_t, w_out = feats.get(), cots.get(), w_in_t.get(), w_out.get()

    chan, units = lax.axis_index("chan"), gpre_own.ref.shape[0]

    def others(k, carry):
        rows = pl.ds(pl.multiple_of((chan ^ k) * units, units), units)
        for part_of in column_steps(feats):
            pre = dot(w_in_t[rows, :], feats[:, part_of])
            slope = gelu_slope(pre, normal_below(pre))
            gpre[rows, part_of] = (dot(w_out[rows, :], cots[:, part_of]) * slope).astype(BF16)
        return carry

    lax.fori_loop(1, groups, others, 0)
    gpre[pl.ds(pl.multiple_of(chan * units, units), units), :] = gpre_own.get()[...]
    own = pl.ds(pl.multiple_of(lax.axis_index("chan") * channels, channels), channels)
    grad_ref[...] = dot(w_in.get()[own, :], gpre[...]).astype(BF16)
    halo = halo.get()
    padded_ref[:, :LANES] = halo[:, :LANES]
    padded_ref[:, LANES:LANES + pixels] = x.get()[...]
    padded_ref[:, LANES + pixels:] = halo[:, LANES:2 * LANES]
    spread = spread_map(edge, padded_ref.shape[1])
    side_ref[...] = dot(halo[:, 2 * LANES:], spread).astype(BF16)
    tap_terms(edge, grad_ref, padded_ref, side_ref, tap_ref, turned_all, moved_all)
    halo_adjoint(edge, neighbours, rotations, spread, grad_ref, taps.get(), cot.get(), accum_ref,
                 outs, d_row, d_side, gathered)


def prep_kernel(edge, w_in, x, neighbours, rotations, taps, w_in_t_ref, center_ref, nb_ref,
                *map_refs):
    nb_ref[...] = neighbours.get()[...]
    rot = tile_row(rotations)
    pick, slot = side_map([rot[d] for d in SIDES], edge)
    maps = (*row_halo_maps(rot[1], rot[6], edge), pick, slot, column_map(edge))
    for ref, values in zip(map_refs, maps):
        ref[...] = values
    w_in_t_ref[...] = w_in.get()[...].astype(F32).T.astype(BF16)
    center_conv(edge, x.get(), taps.get(), center_ref)


def join_kernel(w_in_t, w_out, *refs):
    pieces, (out_ref, part_in_ref, part_out_ref) = refs[:-3], refs[-3:]
    chan = lax.axis_index("chan")
    for k, piece in enumerate(pieces):
        piece = piece.get()
        channels = piece.shape[0]
        start = pl.multiple_of((chan ^ k) * channels, channels)
        out_ref[pl.ds(start, channels), :] = piece[...]
    units = part_in_ref.shape[0]
    mine = pl.ds(pl.multiple_of(chan * units, units), units)
    part_in_ref[...] = w_in_t.get()[mine, :]
    part_out_ref[...] = w_out.get()[mine, :]


def tap_terms(edge, grad_ref, padded_ref, side_ref, tap_ref, turned_all, moved_all):
    channels, pixels = grad_ref.shape
    wide = pixels + 2 * LANES
    moved_all[KSIZE * 16:, :] = jnp.zeros((LANES - KSIZE * 16, wide), BF16)
    same = (lax.broadcasted_iota(jnp.int32, (16, KSIZE * LANES), 1) % 16
            == lax.broadcasted_iota(jnp.int32, (16, KSIZE * LANES), 0))
    line = lax.broadcasted_iota(jnp.int32, (KSIZE * LANES, LANES), 0)
    tap = lax.broadcasted_iota(jnp.int32, (KSIZE * LANES, LANES), 1)
    used = line % LANES < KSIZE * 16
    pick = jnp.where(used & (line // LANES * KSIZE + line % LANES // 16 == tap), 1.0, 0.0).astype(BF16)
    mask = {b: side_mask(b - HALO, (16, wide), edge) for b in range(KSIZE) if b != HALO}
    lane = lax.broadcasted_iota(jnp.int32, (16, LANES), 1)
    zeros = jnp.zeros((16, LANES), F32)
    found = []
    for at in range(0, channels, 16):
        g = jnp.concatenate([zeros, grad_ref[at:at + 16, :].astype(F32), zeros], axis=1)
        x = padded_ref[at:at + 16, :].astype(F32)
        h = side_ref[at:at + 16, :].astype(F32)
        for a in range(KSIZE):
            shift = a - HALO
            turned_all[a * 16:a * 16 + 16, :] = roll(g, shift * edge).astype(BF16)
            moved = roll(jnp.where(mask[a], h, x), -shift) if shift else x
            moved_all[a * 16:a * 16 + 16, :] = moved.astype(BF16)
        products = dot_nt(turned_all[...], moved_all[...])
        side_by_side = jnp.concatenate(
            [products[a * 16:a * 16 + 16, :] for a in range(KSIZE)], axis=1)
        taps = dot(jnp.where(same, side_by_side, 0.0).astype(BF16), pick)
        place = at // 16 % 4
        taps = jnp.where(lane // 32 == place, roll(taps, 32 * place), 0.0)
        if place == 0:
            found.append(taps)
        else:
            found[-1] = found[-1] + taps
    tap_ref[...] = jnp.concatenate(found, axis=0).astype(BF16)


def halo_adjoint(edge, neighbours, rotations, spread, grad_ref, taps_ref, cot_ref, accum_ref, outs,
                 d_row, d_side, gathered):
    channels, pixels = grad_ref.shape
    wide = pixels + 2 * LANES
    tiles = gathered.shape[0]

    def block(i, carry):
        at = pl.multiple_of(i * 16, 16)
        gs = grad_ref[pl.ds(at, 16), :].astype(F32)
        taps_of = [taps_ref[tap, pl.ds(at, 16), :].astype(F32) for tap in range(KSIZE * KSIZE)]
        zeros = jnp.zeros((8, LANES), F32)
        rows, sides = [], []
        for half in (0, 8):
            g = jnp.concatenate([zeros, gs[half:half + 8], zeros], axis=1)
            turned = [roll(g, (a - HALO) * edge) for a in range(KSIZE)]
            d_x = d_h = None
            for b in range(KSIZE):
                shift = b - HALO
                back = None
                for a in range(KSIZE):
                    weight = taps_of[a * KSIZE + b][half:half + 8]
                    term = jnp.tile(weight, (1, wide // LANES)) * turned[a]
                    back = term if back is None else back + term
                back = roll(back, shift)
                if shift:
                    mask = side_mask(shift, back.shape, edge)
                    inside = jnp.where(mask, 0.0, back)
                    outside = jnp.where(mask, back, 0.0)
                    d_h = outside if d_h is None else d_h + outside
                    d_x = inside if d_x is None else d_x + inside
                else:
                    d_x = back if d_x is None else d_x + back
            rows.append(d_x)
            sides.append(d_h)
        d_x = jnp.concatenate(rows, axis=0)
        accum_ref[pl.ds(at, 16), :] = d_x[:, LANES:LANES + pixels]
        d_row[pl.ds(at, 16), :LANES] = d_x[:, :LANES].astype(BF16)
        d_row[pl.ds(at, 16), LANES:] = d_x[:, LANES + pixels:].astype(BF16)
        d_side[pl.ds(at, 16), :] = jnp.concatenate(sides, axis=0).astype(BF16)
        return carry

    lax.fori_loop(0, channels // 16, block, 0)
    accum_ref[...] += cot_ref[...].astype(F32)
    nb, rot = tile_row(neighbours), tile_row(rotations)
    gathered[...] = jnp.zeros(gathered.shape, F32)
    top, low = row_halo_maps(rot[1], rot[6], edge)
    gathered[slot_of(nb[1], tiles)] += dot_nt(d_row[:, :LANES], top)
    gathered[slot_of(nb[6], tiles)] += dot_nt(d_row[:, LANES:], low)
    packed = dot_nt(d_side[...], spread)
    pick, slot = side_map([rot[d] for d in SIDES], edge)
    for position, d in enumerate(SIDES):
        own = jnp.where(slot == position, packed, 0.0).astype(BF16)
        gathered[slot_of(nb[d], tiles)] += dot_nt(own, pick)
    store_parts(gathered, outs)


def store_parts(values, outs):
    for part, out in enumerate(outs):
        out = out.ref if isinstance(out, Stored) else out
        rows = out.shape[0]

        def store(t, carry, out=out, first=part * rows):
            out[t] = values[first + t].astype(BF16)
            return carry

        lax.fori_loop(0, rows, store, 0)


def halves(tiles):
    return tiles > 1 and tiles & (tiles - 1) == 0


def slot_of(tile, tiles):
    if not halves(tiles):
        return tile
    apart, slot = tile ^ lax.axis_index("tile"), 0
    for bit in halving_bits(tiles):
        slot = slot * 2 + jnp.where(apart & bit != 0, 1, 0)
    return slot


def halving_bits(tiles):
    bits = [1 << i for i in range(tiles.bit_length() - 1)]
    return bits[1:2] + bits[:1] + bits[2:]


def pair_kernel(kept, other, *refs):
    outs, total = refs[:-1], refs[-1]
    total[...] = kept.get()[...].astype(F32) + other.get()[...].astype(F32)
    store_parts(total, outs)


def border_kernel(edge, accum, *refs):
    parts, grad_ref = refs[:-1], refs[-1]
    rims = None
    for part in parts:
        more = total_of(part.get())
        rims = more if rims is None else rims + more
    high = rims.astype(BF16)
    low = (rims - high.astype(F32)).astype(BF16)
    pick = one_hot(rim_pixels(edge), edge * edge)
    added = dot_nt(high, pick) + dot_nt(low, pick)
    grad_ref[...] = (accum.get()[...] + added).astype(BF16)


def total_of(ref):
    return lax.fori_loop(1, ref.shape[0], lambda t, so_far: so_far + ref[t].astype(F32),
                         ref[0].astype(F32))


def sum_kernel(recv, tap, out, total, sems):
    recv = recv.get()
    share = recv.shape[1]
    total[:share, :] = total_of(recv).astype(BF16)
    total[share:, :] = tap.get()[...]
    copies = [pltpu.make_async_copy(total, out.at[t], sems.at[t]) for t in range(out.shape[0])]
    for copy in copies:
        copy.start()
    for copy in copies:
        copy.wait()


def compact_kernel(share, values, out):
    values = values.get()
    tiles, rows, _ = values.shape
    for tile in range(tiles):
        out[tile * share:(tile + 1) * share, :] = values[tile, :share, :]
    taps = values[0, share:, :].astype(F32)
    for tile in range(1, tiles):
        taps = taps + values[tile, share:, :].astype(F32)
    out[tiles * share:, :] = taps.astype(BF16)


def final_kernel(which, channels, tap_rows, scale, last, *refs):
    pieces, taps_in = refs[:len(which)], refs[len(which)]
    copies = []
    if last:
        g_in, g_out, g_tap_ref, buf_in, buf_out, sems = refs[-6:]
    else:
        g_in, g_out, g_tap_ref, copied, buf_in, buf_out, sems = refs[-7:]
        copies.append(pltpu.make_async_copy(refs[len(which) + 1].get(), copied, sems.at[0]))
        copies[0].start()
    full, units = buf_in.shape[1:]
    all_taps = taps_in.get()[...]
    row_of = lax.broadcasted_iota(jnp.int32, (full, LANES), 0)
    for i, k in enumerate(which):
        piece = pieces[i].get()
        owner = lax.axis_index("chan") ^ k
        start = pl.multiple_of(owner * units, units)
        used = 0
        for buffer, target in ((buf_in, g_in.at[:, pl.ds(start, units)]),
                               (buf_out, g_out.at[pl.ds(start, units)])):
            height, width = buffer.shape[1:]
            for column in range(0, width, LANES):
                buffer[i, :, column:column + LANES] = piece[used:used + height, :].astype(F32) * scale
                used += height
            copies.append(pltpu.make_async_copy(buffer.at[i], target, sems.at[len(copies)]))
            copies[-1].start()
        taps = piece[piece.shape[0] - tap_rows:, :].astype(F32)
        blocks = []
        for block in range(channels // 16):
            values = taps[block // 4 * 16:block // 4 * 16 + 16, :]
            blocks.append(roll(values, -32 * (block % 4)))
        own = jnp.concatenate(blocks * (full // channels), axis=0)
        all_taps = jnp.where(row_of // channels == owner, own, all_taps)
    if last:
        g_tap_ref[...] = all_taps.T[:KSIZE * KSIZE, :] * scale
    else:
        g_tap_ref[...] = all_taps
    for copy in copies:
        copy.wait()


def swap_chan(values, bit):
    return lax.ppermute(values, "chan", [(i, i ^ bit) for i in range(lax.axis_size("chan"))])


def gather_pieces(own, groups):
    pieces = {0: own}
    bit = groups // 2
    while bit:
        for k in list(pieces):
            pieces[k ^ bit] = swap_chan(pieces[k], bit)
        bit //= 2
    return [pieces[k] for k in range(groups)]


def first_tile(tiles):
    return tiles // 2


def swap_rows(values):
    tiles = lax.axis_size("tile")
    group = [(first_tile(tiles) + i) % tiles for i in range(tiles)]
    return lax.all_to_all(values, "tile", 0, 0, tiled=True, axis_index_groups=[group])


def halve(parts, bit, after):
    kept, given = parts
    half = ((kept.shape[0] // 2, *kept.shape[1:]), BF16, NEAR)
    return call(pair_kernel, [(kept, NEAR), (swap_bit(given, bit), NEAR)], [half] * 2,
                [pltpu.VMEM(kept.shape, F32)], time=0.3, after=after)


def swap_bit(values, bit):
    return lax.ppermute(values, "tile", [(t, t ^ bit) for t in range(lax.axis_size("tile"))])


def body(inputs, grad_out, kernel, w_in, w_out, neighbours, rotations):
    channels, pixels = inputs.shape[1:]
    edge = math.isqrt(pixels)
    full, hidden = w_in.shape
    groups = lax.axis_size("chan")
    tiles = lax.axis_size("tile")
    wide = pixels + 2 * LANES
    rim = 4 * HALO * edge
    units = hidden // groups
    scale = (tiles * pixels) ** -0.5
    x, cot = inputs[0], grad_out[0]

    [rims] = call(functools.partial(pack_kernel, edge), [(x, FAR)],
                  [((tiles, channels, rim), BF16, RAW)],
                  [pltpu.VMEM((channels, rim), BF16), pltpu.SemaphoreType.DMA((tiles,))])
    _, kernel = lax.optimization_barrier((rims, kernel))
    taps = jnp.broadcast_to(kernel[:, :, None], (KSIZE * KSIZE, channels, LANES))
    cot_pieces = gather_pieces(cot, groups)
    table = neighbours.shape
    w_in_t, center, nb_near, *maps = call(
        functools.partial(prep_kernel, edge),
        [(w_in, NEAR), (x, FAR), (neighbours, NEAR), (rotations, NEAR), (taps, NEAR)],
        [((hidden, full), BF16, NEAR), ((channels, pixels), F32, NEAR),
         (neighbours.shape, jnp.int32, NEAR), ((rim, LANES), BF16, NEAR), ((rim, LANES), BF16, NEAR),
         ((rim, 2 * LANES), BF16, NEAR), ((1, 2 * LANES), jnp.int32, NEAR),
         ((2 * HALO * edge, pixels), BF16, NEAR)], time=2.0, after=[(rims, RAW)])
    rims = swap_rows(rims)

    hid, halo = call(
        functools.partial(conv_kernel, edge),
        [(a, NEAR) for a in (nb_near, *maps, center, rims, taps)],
        [((channels, pixels), BF16, NEAR), ((channels, 4 * LANES), BF16, FAR)],
        [pltpu.VMEM((len(SIDES) * channels, rim), BF16),
         pltpu.VMEM((channels, 2 * HALO * edge), F32)], time=1.0, after=[(w_in_t, NEAR)])
    feats = lax.all_gather(hid, "chan", axis=0, tiled=True)
    cots, part_in, part_out = call(
        join_kernel, [(w_in_t, NEAR), (w_out, NEAR)] + [(piece, NEAR) for piece in cot_pieces],
        [((full, pixels), BF16, NEAR)] + [((units, full), BF16, NEAR)] * 2, time=0.6,
        after=[(feats, NEAR)])

    used = 2 * full * units // LANES
    share = -(-used // (16 * tiles)) * 16
    tap_rows = -(-channels // 64) * 16
    block = 2 * LANES
    part, gpre = call(
        weight_kernel,
        [(feats, NEAR), (cots, NEAR), (part_in, NEAR), (part_out, NEAR)],
        [((tiles * share, LANES), BF16, RAW), ((units, pixels), BF16, NEAR)],
        [pltpu.VMEM((units, pixels), BF16)]
        + [pltpu.VMEM((tiles * share, LANES), BF16), pltpu.SemaphoreType.DMA((3,))],
        time=2.2)
    part = swap_rows(part.reshape(tiles, share, LANES))

    parts = 2 if halves(tiles) else 1
    placed = ((tiles // parts, channels, rim), BF16, NEAR if parts > 1 else FAR)
    accum, tap_part, *border = call(
        functools.partial(back_kernel, edge, groups, tiles),
        [(feats, NEAR), (cots, NEAR), (w_in, FAR), (w_in_t, NEAR), (w_out, NEAR), (gpre, FAR), (x, FAR),
         (halo, FAR), (cot, FAR), (neighbours, NEAR), (rotations, NEAR), (taps, NEAR)],
        [((channels, pixels), F32, NEAR), ((tap_rows, LANES), BF16, NEAR)] + [placed] * parts,
        [pltpu.VMEM((hidden, pixels), BF16), pltpu.VMEM((channels, pixels), BF16),
         pltpu.VMEM((channels, wide), BF16), pltpu.VMEM((channels, wide), BF16),
         pltpu.VMEM((KSIZE * 16, wide), BF16), pltpu.VMEM((LANES, wide), BF16),
         pltpu.VMEM((channels, 2 * LANES), BF16), pltpu.VMEM((channels, wide), BF16),
         pltpu.VMEM((tiles, channels, rim), F32)], time=7.5, limit=32)
    [mine] = call(sum_kernel, [(part, NEAR), (tap_part, NEAR)],
                  [((tiles, share + tap_rows, LANES), BF16, RAW)],
                  [pltpu.VMEM((share + tap_rows, LANES), BF16), pltpu.SemaphoreType.DMA((tiles,))])
    [weights] = call(functools.partial(compact_kernel, share), [(swap_rows(mine), NEAR)],
                     [((tiles * share + tap_rows, LANES), BF16, NEAR)], time=0.1)

    [outputs] = call(
        functools.partial(out_kernel, block),
        [(feats, NEAR), (w_in_t, NEAR), (w_out, NEAR), (x, FAR)], [((channels, pixels), BF16, FAR)],
        [pltpu.VMEM((hidden, pixels), BF16)], time=4.0, limit=32, after=[(mine, RAW)])
    bits = halving_bits(tiles) if parts > 1 else [0]
    for step, bit in enumerate(bits[:-1]):
        border = halve(border, bit, [(outputs, RAW)] if step else [])
    weights, outputs, *border = lax.optimization_barrier((weights, outputs, *border))
    border = [border[0], swap_bit(border[1], bits[-1])] if parts > 1 else [
        lax.all_to_all(border[0], "tile", 0, 0, tiled=True)]
    [grad_in] = call(functools.partial(border_kernel, edge),
                     [(accum, NEAR)] + [(part, NEAR) for part in border],
                     [((channels, pixels), BF16, PINNED)])

    def place(which, taps_so_far, more, last):
        tap_shape = (KSIZE * KSIZE, full) if last else (full, LANES)
        copied = [] if last else [(more[0][0].shape, more[0][0].dtype, RAW)]
        return call(
            functools.partial(final_kernel, which, channels, tap_rows, scale, last),
            [(pieces[k], NEAR) for k in which] + [(taps_so_far, NEAR)] + more,
            [((full, hidden), F32, RAW), ((hidden, full), F32, RAW), (tap_shape, F32, NEAR)] + copied,
            [pltpu.VMEM((len(which), full, units), F32), pltpu.VMEM((len(which), units, full), F32),
             pltpu.SemaphoreType.DMA((2 * len(which) + 1,))],
            time=1.2, aliases={1 + len(which): 0, 2 + len(which): 1} if last else None)

    pieces = {0: weights}
    bit = groups // 2
    while bit > 1:
        for k in [k for k in pieces if k % 2 == 0]:
            pieces[k ^ bit] = swap_chan(pieces[k], bit)
        bit //= 2
    pieces[1] = swap_chan(weights, 1)
    even, odd = list(range(2, groups, 2)), list(range(3, groups, 2))
    for k in even:
        pieces[k], grad_in = lax.optimization_barrier((pieces[k], grad_in))
    for k in odd:
        pieces[k] = swap_chan(pieces[k ^ 1], 1)
    g_in, g_out, taps_so_far, grad_in = place(
        [0, 1, *even], jnp.zeros((full, LANES), F32), [(grad_in, NEAR)], False)
    grads = place(odd, taps_so_far, [(g_in, RAW), (g_out, RAW)], True)
    return (outputs[None], grad_in[None], *grads)


def solution(mesh):
    return jax.shard_map(
        body,
        mesh=mesh,
        in_specs=(
            P("tile", "chan", None),
            P("tile", "chan", None),
            P(None, "chan"),
            P(),
            P(),
            P(),
            P(),
        ),
        out_specs=(P("tile", "chan", None), P("tile", "chan", None), P(), P(), P()),
        check_vma=False,
    )
```

```python
import functools
import math

import jax
import jax.numpy as jnp
from jax import lax
from jax.experimental import pallas as pl
from jax.experimental.pallas import tpu as pltpu
from jax.sharding import PartitionSpec as P

KSIZE = 5
HALO = KSIZE // 2
LANES = 128
SIDES = (0, 2, 3, 4, 5, 7)
BF16 = jnp.bfloat16
F32 = jnp.float32

NEAR, FAR, RAW, PINNED = "near", "far", "raw", "pinned"
SPACES = {NEAR: pltpu.VMEM, FAR: pltpu.HBM, RAW: pltpu.HBM, PINNED: pltpu.VMEM}


class Loaded:
    def __init__(self, ref, copy=None):
        self.ref, self.copy = ref, copy
        if copy is not None:
            copy.start()

    def get(self):
        if self.copy is not None:
            self.copy.wait()
            self.copy = None
        return self.ref


class Stored:
    def __init__(self, ref, copy):
        self.ref, self.copy, self.started = ref, copy, False

    def send(self):
        if not self.started:
            self.copy.start()
            self.started = True


def call(kernel, ins, outs, scratch=(), time=1.0, after=(), aliases=None, limit=16):
    ins = list(ins) + list(after)
    buffers = []
    for shape, dtype, place in [(a.shape, a.dtype, p) for a, p in ins] + list(outs):
        if place == FAR:
            buffers += [pltpu.VMEM(shape, dtype), pltpu.SemaphoreType.DMA]

    def run(*refs):
        ends = len(ins), len(ins) + len(outs), len(ins) + len(outs) + len(buffers)
        spare = list(refs[ends[1]:ends[2]])
        operands, results = [], []
        for ref, (_, place) in zip(refs, ins):
            if place == FAR:
                buffer, sem = spare.pop(0), spare.pop(0)
                operands.append(Loaded(buffer, pltpu.make_async_copy(ref, buffer, sem)))
            else:
                operands.append(Loaded(ref) if place == NEAR else ref)
        for ref, (_, _, place) in zip(refs[ends[0]:], outs):
            if place == FAR:
                buffer, sem = spare.pop(0), spare.pop(0)
                results.append(Stored(buffer, pltpu.make_async_copy(buffer, ref, sem)))
            else:
                results.append(ref)
        kernel(*operands[:len(ins) - len(after)], *results, *refs[ends[2]:])
        far = [result for result in results if isinstance(result, Stored)]
        for result in far:
            result.send()
        for result in far:
            result.copy.wait()

    return pl.pallas_call(
        run,
        out_shape=[SPACES[p](s, d) if p != NEAR else jax.ShapeDtypeStruct(s, d)
                   for s, d, p in outs],
        in_specs=[pl.BlockSpec(memory_space=SPACES[p]) for _, p in ins],
        out_specs=[pl.BlockSpec(memory_space=SPACES[p]) for _, _, p in outs],
        scratch_shapes=buffers + list(scratch),
        input_output_aliases=aliases or {},
        cost_estimate=pl.CostEstimate(
            flops=int(time * 1e9), bytes_accessed=int(time * 3.5e6), transcendentals=0),
        compiler_params=pltpu.CompilerParams(vmem_limit_bytes=limit * 1024 * 1024),
    )(*[pltpu.with_memory_space_constraint(a, pltpu.HBM) if p in (FAR, RAW) else a
        for a, p in ins])


def tile_row(table):
    row = table.get()[pl.ds(lax.axis_index("tile"), 1), :]
    return [row[0, d] for d in range(8)]


def dot(a, b):
    return lax.dot_general(a, b, (((1,), (0,)), ((), ())), preferred_element_type=F32)


def dot_nt(a, b):
    return lax.dot_general(a, b, (((1,), (1,)), ((), ())), preferred_element_type=F32)


def one_hot(index, rows):
    row = lax.broadcasted_iota(jnp.int32, (rows, index.shape[1]), 0)
    return jnp.where(row == index, 1.0, 0.0).astype(BF16)


def rim_pixels(edge):
    band_len = HALO * edge
    lane = lax.broadcasted_iota(jnp.int32, (1, 4 * band_len), 1)
    band, at = lane // band_len, lane % band_len
    side = (at // HALO) * edge + at % HALO
    pixel = jnp.where(band == 0, at, (edge - HALO) * edge + at)
    return jnp.where(band == 2, side, jnp.where(band == 3, side + edge - HALO, pixel))


def rim_lane(row, col, edge):
    band_len = HALO * edge
    side = jnp.where(col < HALO, 2 * band_len + row * HALO + col,
                     3 * band_len + row * HALO + col - (edge - HALO))
    side = jnp.where(row >= edge - HALO, band_len + (row - (edge - HALO)) * edge + col, side)
    return jnp.where(row < HALO, row * edge + col, side)


def turned_lane(row, col, quarter, edge):
    last = edge - 1
    from_row = jnp.where(quarter == 1, col, jnp.where(
        quarter == 2, last - row, jnp.where(quarter == 3, last - col, row)))
    from_col = jnp.where(quarter == 1, last - row, jnp.where(
        quarter == 2, last - col, jnp.where(quarter == 3, row, col)))
    return rim_lane(from_row, from_col, edge)


def row_halo_maps(top_turn, bottom_turn, edge):
    rim = 4 * HALO * edge
    lane = lax.broadcasted_iota(jnp.int32, (1, LANES), 1)
    up = lane - (LANES - HALO * edge)
    top = turned_lane(edge - HALO + up // edge, up % edge, top_turn, edge)
    low = turned_lane(lane // edge, lane % edge, bottom_turn, edge)
    top = jnp.where(up >= 0, top, -1)
    low = jnp.where(lane < HALO * edge, low, -1)
    return one_hot(top, rim), one_hot(low, rim)


def side_map(turns, edge):
    rim = 4 * HALO * edge
    lane = lax.broadcasted_iota(jnp.int32, (1, 2 * LANES), 1)
    row, k = lane // (2 * HALO), lane % (2 * HALO)
    above, below, right = row < HALO, row >= HALO + edge, k >= HALO
    b_row = jnp.where(above, edge - HALO + row, jnp.where(below, row - HALO - edge, row - HALO))
    b_col = jnp.where(right, k - HALO, edge - HALO + k)
    slot = jnp.where(above, 0, jnp.where(below, 4, 2)) + right.astype(jnp.int32)
    quarter = jnp.zeros_like(slot)
    for position in range(len(SIDES)):
        quarter = jnp.where(slot == position, turns[position], quarter)
    index = turned_lane(b_row, b_col, quarter, edge)
    index = jnp.where(row < edge + 2 * HALO, index, -1)
    return one_hot(index, rim), slot


def spread_map(edge, wide):
    lane = lax.broadcasted_iota(jnp.int32, (1, wide), 1)
    row = lane // edge - (LANES // edge - HALO)
    col = lane % edge
    right_row, left_row = row - 1, row + 1
    rows = edge + 2 * HALO
    right = jnp.where((right_row >= 0) & (right_row < rows), right_row * 2 * HALO + HALO + col, -1)
    left = jnp.where((left_row >= 0) & (left_row < rows),
                     left_row * 2 * HALO + col - (edge - HALO), -1)
    index = jnp.where(col < HALO, right, jnp.where(col >= edge - HALO, left, -1))
    return one_hot(index, 2 * LANES)


def side_mask(shift, shape, edge):
    col = lax.broadcasted_iota(jnp.int32, shape, 1) % edge
    return col < shift if shift > 0 else col >= edge + shift


def roll(values, shift):
    size = values.shape[1]
    return values if shift % size == 0 else pltpu.roll(values, shift % size, axis=1)


def pack_kernel(edge, x, rims, rim, sems):
    pick = one_hot(rim_pixels(edge), edge * edge)
    rim[...] = dot(x.get()[...], pick).astype(BF16)
    copies = [pltpu.make_async_copy(rim, rims.at[t], sems.at[t]) for t in range(rims.shape[0])]
    for copy in copies:
        copy.start()
    for copy in copies:
        copy.wait()


def shifted(values, shift, edge):
    if not shift:
        return values
    return roll(jnp.where(side_mask(shift, values.shape, edge), 0.0, values), -shift)


def tap_rows_of(taps_ref, at):
    return [taps_ref[tap, pl.ds(at, 16), :].astype(F32) for tap in range(KSIZE * KSIZE)]


def center_conv(edge, x_ref, taps_ref, out_ref):
    channels, pixels = x_ref.shape
    wide = pixels + 2 * LANES

    def block(i, carry):
        at = pl.multiple_of(i * 16, 16)
        xs = x_ref[pl.ds(at, 16), :].astype(F32)
        taps = tap_rows_of(taps_ref, at)
        zeros = jnp.zeros((8, LANES), F32)
        halves = []
        for half in (0, 8):
            x = jnp.concatenate([zeros, xs[half:half + 8], zeros], axis=1)
            sums = [None] * KSIZE
            for b in range(KSIZE):
                moved = shifted(x, b - HALO, edge)
                for a in range(KSIZE):
                    term = jnp.tile(taps[a * KSIZE + b][half:half + 8], (1, wide // LANES)) * moved
                    sums[a] = term if sums[a] is None else sums[a] + term
            total = None
            for a in range(KSIZE):
                part = roll(sums[a], -(a - HALO) * edge)[:, LANES:LANES + pixels]
                total = part if total is None else total + part
            halves.append(total)
        out_ref[pl.ds(at, 16), :] = jnp.concatenate(halves, axis=0)
        return carry

    lax.fori_loop(0, channels // 16, block, 0)


def row_terms(rows, taps, edge, below):
    lane = lax.broadcasted_iota(jnp.int32, rows.shape, 1)
    total = None
    for a in range(KSIZE):
        far = a - HALO if below else HALO - a
        if far <= 0:
            continue
        sums = None
        for b in range(KSIZE):
            term = taps[a * KSIZE + b] * shifted(rows, b - HALO, edge)
            sums = term if sums is None else sums + term
        if below:
            part = jnp.where(lane >= LANES - far * edge, roll(sums, LANES - far * edge), 0.0)
        else:
            part = jnp.where(lane < far * edge, roll(sums, far * edge - LANES), 0.0)
        total = part if total is None else total + part
    return total


def side_terms(packed, taps, edge):
    place = lax.broadcasted_iota(jnp.int32, packed.shape, 1) % (2 * HALO)
    beside = jnp.where(place == 0, roll(packed, -1), jnp.where(place == 3, roll(packed, 1), 0.0))
    total = None
    for a in range(KSIZE):
        def tap(b):
            return jnp.tile(taps[a * KSIZE + b], (1, packed.shape[1] // LANES))

        terms = (jnp.where(place < HALO, tap(0), tap(4)) * packed
                 + jnp.where(place == 0, tap(1), tap(3)) * beside)
        part = roll(terms, -a * 2 * HALO)[:, :2 * HALO * edge]
        total = part if total is None else total + part
    return total


def column_map(edge):
    pixel = lax.broadcasted_iota(jnp.int32, (1, edge * edge), 1)
    row, col = pixel // edge, pixel % edge
    index = jnp.where(col < HALO, row * 2 * HALO + col, row * 2 * HALO + col - (edge - 2 * HALO))
    return one_hot(jnp.where((col < HALO) | (col >= edge - HALO), index, -1), 2 * HALO * edge)


def conv_kernel(edge, neighbours, top, low, pick, slot, columns, center, rims, taps,
                hidden_ref, halo, gathered, sides):
    rims_ref, taps_ref, halo_ref = rims.get(), taps.get(), halo.ref
    channels, pixels = hidden_ref.shape
    tiles = rims_ref.shape[0]
    nb = [lax.rem(tile + tiles - first_tile(tiles), tiles) for tile in tile_row(neighbours)]
    halo_ref[:, :LANES] = dot(rims_ref[nb[1]], top.get()[...]).astype(BF16)
    halo_ref[:, LANES:2 * LANES] = dot(rims_ref[nb[6]], low.get()[...]).astype(BF16)
    for position, d in enumerate(SIDES):
        gathered[position * channels:(position + 1) * channels, :] = rims_ref[nb[d]]
    candidates, slot = dot(gathered[...], pick.get()[...]), slot.get()[...]
    packed = candidates[:channels, :]
    for position in range(1, len(SIDES)):
        packed = jnp.where(slot == position,
                           candidates[position * channels:(position + 1) * channels, :], packed)
    halo_ref[:, 2 * LANES:] = packed.astype(BF16)
    halo.send()
    center = center.get()
    ends = []
    for at in range(0, channels, 16):
        halos = halo_ref[at:at + 16, :].astype(F32)
        taps_of = tap_rows_of(taps_ref, at)
        ends.append((row_terms(halos[:, :LANES], taps_of, edge, False),
                     row_terms(halos[:, LANES:2 * LANES], taps_of, edge, True)))
        sides[at:at + 16, :] = side_terms(halos[:, 2 * LANES:], taps_of, edge)
    high = sides[...].astype(BF16)
    low = (sides[...] - high.astype(F32)).astype(BF16)
    columns = columns.get()[...]
    hidden = center[...] + dot(high, columns) + dot(low, columns)
    hidden_ref[:, LANES:pixels - LANES] = hidden[:, LANES:pixels - LANES].astype(BF16)
    first = jnp.concatenate([end[0] for end in ends], axis=0)
    last = jnp.concatenate([end[1] for end in ends], axis=0)
    hidden_ref[:, :LANES] = (hidden[:, :LANES] + first).astype(BF16)
    hidden_ref[:, pixels - LANES:] = (hidden[:, pixels - LANES:] + last).astype(BF16)


def normal_below(values):
    return 0.5 * (1.0 + lax.erf(values * 0.7071067811865476))


def gelu_slope(values, below):
    return below + values * jnp.exp(-0.5 * values * values) * 0.3989422804014327


def column_steps(ref):
    return [slice(at, at + 2 * LANES) for at in range(0, ref.shape[1], 2 * LANES)]


def over_units(units, block, body):
    def step(i, carry):
        body(pl.ds(pl.multiple_of(i * block, block), block))
        return carry

    lax.fori_loop(0, units // block, step, 0)


def weight_kernel(feats, cots, w_in_t, w_out, part, gpre, act, stack, sems):
    feats, cots = feats.get(), cots.get()
    full, units = feats.shape[0], act.shape[0]
    w_in_t, w_out = w_in_t.get()[...], w_out.get()[...]
    for part_of in column_steps(feats):
        pre = dot(w_in_t, feats[:, part_of])
        below = normal_below(pre)
        act[:, part_of] = (pre * below).astype(BF16)
        slope = gelu_slope(pre, below)
        gpre[:, part_of] = (dot(w_out, cots[:, part_of]) * slope).astype(BF16)
    used, copies = 0, []
    for values, height in ((dot_nt(feats[...], gpre[...]), full),
                           (dot_nt(act[...], cots[...]), units)):
        first = used
        for column in range(0, values.shape[1], LANES):
            stack[used:used + height, :] = values[:, column:column + LANES].astype(BF16)
            used += height
        copies.append(pltpu.make_async_copy(
            stack.at[first:used], part.at[first:used], sems.at[len(copies)]))
        copies[-1].start()
    if used < part.shape[0]:
        stack[used:, :] = jnp.zeros((part.shape[0] - used, LANES), BF16)
        copies.append(pltpu.make_async_copy(stack.at[used:], part.at[used:], sems.at[2]))
        copies[-1].start()
    for copy in copies:
        copy.wait()


def out_kernel(block, feats, w_in_t, w_out, x, out, act):
    feats, w_in_t, w_out = feats.get(), w_in_t.get(), w_out.get()

    def units(rows):
        for part_of in column_steps(feats):
            pre = dot(w_in_t[rows, :], feats[:, part_of])
            act[rows, part_of] = (pre * normal_below(pre)).astype(BF16)

    over_units(w_out.shape[0], block, units)
    channels = out.ref.shape[0]
    row = lax.broadcasted_iota(jnp.int32, (channels, w_out.shape[1]), 0)
    column = lax.broadcasted_iota(jnp.int32, (channels, w_out.shape[1]), 1)
    pick = jnp.where(column == row + lax.axis_index("chan") * channels, 1.0, 0.0).astype(BF16)
    branch = dot(dot_nt(pick, w_out[...]).astype(BF16), act[...])
    out.ref[...] = (x.get()[...].astype(F32) + branch.astype(BF16).astype(F32)).astype(BF16)


def back_kernel(edge, groups, tiles, feats, cots, w_in, w_in_t, w_out, gpre_own, x, halo, cot,
                neighbours, rotations, taps, accum_ref, tap_ref, *refs):
    outs, (gpre, grad_ref, padded_ref, side_ref, turned_all, moved_all, d_row, d_side, gathered) = (
        refs[:-9], refs[-9:])
    channels, pixels = grad_ref.shape
    feats, cots, w_in_t, w_out = feats.get(), cots.get(), w_in_t.get(), w_out.get()

    chan, units = lax.axis_index("chan"), gpre_own.ref.shape[0]

    def others(k, carry):
        rows = pl.ds(pl.multiple_of((chan ^ k) * units, units), units)
        for part_of in column_steps(feats):
            pre = dot(w_in_t[rows, :], feats[:, part_of])
            slope = gelu_slope(pre, normal_below(pre))
            gpre[rows, part_of] = (dot(w_out[rows, :], cots[:, part_of]) * slope).astype(BF16)
        return carry

    lax.fori_loop(1, groups, others, 0)
    gpre[pl.ds(pl.multiple_of(chan * units, units), units), :] = gpre_own.get()[...]
    own = pl.ds(pl.multiple_of(lax.axis_index("chan") * channels, channels), channels)
    grad_ref[...] = dot(w_in.get()[own, :], gpre[...]).astype(BF16)
    halo = halo.get()
    padded_ref[:, :LANES] = halo[:, :LANES]
    padded_ref[:, LANES:LANES + pixels] = x.get()[...]
    padded_ref[:, LANES + pixels:] = halo[:, LANES:2 * LANES]
    spread = spread_map(edge, padded_ref.shape[1])
    side_ref[...] = dot(halo[:, 2 * LANES:], spread).astype(BF16)
    tap_terms(edge, grad_ref, padded_ref, side_ref, tap_ref, turned_all, moved_all)
    halo_adjoint(edge, neighbours, rotations, spread, grad_ref, taps.get(), cot.get(), accum_ref,
                 outs, d_row, d_side, gathered)


def prep_kernel(edge, w_in, x, neighbours, rotations, taps, w_in_t_ref, center_ref, nb_ref,
                *map_refs):
    nb_ref[...] = neighbours.get()[...]
    rot = tile_row(rotations)
    pick, slot = side_map([rot[d] for d in SIDES], edge)
    maps = (*row_halo_maps(rot[1], rot[6], edge), pick, slot, column_map(edge))
    for ref, values in zip(map_refs, maps):
        ref[...] = values
    w_in_t_ref[...] = w_in.get()[...].astype(F32).T.astype(BF16)
    center_conv(edge, x.get(), taps.get(), center_ref)


def join_kernel(w_in_t, w_out, *refs):
    pieces, (out_ref, part_in_ref, part_out_ref) = refs[:-3], refs[-3:]
    chan = lax.axis_index("chan")
    for k, piece in enumerate(pieces):
        piece = piece.get()
        channels = piece.shape[0]
        start = pl.multiple_of((chan ^ k) * channels, channels)
        out_ref[pl.ds(start, channels), :] = piece[...]
    units = part_in_ref.shape[0]
    mine = pl.ds(pl.multiple_of(chan * units, units), units)
    part_in_ref[...] = w_in_t.get()[mine, :]
    part_out_ref[...] = w_out.get()[mine, :]


def tap_terms(edge, grad_ref, padded_ref, side_ref, tap_ref, turned_all, moved_all):
    channels, pixels = grad_ref.shape
    wide = pixels + 2 * LANES
    moved_all[KSIZE * 16:, :] = jnp.zeros((LANES - KSIZE * 16, wide), BF16)
    same = (lax.broadcasted_iota(jnp.int32, (16, KSIZE * LANES), 1) % 16
            == lax.broadcasted_iota(jnp.int32, (16, KSIZE * LANES), 0))
    line = lax.broadcasted_iota(jnp.int32, (KSIZE * LANES, LANES), 0)
    tap = lax.broadcasted_iota(jnp.int32, (KSIZE * LANES, LANES), 1)
    used = line % LANES < KSIZE * 16
    pick = jnp.where(used & (line // LANES * KSIZE + line % LANES // 16 == tap), 1.0, 0.0).astype(BF16)
    mask = {b: side_mask(b - HALO, (16, wide), edge) for b in range(KSIZE) if b != HALO}
    lane = lax.broadcasted_iota(jnp.int32, (16, LANES), 1)
    zeros = jnp.zeros((16, LANES), F32)
    found = []
    for at in range(0, channels, 16):
        g = jnp.concatenate([zeros, grad_ref[at:at + 16, :].astype(F32), zeros], axis=1)
        x = padded_ref[at:at + 16, :].astype(F32)
        h = side_ref[at:at + 16, :].astype(F32)
        for a in range(KSIZE):
            shift = a - HALO
            turned_all[a * 16:a * 16 + 16, :] = roll(g, shift * edge).astype(BF16)
            moved = roll(jnp.where(mask[a], h, x), -shift) if shift else x
            moved_all[a * 16:a * 16 + 16, :] = moved.astype(BF16)
        products = dot_nt(turned_all[...], moved_all[...])
        side_by_side = jnp.concatenate(
            [products[a * 16:a * 16 + 16, :] for a in range(KSIZE)], axis=1)
        taps = dot(jnp.where(same, side_by_side, 0.0).astype(BF16), pick)
        place = at // 16 % 4
        taps = jnp.where(lane // 32 == place, roll(taps, 32 * place), 0.0)
        if place == 0:
            found.append(taps)
        else:
            found[-1] = found[-1] + taps
    tap_ref[...] = jnp.concatenate(found, axis=0).astype(BF16)


def halo_adjoint(edge, neighbours, rotations, spread, grad_ref, taps_ref, cot_ref, accum_ref, outs,
                 d_row, d_side, gathered):
    channels, pixels = grad_ref.shape
    wide = pixels + 2 * LANES
    tiles = gathered.shape[0]

    def block(i, carry):
        at = pl.multiple_of(i * 16, 16)
        gs = grad_ref[pl.ds(at, 16), :].astype(F32)
        taps_of = [taps_ref[tap, pl.ds(at, 16), :].astype(F32) for tap in range(KSIZE * KSIZE)]
        zeros = jnp.zeros((8, LANES), F32)
        rows, sides = [], []
        for half in (0, 8):
            g = jnp.concatenate([zeros, gs[half:half + 8], zeros], axis=1)
            turned = [roll(g, (a - HALO) * edge) for a in range(KSIZE)]
            d_x = d_h = None
            for b in range(KSIZE):
                shift = b - HALO
                back = None
                for a in range(KSIZE):
                    weight = taps_of[a * KSIZE + b][half:half + 8]
                    term = jnp.tile(weight, (1, wide // LANES)) * turned[a]
                    back = term if back is None else back + term
                back = roll(back, shift)
                if shift:
                    mask = side_mask(shift, back.shape, edge)
                    inside = jnp.where(mask, 0.0, back)
                    outside = jnp.where(mask, back, 0.0)
                    d_h = outside if d_h is None else d_h + outside
                    d_x = inside if d_x is None else d_x + inside
                else:
                    d_x = back if d_x is None else d_x + back
            rows.append(d_x)
            sides.append(d_h)
        d_x = jnp.concatenate(rows, axis=0)
        accum_ref[pl.ds(at, 16), :] = d_x[:, LANES:LANES + pixels]
        d_row[pl.ds(at, 16), :LANES] = d_x[:, :LANES].astype(BF16)
        d_row[pl.ds(at, 16), LANES:] = d_x[:, LANES + pixels:].astype(BF16)
        d_side[pl.ds(at, 16), :] = jnp.concatenate(sides, axis=0).astype(BF16)
        return carry

    lax.fori_loop(0, channels // 16, block, 0)
    accum_ref[...] += cot_ref[...].astype(F32)
    nb, rot = tile_row(neighbours), tile_row(rotations)
    gathered[...] = jnp.zeros(gathered.shape, F32)
    top, low = row_halo_maps(rot[1], rot[6], edge)
    gathered[slot_of(nb[1], tiles)] += dot_nt(d_row[:, :LANES], top)
    gathered[slot_of(nb[6], tiles)] += dot_nt(d_row[:, LANES:], low)
    packed = dot_nt(d_side[...], spread)
    pick, slot = side_map([rot[d] for d in SIDES], edge)
    for position, d in enumerate(SIDES):
        own = jnp.where(slot == position, packed, 0.0).astype(BF16)
        gathered[slot_of(nb[d], tiles)] += dot_nt(own, pick)
    store_parts(gathered, outs)


def store_parts(values, outs):
    for part, out in enumerate(outs):
        out = out.ref if isinstance(out, Stored) else out
        rows = out.shape[0]

        def store(t, carry, out=out, first=part * rows):
            out[t] = values[first + t].astype(BF16)
            return carry

        lax.fori_loop(0, rows, store, 0)


def halves(tiles):
    return tiles > 1 and tiles & (tiles - 1) == 0


def slot_of(tile, tiles):
    if not halves(tiles):
        return tile
    apart, slot = tile ^ lax.axis_index("tile"), 0
    for bit in halving_bits(tiles):
        slot = slot * 2 + jnp.where(apart & bit != 0, 1, 0)
    return slot


def halving_bits(tiles):
    bits = [1 << i for i in range(tiles.bit_length() - 1)]
    return bits[1:2] + bits[:1] + bits[2:]


def pair_kernel(kept, other, *refs):
    outs, total = refs[:-1], refs[-1]
    total[...] = kept.get()[...].astype(F32) + other.get()[...].astype(F32)
    store_parts(total, outs)


def border_kernel(edge, accum, *refs):
    parts, grad_ref = refs[:-1], refs[-1]
    rims = None
    for part in parts:
        more = total_of(part.get())
        rims = more if rims is None else rims + more
    high = rims.astype(BF16)
    low = (rims - high.astype(F32)).astype(BF16)
    pick = one_hot(rim_pixels(edge), edge * edge)
    added = dot_nt(high, pick) + dot_nt(low, pick)
    grad_ref[...] = (accum.get()[...] + added).astype(BF16)


def total_of(ref):
    return lax.fori_loop(1, ref.shape[0], lambda t, so_far: so_far + ref[t].astype(F32),
                         ref[0].astype(F32))


def sum_kernel(recv, tap, out, total, sems):
    recv = recv.get()
    share = recv.shape[1]
    total[:share, :] = total_of(recv).astype(BF16)
    total[share:, :] = tap.get()[...]
    copies = [pltpu.make_async_copy(total, out.at[t], sems.at[t]) for t in range(out.shape[0])]
    for copy in copies:
        copy.start()
    for copy in copies:
        copy.wait()


def compact_kernel(share, values, out):
    values = values.get()
    tiles, rows, _ = values.shape
    for tile in range(tiles):
        out[tile * share:(tile + 1) * share, :] = values[tile, :share, :]
    taps = values[0, share:, :].astype(F32)
    for tile in range(1, tiles):
        taps = taps + values[tile, share:, :].astype(F32)
    out[tiles * share:, :] = taps.astype(BF16)


def final_kernel(which, channels, tap_rows, scale, last, *refs):
    pieces, taps_in = refs[:len(which)], refs[len(which)]
    copies = []
    if last:
        g_in, g_out, g_tap_ref, buf_in, buf_out, sems = refs[-6:]
    else:
        g_in, g_out, g_tap_ref, copied, buf_in, buf_out, sems = refs[-7:]
        copies.append(pltpu.make_async_copy(refs[len(which) + 1].get(), copied, sems.at[0]))
        copies[0].start()
    full, units = buf_in.shape[1:]
    all_taps = taps_in.get()[...]
    row_of = lax.broadcasted_iota(jnp.int32, (full, LANES), 0)
    for i, k in enumerate(which):
        piece = pieces[i].get()
        owner = lax.axis_index("chan") ^ k
        start = pl.multiple_of(owner * units, units)
        used = 0
        for buffer, target in ((buf_in, g_in.at[:, pl.ds(start, units)]),
                               (buf_out, g_out.at[pl.ds(start, units)])):
            height, width = buffer.shape[1:]
            for column in range(0, width, LANES):
                buffer[i, :, column:column + LANES] = piece[used:used + height, :].astype(F32) * scale
                used += height
            copies.append(pltpu.make_async_copy(buffer.at[i], target, sems.at[len(copies)]))
            copies[-1].start()
        taps = piece[piece.shape[0] - tap_rows:, :].astype(F32)
        blocks = []
        for block in range(channels // 16):
            values = taps[block // 4 * 16:block // 4 * 16 + 16, :]
            blocks.append(roll(values, -32 * (block % 4)))
        own = jnp.concatenate(blocks * (full // channels), axis=0)
        all_taps = jnp.where(row_of // channels == owner, own, all_taps)
    if last:
        g_tap_ref.ref[...] = all_taps.T[:KSIZE * KSIZE, :] * scale
        g_tap_ref.send()
    else:
        g_tap_ref[...] = all_taps
    for copy in copies:
        copy.wait()


def swap_chan(values, bit):
    return lax.ppermute(values, "chan", [(i, i ^ bit) for i in range(lax.axis_size("chan"))])


def gather_pieces(own, groups):
    pieces = {0: own}
    bit = groups // 2
    while bit:
        for k in list(pieces):
            pieces[k ^ bit] = swap_chan(pieces[k], bit)
        bit //= 2
    return [pieces[k] for k in range(groups)]


def first_tile(tiles):
    return tiles // 2


def swap_rows(values):
    tiles = lax.axis_size("tile")
    group = [(first_tile(tiles) + i) % tiles for i in range(tiles)]
    return lax.all_to_all(values, "tile", 0, 0, tiled=True, axis_index_groups=[group])


def halve(parts, bit, after):
    kept, given = parts
    half = ((kept.shape[0] // 2, *kept.shape[1:]), BF16, NEAR)
    return call(pair_kernel, [(kept, NEAR), (swap_bit(given, bit), NEAR)], [half] * 2,
                [pltpu.VMEM(kept.shape, F32)], time=0.3, after=after)


def swap_bit(values, bit):
    return lax.ppermute(values, "tile", [(t, t ^ bit) for t in range(lax.axis_size("tile"))])


def body(inputs, grad_out, kernel, w_in, w_out, neighbours, rotations):
    channels, pixels = inputs.shape[1:]
    edge = math.isqrt(pixels)
    full, hidden = w_in.shape
    groups = lax.axis_size("chan")
    tiles = lax.axis_size("tile")
    wide = pixels + 2 * LANES
    rim = 4 * HALO * edge
    units = hidden // groups
    scale = (tiles * pixels) ** -0.5
    x, cot = inputs[0], grad_out[0]

    [rims] = call(functools.partial(pack_kernel, edge), [(x, FAR)],
                  [((tiles, channels, rim), BF16, RAW)],
                  [pltpu.VMEM((channels, rim), BF16), pltpu.SemaphoreType.DMA((tiles,))])
    _, kernel = lax.optimization_barrier((rims, kernel))
    taps = jnp.broadcast_to(kernel[:, :, None], (KSIZE * KSIZE, channels, LANES))
    cot_pieces = gather_pieces(cot, groups)
    table = neighbours.shape
    w_in_t, center, nb_near, *maps = call(
        functools.partial(prep_kernel, edge),
        [(w_in, NEAR), (x, FAR), (neighbours, NEAR), (rotations, NEAR), (taps, NEAR)],
        [((hidden, full), BF16, NEAR), ((channels, pixels), F32, NEAR),
         (neighbours.shape, jnp.int32, NEAR), ((rim, LANES), BF16, NEAR), ((rim, LANES), BF16, NEAR),
         ((rim, 2 * LANES), BF16, NEAR), ((1, 2 * LANES), jnp.int32, NEAR),
         ((2 * HALO * edge, pixels), BF16, NEAR)], time=2.0, after=[(rims, RAW)])
    rims = swap_rows(rims)

    hid, halo = call(
        functools.partial(conv_kernel, edge),
        [(a, NEAR) for a in (nb_near, *maps, center, rims, taps)],
        [((channels, pixels), BF16, NEAR), ((channels, 4 * LANES), BF16, FAR)],
        [pltpu.VMEM((len(SIDES) * channels, rim), BF16),
         pltpu.VMEM((channels, 2 * HALO * edge), F32)], time=1.0, after=[(w_in_t, NEAR)])
    feats = lax.all_gather(hid, "chan", axis=0, tiled=True)
    cots, part_in, part_out = call(
        join_kernel, [(w_in_t, NEAR), (w_out, NEAR)] + [(piece, NEAR) for piece in cot_pieces],
        [((full, pixels), BF16, NEAR)] + [((units, full), BF16, NEAR)] * 2, time=0.6,
        after=[(feats, NEAR)])

    used = 2 * full * units // LANES
    share = -(-used // (16 * tiles)) * 16
    tap_rows = -(-channels // 64) * 16
    block = 2 * LANES
    part, gpre = call(
        weight_kernel,
        [(feats, NEAR), (cots, NEAR), (part_in, NEAR), (part_out, NEAR)],
        [((tiles * share, LANES), BF16, RAW), ((units, pixels), BF16, NEAR)],
        [pltpu.VMEM((units, pixels), BF16)]
        + [pltpu.VMEM((tiles * share, LANES), BF16), pltpu.SemaphoreType.DMA((3,))],
        time=2.2)
    part = swap_rows(part.reshape(tiles, share, LANES))

    parts = 2 if halves(tiles) else 1
    placed = ((tiles // parts, channels, rim), BF16, NEAR if parts > 1 else FAR)
    accum, tap_part, *border = call(
        functools.partial(back_kernel, edge, groups, tiles),
        [(feats, NEAR), (cots, NEAR), (w_in, FAR), (w_in_t, NEAR), (w_out, NEAR), (gpre, FAR), (x, FAR),
         (halo, FAR), (cot, FAR), (neighbours, NEAR), (rotations, NEAR), (taps, NEAR)],
        [((channels, pixels), F32, NEAR), ((tap_rows, LANES), BF16, NEAR)] + [placed] * parts,
        [pltpu.VMEM((hidden, pixels), BF16), pltpu.VMEM((channels, pixels), BF16),
         pltpu.VMEM((channels, wide), BF16), pltpu.VMEM((channels, wide), BF16),
         pltpu.VMEM((KSIZE * 16, wide), BF16), pltpu.VMEM((LANES, wide), BF16),
         pltpu.VMEM((channels, 2 * LANES), BF16), pltpu.VMEM((channels, wide), BF16),
         pltpu.VMEM((tiles, channels, rim), F32)], time=7.5, limit=32)
    [mine] = call(sum_kernel, [(part, NEAR), (tap_part, NEAR)],
                  [((tiles, share + tap_rows, LANES), BF16, RAW)],
                  [pltpu.VMEM((share + tap_rows, LANES), BF16), pltpu.SemaphoreType.DMA((tiles,))])
    [weights] = call(functools.partial(compact_kernel, share), [(swap_rows(mine), NEAR)],
                     [((tiles * share + tap_rows, LANES), BF16, NEAR)], time=0.1)

    [outputs] = call(
        functools.partial(out_kernel, block),
        [(feats, NEAR), (w_in_t, NEAR), (w_out, NEAR), (x, FAR)], [((channels, pixels), BF16, FAR)],
        [pltpu.VMEM((hidden, pixels), BF16)], time=4.0, limit=32, after=[(mine, RAW)])
    bits = halving_bits(tiles) if parts > 1 else [0]
    for step, bit in enumerate(bits[:-1]):
        border = halve(border, bit, [(outputs, RAW)] if step else [])
    weights, outputs, *border = lax.optimization_barrier((weights, outputs, *border))
    border = [border[0], swap_bit(border[1], bits[-1])] if parts > 1 else [
        lax.all_to_all(border[0], "tile", 0, 0, tiled=True)]
    [grad_in] = call(functools.partial(border_kernel, edge),
                     [(accum, NEAR)] + [(part, NEAR) for part in border],
                     [((channels, pixels), BF16, PINNED)])

    def place(which, taps_so_far, more, last):
        tap_shape = (KSIZE * KSIZE, full) if last else (full, LANES)
        copied = [] if last else [(more[0][0].shape, more[0][0].dtype, RAW)]
        return call(
            functools.partial(final_kernel, which, channels, tap_rows, scale, last),
            [(pieces[k], NEAR) for k in which] + [(taps_so_far, NEAR)] + more,
            [((full, hidden), F32, RAW), ((hidden, full), F32, RAW), (tap_shape, F32, FAR if last else NEAR)]
            + copied,
            [pltpu.VMEM((len(which), full, units), F32), pltpu.VMEM((len(which), units, full), F32),
             pltpu.SemaphoreType.DMA((2 * len(which) + 1,))],
            time=1.2, aliases={1 + len(which): 0, 2 + len(which): 1} if last else None)

    pieces = {0: weights}
    bit = groups // 2
    while bit > 1:
        for k in [k for k in pieces if k % 2 == 0]:
            pieces[k ^ bit] = swap_chan(pieces[k], bit)
        bit //= 2
    pieces[1] = swap_chan(weights, 1)
    even, odd = list(range(2, groups, 2)), list(range(3, groups, 2))
    for k in even:
        pieces[k], grad_in = lax.optimization_barrier((pieces[k], grad_in))
    for k in odd:
        pieces[k] = swap_chan(pieces[k ^ 1], 1)
    g_in, g_out, taps_so_far, grad_in = place(
        [0, 1, *even], jnp.zeros((full, LANES), F32), [(grad_in, NEAR)], False)
    grads = place(odd, taps_so_far, [(g_in, RAW), (g_out, RAW)], True)
    return (outputs[None], grad_in[None], *grads)


def solution(mesh):
    return jax.shard_map(
        body,
        mesh=mesh,
        in_specs=(
            P("tile", "chan", None),
            P("tile", "chan", None),
            P(None, "chan"),
            P(),
            P(),
            P(),
            P(),
        ),
        out_specs=(P("tile", "chan", None), P("tile", "chan", None), P(), P(), P()),
        check_vma=False,
    )
```

```python
import functools
import math

import jax
import jax.numpy as jnp
from jax import lax
from jax.experimental import pallas as pl
from jax.experimental.pallas import tpu as pltpu
from jax.sharding import PartitionSpec as P

KSIZE = 5
HALO = KSIZE // 2
LANES = 128
SIDES = (0, 2, 3, 4, 5, 7)
BF16 = jnp.bfloat16
F32 = jnp.float32

NEAR, FAR, RAW, PINNED = "near", "far", "raw", "pinned"
SPACES = {NEAR: pltpu.VMEM, FAR: pltpu.HBM, RAW: pltpu.HBM, PINNED: pltpu.VMEM}


class Loaded:
    def __init__(self, ref, copy=None):
        self.ref, self.copy = ref, copy
        if copy is not None:
            copy.start()

    def get(self):
        if self.copy is not None:
            self.copy.wait()
            self.copy = None
        return self.ref


class Stored:
    def __init__(self, ref, copy):
        self.ref, self.copy, self.started = ref, copy, False

    def send(self):
        if not self.started:
            self.copy.start()
            self.started = True


def call(kernel, ins, outs, scratch=(), time=1.0, after=(), aliases=None, limit=16):
    ins = list(ins) + list(after)
    buffers = []
    for shape, dtype, place in [(a.shape, a.dtype, p) for a, p in ins] + list(outs):
        if place == FAR:
            buffers += [pltpu.VMEM(shape, dtype), pltpu.SemaphoreType.DMA]

    def run(*refs):
        ends = len(ins), len(ins) + len(outs), len(ins) + len(outs) + len(buffers)
        spare = list(refs[ends[1]:ends[2]])
        operands, results = [], []
        for ref, (_, place) in zip(refs, ins):
            if place == FAR:
                buffer, sem = spare.pop(0), spare.pop(0)
                operands.append(Loaded(buffer, pltpu.make_async_copy(ref, buffer, sem)))
            else:
                operands.append(Loaded(ref) if place == NEAR else ref)
        for ref, (_, _, place) in zip(refs[ends[0]:], outs):
            if place == FAR:
                buffer, sem = spare.pop(0), spare.pop(0)
                results.append(Stored(buffer, pltpu.make_async_copy(buffer, ref, sem)))
            else:
                results.append(ref)
        kernel(*operands[:len(ins) - len(after)], *results, *refs[ends[2]:])
        far = [result for result in results if isinstance(result, Stored)]
        for result in far:
            result.send()
        for result in far:
            result.copy.wait()

    return pl.pallas_call(
        run,
        out_shape=[SPACES[p](s, d) if p != NEAR else jax.ShapeDtypeStruct(s, d)
                   for s, d, p in outs],
        in_specs=[pl.BlockSpec(memory_space=SPACES[p]) for _, p in ins],
        out_specs=[pl.BlockSpec(memory_space=SPACES[p]) for _, _, p in outs],
        scratch_shapes=buffers + list(scratch),
        input_output_aliases=aliases or {},
        cost_estimate=pl.CostEstimate(
            flops=int(time * 1e9), bytes_accessed=int(time * 3.5e6), transcendentals=0),
        compiler_params=pltpu.CompilerParams(vmem_limit_bytes=limit * 1024 * 1024),
    )(*[pltpu.with_memory_space_constraint(a, pltpu.HBM) if p in (FAR, RAW) else a
        for a, p in ins])


def tile_row(table):
    row = table.get()[pl.ds(lax.axis_index("tile"), 1), :]
    return [row[0, d] for d in range(8)]


def dot(a, b):
    return lax.dot_general(a, b, (((1,), (0,)), ((), ())), preferred_element_type=F32)


def dot_nt(a, b):
    return lax.dot_general(a, b, (((1,), (1,)), ((), ())), preferred_element_type=F32)


def one_hot(index, rows):
    row = lax.broadcasted_iota(jnp.int32, (rows, index.shape[1]), 0)
    return jnp.where(row == index, 1.0, 0.0).astype(BF16)


def rim_pixels(edge):
    band_len = HALO * edge
    lane = lax.broadcasted_iota(jnp.int32, (1, 4 * band_len), 1)
    band, at = lane // band_len, lane % band_len
    side = (at // HALO) * edge + at % HALO
    pixel = jnp.where(band == 0, at, (edge - HALO) * edge + at)
    return jnp.where(band == 2, side, jnp.where(band == 3, side + edge - HALO, pixel))


def rim_lane(row, col, edge):
    band_len = HALO * edge
    side = jnp.where(col < HALO, 2 * band_len + row * HALO + col,
                     3 * band_len + row * HALO + col - (edge - HALO))
    side = jnp.where(row >= edge - HALO, band_len + (row - (edge - HALO)) * edge + col, side)
    return jnp.where(row < HALO, row * edge + col, side)


def turned_lane(row, col, quarter, edge):
    last = edge - 1
    from_row = jnp.where(quarter == 1, col, jnp.where(
        quarter == 2, last - row, jnp.where(quarter == 3, last - col, row)))
    from_col = jnp.where(quarter == 1, last - row, jnp.where(
        quarter == 2, last - col, jnp.where(quarter == 3, row, col)))
    return rim_lane(from_row, from_col, edge)


def row_halo_maps(top_turn, bottom_turn, edge):
    rim = 4 * HALO * edge
    lane = lax.broadcasted_iota(jnp.int32, (1, LANES), 1)
    up = lane - (LANES - HALO * edge)
    top = turned_lane(edge - HALO + up // edge, up % edge, top_turn, edge)
    low = turned_lane(lane // edge, lane % edge, bottom_turn, edge)
    top = jnp.where(up >= 0, top, -1)
    low = jnp.where(lane < HALO * edge, low, -1)
    return one_hot(top, rim), one_hot(low, rim)


def side_map(turns, edge):
    rim = 4 * HALO * edge
    lane = lax.broadcasted_iota(jnp.int32, (1, 2 * LANES), 1)
    row, k = lane // (2 * HALO), lane % (2 * HALO)
    above, below, right = row < HALO, row >= HALO + edge, k >= HALO
    b_row = jnp.where(above, edge - HALO + row, jnp.where(below, row - HALO - edge, row - HALO))
    b_col = jnp.where(right, k - HALO, edge - HALO + k)
    slot = jnp.where(above, 0, jnp.where(below, 4, 2)) + right.astype(jnp.int32)
    quarter = jnp.zeros_like(slot)
    for position in range(len(SIDES)):
        quarter = jnp.where(slot == position, turns[position], quarter)
    index = turned_lane(b_row, b_col, quarter, edge)
    index = jnp.where(row < edge + 2 * HALO, index, -1)
    return one_hot(index, rim), slot


def spread_map(edge, wide):
    lane = lax.broadcasted_iota(jnp.int32, (1, wide), 1)
    row = lane // edge - (LANES // edge - HALO)
    col = lane % edge
    right_row, left_row = row - 1, row + 1
    rows = edge + 2 * HALO
    right = jnp.where((right_row >= 0) & (right_row < rows), right_row * 2 * HALO + HALO + col, -1)
    left = jnp.where((left_row >= 0) & (left_row < rows),
                     left_row * 2 * HALO + col - (edge - HALO), -1)
    index = jnp.where(col < HALO, right, jnp.where(col >= edge - HALO, left, -1))
    return one_hot(index, 2 * LANES)


def side_mask(shift, shape, edge):
    col = lax.broadcasted_iota(jnp.int32, shape, 1) % edge
    return col < shift if shift > 0 else col >= edge + shift


def roll(values, shift):
    size = values.shape[1]
    return values if shift % size == 0 else pltpu.roll(values, shift % size, axis=1)


def pack_kernel(edge, x, rims, rim, sems):
    pick = one_hot(rim_pixels(edge), edge * edge)
    rim[...] = dot(x.get()[...], pick).astype(BF16)
    copies = [pltpu.make_async_copy(rim, rims.at[t], sems.at[t]) for t in range(rims.shape[0])]
    for copy in copies:
        copy.start()
    for copy in copies:
        copy.wait()


def shifted(values, shift, edge):
    if not shift:
        return values
    return roll(jnp.where(side_mask(shift, values.shape, edge), 0.0, values), -shift)


def tap_rows_of(taps_ref, at):
    return [taps_ref[tap, pl.ds(at, 16), :].astype(F32) for tap in range(KSIZE * KSIZE)]


def center_conv(edge, x_ref, taps_ref, out_ref):
    channels, pixels = x_ref.shape
    wide = pixels + 2 * LANES

    def block(i, carry):
        at = pl.multiple_of(i * 16, 16)
        xs = x_ref[pl.ds(at, 16), :].astype(F32)
        taps = tap_rows_of(taps_ref, at)
        zeros = jnp.zeros((8, LANES), F32)
        halves = []
        for half in (0, 8):
            x = jnp.concatenate([zeros, xs[half:half + 8], zeros], axis=1)
            sums = [None] * KSIZE
            for b in range(KSIZE):
                moved = shifted(x, b - HALO, edge)
                for a in range(KSIZE):
                    term = jnp.tile(taps[a * KSIZE + b][half:half + 8], (1, wide // LANES)) * moved
                    sums[a] = term if sums[a] is None else sums[a] + term
            total = None
            for a in range(KSIZE):
                part = roll(sums[a], -(a - HALO) * edge)[:, LANES:LANES + pixels]
                total = part if total is None else total + part
            halves.append(total)
        out_ref[pl.ds(at, 16), :] = jnp.concatenate(halves, axis=0)
        return carry

    lax.fori_loop(0, channels // 16, block, 0)


def row_terms(rows, taps, edge, below):
    lane = lax.broadcasted_iota(jnp.int32, rows.shape, 1)
    total = None
    for a in range(KSIZE):
        far = a - HALO if below else HALO - a
        if far <= 0:
            continue
        sums = None
        for b in range(KSIZE):
            term = taps[a * KSIZE + b] * shifted(rows, b - HALO, edge)
            sums = term if sums is None else sums + term
        if below:
            part = jnp.where(lane >= LANES - far * edge, roll(sums, LANES - far * edge), 0.0)
        else:
            part = jnp.where(lane < far * edge, roll(sums, far * edge - LANES), 0.0)
        total = part if total is None else total + part
    return total


def side_terms(packed, taps, edge):
    place = lax.broadcasted_iota(jnp.int32, packed.shape, 1) % (2 * HALO)
    beside = jnp.where(place == 0, roll(packed, -1), jnp.where(place == 3, roll(packed, 1), 0.0))
    total = None
    for a in range(KSIZE):
        def tap(b):
            return jnp.tile(taps[a * KSIZE + b], (1, packed.shape[1] // LANES))

        terms = (jnp.where(place < HALO, tap(0), tap(4)) * packed
                 + jnp.where(place == 0, tap(1), tap(3)) * beside)
        part = roll(terms, -a * 2 * HALO)[:, :2 * HALO * edge]
        total = part if total is None else total + part
    return total


def column_map(edge):
    pixel = lax.broadcasted_iota(jnp.int32, (1, edge * edge), 1)
    row, col = pixel // edge, pixel % edge
    index = jnp.where(col < HALO, row * 2 * HALO + col, row * 2 * HALO + col - (edge - 2 * HALO))
    return one_hot(jnp.where((col < HALO) | (col >= edge - HALO), index, -1), 2 * HALO * edge)


def conv_kernel(edge, neighbours, top, low, pick, slot, columns, center, rims, taps,
                hidden_ref, halo, gathered, sides):
    rims_ref, taps_ref, halo_ref = rims.get(), taps.get(), halo.ref
    channels, pixels = hidden_ref.shape
    tiles = rims_ref.shape[0]
    nb = [lax.rem(tile + tiles - first_tile(tiles), tiles) for tile in tile_row(neighbours)]
    halo_ref[:, :LANES] = dot(rims_ref[nb[1]], top.get()[...]).astype(BF16)
    halo_ref[:, LANES:2 * LANES] = dot(rims_ref[nb[6]], low.get()[...]).astype(BF16)
    for position, d in enumerate(SIDES):
        gathered[position * channels:(position + 1) * channels, :] = rims_ref[nb[d]]
    candidates, slot = dot(gathered[...], pick.get()[...]), slot.get()[...]
    packed = candidates[:channels, :]
    for position in range(1, len(SIDES)):
        packed = jnp.where(slot == position,
                           candidates[position * channels:(position + 1) * channels, :], packed)
    halo_ref[:, 2 * LANES:] = packed.astype(BF16)
    halo.send()
    center = center.get()
    ends = []
    for at in range(0, channels, 16):
        halos = halo_ref[at:at + 16, :].astype(F32)
        taps_of = tap_rows_of(taps_ref, at)
        ends.append((row_terms(halos[:, :LANES], taps_of, edge, False),
                     row_terms(halos[:, LANES:2 * LANES], taps_of, edge, True)))
        sides[at:at + 16, :] = side_terms(halos[:, 2 * LANES:], taps_of, edge)
    high = sides[...].astype(BF16)
    low = (sides[...] - high.astype(F32)).astype(BF16)
    columns = columns.get()[...]
    hidden = center[...] + dot(high, columns) + dot(low, columns)
    hidden_ref[:, LANES:pixels - LANES] = hidden[:, LANES:pixels - LANES].astype(BF16)
    first = jnp.concatenate([end[0] for end in ends], axis=0)
    last = jnp.concatenate([end[1] for end in ends], axis=0)
    hidden_ref[:, :LANES] = (hidden[:, :LANES] + first).astype(BF16)
    hidden_ref[:, pixels - LANES:] = (hidden[:, pixels - LANES:] + last).astype(BF16)


def normal_below(values):
    return 0.5 * (1.0 + lax.erf(values * 0.7071067811865476))


def gelu_slope(values, below):
    return below + values * jnp.exp(-0.5 * values * values) * 0.3989422804014327


def column_steps(ref):
    return [slice(at, at + 2 * LANES) for at in range(0, ref.shape[1], 2 * LANES)]


def over_units(units, block, body):
    def step(i, carry):
        body(pl.ds(pl.multiple_of(i * block, block), block))
        return carry

    lax.fori_loop(0, units // block, step, 0)


def weight_kernel(feats, cots, w_in_t, w_out, part, gpre, act, stack, sems):
    feats, cots = feats.get(), cots.get()
    full, units = feats.shape[0], act.shape[0]
    w_in_t, w_out = w_in_t.get()[...], w_out.get()[...]
    for part_of in column_steps(feats):
        pre = dot(w_in_t, feats[:, part_of])
        below = normal_below(pre)
        act[:, part_of] = (pre * below).astype(BF16)
        slope = gelu_slope(pre, below)
        gpre[:, part_of] = (dot(w_out, cots[:, part_of]) * slope).astype(BF16)
    used, copies = 0, []
    for values, height in ((dot_nt(feats[...], gpre[...]), full),
                           (dot_nt(act[...], cots[...]), units)):
        first = used
        for column in range(0, values.shape[1], LANES):
            stack[used:used + height, :] = values[:, column:column + LANES].astype(BF16)
            used += height
        copies.append(pltpu.make_async_copy(
            stack.at[first:used], part.at[first:used], sems.at[len(copies)]))
        copies[-1].start()
    if used < part.shape[0]:
        stack[used:, :] = jnp.zeros((part.shape[0] - used, LANES), BF16)
        copies.append(pltpu.make_async_copy(stack.at[used:], part.at[used:], sems.at[2]))
        copies[-1].start()
    for copy in copies:
        copy.wait()


def out_kernel(block, feats, w_in_t, w_out, x, out, act):
    feats, w_in_t, w_out = feats.get(), w_in_t.get(), w_out.get()

    def units(rows):
        for part_of in column_steps(feats):
            pre = dot(w_in_t[rows, :], feats[:, part_of])
            act[rows, part_of] = (pre * normal_below(pre)).astype(BF16)

    over_units(w_out.shape[0], block, units)
    channels = out.ref.shape[0]
    row = lax.broadcasted_iota(jnp.int32, (channels, w_out.shape[1]), 0)
    column = lax.broadcasted_iota(jnp.int32, (channels, w_out.shape[1]), 1)
    pick = jnp.where(column == row + lax.axis_index("chan") * channels, 1.0, 0.0).astype(BF16)
    branch = dot(dot_nt(pick, w_out[...]).astype(BF16), act[...])
    out.ref[...] = (x.get()[...].astype(F32) + branch.astype(BF16).astype(F32)).astype(BF16)


def back_kernel(edge, groups, tiles, feats, cots, w_in, w_in_t, w_out, gpre_own, x, halo, cot,
                neighbours, rotations, taps, accum_ref, tap_ref, *refs):
    outs, (gpre, grad_ref, padded_ref, side_ref, turned_all, moved_all, d_row, d_side, gathered) = (
        refs[:-9], refs[-9:])
    channels, pixels = grad_ref.shape
    feats, cots, w_in_t, w_out = feats.get(), cots.get(), w_in_t.get(), w_out.get()

    chan, units = lax.axis_index("chan"), gpre_own.ref.shape[0]

    def others(k, carry):
        rows = pl.ds(pl.multiple_of((chan ^ k) * units, units), units)
        for part_of in column_steps(feats):
            pre = dot(w_in_t[rows, :], feats[:, part_of])
            slope = gelu_slope(pre, normal_below(pre))
            gpre[rows, part_of] = (dot(w_out[rows, :], cots[:, part_of]) * slope).astype(BF16)
        return carry

    lax.fori_loop(1, groups, others, 0)
    gpre[pl.ds(pl.multiple_of(chan * units, units), units), :] = gpre_own.get()[...]
    own = pl.ds(pl.multiple_of(lax.axis_index("chan") * channels, channels), channels)
    grad_ref[...] = dot(w_in.get()[own, :], gpre[...]).astype(BF16)
    halo = halo.get()
    padded_ref[:, :LANES] = halo[:, :LANES]
    padded_ref[:, LANES:LANES + pixels] = x.get()[...]
    padded_ref[:, LANES + pixels:] = halo[:, LANES:2 * LANES]
    spread = spread_map(edge, padded_ref.shape[1])
    side_ref[...] = dot(halo[:, 2 * LANES:], spread).astype(BF16)
    tap_terms(edge, grad_ref, padded_ref, side_ref, tap_ref, turned_all, moved_all)
    halo_adjoint(edge, neighbours, rotations, spread, grad_ref, taps.get(), cot.get(), accum_ref,
                 outs, d_row, d_side, gathered)


def prep_kernel(edge, w_in, x, neighbours, rotations, taps, w_in_t_ref, center_ref, nb_ref,
                *map_refs):
    nb_ref[...] = neighbours.get()[...]
    rot = tile_row(rotations)
    pick, slot = side_map([rot[d] for d in SIDES], edge)
    maps = (*row_halo_maps(rot[1], rot[6], edge), pick, slot, column_map(edge))
    for ref, values in zip(map_refs, maps):
        ref[...] = values
    w_in_t_ref[...] = w_in.get()[...].astype(F32).T.astype(BF16)
    center_conv(edge, x.get(), taps.get(), center_ref)


def join_kernel(w_in_t, w_out, *refs):
    pieces, (out_ref, part_in_ref, part_out_ref) = refs[:-3], refs[-3:]
    chan = lax.axis_index("chan")
    for k, piece in enumerate(pieces):
        piece = piece.get()
        channels = piece.shape[0]
        start = pl.multiple_of((chan ^ k) * channels, channels)
        out_ref[pl.ds(start, channels), :] = piece[...]
    units = part_in_ref.shape[0]
    mine = pl.ds(pl.multiple_of(chan * units, units), units)
    part_in_ref[...] = w_in_t.get()[mine, :]
    part_out_ref[...] = w_out.get()[mine, :]


def tap_terms(edge, grad_ref, padded_ref, side_ref, tap_ref, turned_all, moved_all):
    channels, pixels = grad_ref.shape
    wide = pixels + 2 * LANES
    moved_all[KSIZE * 16:, :] = jnp.zeros((LANES - KSIZE * 16, wide), BF16)
    same = (lax.broadcasted_iota(jnp.int32, (16, KSIZE * LANES), 1) % 16
            == lax.broadcasted_iota(jnp.int32, (16, KSIZE * LANES), 0))
    line = lax.broadcasted_iota(jnp.int32, (KSIZE * LANES, LANES), 0)
    tap = lax.broadcasted_iota(jnp.int32, (KSIZE * LANES, LANES), 1)
    used = line % LANES < KSIZE * 16
    pick = jnp.where(used & (line // LANES * KSIZE + line % LANES // 16 == tap), 1.0, 0.0).astype(BF16)
    mask = {b: side_mask(b - HALO, (16, wide), edge) for b in range(KSIZE) if b != HALO}
    lane = lax.broadcasted_iota(jnp.int32, (16, LANES), 1)
    zeros = jnp.zeros((16, LANES), F32)
    found = []
    for at in range(0, channels, 16):
        g = jnp.concatenate([zeros, grad_ref[at:at + 16, :].astype(F32), zeros], axis=1)
        x = padded_ref[at:at + 16, :].astype(F32)
        h = side_ref[at:at + 16, :].astype(F32)
        for a in range(KSIZE):
            shift = a - HALO
            turned_all[a * 16:a * 16 + 16, :] = roll(g, shift * edge).astype(BF16)
            moved = roll(jnp.where(mask[a], h, x), -shift) if shift else x
            moved_all[a * 16:a * 16 + 16, :] = moved.astype(BF16)
        products = dot_nt(turned_all[...], moved_all[...])
        side_by_side = jnp.concatenate(
            [products[a * 16:a * 16 + 16, :] for a in range(KSIZE)], axis=1)
        taps = dot(jnp.where(same, side_by_side, 0.0).astype(BF16), pick)
        place = at // 16 % 4
        taps = jnp.where(lane // 32 == place, roll(taps, 32 * place), 0.0)
        if place == 0:
            found.append(taps)
        else:
            found[-1] = found[-1] + taps
    tap_ref[...] = jnp.concatenate(found, axis=0).astype(BF16)


def halo_adjoint(edge, neighbours, rotations, spread, grad_ref, taps_ref, cot_ref, accum_ref, outs,
                 d_row, d_side, gathered):
    channels, pixels = grad_ref.shape
    wide = pixels + 2 * LANES
    tiles = gathered.shape[0]

    def block(i, carry):
        at = pl.multiple_of(i * 16, 16)
        gs = grad_ref[pl.ds(at, 16), :].astype(F32)
        taps_of = [taps_ref[tap, pl.ds(at, 16), :].astype(F32) for tap in range(KSIZE * KSIZE)]
        zeros = jnp.zeros((8, LANES), F32)
        rows, sides = [], []
        for half in (0, 8):
            g = jnp.concatenate([zeros, gs[half:half + 8], zeros], axis=1)
            turned = [roll(g, (a - HALO) * edge) for a in range(KSIZE)]
            d_x = d_h = None
            for b in range(KSIZE):
                shift = b - HALO
                back = None
                for a in range(KSIZE):
                    weight = taps_of[a * KSIZE + b][half:half + 8]
                    term = jnp.tile(weight, (1, wide // LANES)) * turned[a]
                    back = term if back is None else back + term
                back = roll(back, shift)
                if shift:
                    mask = side_mask(shift, back.shape, edge)
                    inside = jnp.where(mask, 0.0, back)
                    outside = jnp.where(mask, back, 0.0)
                    d_h = outside if d_h is None else d_h + outside
                    d_x = inside if d_x is None else d_x + inside
                else:
                    d_x = back if d_x is None else d_x + back
            rows.append(d_x)
            sides.append(d_h)
        d_x = jnp.concatenate(rows, axis=0)
        accum_ref[pl.ds(at, 16), :] = d_x[:, LANES:LANES + pixels]
        d_row[pl.ds(at, 16), :LANES] = d_x[:, :LANES].astype(BF16)
        d_row[pl.ds(at, 16), LANES:] = d_x[:, LANES + pixels:].astype(BF16)
        d_side[pl.ds(at, 16), :] = jnp.concatenate(sides, axis=0).astype(BF16)
        return carry

    lax.fori_loop(0, channels // 16, block, 0)
    accum_ref[...] += cot_ref[...].astype(F32)
    nb, rot = tile_row(neighbours), tile_row(rotations)
    gathered[...] = jnp.zeros(gathered.shape, F32)
    top, low = row_halo_maps(rot[1], rot[6], edge)
    gathered[slot_of(nb[1], tiles)] += dot_nt(d_row[:, :LANES], top)
    gathered[slot_of(nb[6], tiles)] += dot_nt(d_row[:, LANES:], low)
    packed = dot_nt(d_side[...], spread)
    pick, slot = side_map([rot[d] for d in SIDES], edge)
    own = jnp.concatenate(
        [jnp.where(slot == position, packed, 0.0) for position in range(len(SIDES))], axis=0)
    placed = dot_nt(own.astype(BF16), pick)
    for position, d in enumerate(SIDES):
        gathered[slot_of(nb[d], tiles)] += placed[position * channels:(position + 1) * channels, :]
    store_parts(gathered, outs)


def store_parts(values, outs):
    for part, out in enumerate(outs):
        out = out.ref if isinstance(out, Stored) else out
        rows = out.shape[0]

        def store(t, carry, out=out, first=part * rows):
            out[t] = values[first + t].astype(BF16)
            return carry

        lax.fori_loop(0, rows, store, 0)


def halves(tiles):
    return tiles > 1 and tiles & (tiles - 1) == 0


def slot_of(tile, tiles):
    if not halves(tiles):
        return tile
    apart, slot = tile ^ lax.axis_index("tile"), 0
    for bit in halving_bits(tiles):
        slot = slot * 2 + jnp.where(apart & bit != 0, 1, 0)
    return slot


def halving_bits(tiles):
    bits = [1 << i for i in range(tiles.bit_length() - 1)]
    return bits[1:2] + bits[:1] + bits[2:]


def pair_kernel(kept, other, *refs):
    outs, total = refs[:-1], refs[-1]
    total[...] = kept.get()[...].astype(F32) + other.get()[...].astype(F32)
    store_parts(total, outs)


def border_kernel(edge, accum, *refs):
    parts, grad_ref = refs[:-1], refs[-1]
    rims = None
    for part in parts:
        more = total_of(part.get())
        rims = more if rims is None else rims + more
    high = rims.astype(BF16)
    low = (rims - high.astype(F32)).astype(BF16)
    pick = one_hot(rim_pixels(edge), edge * edge)
    added = dot_nt(high, pick) + dot_nt(low, pick)
    grad_ref[...] = (accum.get()[...] + added).astype(BF16)


def total_of(ref):
    return lax.fori_loop(1, ref.shape[0], lambda t, so_far: so_far + ref[t].astype(F32),
                         ref[0].astype(F32))


def sum_kernel(recv, tap, out, total, sems):
    recv = recv.get()
    share = recv.shape[1]
    total[:share, :] = total_of(recv).astype(BF16)
    total[share:, :] = tap.get()[...]
    copies = [pltpu.make_async_copy(total, out.at[t], sems.at[t]) for t in range(out.shape[0])]
    for copy in copies:
        copy.start()
    for copy in copies:
        copy.wait()


def compact_kernel(share, values, out):
    values = values.get()
    tiles, rows, _ = values.shape
    for tile in range(tiles):
        out[tile * share:(tile + 1) * share, :] = values[tile, :share, :]
    taps = values[0, share:, :].astype(F32)
    for tile in range(1, tiles):
        taps = taps + values[tile, share:, :].astype(F32)
    out[tiles * share:, :] = taps.astype(BF16)


def final_kernel(which, channels, tap_rows, scale, last, *refs):
    pieces, taps_in = refs[:len(which)], refs[len(which)]
    copies = []
    if last:
        g_in, g_out, g_tap_ref, buf_in, buf_out, sems = refs[-6:]
    else:
        g_in, g_out, g_tap_ref, copied, buf_in, buf_out, sems = refs[-7:]
        copies.append(pltpu.make_async_copy(refs[len(which) + 1].get(), copied, sems.at[0]))
        copies[0].start()
    full, units = buf_in.shape[1:]
    all_taps = taps_in.get()[...]
    row_of = lax.broadcasted_iota(jnp.int32, (full, LANES), 0)
    for i, k in enumerate(which):
        piece = pieces[i].get()
        owner = lax.axis_index("chan") ^ k
        start = pl.multiple_of(owner * units, units)
        used = 0
        for buffer, target in ((buf_in, g_in.at[:, pl.ds(start, units)]),
                               (buf_out, g_out.at[pl.ds(start, units)])):
            height, width = buffer.shape[1:]
            for column in range(0, width, LANES):
                buffer[i, :, column:column + LANES] = piece[used:used + height, :].astype(F32) * scale
                used += height
            copies.append(pltpu.make_async_copy(buffer.at[i], target, sems.at[len(copies)]))
            copies[-1].start()
        taps = piece[piece.shape[0] - tap_rows:, :].astype(F32)
        blocks = []
        for block in range(channels // 16):
            values = taps[block // 4 * 16:block // 4 * 16 + 16, :]
            blocks.append(roll(values, -32 * (block % 4)))
        own = jnp.concatenate(blocks * (full // channels), axis=0)
        all_taps = jnp.where(row_of // channels == owner, own, all_taps)
    if last:
        g_tap_ref.ref[...] = all_taps.T[:KSIZE * KSIZE, :] * scale
        g_tap_ref.send()
    else:
        g_tap_ref[...] = all_taps
    for copy in copies:
        copy.wait()


def swap_chan(values, bit):
    return lax.ppermute(values, "chan", [(i, i ^ bit) for i in range(lax.axis_size("chan"))])


def gather_pieces(own, groups):
    pieces = {0: own}
    bit = groups // 2
    while bit:
        for k in list(pieces):
            pieces[k ^ bit] = swap_chan(pieces[k], bit)
        bit //= 2
    return [pieces[k] for k in range(groups)]


def first_tile(tiles):
    return tiles // 2


def swap_rows(values):
    tiles = lax.axis_size("tile")
    group = [(first_tile(tiles) + i) % tiles for i in range(tiles)]
    return lax.all_to_all(values, "tile", 0, 0, tiled=True, axis_index_groups=[group])


def halve(parts, bit, after):
    kept, given = parts
    half = ((kept.shape[0] // 2, *kept.shape[1:]), BF16, NEAR)
    return call(pair_kernel, [(kept, NEAR), (swap_bit(given, bit), NEAR)], [half] * 2,
                [pltpu.VMEM(kept.shape, F32)], time=0.3, after=after)


def swap_bit(values, bit):
    return lax.ppermute(values, "tile", [(t, t ^ bit) for t in range(lax.axis_size("tile"))])


def body(inputs, grad_out, kernel, w_in, w_out, neighbours, rotations):
    channels, pixels = inputs.shape[1:]
    edge = math.isqrt(pixels)
    full, hidden = w_in.shape
    groups = lax.axis_size("chan")
    tiles = lax.axis_size("tile")
    wide = pixels + 2 * LANES
    rim = 4 * HALO * edge
    units = hidden // groups
    scale = (tiles * pixels) ** -0.5
    x, cot = inputs[0], grad_out[0]

    [rims] = call(functools.partial(pack_kernel, edge), [(x, FAR)],
                  [((tiles, channels, rim), BF16, RAW)],
                  [pltpu.VMEM((channels, rim), BF16), pltpu.SemaphoreType.DMA((tiles,))])
    _, kernel = lax.optimization_barrier((rims, kernel))
    taps = jnp.broadcast_to(kernel[:, :, None], (KSIZE * KSIZE, channels, LANES))
    cot_pieces = gather_pieces(cot, groups)
    table = neighbours.shape
    w_in_t, center, nb_near, *maps = call(
        functools.partial(prep_kernel, edge),
        [(w_in, NEAR), (x, FAR), (neighbours, NEAR), (rotations, NEAR), (taps, NEAR)],
        [((hidden, full), BF16, NEAR), ((channels, pixels), F32, NEAR),
         (neighbours.shape, jnp.int32, NEAR), ((rim, LANES), BF16, NEAR), ((rim, LANES), BF16, NEAR),
         ((rim, 2 * LANES), BF16, NEAR), ((1, 2 * LANES), jnp.int32, NEAR),
         ((2 * HALO * edge, pixels), BF16, NEAR)], time=2.0, after=[(rims, RAW)])
    rims = swap_rows(rims)

    hid, halo = call(
        functools.partial(conv_kernel, edge),
        [(a, NEAR) for a in (nb_near, *maps, center, rims, taps)],
        [((channels, pixels), BF16, NEAR), ((channels, 4 * LANES), BF16, FAR)],
        [pltpu.VMEM((len(SIDES) * channels, rim), BF16),
         pltpu.VMEM((channels, 2 * HALO * edge), F32)], time=1.0, after=[(w_in_t, NEAR)])
    feats = lax.all_gather(hid, "chan", axis=0, tiled=True)
    cots, part_in, part_out = call(
        join_kernel, [(w_in_t, NEAR), (w_out, NEAR)] + [(piece, NEAR) for piece in cot_pieces],
        [((full, pixels), BF16, NEAR)] + [((units, full), BF16, NEAR)] * 2, time=0.6,
        after=[(feats, NEAR)])

    used = 2 * full * units // LANES
    share = -(-used // (16 * tiles)) * 16
    tap_rows = -(-channels // 64) * 16
    block = 2 * LANES
    part, gpre = call(
        weight_kernel,
        [(feats, NEAR), (cots, NEAR), (part_in, NEAR), (part_out, NEAR)],
        [((tiles * share, LANES), BF16, RAW), ((units, pixels), BF16, NEAR)],
        [pltpu.VMEM((units, pixels), BF16)]
        + [pltpu.VMEM((tiles * share, LANES), BF16), pltpu.SemaphoreType.DMA((3,))],
        time=2.2)
    part = swap_rows(part.reshape(tiles, share, LANES))

    parts = 2 if halves(tiles) else 1
    placed = ((tiles // parts, channels, rim), BF16, NEAR if parts > 1 else FAR)
    accum, tap_part, *border = call(
        functools.partial(back_kernel, edge, groups, tiles),
        [(feats, NEAR), (cots, NEAR), (w_in, FAR), (w_in_t, NEAR), (w_out, NEAR), (gpre, FAR), (x, FAR),
         (halo, FAR), (cot, FAR), (neighbours, NEAR), (rotations, NEAR), (taps, NEAR)],
        [((channels, pixels), F32, NEAR), ((tap_rows, LANES), BF16, NEAR)] + [placed] * parts,
        [pltpu.VMEM((hidden, pixels), BF16), pltpu.VMEM((channels, pixels), BF16),
         pltpu.VMEM((channels, wide), BF16), pltpu.VMEM((channels, wide), BF16),
         pltpu.VMEM((KSIZE * 16, wide), BF16), pltpu.VMEM((LANES, wide), BF16),
         pltpu.VMEM((channels, 2 * LANES), BF16), pltpu.VMEM((channels, wide), BF16),
         pltpu.VMEM((tiles, channels, rim), F32)], time=7.5, limit=32)
    [mine] = call(sum_kernel, [(part, NEAR), (tap_part, NEAR)],
                  [((tiles, share + tap_rows, LANES), BF16, RAW)],
                  [pltpu.VMEM((share + tap_rows, LANES), BF16), pltpu.SemaphoreType.DMA((tiles,))])
    [weights] = call(functools.partial(compact_kernel, share), [(swap_rows(mine), NEAR)],
                     [((tiles * share + tap_rows, LANES), BF16, NEAR)], time=0.1)

    [outputs] = call(
        functools.partial(out_kernel, block),
        [(feats, NEAR), (w_in_t, NEAR), (w_out, NEAR), (x, FAR)], [((channels, pixels), BF16, FAR)],
        [pltpu.VMEM((hidden, pixels), BF16)], time=4.0, limit=32, after=[(mine, RAW)])
    bits = halving_bits(tiles) if parts > 1 else [0]
    for step, bit in enumerate(bits[:-1]):
        border = halve(border, bit, [(outputs, RAW)] if step else [])
    weights, outputs, *border = lax.optimization_barrier((weights, outputs, *border))
    border = [border[0], swap_bit(border[1], bits[-1])] if parts > 1 else [
        lax.all_to_all(border[0], "tile", 0, 0, tiled=True)]
    [grad_in] = call(functools.partial(border_kernel, edge),
                     [(accum, NEAR)] + [(part, NEAR) for part in border],
                     [((channels, pixels), BF16, PINNED)])

    def place(which, taps_so_far, more, last):
        tap_shape = (KSIZE * KSIZE, full) if last else (full, LANES)
        copied = [] if last else [(more[0][0].shape, more[0][0].dtype, RAW)]
        return call(
            functools.partial(final_kernel, which, channels, tap_rows, scale, last),
            [(pieces[k], NEAR) for k in which] + [(taps_so_far, NEAR)] + more,
            [((full, hidden), F32, RAW), ((hidden, full), F32, RAW), (tap_shape, F32, FAR if last else NEAR)]
            + copied,
            [pltpu.VMEM((len(which), full, units), F32), pltpu.VMEM((len(which), units, full), F32),
             pltpu.SemaphoreType.DMA((2 * len(which) + 1,))],
            time=1.2, aliases={1 + len(which): 0, 2 + len(which): 1} if last else None)

    pieces = {0: weights}
    bit = groups // 2
    while bit > 1:
        for k in [k for k in pieces if k % 2 == 0]:
            pieces[k ^ bit] = swap_chan(pieces[k], bit)
        bit //= 2
    pieces[1] = swap_chan(weights, 1)
    even, odd = list(range(2, groups, 2)), list(range(3, groups, 2))
    for k in even:
        pieces[k], grad_in = lax.optimization_barrier((pieces[k], grad_in))
    for k in odd:
        pieces[k] = swap_chan(pieces[k ^ 1], 1)
    g_in, g_out, taps_so_far, grad_in = place(
        [0, 1, *even], jnp.zeros((full, LANES), F32), [(grad_in, NEAR)], False)
    grads = place(odd, taps_so_far, [(g_in, RAW), (g_out, RAW)], True)
    return (outputs[None], grad_in[None], *grads)


def solution(mesh):
    return jax.shard_map(
        body,
        mesh=mesh,
        in_specs=(
            P("tile", "chan", None),
            P("tile", "chan", None),
            P(None, "chan"),
            P(),
            P(),
            P(),
            P(),
        ),
        out_specs=(P("tile", "chan", None), P("tile", "chan", None), P(), P(), P()),
        check_vma=False,
    )
```

```python
import functools
import math

import jax
import jax.numpy as jnp
from jax import lax
from jax.experimental import pallas as pl
from jax.experimental.pallas import tpu as pltpu
from jax.sharding import PartitionSpec as P

KSIZE = 5
HALO = KSIZE // 2
LANES = 128
SIDES = (0, 2, 3, 4, 5, 7)
BF16 = jnp.bfloat16
F32 = jnp.float32

NEAR, FAR, RAW, PINNED = "near", "far", "raw", "pinned"
SPACES = {NEAR: pltpu.VMEM, FAR: pltpu.HBM, RAW: pltpu.HBM, PINNED: pltpu.VMEM}


class Loaded:
    def __init__(self, ref, copy=None):
        self.ref, self.copy = ref, copy
        if copy is not None:
            copy.start()

    def get(self):
        if self.copy is not None:
            self.copy.wait()
            self.copy = None
        return self.ref


class Stored:
    def __init__(self, ref, copy):
        self.ref, self.copy, self.started = ref, copy, False

    def send(self):
        if not self.started:
            self.copy.start()
            self.started = True


def call(kernel, ins, outs, scratch=(), time=1.0, after=(), aliases=None, limit=16):
    ins = list(ins) + list(after)
    buffers = []
    for shape, dtype, place in [(a.shape, a.dtype, p) for a, p in ins] + list(outs):
        if place == FAR:
            buffers += [pltpu.VMEM(shape, dtype), pltpu.SemaphoreType.DMA]

    def run(*refs):
        ends = len(ins), len(ins) + len(outs), len(ins) + len(outs) + len(buffers)
        spare = list(refs[ends[1]:ends[2]])
        operands, results = [], []
        for ref, (_, place) in zip(refs, ins):
            if place == FAR:
                buffer, sem = spare.pop(0), spare.pop(0)
                operands.append(Loaded(buffer, pltpu.make_async_copy(ref, buffer, sem)))
            else:
                operands.append(Loaded(ref) if place == NEAR else ref)
        for ref, (_, _, place) in zip(refs[ends[0]:], outs):
            if place == FAR:
                buffer, sem = spare.pop(0), spare.pop(0)
                results.append(Stored(buffer, pltpu.make_async_copy(buffer, ref, sem)))
            else:
                results.append(ref)
        kernel(*operands[:len(ins) - len(after)], *results, *refs[ends[2]:])
        far = [result for result in results if isinstance(result, Stored)]
        for result in far:
            result.send()
        for result in far:
            result.copy.wait()

    return pl.pallas_call(
        run,
        out_shape=[SPACES[p](s, d) if p != NEAR else jax.ShapeDtypeStruct(s, d)
                   for s, d, p in outs],
        in_specs=[pl.BlockSpec(memory_space=SPACES[p]) for _, p in ins],
        out_specs=[pl.BlockSpec(memory_space=SPACES[p]) for _, _, p in outs],
        scratch_shapes=buffers + list(scratch),
        input_output_aliases=aliases or {},
        cost_estimate=pl.CostEstimate(
            flops=int(time * 1e9), bytes_accessed=int(time * 3.5e6), transcendentals=0),
        compiler_params=pltpu.CompilerParams(vmem_limit_bytes=limit * 1024 * 1024),
    )(*[pltpu.with_memory_space_constraint(a, pltpu.HBM) if p in (FAR, RAW) else a
        for a, p in ins])


def tile_row(table):
    row = table.get()[pl.ds(lax.axis_index("tile"), 1), :]
    return [row[0, d] for d in range(8)]


def dot(a, b):
    return lax.dot_general(a, b, (((1,), (0,)), ((), ())), preferred_element_type=F32)


def dot_nt(a, b):
    return lax.dot_general(a, b, (((1,), (1,)), ((), ())), preferred_element_type=F32)


def one_hot(index, rows):
    row = lax.broadcasted_iota(jnp.int32, (rows, index.shape[1]), 0)
    return jnp.where(row == index, 1.0, 0.0).astype(BF16)


def rim_pixels(edge):
    band_len = HALO * edge
    lane = lax.broadcasted_iota(jnp.int32, (1, 4 * band_len), 1)
    band, at = lane // band_len, lane % band_len
    side = (at // HALO) * edge + at % HALO
    pixel = jnp.where(band == 0, at, (edge - HALO) * edge + at)
    return jnp.where(band == 2, side, jnp.where(band == 3, side + edge - HALO, pixel))


def rim_lane(row, col, edge):
    band_len = HALO * edge
    side = jnp.where(col < HALO, 2 * band_len + row * HALO + col,
                     3 * band_len + row * HALO + col - (edge - HALO))
    side = jnp.where(row >= edge - HALO, band_len + (row - (edge - HALO)) * edge + col, side)
    return jnp.where(row < HALO, row * edge + col, side)


def turned_lane(row, col, quarter, edge):
    last = edge - 1
    from_row = jnp.where(quarter == 1, col, jnp.where(
        quarter == 2, last - row, jnp.where(quarter == 3, last - col, row)))
    from_col = jnp.where(quarter == 1, last - row, jnp.where(
        quarter == 2, last - col, jnp.where(quarter == 3, row, col)))
    return rim_lane(from_row, from_col, edge)


def row_halo_maps(top_turn, bottom_turn, edge):
    rim = 4 * HALO * edge
    lane = lax.broadcasted_iota(jnp.int32, (1, LANES), 1)
    up = lane - (LANES - HALO * edge)
    top = turned_lane(edge - HALO + up // edge, up % edge, top_turn, edge)
    low = turned_lane(lane // edge, lane % edge, bottom_turn, edge)
    top = jnp.where(up >= 0, top, -1)
    low = jnp.where(lane < HALO * edge, low, -1)
    return one_hot(top, rim), one_hot(low, rim)


def side_map(turns, edge):
    rim = 4 * HALO * edge
    lane = lax.broadcasted_iota(jnp.int32, (1, 2 * LANES), 1)
    row, k = lane // (2 * HALO), lane % (2 * HALO)
    above, below, right = row < HALO, row >= HALO + edge, k >= HALO
    b_row = jnp.where(above, edge - HALO + row, jnp.where(below, row - HALO - edge, row - HALO))
    b_col = jnp.where(right, k - HALO, edge - HALO + k)
    slot = jnp.where(above, 0, jnp.where(below, 4, 2)) + right.astype(jnp.int32)
    quarter = jnp.zeros_like(slot)
    for position in range(len(SIDES)):
        quarter = jnp.where(slot == position, turns[position], quarter)
    index = turned_lane(b_row, b_col, quarter, edge)
    index = jnp.where(row < edge + 2 * HALO, index, -1)
    return one_hot(index, rim), slot


def spread_map(edge, wide):
    lane = lax.broadcasted_iota(jnp.int32, (1, wide), 1)
    row = lane // edge - (LANES // edge - HALO)
    col = lane % edge
    right_row, left_row = row - 1, row + 1
    rows = edge + 2 * HALO
    right = jnp.where((right_row >= 0) & (right_row < rows), right_row * 2 * HALO + HALO + col, -1)
    left = jnp.where((left_row >= 0) & (left_row < rows),
                     left_row * 2 * HALO + col - (edge - HALO), -1)
    index = jnp.where(col < HALO, right, jnp.where(col >= edge - HALO, left, -1))
    return one_hot(index, 2 * LANES)


def side_mask(shift, shape, edge):
    col = lax.broadcasted_iota(jnp.int32, shape, 1) % edge
    return col < shift if shift > 0 else col >= edge + shift


def roll(values, shift):
    size = values.shape[1]
    return values if shift % size == 0 else pltpu.roll(values, shift % size, axis=1)


def pack_kernel(edge, x, rims, rim, sems):
    pick = one_hot(rim_pixels(edge), edge * edge)
    rim[...] = dot(x.get()[...], pick).astype(BF16)
    copies = [pltpu.make_async_copy(rim, rims.at[t], sems.at[t]) for t in range(rims.shape[0])]
    for copy in copies:
        copy.start()
    for copy in copies:
        copy.wait()


def shifted(values, shift, edge):
    if not shift:
        return values
    return roll(jnp.where(side_mask(shift, values.shape, edge), 0.0, values), -shift)


def tap_rows_of(taps_ref, at):
    return [taps_ref[tap, pl.ds(at, 16), :].astype(F32) for tap in range(KSIZE * KSIZE)]


def center_conv(edge, x_ref, taps_ref, out_ref):
    channels, pixels = x_ref.shape
    wide = pixels + 2 * LANES

    def block(i, carry):
        at = pl.multiple_of(i * 16, 16)
        xs = x_ref[pl.ds(at, 16), :].astype(F32)
        taps = tap_rows_of(taps_ref, at)
        zeros = jnp.zeros((8, LANES), F32)
        halves = []
        for half in (0, 8):
            x = jnp.concatenate([zeros, xs[half:half + 8], zeros], axis=1)
            sums = [None] * KSIZE
            for b in range(KSIZE):
                moved = shifted(x, b - HALO, edge)
                for a in range(KSIZE):
                    term = jnp.tile(taps[a * KSIZE + b][half:half + 8], (1, wide // LANES)) * moved
                    sums[a] = term if sums[a] is None else sums[a] + term
            total = None
            for a in range(KSIZE):
                part = roll(sums[a], -(a - HALO) * edge)[:, LANES:LANES + pixels]
                total = part if total is None else total + part
            halves.append(total)
        out_ref[pl.ds(at, 16), :] = jnp.concatenate(halves, axis=0)
        return carry

    lax.fori_loop(0, channels // 16, block, 0)


def row_terms(rows, taps, edge, below):
    lane = lax.broadcasted_iota(jnp.int32, rows.shape, 1)
    total = None
    for a in range(KSIZE):
        far = a - HALO if below else HALO - a
        if far <= 0:
            continue
        sums = None
        for b in range(KSIZE):
            term = taps[a * KSIZE + b] * shifted(rows, b - HALO, edge)
            sums = term if sums is None else sums + term
        if below:
            part = jnp.where(lane >= LANES - far * edge, roll(sums, LANES - far * edge), 0.0)
        else:
            part = jnp.where(lane < far * edge, roll(sums, far * edge - LANES), 0.0)
        total = part if total is None else total + part
    return total


def side_terms(packed, taps, edge):
    place = lax.broadcasted_iota(jnp.int32, packed.shape, 1) % (2 * HALO)
    beside = jnp.where(place == 0, roll(packed, -1), jnp.where(place == 3, roll(packed, 1), 0.0))
    total = None
    for a in range(KSIZE):
        def tap(b):
            return jnp.tile(taps[a * KSIZE + b], (1, packed.shape[1] // LANES))

        terms = (jnp.where(place < HALO, tap(0), tap(4)) * packed
                 + jnp.where(place == 0, tap(1), tap(3)) * beside)
        part = roll(terms, -a * 2 * HALO)[:, :2 * HALO * edge]
        total = part if total is None else total + part
    return total


def column_map(edge):
    pixel = lax.broadcasted_iota(jnp.int32, (1, edge * edge), 1)
    row, col = pixel // edge, pixel % edge
    index = jnp.where(col < HALO, row * 2 * HALO + col, row * 2 * HALO + col - (edge - 2 * HALO))
    return one_hot(jnp.where((col < HALO) | (col >= edge - HALO), index, -1), 2 * HALO * edge)


def conv_kernel(edge, neighbours, top, low, pick, slot, columns, center, rims, taps,
                hidden_ref, halo, gathered, sides):
    rims_ref, taps_ref, halo_ref = rims.get(), taps.get(), halo.ref
    channels, pixels = hidden_ref.shape
    tiles = rims_ref.shape[0]
    nb = [lax.rem(tile + tiles - first_tile(tiles), tiles) for tile in tile_row(neighbours)]
    halo_ref[:, :LANES] = dot(rims_ref[nb[1]], top.get()[...]).astype(BF16)
    halo_ref[:, LANES:2 * LANES] = dot(rims_ref[nb[6]], low.get()[...]).astype(BF16)
    for position, d in enumerate(SIDES):
        gathered[position * channels:(position + 1) * channels, :] = rims_ref[nb[d]]
    candidates, slot = dot(gathered[...], pick.get()[...]), slot.get()[...]
    packed = candidates[:channels, :]
    for position in range(1, len(SIDES)):
        packed = jnp.where(slot == position,
                           candidates[position * channels:(position + 1) * channels, :], packed)
    halo_ref[:, 2 * LANES:] = packed.astype(BF16)
    halo.send()
    center = center.get()
    ends = []
    for at in range(0, channels, 16):
        halos = halo_ref[at:at + 16, :].astype(F32)
        taps_of = tap_rows_of(taps_ref, at)
        ends.append((row_terms(halos[:, :LANES], taps_of, edge, False),
                     row_terms(halos[:, LANES:2 * LANES], taps_of, edge, True)))
        sides[at:at + 16, :] = side_terms(halos[:, 2 * LANES:], taps_of, edge)
    high = sides[...].astype(BF16)
    low = (sides[...] - high.astype(F32)).astype(BF16)
    columns = columns.get()[...]
    hidden = center[...] + dot(high, columns) + dot(low, columns)
    hidden_ref[:, LANES:pixels - LANES] = hidden[:, LANES:pixels - LANES].astype(BF16)
    first = jnp.concatenate([end[0] for end in ends], axis=0)
    last = jnp.concatenate([end[1] for end in ends], axis=0)
    hidden_ref[:, :LANES] = (hidden[:, :LANES] + first).astype(BF16)
    hidden_ref[:, pixels - LANES:] = (hidden[:, pixels - LANES:] + last).astype(BF16)


def normal_below(values):
    return 0.5 * (1.0 + lax.erf(values * 0.7071067811865476))


def gelu_slope(values, below):
    return below + values * jnp.exp(-0.5 * values * values) * 0.3989422804014327


def column_steps(ref):
    return [slice(at, at + 2 * LANES) for at in range(0, ref.shape[1], 2 * LANES)]


def over_units(units, block, body):
    def step(i, carry):
        body(pl.ds(pl.multiple_of(i * block, block), block))
        return carry

    lax.fori_loop(0, units // block, step, 0)


def weight_kernel(feats, cots, w_in_t, w_out, part, gpre, act, stack, sems):
    feats, cots = feats.get(), cots.get()
    full, units = feats.shape[0], act.shape[0]
    w_in_t, w_out = w_in_t.get()[...], w_out.get()[...]
    for part_of in column_steps(feats):
        pre = dot(w_in_t, feats[:, part_of])
        below = normal_below(pre)
        act[:, part_of] = (pre * below).astype(BF16)
        slope = gelu_slope(pre, below)
        gpre[:, part_of] = (dot(w_out, cots[:, part_of]) * slope).astype(BF16)
    used, copies = 0, []
    for values, height in ((dot_nt(feats[...], gpre[...]), full),
                           (dot_nt(act[...], cots[...]), units)):
        first = used
        for column in range(0, values.shape[1], LANES):
            stack[used:used + height, :] = values[:, column:column + LANES].astype(BF16)
            used += height
        copies.append(pltpu.make_async_copy(
            stack.at[first:used], part.at[first:used], sems.at[len(copies)]))
        copies[-1].start()
    if used < part.shape[0]:
        stack[used:, :] = jnp.zeros((part.shape[0] - used, LANES), BF16)
        copies.append(pltpu.make_async_copy(stack.at[used:], part.at[used:], sems.at[2]))
        copies[-1].start()
    for copy in copies:
        copy.wait()


def out_kernel(block, feats, w_in_t, w_out, x, out, act):
    feats, w_in_t, w_out = feats.get(), w_in_t.get(), w_out.get()

    def units(rows):
        for part_of in column_steps(feats):
            pre = dot(w_in_t[rows, :], feats[:, part_of])
            act[rows, part_of] = (pre * normal_below(pre)).astype(BF16)

    over_units(w_out.shape[0], block, units)
    channels = out.ref.shape[0]
    row = lax.broadcasted_iota(jnp.int32, (channels, w_out.shape[1]), 0)
    column = lax.broadcasted_iota(jnp.int32, (channels, w_out.shape[1]), 1)
    pick = jnp.where(column == row + lax.axis_index("chan") * channels, 1.0, 0.0).astype(BF16)
    branch = dot(dot_nt(pick, w_out[...]).astype(BF16), act[...])
    out.ref[...] = (x.get()[...].astype(F32) + branch.astype(BF16).astype(F32)).astype(BF16)


def back_kernel(edge, groups, tiles, feats, cots, w_in, w_in_t, w_out, gpre_own, x, halo, spread, cot,
                neighbours, rotations, taps, accum_ref, tap_ref, *refs):
    outs, (gpre, grad_ref, padded_ref, side_ref, turned_all, moved_all, d_row, d_side, gathered) = (
        refs[:-9], refs[-9:])
    channels, pixels = grad_ref.shape
    feats, cots, w_in_t, w_out = feats.get(), cots.get(), w_in_t.get(), w_out.get()

    chan, units = lax.axis_index("chan"), gpre_own.ref.shape[0]

    def others(k, carry):
        rows = pl.ds(pl.multiple_of((chan ^ k) * units, units), units)
        for part_of in column_steps(feats):
            pre = dot(w_in_t[rows, :], feats[:, part_of])
            slope = gelu_slope(pre, normal_below(pre))
            gpre[rows, part_of] = (dot(w_out[rows, :], cots[:, part_of]) * slope).astype(BF16)
        return carry

    lax.fori_loop(1, groups, others, 0)
    gpre[pl.ds(pl.multiple_of(chan * units, units), units), :] = gpre_own.get()[...]
    own = pl.ds(pl.multiple_of(lax.axis_index("chan") * channels, channels), channels)
    grad_ref[...] = dot(w_in.get()[own, :], gpre[...]).astype(BF16)
    halo = halo.get()
    padded_ref[:, :LANES] = halo[:, :LANES]
    padded_ref[:, LANES:LANES + pixels] = x.get()[...]
    padded_ref[:, LANES + pixels:] = halo[:, LANES:2 * LANES]
    spread = spread.get()[...]
    side_ref[...] = dot(halo[:, 2 * LANES:], spread).astype(BF16)
    tap_terms(edge, grad_ref, padded_ref, side_ref, tap_ref, turned_all, moved_all)
    halo_adjoint(edge, neighbours, rotations, spread, grad_ref, taps.get(), cot.get(), accum_ref,
                 outs, d_row, d_side, gathered)


def prep_kernel(edge, w_in, x, neighbours, rotations, taps, w_in_t_ref, center_ref, nb_ref,
                top_ref, low_ref, pick_ref, slot_ref, columns_ref, spread):
    nb_ref[...] = neighbours.get()[...]
    rot = tile_row(rotations)
    pick, slot = side_map([rot[d] for d in SIDES], edge)
    spread.ref[...] = spread_map(edge, edge * edge + 2 * LANES)
    spread.send()
    top_ref[...], low_ref[...] = row_halo_maps(rot[1], rot[6], edge)
    pick_ref[...], slot_ref[...], columns_ref[...] = pick, slot, column_map(edge)
    w_in_t_ref[...] = w_in.get()[...].astype(F32).T.astype(BF16)
    center_conv(edge, x.get(), taps.get(), center_ref)


def join_kernel(w_in_t, w_out, *refs):
    pieces, (out_ref, part_in_ref, part_out_ref) = refs[:-3], refs[-3:]
    chan = lax.axis_index("chan")
    for k, piece in enumerate(pieces):
        piece = piece.get()
        channels = piece.shape[0]
        start = pl.multiple_of((chan ^ k) * channels, channels)
        out_ref[pl.ds(start, channels), :] = piece[...]
    units = part_in_ref.shape[0]
    mine = pl.ds(pl.multiple_of(chan * units, units), units)
    part_in_ref[...] = w_in_t.get()[mine, :]
    part_out_ref[...] = w_out.get()[mine, :]


def tap_terms(edge, grad_ref, padded_ref, side_ref, tap_ref, turned_all, moved_all):
    channels, pixels = grad_ref.shape
    wide = pixels + 2 * LANES
    moved_all[KSIZE * 16:, :] = jnp.zeros((LANES - KSIZE * 16, wide), BF16)
    same = (lax.broadcasted_iota(jnp.int32, (16, KSIZE * LANES), 1) % 16
            == lax.broadcasted_iota(jnp.int32, (16, KSIZE * LANES), 0))
    line = lax.broadcasted_iota(jnp.int32, (KSIZE * LANES, LANES), 0)
    tap = lax.broadcasted_iota(jnp.int32, (KSIZE * LANES, LANES), 1)
    used = line % LANES < KSIZE * 16
    pick = jnp.where(used & (line // LANES * KSIZE + line % LANES // 16 == tap), 1.0, 0.0).astype(BF16)
    mask = {b: side_mask(b - HALO, (16, wide), edge) for b in range(KSIZE) if b != HALO}
    lane = lax.broadcasted_iota(jnp.int32, (16, LANES), 1)
    zeros = jnp.zeros((16, LANES), F32)
    found = []
    for at in range(0, channels, 16):
        g = jnp.concatenate([zeros, grad_ref[at:at + 16, :].astype(F32), zeros], axis=1)
        x = padded_ref[at:at + 16, :].astype(F32)
        h = side_ref[at:at + 16, :].astype(F32)
        for a in range(KSIZE):
            shift = a - HALO
            turned_all[a * 16:a * 16 + 16, :] = roll(g, shift * edge).astype(BF16)
            moved = roll(jnp.where(mask[a], h, x), -shift) if shift else x
            moved_all[a * 16:a * 16 + 16, :] = moved.astype(BF16)
        products = dot_nt(turned_all[...], moved_all[...])
        side_by_side = jnp.concatenate(
            [products[a * 16:a * 16 + 16, :] for a in range(KSIZE)], axis=1)
        taps = dot(jnp.where(same, side_by_side, 0.0).astype(BF16), pick)
        place = at // 16 % 4
        taps = jnp.where(lane // 32 == place, roll(taps, 32 * place), 0.0)
        if place == 0:
            found.append(taps)
        else:
            found[-1] = found[-1] + taps
    tap_ref[...] = jnp.concatenate(found, axis=0).astype(BF16)


def halo_adjoint(edge, neighbours, rotations, spread, grad_ref, taps_ref, cot_ref, accum_ref, outs,
                 d_row, d_side, gathered):
    channels, pixels = grad_ref.shape
    wide = pixels + 2 * LANES
    tiles = gathered.shape[0]

    def block(i, carry):
        at = pl.multiple_of(i * 16, 16)
        gs = grad_ref[pl.ds(at, 16), :].astype(F32)
        taps_of = [taps_ref[tap, pl.ds(at, 16), :].astype(F32) for tap in range(KSIZE * KSIZE)]
        zeros = jnp.zeros((8, LANES), F32)
        rows, sides = [], []
        for half in (0, 8):
            g = jnp.concatenate([zeros, gs[half:half + 8], zeros], axis=1)
            turned = [roll(g, (a - HALO) * edge) for a in range(KSIZE)]
            d_x = d_h = None
            for b in range(KSIZE):
                shift = b - HALO
                back = None
                for a in range(KSIZE):
                    weight = taps_of[a * KSIZE + b][half:half + 8]
                    term = jnp.tile(weight, (1, wide // LANES)) * turned[a]
                    back = term if back is None else back + term
                back = roll(back, shift)
                if shift:
                    mask = side_mask(shift, back.shape, edge)
                    inside = jnp.where(mask, 0.0, back)
                    outside = jnp.where(mask, back, 0.0)
                    d_h = outside if d_h is None else d_h + outside
                    d_x = inside if d_x is None else d_x + inside
                else:
                    d_x = back if d_x is None else d_x + back
            rows.append(d_x)
            sides.append(d_h)
        d_x = jnp.concatenate(rows, axis=0)
        accum_ref[pl.ds(at, 16), :] = d_x[:, LANES:LANES + pixels]
        d_row[pl.ds(at, 16), :LANES] = d_x[:, :LANES].astype(BF16)
        d_row[pl.ds(at, 16), LANES:] = d_x[:, LANES + pixels:].astype(BF16)
        d_side[pl.ds(at, 16), :] = jnp.concatenate(sides, axis=0).astype(BF16)
        return carry

    lax.fori_loop(0, channels // 16, block, 0)
    accum_ref[...] += cot_ref[...].astype(F32)
    nb, rot = tile_row(neighbours), tile_row(rotations)
    gathered[...] = jnp.zeros(gathered.shape, F32)
    top, low = row_halo_maps(rot[1], rot[6], edge)
    gathered[slot_of(nb[1], tiles)] += dot_nt(d_row[:, :LANES], top)
    gathered[slot_of(nb[6], tiles)] += dot_nt(d_row[:, LANES:], low)
    packed = dot_nt(d_side[...], spread)
    pick, slot = side_map([rot[d] for d in SIDES], edge)
    own = jnp.concatenate(
        [jnp.where(slot == position, packed, 0.0) for position in range(len(SIDES))], axis=0)
    placed = dot_nt(own.astype(BF16), pick)
    for position, d in enumerate(SIDES):
        gathered[slot_of(nb[d], tiles)] += placed[position * channels:(position + 1) * channels, :]
    store_parts(gathered, outs)


def store_parts(values, outs):
    for part, out in enumerate(outs):
        out = out.ref if isinstance(out, Stored) else out
        rows = out.shape[0]

        def store(t, carry, out=out, first=part * rows):
            out[t] = values[first + t].astype(BF16)
            return carry

        lax.fori_loop(0, rows, store, 0)


def halves(tiles):
    return tiles > 1 and tiles & (tiles - 1) == 0


def slot_of(tile, tiles):
    if not halves(tiles):
        return tile
    apart, slot = tile ^ lax.axis_index("tile"), 0
    for bit in halving_bits(tiles):
        slot = slot * 2 + jnp.where(apart & bit != 0, 1, 0)
    return slot


def halving_bits(tiles):
    bits = [1 << i for i in range(tiles.bit_length() - 1)]
    return bits[1:2] + bits[:1] + bits[2:]


def pair_kernel(kept, other, *refs):
    outs, total = refs[:-1], refs[-1]
    total[...] = kept.get()[...].astype(F32) + other.get()[...].astype(F32)
    store_parts(total, outs)


def border_kernel(edge, accum, *refs):
    parts, grad_ref = refs[:-1], refs[-1]
    rims = None
    for part in parts:
        more = total_of(part.get())
        rims = more if rims is None else rims + more
    high = rims.astype(BF16)
    low = (rims - high.astype(F32)).astype(BF16)
    pick = one_hot(rim_pixels(edge), edge * edge)
    added = dot_nt(high, pick) + dot_nt(low, pick)
    grad_ref[...] = (accum.get()[...] + added).astype(BF16)


def total_of(ref):
    return lax.fori_loop(1, ref.shape[0], lambda t, so_far: so_far + ref[t].astype(F32),
                         ref[0].astype(F32))


def sum_kernel(recv, tap, out, total, sems):
    recv = recv.get()
    share = recv.shape[1]
    total[:share, :] = total_of(recv).astype(BF16)
    total[share:, :] = tap.get()[...]
    copies = [pltpu.make_async_copy(total, out.at[t], sems.at[t]) for t in range(out.shape[0])]
    for copy in copies:
        copy.start()
    for copy in copies:
        copy.wait()


def compact_kernel(share, values, out):
    values = values.get()
    tiles, rows, _ = values.shape
    for tile in range(tiles):
        out[tile * share:(tile + 1) * share, :] = values[tile, :share, :]
    taps = values[0, share:, :].astype(F32)
    for tile in range(1, tiles):
        taps = taps + values[tile, share:, :].astype(F32)
    out[tiles * share:, :] = taps.astype(BF16)


def final_kernel(which, channels, tap_rows, scale, last, *refs):
    pieces, taps_in = refs[:len(which)], refs[len(which)]
    copies = []
    if last:
        g_in, g_out, g_tap_ref, buf_in, buf_out, sems = refs[-6:]
    else:
        g_in, g_out, g_tap_ref, copied, buf_in, buf_out, sems = refs[-7:]
        copies.append(pltpu.make_async_copy(refs[len(which) + 1].get(), copied, sems.at[0]))
        copies[0].start()
    full, units = buf_in.shape[1:]
    all_taps = taps_in.get()[...]
    row_of = lax.broadcasted_iota(jnp.int32, (full, LANES), 0)
    for i, k in enumerate(which):
        piece = pieces[i].get()
        owner = lax.axis_index("chan") ^ k
        start = pl.multiple_of(owner * units, units)
        used = 0
        for buffer, target in ((buf_in, g_in.at[:, pl.ds(start, units)]),
                               (buf_out, g_out.at[pl.ds(start, units)])):
            height, width = buffer.shape[1:]
            for column in range(0, width, LANES):
                buffer[i, :, column:column + LANES] = piece[used:used + height, :].astype(F32) * scale
                used += height
            copies.append(pltpu.make_async_copy(buffer.at[i], target, sems.at[len(copies)]))
            copies[-1].start()
        taps = piece[piece.shape[0] - tap_rows:, :].astype(F32)
        blocks = []
        for block in range(channels // 16):
            values = taps[block // 4 * 16:block // 4 * 16 + 16, :]
            blocks.append(roll(values, -32 * (block % 4)))
        own = jnp.concatenate(blocks * (full // channels), axis=0)
        all_taps = jnp.where(row_of // channels == owner, own, all_taps)
    if last:
        g_tap_ref.ref[...] = all_taps.T[:KSIZE * KSIZE, :] * scale
        g_tap_ref.send()
    else:
        g_tap_ref[...] = all_taps
    for copy in copies:
        copy.wait()


def swap_chan(values, bit):
    return lax.ppermute(values, "chan", [(i, i ^ bit) for i in range(lax.axis_size("chan"))])


def gather_pieces(own, groups):
    pieces = {0: own}
    bit = groups // 2
    while bit:
        for k in list(pieces):
            pieces[k ^ bit] = swap_chan(pieces[k], bit)
        bit //= 2
    return [pieces[k] for k in range(groups)]


def first_tile(tiles):
    return tiles // 2


def swap_rows(values):
    tiles = lax.axis_size("tile")
    group = [(first_tile(tiles) + i) % tiles for i in range(tiles)]
    return lax.all_to_all(values, "tile", 0, 0, tiled=True, axis_index_groups=[group])


def halve(parts, bit, after):
    kept, given = parts
    half = ((kept.shape[0] // 2, *kept.shape[1:]), BF16, NEAR)
    return call(pair_kernel, [(kept, NEAR), (swap_bit(given, bit), NEAR)], [half] * 2,
                [pltpu.VMEM(kept.shape, F32)], time=0.3, after=after)


def swap_bit(values, bit):
    return lax.ppermute(values, "tile", [(t, t ^ bit) for t in range(lax.axis_size("tile"))])


def body(inputs, grad_out, kernel, w_in, w_out, neighbours, rotations):
    channels, pixels = inputs.shape[1:]
    edge = math.isqrt(pixels)
    full, hidden = w_in.shape
    groups = lax.axis_size("chan")
    tiles = lax.axis_size("tile")
    wide = pixels + 2 * LANES
    rim = 4 * HALO * edge
    units = hidden // groups
    scale = (tiles * pixels) ** -0.5
    x, cot = inputs[0], grad_out[0]

    [rims] = call(functools.partial(pack_kernel, edge), [(x, FAR)],
                  [((tiles, channels, rim), BF16, RAW)],
                  [pltpu.VMEM((channels, rim), BF16), pltpu.SemaphoreType.DMA((tiles,))])
    _, kernel = lax.optimization_barrier((rims, kernel))
    taps = jnp.broadcast_to(kernel[:, :, None], (KSIZE * KSIZE, channels, LANES))
    cot_pieces = gather_pieces(cot, groups)
    table = neighbours.shape
    w_in_t, center, nb_near, *maps = call(
        functools.partial(prep_kernel, edge),
        [(w_in, NEAR), (x, FAR), (neighbours, NEAR), (rotations, NEAR), (taps, NEAR)],
        [((hidden, full), BF16, NEAR), ((channels, pixels), F32, NEAR),
         (neighbours.shape, jnp.int32, NEAR), ((rim, LANES), BF16, NEAR), ((rim, LANES), BF16, NEAR),
         ((rim, 2 * LANES), BF16, NEAR), ((1, 2 * LANES), jnp.int32, NEAR),
         ((2 * HALO * edge, pixels), BF16, NEAR), ((2 * LANES, wide), BF16, FAR)], time=2.0,
        after=[(rims, RAW)])
    spread = maps.pop()
    rims = swap_rows(rims)

    hid, halo = call(
        functools.partial(conv_kernel, edge),
        [(a, NEAR) for a in (nb_near, *maps, center, rims, taps)],
        [((channels, pixels), BF16, NEAR), ((channels, 4 * LANES), BF16, FAR)],
        [pltpu.VMEM((len(SIDES) * channels, rim), BF16),
         pltpu.VMEM((channels, 2 * HALO * edge), F32)], time=1.0, after=[(w_in_t, NEAR)])
    feats = lax.all_gather(hid, "chan", axis=0, tiled=True)
    cots, part_in, part_out = call(
        join_kernel, [(w_in_t, NEAR), (w_out, NEAR)] + [(piece, NEAR) for piece in cot_pieces],
        [((full, pixels), BF16, NEAR)] + [((units, full), BF16, NEAR)] * 2, time=0.6,
        after=[(feats, NEAR)])

    used = 2 * full * units // LANES
    share = -(-used // (16 * tiles)) * 16
    tap_rows = -(-channels // 64) * 16
    block = 2 * LANES
    part, gpre = call(
        weight_kernel,
        [(feats, NEAR), (cots, NEAR), (part_in, NEAR), (part_out, NEAR)],
        [((tiles * share, LANES), BF16, RAW), ((units, pixels), BF16, NEAR)],
        [pltpu.VMEM((units, pixels), BF16)]
        + [pltpu.VMEM((tiles * share, LANES), BF16), pltpu.SemaphoreType.DMA((3,))],
        time=2.2)
    part = swap_rows(part.reshape(tiles, share, LANES))

    parts = 2 if halves(tiles) else 1
    placed = ((tiles // parts, channels, rim), BF16, NEAR if parts > 1 else FAR)
    accum, tap_part, *border = call(
        functools.partial(back_kernel, edge, groups, tiles),
        [(feats, NEAR), (cots, NEAR), (w_in, FAR), (w_in_t, NEAR), (w_out, NEAR), (gpre, FAR), (x, FAR),
         (halo, FAR), (spread, FAR), (cot, FAR), (neighbours, NEAR), (rotations, NEAR), (taps, NEAR)],
        [((channels, pixels), F32, NEAR), ((tap_rows, LANES), BF16, NEAR)] + [placed] * parts,
        [pltpu.VMEM((hidden, pixels), BF16), pltpu.VMEM((channels, pixels), BF16),
         pltpu.VMEM((channels, wide), BF16), pltpu.VMEM((channels, wide), BF16),
         pltpu.VMEM((KSIZE * 16, wide), BF16), pltpu.VMEM((LANES, wide), BF16),
         pltpu.VMEM((channels, 2 * LANES), BF16), pltpu.VMEM((channels, wide), BF16),
         pltpu.VMEM((tiles, channels, rim), F32)], time=7.5, limit=32)
    [mine] = call(sum_kernel, [(part, NEAR), (tap_part, NEAR)],
                  [((tiles, share + tap_rows, LANES), BF16, RAW)],
                  [pltpu.VMEM((share + tap_rows, LANES), BF16), pltpu.SemaphoreType.DMA((tiles,))])
    [weights] = call(functools.partial(compact_kernel, share), [(swap_rows(mine), NEAR)],
                     [((tiles * share + tap_rows, LANES), BF16, NEAR)], time=0.1)

    [outputs] = call(
        functools.partial(out_kernel, block),
        [(feats, NEAR), (w_in_t, NEAR), (w_out, NEAR), (x, FAR)], [((channels, pixels), BF16, FAR)],
        [pltpu.VMEM((hidden, pixels), BF16)], time=4.0, limit=32, after=[(mine, RAW)])
    bits = halving_bits(tiles) if parts > 1 else [0]
    for step, bit in enumerate(bits[:-1]):
        border = halve(border, bit, [(outputs, RAW)] if step else [])
    weights, outputs, *border = lax.optimization_barrier((weights, outputs, *border))
    border = [border[0], swap_bit(border[1], bits[-1])] if parts > 1 else [
        lax.all_to_all(border[0], "tile", 0, 0, tiled=True)]
    [grad_in] = call(functools.partial(border_kernel, edge),
                     [(accum, NEAR)] + [(part, NEAR) for part in border],
                     [((channels, pixels), BF16, PINNED)])

    def place(which, taps_so_far, more, last):
        tap_shape = (KSIZE * KSIZE, full) if last else (full, LANES)
        copied = [] if last else [(more[0][0].shape, more[0][0].dtype, RAW)]
        return call(
            functools.partial(final_kernel, which, channels, tap_rows, scale, last),
            [(pieces[k], NEAR) for k in which] + [(taps_so_far, NEAR)] + more,
            [((full, hidden), F32, RAW), ((hidden, full), F32, RAW), (tap_shape, F32, FAR if last else NEAR)]
            + copied,
            [pltpu.VMEM((len(which), full, units), F32), pltpu.VMEM((len(which), units, full), F32),
             pltpu.SemaphoreType.DMA((2 * len(which) + 1,))],
            time=1.2, aliases={1 + len(which): 0, 2 + len(which): 1} if last else None)

    pieces = {0: weights}
    bit = groups // 2
    while bit > 1:
        for k in [k for k in pieces if k % 2 == 0]:
            pieces[k ^ bit] = swap_chan(pieces[k], bit)
        bit //= 2
    pieces[1] = swap_chan(weights, 1)
    even, odd = list(range(2, groups, 2)), list(range(3, groups, 2))
    for k in even:
        pieces[k], grad_in = lax.optimization_barrier((pieces[k], grad_in))
    for k in odd:
        pieces[k] = swap_chan(pieces[k ^ 1], 1)
    g_in, g_out, taps_so_far, grad_in = place(
        [0, 1, *even], jnp.zeros((full, LANES), F32), [(grad_in, NEAR)], False)
    grads = place(odd, taps_so_far, [(g_in, RAW), (g_out, RAW)], True)
    return (outputs[None], grad_in[None], *grads)


def solution(mesh):
    return jax.shard_map(
        body,
        mesh=mesh,
        in_specs=(
            P("tile", "chan", None),
            P("tile", "chan", None),
            P(None, "chan"),
            P(),
            P(),
            P(),
            P(),
        ),
        out_specs=(P("tile", "chan", None), P("tile", "chan", None), P(), P(), P()),
        check_vma=False,
    )
```
